32 devices in a mesh: dp: 8 (over y, x, core), seq: 4 (over z).
Axes of the slice: x: 2, y: 2, z: 4, core: 2. Of those that a mesh axis runs over, the one named last changes fastest.
Arguments:
- features: bfloat16 [8, 512, 1024], P('dp', 'seq'), may hold values from -6 to 6
- utterance_ends: int32 [8, 4], P('dp'), may hold values from 64 to 512, as said below
- kernel_weight: bfloat16 [1024, 8192], P(('dp', 'seq')), may hold values from -0.0625 to 0.0625
- position_bias: bfloat16 [1024], P(('dp', 'seq')), may hold values from -1.75 to 1.75
- entry_gain: bfloat16 [1024], P(('dp', 'seq')), may hold values from 0.5 to 1.5
- base_shift: bfloat16 [1024], P(('dp', 'seq')), may hold values from -1.25 to 1.25
- joint_weight: bfloat16 [2, 1024, 3072], P(None, ('dp', 'seq')), may hold values from -0.1875 to 0.1875
- query_bias: bfloat16 [2, 1024], P(None, ('dp', 'seq')), may hold values from -3 to 3
- value_bias: bfloat16 [2, 1024], P(None, ('dp', 'seq')), may hold values from -1.75 to 1.75
- output_weight: bfloat16 [2, 1024, 1024], P(None, ('dp', 'seq')), may hold values from -3 to 3
- attend_bias: bfloat16 [2, 1024], P(None, ('dp', 'seq')), may hold values from -1.75 to 1.75
- middle_gain: bfloat16 [2, 1024], P(None, ('dp', 'seq')), may hold values from 0.5 to 1.5
- lower_shift: bfloat16 [2, 1024], P(None, ('dp', 'seq')), may hold values from -1.25 to 1.25
- expand_weight: bfloat16 [2, 1024, 4096], P(None, ('dp', 'seq')), may hold values from -0.1875 to 0.1875
- hidden_bias: bfloat16 [2, 4096], P(None, ('dp', 'seq')), may hold values from -1.75 to 1.75
- reduce_weight: bfloat16 [2, 4096, 1024], P(None, ('dp', 'seq')), may hold values from -0.09375 to 0.09375
- return_bias: bfloat16 [2, 1024], P(None, ('dp', 'seq')), may hold values from -1.75 to 1.75
- final_gain: bfloat16 [2, 1024], P(None, ('dp', 'seq')), may hold values from 0.5 to 1.5
- upper_shift: bfloat16 [2, 1024], P(None, ('dp', 'seq')), may hold values from -1.25 to 1.25
- head_weight: bfloat16 [1024, 32], P(('dp', 'seq')), may hold values from -0.1875 to 0.1875
- vocab_bias: bfloat16 [32], replicated, may hold values from -3 to 3
- cotangent: bfloat16 [8, 512, 32], P('dp', 'seq'), may hold values from -6 to 6
Outputs:
- logits: float32 [8, 512, 32], P('dp', 'seq')
- features_grad: float32 [8, 512, 1024], P('dp', 'seq')
- kernel_grad: float32 [1024, 8192], P(('dp', 'seq'))
- position_grad: float32 [1024], P(('dp', 'seq'))
- entry_grad: float32 [1024], P(('dp', 'seq'))
- base_grad: float32 [1024], P(('dp', 'seq'))
- joint_grad: float32 [2, 1024, 3072], P(None, ('dp', 'seq'))
- query_grad: float32 [2, 1024], P(None, ('dp', 'seq'))
- value_grad: float32 [2, 1024], P(None, ('dp', 'seq'))
- output_grad: float32 [2, 1024, 1024], P(None, ('dp', 'seq'))
- attend_grad: float32 [2, 1024], P(None, ('dp', 'seq'))
- middle_grad: float32 [2, 1024], P(None, ('dp', 'seq'))
- lower_grad: float32 [2, 1024], P(None, ('dp', 'seq'))
- expand_grad: float32 [2, 1024, 4096], P(None, ('dp', 'seq'))
- hidden_grad: float32 [2, 4096], P(None, ('dp', 'seq'))
- reduce_grad: float32 [2, 4096, 1024], P(None, ('dp', 'seq'))
- return_grad: float32 [2, 1024], P(None, ('dp', 'seq'))
- final_grad: float32 [2, 1024], P(None, ('dp', 'seq'))
- upper_grad: float32 [2, 1024], P(None, ('dp', 'seq'))
- head_grad: float32 [1024, 32], P(('dp', 'seq'))
- vocab_grad: float32 [32], replicated
The draws below stay inside these ranges and needn't reach their ends.
Inputs may be any that keep to these rules, and one draw needn't show every extreme that they name: The ends of a row never fall; utterance j holds the frames from utterance_ends[r, j - 1] (0 for j = 0) up to utterance_ends[r, j] - 1, so a repeated end is an empty slot; frames from utterance_ends[r, 3] on are padding, and one row is filled to its last frame. Each row holds one to three utterances, and in every row one utterance begins on the first device along seq and ends on the last.
All inputs are finite; a program needn't handle non-finite values.
Results may differ from the reference program's by a relative error of at most 0.017.
Values may be sent and summed in bfloat16 or wider, within the bound.
A program may use at most 640 MiB of HBM per device.

```python
import math
import jax
import jax.numpy as jnp
from jax import lax

D = 1024
HEADS = 16
FF = 4096
VOCAB = 32
CONV_K = 128
CONV_G = 16
LAYERS = 2
SEGS = 4
FR_DEV = 128
HEAD_DIM = 64
FRAMES = 512
ROWS = 8


def draw_utterance_ends(key, part):
    key = jax.random.fold_in(key, 11)
    subkeys = jax.random.split(key, 6)
    rows_at = jnp.arange(ROWS)
    has_lead = jax.random.randint(subkeys[0], (ROWS,), 0, 2)
    lead_len = jax.random.randint(subkeys[1], (ROWS,), FR_DEV // 2, FR_DEV)
    lead_row = jax.random.randint(subkeys[2], (), 0, ROWS)
    full_row = jax.random.randint(subkeys[3], (), 0, ROWS)
    has_lead = jnp.where(rows_at == lead_row, 1, has_lead)
    lead_len = jnp.where(rows_at == lead_row, FR_DEV // 2, lead_len)
    span_end = jax.random.randint(subkeys[4], (ROWS,), FRAMES - FR_DEV + 1, FRAMES + 1)
    tail_end = jax.random.randint(subkeys[5], (ROWS,), span_end, FRAMES + 1)
    tail_end = jnp.where(rows_at == full_row, FRAMES, tail_end)
    first_end = jnp.where(has_lead == 1, lead_len, span_end)
    second_end = jnp.where(has_lead == 1, span_end, tail_end)
    column = jnp.arange(SEGS)[None, :]
    result = jnp.where(column == 0, first_end[:, None], jnp.where(column == 1, second_end[:, None], tail_end[:, None]))
    return result.astype(jnp.int32)


def level_of(own_key, dims, shards, low, top_value):
    def one(position, shards_of):
        draws = jax.random.uniform(jax.random.fold_in(jax.random.fold_in(own_key, 6), position), (shards_of,), jnp.float32, low / len(shards), top_value / len(shards))
        return jnp.repeat(jnp.exp(draws), dims[position] // shards_of).reshape((-1,) + (1,) * (len(dims) - position - 1))

    gain = one(*shards[0])
    for cut in shards[1:]:
        gain = gain * one(*cut)
    return gain


def noise(stream_key, extent, width, most, cuts=(), kind=jnp.bfloat16):
    array = width * jax.random.normal(stream_key, extent, jnp.float32)
    if cuts:
        array = array * level_of(stream_key, extent, cuts, -0.22, 0.18)
    return jnp.clip(array, -most, most).astype(kind)


def setup_inputs(seed: int = 0) -> dict:
    arg_keys = jax.random.split(jax.random.key(seed), 23)
    return {
        "features": noise(arg_keys[0], (ROWS, FRAMES, D), 1.0, 6.0, ((0, 8), (1, 4))),
        "utterance_ends": draw_utterance_ends(jax.random.fold_in(arg_keys[22], 71), 0),
        "kernel_weight": noise(arg_keys[2], (D, CONV_K * (D // CONV_G)), (CONV_K * (D // CONV_G)) ** -0.5, 0.0625, ((0, 32),)),
        "position_bias": noise(arg_keys[3], (D,), 0.3, 1.75, ((0, 32),)),
        "entry_gain": jnp.clip(1.0 + 0.1 * jax.random.normal(arg_keys[4], (D,), jnp.float32), 0.5, 1.5).astype(jnp.bfloat16),
        "base_shift": noise(arg_keys[5], (D,), 0.2, 1.25, ((0, 32),)),
        "joint_weight": noise(arg_keys[6], (LAYERS, D, 3 * D), D ** -0.5, 0.1875, ((1, 32),)),
        "query_bias": noise(arg_keys[7], (LAYERS, D), 0.5, 3.0, ((1, 32),)),
        "value_bias": noise(arg_keys[8], (LAYERS, D), 0.3, 1.75, ((1, 32),)),
        "output_weight": noise(arg_keys[9], (LAYERS, D, D), (D // 256) ** -0.5, 3.0, ((1, 32),)),
        "attend_bias": noise(arg_keys[10], (LAYERS, D), 0.3, 1.75, ((1, 32),)),
        "middle_gain": jnp.clip(1.0 + 0.1 * jax.random.normal(arg_keys[11], (LAYERS, D), jnp.float32), 0.5, 1.5).astype(jnp.bfloat16),
        "lower_shift": noise(arg_keys[12], (LAYERS, D), 0.2, 1.25, ((1, 32),)),
        "expand_weight": noise(arg_keys[13], (LAYERS, D, FF), D ** -0.5, 0.1875, ((1, 32),)),
        "hidden_bias": noise(arg_keys[14], (LAYERS, FF), 0.3, 1.75, ((1, 32),)),
        "reduce_weight": noise(arg_keys[15], (LAYERS, FF, D), FF ** -0.5, 0.09375, ((1, 32),)),
        "return_bias": noise(arg_keys[16], (LAYERS, D), 0.3, 1.75, ((1, 32),)),
        "final_gain": jnp.clip(1.0 + 0.1 * jax.random.normal(arg_keys[17], (LAYERS, D), jnp.float32), 0.5, 1.5).astype(jnp.bfloat16),
        "upper_shift": noise(arg_keys[18], (LAYERS, D), 0.2, 1.25, ((1, 32),)),
        "head_weight": noise(arg_keys[19], (D, VOCAB), D ** -0.5, 0.1875, ((0, 32),)),
        "vocab_bias": noise(arg_keys[20], (VOCAB,), 0.5, 3.0),
        "cotangent": noise(arg_keys[21], (ROWS, FRAMES, VOCAB), 1.0, 6.0, ((0, 8), (1, 4))),
    }


@jax.custom_vjp
def low(v):
    return lax.optimization_barrier(v.astype(jnp.bfloat16)).astype(jnp.float32)

@jax.custom_vjp
def low_back(v):
    return v

def low_keep(v):
    return (low(v), None)

def low_pass(kept, grad):
    return (grad,)

def back_keep(v):
    return (v, None)

def back_low(kept, grad):
    return (low(grad),)
low.defvjp(low_keep, low_pass)
low_back.defvjp(back_keep, back_low)
epsilon = 1e-05
masked_score = -1e+30
highest = lax.Precision.HIGHEST

def product(left, right):
    return jnp.dot(left, right, precision=highest, preferred_element_type=jnp.float32)

def layer_norm(tensor, scaling, shifts):
    average = lax.optimization_barrier(jnp.mean(tensor, axis=-1, keepdims=True))
    centred = tensor - average
    spread = lax.optimization_barrier(jnp.mean(centred * centred, axis=-1, keepdims=True))
    return centred * lax.rsqrt(spread + epsilon) * scaling + shifts

def gelu_exact(tensor):
    return jax.nn.gelu(tensor, approximate=False)

def segment_ids(positions, ends_row):
    return lax.optimization_barrier(jnp.sum((positions[:, None] >= ends_row[None, :]).astype(jnp.int32), axis=1))

def masked_conv(row_feats, frame_ids, kernel):
    groups = CONV_G
    group_width = D // CONV_G
    tap_count = CONV_K
    half_taps = tap_count // 2
    padded = jnp.pad(row_feats, ((half_taps, half_taps), (0, 0)))
    padded_ids = jnp.pad(frame_ids, (half_taps, half_taps), constant_values=-1)
    kernel_grid = kernel.reshape(groups, group_width, tap_count, group_width)
    block_len = math.gcd(FRAMES, 64)

    def one_block(anchor):
        frame_at = anchor + jnp.arange(block_len, dtype=jnp.int32)
        taps_at = frame_at[:, None] + jnp.arange(tap_count, dtype=jnp.int32)[None, :]
        window = padded[taps_at]
        own_ids = lax.dynamic_slice_in_dim(frame_ids, anchor, block_len)
        linked = padded_ids[taps_at] == own_ids[:, None]
        window = jnp.where(linked[:, :, None], window, 0.0)
        window = window.reshape(block_len, tap_count, groups, group_width)
        result = jnp.einsum('tkgi,goki->tgo', window, kernel_grid, precision=highest)
        return result.reshape(block_len, D)
    starts = jnp.arange(FRAMES // block_len, dtype=jnp.int32) * block_len
    return lax.map(jax.checkpoint(one_block), starts).reshape(FRAMES, D)

def encoder_layer(hidden, linked_pairs, joint_w, query_b, value_b, output_w, attend_b, middle_g, lower_s, expand_w, hidden_b, reduce_w, return_b, final_g, upper_s):
    query_scale = HEAD_DIM ** (-0.5)
    inputs = low(hidden)
    joint_out = product(inputs, joint_w)
    queries = low(low_back((joint_out[:, :D] + query_b) * query_scale))
    keyed = low(low_back(joint_out[:, D:2 * D]))
    values_low = low(low_back(joint_out[:, 2 * D:] + value_b))
    queries = queries.reshape(FRAMES, HEADS, HEAD_DIM)
    keyed = keyed.reshape(FRAMES, HEADS, HEAD_DIM)
    values_low = values_low.reshape(FRAMES, HEADS, HEAD_DIM)
    scores = low_back(jnp.einsum('qhd,khd->hqk', queries, keyed, precision=highest))
    scores = jnp.where(linked_pairs[None], scores, masked_score)
    row_peak = lax.optimization_barrier(jnp.max(scores, axis=-1, keepdims=True))
    exponent = jnp.exp(scores - row_peak)
    weights_low = low(exponent / lax.optimization_barrier(jnp.sum(exponent, axis=-1, keepdims=True)))
    context = jnp.einsum('hqk,khd->qhd', weights_low, values_low, precision=highest).reshape(FRAMES, D)
    context = low(low_back(context))
    attended = low_back(product(context, output_w) + attend_b)
    middle = layer_norm(hidden + attended, middle_g, lower_s)
    inner_pre = low_back(product(low(middle), expand_w) + hidden_b)
    activated = low(gelu_exact(inner_pre))
    fed_out = low_back(product(activated, reduce_w) + return_b)
    return layer_norm(middle + fed_out, final_g, upper_s)

def encode_row(row_feats, ends_row, params):
    kernel, position_b, entry_g, base_s, joint_w, query_b, value_b, output_w, attend_b, middle_g, lower_s, expand_w, hidden_b, reduce_w, return_b, final_g, upper_s, head_w, vocab_b = params
    frame_ids = segment_ids(jnp.arange(FRAMES, dtype=jnp.int32), ends_row)
    conv_pre = low_back(masked_conv(row_feats, frame_ids, kernel) + position_b)
    hidden = layer_norm(row_feats + gelu_exact(conv_pre), entry_g, base_s)
    linked_pairs = frame_ids[:, None] == frame_ids[None, :]
    for layer_at in range(LAYERS):
        hidden = encoder_layer(hidden, linked_pairs, joint_w[layer_at], query_b[layer_at], value_b[layer_at], output_w[layer_at], attend_b[layer_at], middle_g[layer_at], lower_s[layer_at], expand_w[layer_at], hidden_b[layer_at], reduce_w[layer_at], return_b[layer_at], final_g[layer_at], upper_s[layer_at])
    return product(low(hidden), head_w) + vocab_b

def reference(features, utterance_ends, kernel_weight, position_bias, entry_gain, base_shift, joint_weight, query_bias, value_bias, output_weight, attend_bias, middle_gain, lower_shift, expand_weight, hidden_bias, reduce_weight, return_bias, final_gain, upper_shift, head_weight, vocab_bias, cotangent):
    params = tuple((tensor.astype(jnp.float32) for tensor in (kernel_weight, position_bias, entry_gain, base_shift, joint_weight, query_bias, value_bias, output_weight, attend_bias, middle_gain, lower_shift, expand_weight, hidden_bias, reduce_weight, return_bias, final_gain, upper_shift, head_weight, vocab_bias)))

    def forward(inputs, weights):

        def one_row(row_pair):
            return encode_row(row_pair[0], row_pair[1], weights)
        return lax.map(jax.checkpoint(one_row), (inputs, utterance_ends))
    logits, pullback = jax.vjp(forward, features.astype(jnp.float32), params)
    input_grads, gradients = pullback(cotangent.astype(jnp.float32))
    return (logits, input_grads, gradients[0], gradients[1], gradients[2], gradients[3], gradients[4], gradients[5], gradients[6], gradients[7], gradients[8], gradients[9], gradients[10], gradients[11], gradients[12], gradients[13], gradients[14], gradients[15], gradients[16], gradients[17], gradients[18])
```

```python
import functools
import math

import jax
import jax.numpy as jnp
from jax import lax
from jax.experimental import pallas as pl
from jax.experimental.pallas import tpu as pltpu
from jax.sharding import PartitionSpec as P

HEADS = 16
CONV_G = 16


epsilon = 1e-05
masked_score = -1e30


def with_halo(cells, sides, width):
    for axis, dim in sides:
        count = lax.axis_size(axis)
        ends = count - 1
        head = lax.slice_in_dim(cells, 0, width, axis=dim)
        tail = lax.slice_in_dim(cells, cells.shape[dim] - width, cells.shape[dim], axis=dim)
        cells = jnp.concatenate(
            [
                lax.ppermute(tail, axis, [(i, (i + 1) % count) for i in range(ends)]),
                cells,
                lax.ppermute(head, axis, [((i + 1) % count, i) for i in range(ends)]),
            ],
            axis=dim,
        )
    return cells


def layer_norm(tensor, scaling, shifts):
    average = jnp.mean(tensor, axis=-1, keepdims=True)
    centred = tensor - average
    spread = jnp.mean(centred * centred, axis=-1, keepdims=True)
    return centred * lax.rsqrt(spread + epsilon) * scaling + shifts


def norm_pullback(tensor, scaling, upstream):
    _, pullback = jax.vjp(layer_norm, tensor, scaling, jnp.zeros_like(scaling))
    return pullback(upstream)


def gelu_exact(tensor):
    return jax.nn.gelu(tensor, approximate=False)


def rounded(tensor):
    return tensor.astype(jnp.bfloat16)


def widened(tensor):
    return tensor.astype(jnp.float32)


def segment_ids(positions, utterance_ends):
    return jnp.sum(
        (positions[None, :, None] >= utterance_ends[:, None, :]).astype(jnp.int32), axis=2
    )


def unfold(source, source_ids, target_ids, anchors):
    length = target_ids.shape[1]
    pieces = [lax.slice_in_dim(source, anchor, anchor + length, axis=1) for anchor in anchors]
    matches = [
        lax.slice_in_dim(source_ids, anchor, anchor + length, axis=1) == target_ids
        for anchor in anchors
    ]
    stacked = jnp.stack(pieces, axis=2)
    keepers = jnp.stack(matches, axis=2)
    return jnp.where(keepers[..., None], stacked, jnp.zeros_like(stacked))


def conv_forward(halo_feats, halo_ids, frame_ids, kernel_grid, tap_block):
    row_count, frame_count = frame_ids.shape
    groups, group_width, tap_count, inner_width = kernel_grid.shape
    summed = jnp.zeros((row_count, frame_count, groups, group_width), jnp.float32)
    for block_at in range(tap_count // tap_block):
        first_tap = block_at * tap_block
        window = unfold(
            halo_feats,
            halo_ids,
            frame_ids,
            [first_tap + inner_tap for inner_tap in range(tap_block)],
        )
        window = window.reshape(row_count, frame_count, tap_block, groups, inner_width)
        summed = summed + jnp.einsum(
            "rtkgi,goki->rtgo",
            window,
            kernel_grid[:, :, first_tap : first_tap + tap_block, :],
            preferred_element_type=jnp.float32,
        )
    return summed.reshape(row_count, frame_count, groups * group_width)


def conv_backward(halo_grads, halo_feats, halo_ids, frame_ids, kernel_grid, tap_block, conv_low):
    row_count, frame_count = frame_ids.shape
    groups, group_width, tap_count, inner_width = kernel_grid.shape
    input_part = jnp.zeros((row_count, frame_count, groups, inner_width), jnp.float32)
    grouped = conv_low.reshape(row_count, frame_count, groups, group_width)
    kernel_parts = []
    for block_at in range(tap_count // tap_block):
        first_tap = block_at * tap_block
        tap_list = [first_tap + inner_tap for inner_tap in range(tap_block)]
        grads_window = unfold(
            halo_grads, halo_ids, frame_ids, [tap_count - tap_at for tap_at in tap_list]
        )
        grads_window = grads_window.reshape(row_count, frame_count, tap_block, groups, group_width)
        input_part = input_part + jnp.einsum(
            "rtkgo,goki->rtgi",
            grads_window,
            kernel_grid[:, :, first_tap : first_tap + tap_block, :],
            preferred_element_type=jnp.float32,
        )
        feats_window = unfold(halo_feats, halo_ids, frame_ids, tap_list)
        feats_window = feats_window.reshape(row_count, frame_count, tap_block, groups, inner_width)
        kernel_parts.append(
            jnp.einsum(
                "rtgo,rtkgi->goki", grouped, feats_window, preferred_element_type=jnp.float32
            )
        )
    kernel_full = jnp.concatenate(kernel_parts, axis=2).reshape(
        groups * group_width, tap_count * inner_width
    )
    return (input_part.reshape(row_count, frame_count, groups * inner_width), kernel_full)


def split_heads(tensor, head_count):
    return tensor.reshape(
        tensor.shape[0], tensor.shape[1], head_count, tensor.shape[2] // head_count
    )


def attend_scores(queries, all_keys, query_ids, key_ids, head_count):
    scores = jnp.einsum(
        "rqhd,rkhd->rhqk",
        split_heads(queries, head_count),
        split_heads(all_keys, head_count),
        preferred_element_type=jnp.float32,
    )
    allowed = query_ids[:, None, :, None] == key_ids[:, None, None, :]
    return jnp.where(allowed, scores, masked_score)


def attend_forward(queries, all_keys, all_values, frame_ids, row_ids, head_count):
    scores = attend_scores(queries, all_keys, frame_ids, row_ids, head_count)
    row_peak = jnp.max(scores, axis=-1, keepdims=True)
    exponent = jnp.exp(scores - row_peak)
    totals = jnp.sum(exponent, axis=-1, keepdims=True)
    weights_low = rounded(exponent / totals)
    context = jnp.einsum(
        "rhqk,rkhd->rqhd",
        weights_low,
        split_heads(all_values, head_count),
        preferred_element_type=jnp.float32,
    )
    return (rounded(context.reshape(queries.shape)), row_peak + jnp.log(totals))


def attend_backward(
    queries, all_keys, all_values, frame_ids, row_ids, head_count, log_totals, context_low
):
    scores = attend_scores(queries, all_keys, frame_ids, row_ids, head_count)
    attention = jnp.exp(scores - log_totals)
    weights_low = rounded(attention)
    grad_heads = split_heads(context_low, head_count)
    prob_grad = jnp.einsum(
        "rqhd,rkhd->rhqk",
        grad_heads,
        split_heads(all_values, head_count),
        preferred_element_type=jnp.float32,
    )
    row_delta = jnp.sum(attention * prob_grad, axis=-1, keepdims=True)
    score_grad = rounded(attention * (prob_grad - row_delta))
    value_part = jnp.einsum(
        "rhqk,rqhd->rkhd", weights_low, grad_heads, preferred_element_type=jnp.float32
    )
    query_part = jnp.einsum(
        "rhqk,rkhd->rqhd",
        score_grad,
        split_heads(all_keys, head_count),
        preferred_element_type=jnp.float32,
    )
    key_part = jnp.einsum(
        "rhqk,rqhd->rkhd",
        score_grad,
        split_heads(queries, head_count),
        preferred_element_type=jnp.float32,
    )
    return (
        query_part.reshape(queries.shape),
        key_part.reshape(all_keys.shape),
        value_part.reshape(all_values.shape),
    )


def local(
    features,
    utterance_ends,
    kernel_weight,
    position_bias,
    entry_gain,
    base_shift,
    joint_weight,
    query_bias,
    value_bias,
    output_weight,
    attend_bias,
    middle_gain,
    lower_shift,
    expand_weight,
    hidden_bias,
    reduce_weight,
    return_bias,
    final_gain,
    upper_shift,
    head_weight,
    vocab_bias,
    cotangent,
):
    row_count, frame_count, model_dim = features.shape
    frames_all = frame_count * lax.axis_size("seq")
    groups = CONV_G
    group_width = model_dim // groups
    tap_count = kernel_weight.shape[1] // group_width
    half_taps = tap_count // 2
    tap_block = math.gcd(tap_count, 16)
    head_count = HEADS
    query_scale = (model_dim // head_count) ** (-0.5)
    layer_count = joint_weight.shape[0]
    rows_share = model_dim // lax.axis_size(("dp", "seq"))
    anchor = lax.axis_index("seq") * frame_count
    frame_ids = segment_ids(anchor + jnp.arange(frame_count, dtype=jnp.int32), utterance_ends)
    row_ids = segment_ids(jnp.arange(frames_all, dtype=jnp.int32), utterance_ends)
    halo_place = anchor - half_taps + jnp.arange(frame_count + tap_count, dtype=jnp.int32)
    inside = (halo_place >= 0) & (halo_place < frames_all)
    halo_ids = jnp.where(inside[None, :], segment_ids(halo_place, utterance_ends), -1)
    stem = (
        lax.all_gather(kernel_weight, ("dp", "seq"), axis=0, tiled=True),
        lax.all_gather(position_bias, ("dp", "seq"), axis=0, tiled=True),
        lax.all_gather(entry_gain, ("dp", "seq"), axis=0, tiled=True),
        lax.all_gather(base_shift, ("dp", "seq"), axis=0, tiled=True),
        lax.all_gather(head_weight, ("dp", "seq"), axis=0, tiled=True),
    )
    kernel_grid = stem[0].reshape(groups, group_width, tap_count, group_width)
    halo_feats = with_halo(features, (("seq", 1),), half_taps)
    conv_pre = conv_forward(halo_feats, halo_ids, frame_ids, kernel_grid, tap_block) + widened(
        stem[1]
    )
    mixed = widened(features) + gelu_exact(conv_pre)
    hidden = layer_norm(mixed, widened(stem[2]), widened(stem[3]))
    saved = []
    for layer_at in range(layer_count):
        (
            joint_full,
            query_full,
            value_full,
            output_full,
            attend_full,
            middle_full,
            lower_full,
            expand_full,
            hidden_full,
            reduce_full,
            return_full,
            final_full,
            upper_full,
        ) = (
            lax.all_gather(joint_weight[layer_at], ("dp", "seq"), axis=0, tiled=True),
            lax.all_gather(query_bias[layer_at], ("dp", "seq"), axis=0, tiled=True),
            lax.all_gather(value_bias[layer_at], ("dp", "seq"), axis=0, tiled=True),
            lax.all_gather(output_weight[layer_at], ("dp", "seq"), axis=0, tiled=True),
            lax.all_gather(attend_bias[layer_at], ("dp", "seq"), axis=0, tiled=True),
            lax.all_gather(middle_gain[layer_at], ("dp", "seq"), axis=0, tiled=True),
            lax.all_gather(lower_shift[layer_at], ("dp", "seq"), axis=0, tiled=True),
            lax.all_gather(expand_weight[layer_at], ("dp", "seq"), axis=0, tiled=True),
            lax.all_gather(hidden_bias[layer_at], ("dp", "seq"), axis=0, tiled=True),
            lax.all_gather(reduce_weight[layer_at], ("dp", "seq"), axis=0, tiled=True),
            lax.all_gather(return_bias[layer_at], ("dp", "seq"), axis=0, tiled=True),
            lax.all_gather(final_gain[layer_at], ("dp", "seq"), axis=0, tiled=True),
            lax.all_gather(upper_shift[layer_at], ("dp", "seq"), axis=0, tiled=True),
        )
        inputs_low = rounded(hidden)
        joint_out = jnp.einsum(
            "rtd,de->rte", inputs_low, joint_full, preferred_element_type=jnp.float32
        )
        queries = rounded((joint_out[..., :model_dim] + widened(query_full)) * query_scale)
        keys_local = rounded(joint_out[..., model_dim : 2 * model_dim])
        values_local = rounded(joint_out[..., 2 * model_dim :] + widened(value_full))
        all_keys, all_values = (
            lax.all_gather(keys_local, "seq", axis=1, tiled=True),
            lax.all_gather(values_local, "seq", axis=1, tiled=True),
        )
        context, log_totals = attend_forward(
            queries, all_keys, all_values, frame_ids, row_ids, head_count
        )
        attended = jnp.einsum(
            "rtc,cd->rtd", context, output_full, preferred_element_type=jnp.float32
        ) + widened(attend_full)
        residual_one = hidden + attended
        middle = layer_norm(residual_one, widened(middle_full), widened(lower_full))
        middle_low = rounded(middle)
        inner_pre = jnp.einsum(
            "rtd,df->rtf", middle_low, expand_full, preferred_element_type=jnp.float32
        ) + widened(hidden_full)
        activated = rounded(gelu_exact(inner_pre))
        outer = (
            middle
            + jnp.einsum("rtf,fd->rtd", activated, reduce_full, preferred_element_type=jnp.float32)
            + widened(return_full)
        )
        kept_weights = None
        saved.append(
            (
                inputs_low,
                queries,
                all_keys,
                all_values,
                log_totals,
                context,
                residual_one,
                middle_low,
                inner_pre,
                activated,
                outer,
                kept_weights,
            )
        )
        hidden = layer_norm(outer, widened(final_full), widened(upper_full))
    final_low = rounded(hidden)
    logits = jnp.einsum(
        "rtd,dv->rtv", final_low, stem[4], preferred_element_type=jnp.float32
    ) + widened(vocab_bias)
    back_stem = (
        lax.all_gather(kernel_weight, ("dp", "seq"), axis=0, tiled=True),
        lax.all_gather(entry_gain, ("dp", "seq"), axis=0, tiled=True),
        lax.all_gather(head_weight, ("dp", "seq"), axis=0, tiled=True),
    )
    vocab_sum = jnp.sum(widened(cotangent), axis=(0, 1))
    head_part = jnp.einsum("rtd,rtv->dv", final_low, cotangent, preferred_element_type=jnp.float32)
    flow_grad = jnp.einsum(
        "rtv,dv->rtd", cotangent, back_stem[2], preferred_element_type=jnp.float32
    )
    layer_grads = [None] * layer_count
    for layer_at in reversed(range(layer_count)):
        (
            inputs_low,
            queries,
            all_keys,
            all_values,
            log_totals,
            context,
            residual_one,
            middle_low,
            inner_pre,
            activated,
            outer,
            kept_weights,
        ) = saved[layer_at]
        back_weights = (
            lax.all_gather(joint_weight[layer_at], ("dp", "seq"), axis=0, tiled=True),
            lax.all_gather(output_weight[layer_at], ("dp", "seq"), axis=0, tiled=True),
            lax.all_gather(expand_weight[layer_at], ("dp", "seq"), axis=0, tiled=True),
            lax.all_gather(reduce_weight[layer_at], ("dp", "seq"), axis=0, tiled=True),
            lax.all_gather(middle_gain[layer_at], ("dp", "seq"), axis=0, tiled=True),
            lax.all_gather(final_gain[layer_at], ("dp", "seq"), axis=0, tiled=True),
        )
        joint_full, output_full, expand_full, reduce_full, middle_full, final_full = back_weights
        outer_grad, final_part, upper_part = norm_pullback(outer, widened(final_full), flow_grad)
        fed_low = rounded(outer_grad)
        return_part = jnp.sum(widened(fed_low), axis=(0, 1))
        active_grad = jnp.einsum(
            "rtd,fd->rtf", fed_low, reduce_full, preferred_element_type=jnp.float32
        )
        _, gelu_pull = jax.vjp(gelu_exact, inner_pre)
        (inner_grad,) = gelu_pull(active_grad)
        inner_low = rounded(inner_grad)
        hidden_part = jnp.sum(widened(inner_low), axis=(0, 1))
        middle_flow = outer_grad + jnp.einsum(
            "rtf,df->rtd", inner_low, expand_full, preferred_element_type=jnp.float32
        )
        residual_grad, middle_part, lower_part = norm_pullback(
            residual_one, widened(middle_full), middle_flow
        )
        attended_low = rounded(residual_grad)
        attend_part = jnp.sum(widened(attended_low), axis=(0, 1))
        context_low = rounded(
            jnp.einsum("rtd,cd->rtc", attended_low, output_full, preferred_element_type=jnp.float32)
        )
        query_raw, key_raw, value_raw = attend_backward(
            queries, all_keys, all_values, frame_ids, row_ids, head_count, log_totals, context_low
        )
        key_sum, value_sum = (
            lax.psum_scatter(
                key_raw.astype(jnp.bfloat16), "seq", scatter_dimension=1, tiled=True
            ).astype(jnp.float32),
            lax.psum_scatter(
                value_raw.astype(jnp.bfloat16), "seq", scatter_dimension=1, tiled=True
            ).astype(jnp.float32),
        )
        query_low = rounded(widened(rounded(query_raw)) * query_scale)
        key_low = rounded(key_sum)
        value_low = rounded(value_sum)
        query_part = jnp.sum(widened(query_low), axis=(0, 1))
        value_part = jnp.sum(widened(value_low), axis=(0, 1))
        joint_low = jnp.concatenate([query_low, key_low, value_low], axis=-1)
        flow_grad = residual_grad + jnp.einsum(
            "rte,de->rtd", joint_low, joint_full, preferred_element_type=jnp.float32
        )
        ratio = hidden_part.shape[0] // model_dim
        vector_rows = jnp.stack(
            [
                query_part,
                value_part,
                attend_part,
                middle_part,
                lower_part,
                return_part,
                final_part,
                upper_part,
            ],
            axis=1,
        )
        hidden_rows = hidden_part.reshape(model_dim, ratio)

        def layer_term(
            start,
            count,
            inputs_low=inputs_low,
            joint_low=joint_low,
            context=context,
            attended_low=attended_low,
            middle_low=middle_low,
            inner_low=inner_low,
            activated=activated,
            fed_low=fed_low,
            vector_rows=vector_rows,
            hidden_rows=hidden_rows,
            ratio=ratio,
        ):
            joint_rows = jnp.einsum(
                "rtd,rte->de", inputs_low, joint_low, preferred_element_type=jnp.float32
            )
            output_rows = jnp.einsum(
                "rtc,rtd->cd", context, attended_low, preferred_element_type=jnp.float32
            )
            expand_rows = jnp.einsum(
                "rtd,rtf->df", middle_low, inner_low, preferred_element_type=jnp.float32
            )
            reduce_rows = jnp.einsum(
                "rtf,rtd->fd", activated, fed_low, preferred_element_type=jnp.float32
            ).reshape(count, ratio * model_dim)
            return jnp.concatenate(
                [joint_rows, output_rows, expand_rows, reduce_rows, vector_rows, hidden_rows],
                axis=1,
            )

        summed = lax.psum_scatter(
            layer_term(jnp.int32(0), rows_share * lax.axis_size(("dp", "seq"))),
            ("dp", "seq"),
            scatter_dimension=0,
            tiled=True,
        )
        ff_width = ratio * model_dim
        first = 3 * model_dim
        second = first + model_dim
        third = second + ff_width
        fourth = third + ratio * model_dim
        joint_own = summed[:, :first]
        output_own = summed[:, first:second]
        expand_own = summed[:, second:third]
        reduce_own = summed[:, third:fourth].reshape(rows_share * ratio, model_dim)
        vector_own = summed[:, fourth : fourth + 8]
        hidden_own = summed[:, fourth + 8 :].reshape(rows_share * ratio)
        layer_grads[layer_at] = (
            joint_own,
            vector_own[:, 0],
            vector_own[:, 1],
            output_own,
            vector_own[:, 2],
            vector_own[:, 3],
            vector_own[:, 4],
            expand_own,
            hidden_own,
            reduce_own,
            vector_own[:, 5],
            vector_own[:, 6],
            vector_own[:, 7],
        )
    mixed_grad, entry_part, base_part = norm_pullback(mixed, widened(back_stem[1]), flow_grad)
    _, gelu_pull = jax.vjp(gelu_exact, conv_pre)
    (conv_grad,) = gelu_pull(mixed_grad)
    conv_low = rounded(conv_grad)
    position_part = jnp.sum(widened(conv_low), axis=(0, 1))
    halo_grads = with_halo(conv_low, (("seq", 1),), half_taps)
    back_grid = back_stem[0].reshape(groups, group_width, tap_count, group_width)
    input_part, kernel_part = conv_backward(
        halo_grads, halo_feats, halo_ids, frame_ids, back_grid, tap_block, conv_low
    )
    features_grad = mixed_grad + input_part
    vocab_tiled = jnp.tile(vocab_sum, lax.axis_size(("dp", "seq")))
    stem_sums = (
        lax.psum_scatter(kernel_part, ("dp", "seq"), scatter_dimension=0, tiled=True),
        lax.psum_scatter(position_part, ("dp", "seq"), scatter_dimension=0, tiled=True),
        lax.psum_scatter(entry_part, ("dp", "seq"), scatter_dimension=0, tiled=True),
        lax.psum_scatter(base_part, ("dp", "seq"), scatter_dimension=0, tiled=True),
        lax.psum_scatter(head_part, ("dp", "seq"), scatter_dimension=0, tiled=True),
        lax.psum_scatter(vocab_tiled, ("dp", "seq"), scatter_dimension=0, tiled=True),
    )
    stacked = [
        jnp.stack([layer_grads[layer_at][member] for layer_at in range(layer_count)])
        for member in range(13)
    ]
    return (
        logits,
        features_grad,
        stem_sums[0],
        stem_sums[1],
        stem_sums[2],
        stem_sums[3],
        stacked[0],
        stacked[1],
        stacked[2],
        stacked[3],
        stacked[4],
        stacked[5],
        stacked[6],
        stacked[7],
        stacked[8],
        stacked[9],
        stacked[10],
        stacked[11],
        stacked[12],
        stem_sums[4],
        stem_sums[5],
    )


MESH_ID = pl.DeviceIdType.MESH
IN_VMEM = pl.BlockSpec(memory_space=pltpu.VMEM)
ANYWHERE = pl.BlockSpec(memory_space=pl.ANY)
AXES = ("a", "t", "z")
PACK = 8
RANKS = 4


def kernel_params(collective=None):
    if collective is None:
        return pltpu.CompilerParams(vmem_limit_bytes=56 * 2**20)
    return pltpu.CompilerParams(
        vmem_limit_bytes=56 * 2**20, collective_id=collective, has_side_effects=True
    )


def cost(micros):
    return pl.CostEstimate(flops=int(micros * 1.1e9), bytes_accessed=2**20, transcendentals=0)


def greet(peers):
    gate = pltpu.get_barrier_semaphore()
    for peer in peers:
        pl.semaphore_signal(gate, inc=1, device_id=peer, device_id_type=MESH_ID)
    pl.semaphore_wait(gate, len(peers))


def remote(source, target, send, receive, peer):
    return pltpu.make_async_remote_copy(
        source, target, send, receive, device_id=peer, device_id_type=MESH_ID
    )


def swap_all(sizes, collective, payloads, places):
    a_size, t_size, z_size = sizes
    total = a_size * t_size * z_size
    count = len(payloads)

    def kernel(*refs):
        sources, targets = refs[:count], refs[count : 2 * count]
        sends, receives, own_sems = refs[2 * count :]
        a, t, z = (lax.axis_index(axis) for axis in AXES)
        me = (a * t_size + t) * z_size + z
        peers = [
            (lax.rem(a + i, a_size), lax.rem(t + j, t_size), lax.rem(z + k, z_size))
            for i in range(a_size)
            for j in range(t_size)
            for k in range(z_size)
        ][1:]
        greet(peers)
        copies = []
        for p in range(count):
            own = pltpu.make_async_copy(
                sources[p].at[places[p](a, t, z)], targets[p].at[me], own_sems.at[p]
            )
            own.start()
            copies.append(own)
            for number, peer in enumerate(peers):
                copy = remote(
                    sources[p].at[places[p](*peer)],
                    targets[p].at[me],
                    sends.at[p, number],
                    receives.at[p, number],
                    peer,
                )
                copy.start()
                copies.append(copy)
        for copy in copies:
            copy.wait()

    return pl.pallas_call(
        kernel,
        out_shape=[
            jax.ShapeDtypeStruct((total,) + payload.shape[1:], payload.dtype)
            for payload in payloads
        ],
        in_specs=[ANYWHERE] * count,
        out_specs=[ANYWHERE] * count,
        scratch_shapes=[
            pltpu.SemaphoreType.DMA((count, total - 1)),
            pltpu.SemaphoreType.DMA((count, total - 1)),
            pltpu.SemaphoreType.DMA((count,)),
        ],
        compiler_params=kernel_params(collective),
        cost_estimate=cost(20),
    )(*payloads)


def rank_lanes(bounds_ref, rows, width):
    lanes = PACK * width
    line = lax.broadcasted_iota(jnp.int32, (rows, lanes), 0) // PACK
    lane = lax.broadcasted_iota(jnp.int32, (rows, lanes), 1) // width
    frame = line * PACK + lane
    rank = jnp.zeros((rows, lanes), jnp.int32)
    for slot in range(bounds_ref.shape[1]):
        rank = rank + (frame >= bounds_ref[:, slot : slot + 1]).astype(jnp.int32)
    return rank


def spread_ranks(wide, packed, rank, first):
    rows = packed.shape[0]
    wide[...] = jnp.zeros_like(wide)
    for number in range(RANKS):
        place = pl.ds(first + number * 64, rows)
        wide[place, :] += jnp.where(rank == number, packed, 0.0)


def collect_ranks(summed, rank, rows):
    result = jnp.zeros((rows, summed.shape[1]), jnp.float32)
    for number in range(RANKS):
        result = jnp.where(rank == number, summed[number * 64 : number * 64 + rows, :], result)
    return result


def toeplitz(even, odd, taps, length):
    total = None
    for step in range(taps.shape[0]):
        source = even if step % 2 == 0 else odd
        part = jnp.dot(
            source[pl.ds((step - step % 2) * 8, length), :],
            taps[step],
            preferred_element_type=jnp.float32,
        )
        total = part if total is None else total + part
    return total


def fill_pair(wide, even, odd):
    length = even.shape[0]
    even[...] = wide[:length, :].astype(jnp.bfloat16)
    odd[...] = wide[8 : 8 + length, :].astype(jnp.bfloat16)


def conv_forward_packed(packed, bounds, taps, bias):
    rows = packed.shape[0]
    length = rows + (RANKS - 1) * 64
    held = length + 128
    steps, depth, width = taps.shape

    def kernel(x_ref, b_ref, k_ref, bias_ref, o_ref, even, odd, wide):
        rank = rank_lanes(b_ref, rows, depth // PACK)
        spread_ranks(wide, x_ref[...].astype(jnp.float32), rank, 64)
        fill_pair(wide, even, odd)
        summed = toeplitz(even, odd, k_ref, length)
        rank_out = rank_lanes(b_ref, rows, width // PACK)
        o_ref[...] = (collect_ranks(summed, rank_out, rows) + bias_ref[...]).astype(jnp.bfloat16)

    return pl.pallas_call(
        kernel,
        out_shape=[
            jax.ShapeDtypeStruct((rows, width), jnp.bfloat16),
            jax.ShapeDtypeStruct((held, depth), jnp.bfloat16),
            jax.ShapeDtypeStruct((held, depth), jnp.bfloat16),
        ],
        in_specs=[IN_VMEM] * 4,
        out_specs=[IN_VMEM] * 3,
        scratch_shapes=[pltpu.VMEM((held + 16, depth), jnp.float32)],
        compiler_params=kernel_params(),
        cost_estimate=cost(10),
    )(packed, bounds, taps, bias)


def conv_backward_packed(packed, own, bounds, taps, even, odd):
    rows, depth = packed.shape
    length = rows + (RANKS - 1) * 64
    held = length + 128
    steps, _, width = taps.shape
    tap_count = (steps - 1) * PACK
    group_width = depth // PACK
    chans = width // PACK

    def kernel(g_ref, own_ref, b_ref, k_ref, even_ref, odd_ref, o_ref, w_ref, s_ref, ge, go, wide, turned):
        rank = rank_lanes(b_ref, rows, depth // PACK)
        spread_ranks(wide, g_ref[...].astype(jnp.float32), rank, 64)
        fill_pair(wide, ge, go)
        summed = toeplitz(ge, go, k_ref, length)
        rank_out = rank_lanes(b_ref, rows, width // PACK)
        o_ref[...] = collect_ranks(summed, rank_out, rows).astype(jnp.bfloat16)
        own_wide = own_ref[...].astype(jnp.float32)
        s_ref[...] = jnp.sum(own_wide, axis=0, keepdims=True)
        spread_ranks(wide.at[:length, :width], own_wide, rank_out, 0)
        across = wide[:length, :width].T.astype(jnp.bfloat16)
        for step in range(steps):
            source = even_ref if step % 2 == 0 else odd_ref
            turned[:, pl.ds(step * depth, depth)] = jnp.dot(
                across,
                source[pl.ds((step - step % 2) * 8, length), :],
                preferred_element_type=jnp.float32,
            )
        total = turned[0:chans, 0 : tap_count * group_width]
        for f in range(1, PACK):
            total = total + turned[
                f * chans : (f + 1) * chans,
                f * group_width : f * group_width + tap_count * group_width,
            ]
        w_ref[...] = total

    return pl.pallas_call(
        kernel,
        out_shape=[
            jax.ShapeDtypeStruct((rows, width), jnp.bfloat16),
            jax.ShapeDtypeStruct((chans, tap_count * group_width), jnp.float32),
            jax.ShapeDtypeStruct((1, width), jnp.float32),
        ],
        in_specs=[IN_VMEM] * 6,
        out_specs=[IN_VMEM] * 3,
        scratch_shapes=[
            pltpu.VMEM((held, depth), jnp.bfloat16),
            pltpu.VMEM((held, depth), jnp.bfloat16),
            pltpu.VMEM((held + 16, depth), jnp.float32),
            pltpu.VMEM((width, steps * depth), jnp.float32),
        ],
        compiler_params=kernel_params(),
        cost_estimate=cost(15),
    )(packed, own, bounds, taps, even, odd)


def shifted_taps(grid):
    taps, depth, width = grid.shape
    steps = 17
    room = steps * PACK
    parts = [
        jnp.pad(grid, ((f, room - taps - f), (0, 0), (0, 0))).reshape(room * depth, width)
        for f in range(PACK)
    ]
    return jnp.concatenate(parts, axis=1).reshape(steps, PACK * depth, PACK * width)


def normed(tensor, gain, shift):
    average = jnp.mean(tensor, axis=-1, keepdims=True)
    centred = tensor - average
    spread = jnp.mean(centred * centred, axis=-1, keepdims=True)
    return centred * lax.rsqrt(spread + epsilon) * gain + shift


def normed_back(tensor, gain, upstream):
    average = jnp.mean(tensor, axis=-1, keepdims=True)
    centred = tensor - average
    spread = jnp.mean(centred * centred, axis=-1, keepdims=True)
    inverse = lax.rsqrt(spread + epsilon)
    unit = centred * inverse
    scaled = upstream * gain
    result = inverse * (
        scaled
        - jnp.mean(scaled, axis=-1, keepdims=True)
        - unit * jnp.mean(scaled * unit, axis=-1, keepdims=True)
    )
    return (
        result,
        jnp.sum(upstream * unit, axis=0, keepdims=True),
        jnp.sum(upstream, axis=0, keepdims=True),
    )


def gelu_pair(tensor):
    half = 0.5 * (1.0 + lax.erf(tensor * (2.0**-0.5)))
    slope = half + tensor * (jnp.exp(-0.5 * tensor * tensor) * ((2.0 * math.pi) ** -0.5))
    return tensor * half, slope


def dot(left, right):
    return jnp.dot(left, right, preferred_element_type=jnp.float32)


def dot_rt(left, right):
    return lax.dot_general(left, right, (((1,), (1,)), ((), ())), preferred_element_type=jnp.float32)


def dot_lt(left, right):
    return lax.dot_general(left, right, (((0,), (0,)), ((), ())), preferred_element_type=jnp.float32)


def group_gather(block, t, sends, receives):
    x_peer, c_peer = lax.bitwise_xor(t, 2), lax.bitwise_xor(t, 1)
    own = block.at[t]
    across = remote(own, own, sends.at[0], receives.at[0], {"t": x_peer})
    across.start()
    beside = remote(own, own, sends.at[1], receives.at[1], {"t": c_peer})
    beside.start()
    across.wait_recv()
    other = block.at[x_peer]
    onward = remote(other, other, sends.at[2], receives.at[2], {"t": c_peer})
    onward.start()
    beside.wait_recv()
    onward.wait_recv()
    across.wait_send()
    beside.wait_send()
    onward.wait_send()


def group_scatter(part, t, send_low, got_low, sends, receives, between=None):
    x_peer, c_peer = lax.bitwise_xor(t, 2), lax.bitwise_xor(t, 1)
    send_low[1] = part(lax.bitwise_xor(t, 3)).astype(jnp.bfloat16)
    first = remote(send_low.at[1], got_low.at[1], sends.at[1], receives.at[1], {"t": c_peer})
    first.start()
    send_low[0] = part(c_peer).astype(jnp.bfloat16)
    second = remote(send_low.at[0], got_low.at[0], sends.at[0], receives.at[0], {"t": c_peer})
    second.start()
    total = part(x_peer)
    first.wait_recv()
    send_low[2] = (total + got_low[1].astype(jnp.float32)).astype(jnp.bfloat16)
    third = remote(send_low.at[2], got_low.at[2], sends.at[2], receives.at[2], {"t": x_peer})
    third.start()
    own = part(t)
    if between is not None:
        between()
    second.wait_recv()
    own = own + got_low[0].astype(jnp.float32)
    third.wait_recv()
    own = own + got_low[2].astype(jnp.float32)
    first.wait_send()
    second.wait_send()
    third.wait_send()
    return own


def scatter_scratch(n, width):
    return [
        pltpu.VMEM((3, n, width), jnp.bfloat16),
        pltpu.VMEM((3, n, width), jnp.bfloat16),
        pltpu.SemaphoreType.DMA((3,)),
        pltpu.SemaphoreType.DMA((3,)),
        pltpu.SemaphoreType.DMA((3,)),
        pltpu.SemaphoreType.DMA((3,)),
    ]


def load_rows(pieces, target, sem, sizes, share, column, width):
    a_size, t_size, z_size = sizes
    a, z = lax.axis_index("a"), lax.axis_index("z")
    for number, piece in enumerate(pieces):
        a_at = lax.bitwise_xor(a, number // z_size)
        z_at = lax.bitwise_xor(z, number % z_size)
        for t_at in range(t_size):
            row = pl.multiple_of(((a_at * t_size + t_at) * z_size + z_at) * share, share)
            pltpu.make_async_copy(
                piece.at[pl.ds(t_at * share, share), pl.ds(column, width)],
                target.at[pl.ds(row, share), :],
                sem,
            ).start()


def load_chunks(pieces, target, sem, sizes, share, column, width):
    a_size, t_size, z_size = sizes
    a, z = lax.axis_index("a"), lax.axis_index("z")
    for number, piece in enumerate(pieces):
        a_at = lax.bitwise_xor(a, number // z_size)
        z_at = lax.bitwise_xor(z, number % z_size)
        row = pl.multiple_of((a_at * z_size + z_at) * share, share)
        for chunk in range(t_size):
            pltpu.make_async_copy(
                piece.at[pl.ds(chunk * share, share), pl.ds(column, width)],
                target.at[pl.ds(row, share), pl.ds(chunk * width, width)],
                sem,
            ).start()


def load_blocks(pieces, target, sem, sizes, first, share):
    a_size, t_size, z_size = sizes
    a, z = lax.axis_index("a"), lax.axis_index("z")
    for number, piece in enumerate(pieces):
        a_at = lax.bitwise_xor(a, number // z_size)
        z_at = lax.bitwise_xor(z, number % z_size)
        row = pl.multiple_of((a_at * z_size + z_at) * share, share)
        pltpu.make_async_copy(
            piece.at[pl.ds(first, share), :], target.at[pl.ds(row, share), :], sem
        ).start()


def settle(target, sem):
    pltpu.make_async_copy(target, target, sem).wait()


def attention_forward(hidden, seg_col, seg_row, query_bias, value_bias, attend_bias, gain, shift, pieces, sizes, collective):
    n, width = hidden.shape
    a_size, t_size, z_size = sizes
    count = t_size * n
    part = width // t_size
    head = width // HEADS
    share = width // (a_size * t_size * z_size)
    scale = head**-0.5

    def kernel(h_ref, sc_ref, sr_ref, qb_ref, vb_ref, ab_ref, g_ref, s_ref, *rest):
        piece_refs = rest[: len(pieces)]
        (x_ref, qkv_ref, p_ref, c_ref, r_ref, m_ref, wj, wo, low, got, gs, gr, ss, sr, ws) = rest[len(pieces) :]
        t = lax.axis_index("t")
        greet([{"t": lax.bitwise_xor(t, 1)}, {"t": lax.bitwise_xor(t, 2)}])
        load_rows(piece_refs, wj, ws.at[0], sizes, share, 0, 3 * part)
        load_chunks(piece_refs, wo, ws.at[1], sizes, share, 3 * part, part)
        x_ref[t] = h_ref[...].astype(jnp.bfloat16)
        group_gather(x_ref, t, gs, gr)
        settle(wj, ws.at[0])
        joint = dot(x_ref[...].reshape(count, width), wj[...])
        qkv_ref[:, 0:part] = ((joint[:, 0:part] + qb_ref[...]) * scale).astype(jnp.bfloat16)
        qkv_ref[:, part : 2 * part] = joint[:, part : 2 * part].astype(jnp.bfloat16)
        qkv_ref[:, 2 * part :] = (joint[:, 2 * part :] + vb_ref[...]).astype(jnp.bfloat16)
        linked = sc_ref[...] == sr_ref[...]
        for at in range(part // head):
            queries = qkv_ref[:, at * head : (at + 1) * head]
            keys = qkv_ref[:, part + at * head : part + (at + 1) * head]
            values = qkv_ref[:, 2 * part + at * head : 2 * part + (at + 1) * head]
            scores = jnp.where(linked, dot_rt(queries, keys), masked_score)
            exponent = jnp.exp(scores - jnp.max(scores, axis=-1, keepdims=True))
            weights = (exponent / jnp.sum(exponent, axis=-1, keepdims=True)).astype(jnp.bfloat16)
            p_ref[at] = weights
            c_ref[:, at * head : (at + 1) * head] = dot(weights, values).astype(jnp.bfloat16)
        settle(wo, ws.at[1])
        attended = group_scatter(
            lambda j: dot(c_ref[pl.ds(pl.multiple_of(j * n, n), n), :], wo[...]), t, low, got, ss, sr
        )
        total = h_ref[...] + (attended + ab_ref[...])
        r_ref[...] = total
        m_ref[...] = normed(total, g_ref[...], s_ref[...])

    return pl.pallas_call(
        kernel,
        out_shape=[
            jax.ShapeDtypeStruct((t_size, n, width), jnp.bfloat16),
            jax.ShapeDtypeStruct((count, 3 * part), jnp.bfloat16),
            jax.ShapeDtypeStruct((part // head, count, count), jnp.bfloat16),
            jax.ShapeDtypeStruct((count, part), jnp.bfloat16),
            jax.ShapeDtypeStruct((n, width), jnp.float32),
            jax.ShapeDtypeStruct((n, width), jnp.float32),
        ],
        in_specs=[IN_VMEM] * 8 + [ANYWHERE] * len(pieces),
        out_specs=[IN_VMEM] * 6,
        scratch_shapes=[
            pltpu.VMEM((width, 3 * part), jnp.bfloat16),
            pltpu.VMEM((part, width), jnp.bfloat16),
        ]
        + scatter_scratch(n, width)
        + [pltpu.SemaphoreType.DMA((2,))],
        compiler_params=kernel_params(collective),
        cost_estimate=cost(25),
    )(hidden, seg_col, seg_row, query_bias, value_bias, attend_bias, gain, shift, *pieces)


def feed_forward(middle, hidden_bias, return_bias, gain, shift, pieces, sizes, collective):
    n, width = middle.shape
    a_size, t_size, z_size = sizes
    count = t_size * n
    inner_width = hidden_bias.shape[1]
    share = width // (a_size * t_size * z_size)
    inner_share = inner_width // (a_size * z_size)

    def kernel(m_ref, hb_ref, rb_ref, g_ref, s_ref, *rest):
        piece_refs = rest[: len(pieces)]
        (x_ref, act_ref, slope_ref, o_ref, h_ref, we, wr, low, got, gs, gr, ss, sr, ws) = rest[len(pieces) :]
        t = lax.axis_index("t")
        greet([{"t": lax.bitwise_xor(t, 1)}, {"t": lax.bitwise_xor(t, 2)}])
        load_rows(piece_refs, we, ws.at[0], sizes, share, 0, inner_width)
        load_blocks(piece_refs, wr, ws.at[1], sizes, t_size * share, inner_share)
        x_ref[t] = m_ref[...].astype(jnp.bfloat16)
        group_gather(x_ref, t, gs, gr)
        settle(we, ws.at[0])
        inner = dot(x_ref[...].reshape(count, width), we[...]) + hb_ref[...]
        active, slope = gelu_pair(inner)
        act_ref[...] = active.astype(jnp.bfloat16)
        slope_ref[...] = slope.astype(jnp.bfloat16)
        settle(wr, ws.at[1])
        fed = group_scatter(
            lambda j: dot(act_ref[pl.ds(pl.multiple_of(j * n, n), n), :], wr[...]), t, low, got, ss, sr
        )
        total = m_ref[...] + fed + rb_ref[...]
        o_ref[...] = total
        h_ref[...] = normed(total, g_ref[...], s_ref[...])

    return pl.pallas_call(
        kernel,
        out_shape=[
            jax.ShapeDtypeStruct((t_size, n, width), jnp.bfloat16),
            jax.ShapeDtypeStruct((count, inner_width), jnp.bfloat16),
            jax.ShapeDtypeStruct((count, inner_width), jnp.bfloat16),
            jax.ShapeDtypeStruct((n, width), jnp.float32),
            jax.ShapeDtypeStruct((n, width), jnp.float32),
        ],
        in_specs=[IN_VMEM] * 5 + [ANYWHERE] * len(pieces),
        out_specs=[IN_VMEM] * 5,
        scratch_shapes=[
            pltpu.VMEM((width, inner_width), jnp.bfloat16),
            pltpu.VMEM((inner_width, width), jnp.bfloat16),
        ]
        + scatter_scratch(n, width)
        + [pltpu.SemaphoreType.DMA((2,))],
        compiler_params=kernel_params(collective),
        cost_estimate=cost(25),
    )(middle, hidden_bias, return_bias, gain, shift, *pieces)


def store_rows(target, grads, sizes, share, column):
    a_size, t_size, z_size = sizes
    a, z = lax.axis_index("a"), lax.axis_index("z")
    width = grads.shape[1]
    for a_at in range(a_size):
        for z_at in range(z_size):
            for t_at in range(t_size):
                row = ((a_at * t_size + t_at) * z_size + z_at) * share
                target[
                    lax.bitwise_xor(a, a_at),
                    lax.bitwise_xor(z, z_at),
                    t_at * share : (t_at + 1) * share,
                    column : column + width,
                ] = grads[row : row + share, :].astype(jnp.bfloat16)


def store_chunks(target, grads, sizes, share, column):
    a_size, t_size, z_size = sizes
    a, z = lax.axis_index("a"), lax.axis_index("z")
    width = grads.shape[1] // t_size
    for a_at in range(a_size):
        for z_at in range(z_size):
            row = (a_at * z_size + z_at) * share
            for chunk in range(t_size):
                target[
                    lax.bitwise_xor(a, a_at),
                    lax.bitwise_xor(z, z_at),
                    chunk * share : (chunk + 1) * share,
                    column : column + width,
                ] = grads[row : row + share, chunk * width : (chunk + 1) * width].astype(jnp.bfloat16)


def store_blocks(target, grads, sizes, first, share):
    a_size, t_size, z_size = sizes
    a, z = lax.axis_index("a"), lax.axis_index("z")
    for a_at in range(a_size):
        for z_at in range(z_size):
            row = (a_at * z_size + z_at) * share
            target[lax.bitwise_xor(a, a_at), lax.bitwise_xor(z, z_at), first : first + share, :] = (
                grads[row : row + share, :].astype(jnp.bfloat16)
            )


def feed_backward(upstream, outer, residual, final_gain, middle_gain, gathered, active, slope, pieces, sizes, collective):
    n, width = upstream.shape
    a_size, t_size, z_size = sizes
    count = t_size * n
    inner_width = active.shape[1]
    share = width // (a_size * t_size * z_size)
    inner_share = inner_width // (a_size * z_size)
    piece_rows = t_size * share + inner_share

    def kernel(u_ref, o_ref, r_ref, fg_ref, mg_ref, x_ref, act_ref, slope_ref, *rest):
        piece_refs = rest[: len(pieces)]
        (res_ref, w_ref, v_ref, hid_ref, fed, inner_low, we, wr, low, got, gs, gr, ss, sr, ws) = rest[len(pieces) :]
        t = lax.axis_index("t")
        greet([{"t": lax.bitwise_xor(t, 1)}, {"t": lax.bitwise_xor(t, 2)}])
        load_blocks(piece_refs, wr, ws.at[1], sizes, t_size * share, inner_share)
        load_rows(piece_refs, we, ws.at[0], sizes, share, 0, inner_width)
        outer_grad, final_part, upper_part = normed_back(o_ref[...], fg_ref[...], u_ref[...])
        fed_low = outer_grad.astype(jnp.bfloat16)
        fed[t] = fed_low
        v_ref[0:1] = final_part
        v_ref[1:2] = upper_part
        v_ref[2:3] = jnp.sum(fed_low.astype(jnp.float32), axis=0, keepdims=True)
        group_gather(fed, t, gs, gr)
        settle(wr, ws.at[1])
        active_grad = dot_rt(fed[...].reshape(count, width), wr[...])
        lowered = (active_grad * slope_ref[...].astype(jnp.float32)).astype(jnp.bfloat16)
        inner_low[...] = lowered
        hid_ref[...] = jnp.sum(lowered.astype(jnp.float32), axis=0, keepdims=True)
        settle(we, ws.at[0])

        def weights():
            store_blocks(
                w_ref, dot_lt(act_ref[...], fed[...].reshape(count, width)), sizes, t_size * share, inner_share
            )
            store_rows(w_ref, dot_lt(x_ref[...].reshape(count, width), inner_low[...]), sizes, share, 0)

        back = group_scatter(
            lambda j: dot_rt(inner_low[pl.ds(pl.multiple_of(j * n, n), n), :], we[...]),
            t,
            low,
            got,
            ss,
            sr,
            weights,
        )
        res_grad, middle_part, lower_part = normed_back(r_ref[...], mg_ref[...], outer_grad + back)
        res_ref[...] = res_grad
        v_ref[3:4] = middle_part
        v_ref[4:5] = lower_part
        v_ref[5:8] = jnp.zeros((3, width), jnp.float32)

    return pl.pallas_call(
        kernel,
        out_shape=[
            jax.ShapeDtypeStruct((n, width), jnp.float32),
            jax.ShapeDtypeStruct((a_size, z_size, piece_rows, width), jnp.bfloat16),
            jax.ShapeDtypeStruct((8, width), jnp.float32),
            jax.ShapeDtypeStruct((1, inner_width), jnp.float32),
        ],
        in_specs=[IN_VMEM] * 8 + [ANYWHERE] * len(pieces),
        out_specs=[IN_VMEM] * 4,
        scratch_shapes=[
            pltpu.VMEM((t_size, n, width), jnp.bfloat16),
            pltpu.VMEM((count, inner_width), jnp.bfloat16),
            pltpu.VMEM((width, inner_width), jnp.bfloat16),
            pltpu.VMEM((inner_width, width), jnp.bfloat16),
        ]
        + scatter_scratch(n, width)
        + [pltpu.SemaphoreType.DMA((2,))],
        compiler_params=kernel_params(collective),
        cost_estimate=cost(30),
    )(upstream, outer, residual, final_gain, middle_gain, gathered, active, slope, *pieces)


def attention_backward(res_grad, gathered, qkv, weights_low, context, pieces, sizes, collective):
    n, width = res_grad.shape
    a_size, t_size, z_size = sizes
    count = t_size * n
    part = width // t_size
    head = width // HEADS
    share = width // (a_size * t_size * z_size)
    scale = head**-0.5

    def kernel(r_ref, x_ref, qkv_ref, p_ref, c_ref, *rest):
        piece_refs = rest[: len(pieces)]
        (g_ref, w_ref, v_ref, b_ref, fed, grad_low, joint, wj, wo, low, got, gs, gr, ss, sr, ws) = rest[len(pieces) :]
        t = lax.axis_index("t")
        greet([{"t": lax.bitwise_xor(t, 1)}, {"t": lax.bitwise_xor(t, 2)}])
        load_chunks(piece_refs, wo, ws.at[1], sizes, share, 3 * part, part)
        load_rows(piece_refs, wj, ws.at[0], sizes, share, 0, 3 * part)
        own_low = r_ref[...].astype(jnp.bfloat16)
        fed[t] = own_low
        v_ref[0:1] = jnp.sum(own_low.astype(jnp.float32), axis=0, keepdims=True)
        v_ref[1:8] = jnp.zeros((7, width), jnp.float32)
        group_gather(fed, t, gs, gr)
        settle(wo, ws.at[1])
        grad_low[...] = dot_rt(fed[...].reshape(count, width), wo[...]).astype(jnp.bfloat16)
        for at in range(part // head):
            mine = slice(at * head, (at + 1) * head)
            queries = qkv_ref[:, mine]
            keys = qkv_ref[:, part + at * head : part + (at + 1) * head]
            values = qkv_ref[:, 2 * part + at * head : 2 * part + (at + 1) * head]
            weights = p_ref[at]
            grads = grad_low[:, mine]
            delta = jnp.sum(
                grads.astype(jnp.float32) * c_ref[:, mine].astype(jnp.float32), axis=-1, keepdims=True
            )
            score_grad = (weights.astype(jnp.float32) * (dot_rt(grads, values) - delta)).astype(jnp.bfloat16)
            joint[:, mine] = (
                dot(score_grad, keys).astype(jnp.bfloat16).astype(jnp.float32) * scale
            ).astype(jnp.bfloat16)
            joint[:, part + at * head : part + (at + 1) * head] = dot_lt(score_grad, queries).astype(jnp.bfloat16)
            joint[:, 2 * part + at * head : 2 * part + (at + 1) * head] = dot_lt(weights, grads).astype(jnp.bfloat16)
        b_ref[...] = jnp.sum(joint[...].astype(jnp.float32), axis=0, keepdims=True)
        settle(wj, ws.at[0])

        def weight_grads():
            store_rows(w_ref, dot_lt(x_ref[...].reshape(count, width), joint[...]), sizes, share, 0)
            store_chunks(
                w_ref, dot_lt(c_ref[...], fed[...].reshape(count, width)), sizes, share, 3 * part
            )

        back = group_scatter(
            lambda j: dot_rt(joint[pl.ds(pl.multiple_of(j * n, n), n), :], wj[...]),
            t,
            low,
            got,
            ss,
            sr,
            weight_grads,
        )
        g_ref[...] = r_ref[...] + back

    return pl.pallas_call(
        kernel,
        out_shape=[
            jax.ShapeDtypeStruct((n, width), jnp.float32),
            jax.ShapeDtypeStruct((a_size, z_size, t_size * share, width), jnp.bfloat16),
            jax.ShapeDtypeStruct((8, width), jnp.float32),
            jax.ShapeDtypeStruct((1, 3 * part), jnp.float32),
        ],
        in_specs=[IN_VMEM] * 5 + [ANYWHERE] * len(pieces),
        out_specs=[IN_VMEM] * 4,
        scratch_shapes=[
            pltpu.VMEM((t_size, n, width), jnp.bfloat16),
            pltpu.VMEM((count, part), jnp.bfloat16),
            pltpu.VMEM((count, 3 * part), jnp.bfloat16),
            pltpu.VMEM((width, 3 * part), jnp.bfloat16),
            pltpu.VMEM((part, width), jnp.bfloat16),
        ]
        + scatter_scratch(n, width)
        + [pltpu.SemaphoreType.DMA((2,))],
        compiler_params=kernel_params(collective),
        cost_estimate=cost(30),
    )(res_grad, gathered, qkv, weights_low, context, *pieces)


def pairs_of(size, mask):
    return [(i, i ^ mask) for i in range(size)]


def spread_weights(own, sizes):
    a_size, _, z_size = sizes
    near = [own] + [lax.ppermute(own, "z", pairs_of(z_size, d)) for d in range(1, z_size)]
    pieces = list(near)
    for d in range(1, a_size):
        pieces += [lax.ppermute(piece, "a", pairs_of(a_size, d)) for piece in near]
    return pieces


def reduce_pieces(parts, sizes):
    a_size, _, z_size = sizes
    summed = widened(parts[0])
    for d in range(1, a_size):
        summed = summed + widened(lax.ppermute(parts[d], "a", pairs_of(a_size, d)))
    sent = rounded(summed)
    result = summed[0]
    for d in range(1, z_size):
        result = result + widened(lax.ppermute(sent[d], "z", pairs_of(z_size, d)))
    return result


def fast_local(sizes, *arguments):
    (
        features,
        utterance_ends,
        kernel_weight,
        position_bias,
        entry_gain,
        base_shift,
        joint_weight,
        query_bias,
        value_bias,
        output_weight,
        attend_bias,
        middle_gain,
        lower_shift,
        expand_weight,
        hidden_bias,
        reduce_weight,
        return_bias,
        final_gain,
        upper_shift,
        head_weight,
        vocab_bias,
        cotangent,
    ) = arguments
    a_size, t_size, z_size = sizes
    devices = a_size * t_size * z_size
    _, n, width = features.shape
    frames = n * z_size
    rows = a_size * t_size
    groups = CONV_G
    group_width = width // groups
    share = width // devices
    taps = kernel_weight.shape[1] // group_width
    layers = joint_weight.shape[0]
    inner_all = expand_weight.shape[2]
    inner = inner_all // t_size
    inner_share = inner_all // devices
    part = width // t_size
    vocab = head_weight.shape[1]
    packs = n // PACK
    a, t, z = (lax.axis_index(axis) for axis in AXES)
    turn = [(i * z_size + j, j * z_size + i) for i in range(t_size) for j in range(z_size)]

    vectors = [attend_bias, middle_gain, lower_shift, return_bias, final_gain, upper_shift]
    whole_rows = jnp.concatenate(
        [entry_gain[None], base_shift[None]]
        + vectors
        + [head_weight.T, query_bias, value_bias, hidden_bias.reshape(layers * inner_share // share, share)],
        axis=0,
    )
    gathered = lax.all_gather(whole_rows, AXES, axis=0)
    vector_count = 2 + 6 * layers
    whole = jnp.swapaxes(gathered[:, : vector_count + vocab], 0, 1).reshape(vector_count + vocab, width)
    entry_full, base_full = widened(whole[0:1]), widened(whole[1:2])

    def vector_of(kind, layer):
        at = 2 + kind * layers + layer
        return widened(whole[at : at + 1])

    head_turned = whole[vector_count:]
    own_rows = lax.dynamic_index_in_dim(
        gathered[:, vector_count + vocab :].reshape(a_size, t_size, z_size, -1, share), t, 1, keepdims=False
    )
    own_rows = jnp.moveaxis(own_rows, 2, 0)
    query_full = widened(own_rows[:layers].reshape(layers, part))
    value_full = widened(own_rows[layers : 2 * layers].reshape(layers, part))
    hidden_full = widened(
        own_rows[2 * layers :]
        .reshape(layers, inner_share // share, a_size, z_size, share)
        .transpose(0, 2, 3, 1, 4)
        .reshape(layers, inner)
    )
    all_ends = lax.all_gather(utterance_ends, ("a", "t"), axis=0, tiled=True)
    row_ends = lax.dynamic_slice_in_dim(all_ends, a * t_size + z, 1, axis=0)
    row_ids = segment_ids(jnp.arange(frames, dtype=jnp.int32), row_ends)
    seg_col, seg_row = row_ids.reshape(frames, 1), row_ids
    before = jnp.concatenate([jnp.zeros((rows, 1), jnp.int32), all_ends[:, :-1]], axis=1)
    bounds = jnp.where(all_ends > before, all_ends, frames)
    bounds = jnp.tile(bounds, (frames // PACK, 1))

    joint_turned = joint_weight.reshape(layers, share, 3, a_size, t_size, part // a_size)
    joint_turned = joint_turned.transpose(4, 0, 1, 2, 3, 5).reshape(t_size, layers, share, 3 * part)
    expand_turned = expand_weight.reshape(layers, share, a_size, t_size, inner // a_size)
    expand_turned = expand_turned.transpose(3, 0, 1, 2, 4).reshape(t_size, layers, share, inner)
    columns = lax.all_to_all(
        jnp.concatenate([joint_turned, expand_turned], axis=-1), "t", 0, 0, tiled=True
    )
    attend_pieces, feed_pieces = [], []
    for layer in range(layers):
        joint_rows = columns[:, layer, :, : 3 * part].reshape(t_size * share, 3 * part)
        output_rows = output_weight[layer].reshape(share, t_size, part)
        output_rows = output_rows.transpose(1, 0, 2).reshape(t_size * share, part)
        attend_pieces.append(
            spread_weights(jnp.concatenate([joint_rows, output_rows], axis=1), sizes)
        )
        expand_rows = columns[:, layer, :, 3 * part :].reshape(t_size * share, inner)
        feed_pieces.append(
            spread_weights(jnp.concatenate([expand_rows, reduce_weight[layer]], axis=0), sizes)
        )

    def by_group(tokens):
        tokens = tokens.reshape(packs, PACK, groups, group_width)
        return tokens.transpose(2, 0, 1, 3).reshape(groups, packs, PACK * group_width)

    def from_channels(received):
        received = received.reshape(devices, packs, PACK, share)
        return received.transpose(1, 2, 0, 3).reshape(n, width)

    def index_of(a_at, t_at, z_at):
        return (a_at * t_size + t_at) * z_size + z_at

    def group_of(a_at, t_at, z_at):
        return index_of(a_at, t_at, z_at) * share // group_width

    def turned_of(a_at, t_at, z_at):
        return (a_at * z_size + z_at) * t_size + t_at

    (arrived,) = swap_all(sizes, 1, [by_group(features[0])], [group_of])
    packed = arrived.reshape(rows, frames // PACK, PACK * group_width)
    packed = packed.transpose(1, 0, 2).reshape(frames // PACK * rows, PACK * group_width)
    grid = kernel_weight.reshape(share, taps, group_width)
    conv_pre, even, odd = conv_forward_packed(
        packed,
        bounds,
        shifted_taps(grid.transpose(1, 2, 0)),
        jnp.tile(widened(position_bias), PACK)[None],
    )

    def by_block(channels):
        channels = channels.reshape(z_size, packs, rows, PACK * share)
        return channels.transpose(2, 0, 1, 3).reshape(devices, packs, PACK * share)

    (pre_parts,) = swap_all(sizes, 2, [by_block(conv_pre)], [turned_of])
    pre = widened(from_channels(pre_parts))
    own_feats = lax.ppermute(features[0], ("t", "z"), turn)
    own_cot = lax.ppermute(cotangent[0], ("t", "z"), turn)
    mixed = widened(own_feats) + gelu_exact(pre)
    hidden = layer_norm(mixed, entry_full, base_full)

    saved = []
    for layer in range(layers):
        gathered_x, qkv, weights_low, context, residual, middle = attention_forward(
            hidden,
            seg_col,
            seg_row,
            query_full[layer : layer + 1],
            value_full[layer : layer + 1],
            vector_of(0, layer),
            vector_of(1, layer),
            vector_of(2, layer),
            attend_pieces[layer],
            sizes,
            10 + 4 * layer,
        )
        gathered_m, active, slope, outer, hidden = feed_forward(
            middle,
            hidden_full[layer : layer + 1],
            vector_of(3, layer),
            vector_of(4, layer),
            vector_of(5, layer),
            feed_pieces[layer],
            sizes,
            11 + 4 * layer,
        )
        saved.append((gathered_x, qkv, weights_low, context, residual, gathered_m, active, slope, outer))
    final_low = rounded(hidden)
    logits = dot_rt(final_low, head_turned) + widened(vocab_bias)
    logits = lax.ppermute(logits, ("t", "z"), turn)
    vocab_sum = jnp.sum(widened(own_cot), axis=0)
    head_part = dot_lt(final_low, own_cot)
    flow = dot(own_cot, head_turned)

    layer_sums = [None] * layers
    token_sums = [None] * layers
    column_sums = [None] * layers
    for layer in reversed(range(layers)):
        gathered_x, qkv, weights_low, context, residual, gathered_m, active, slope, outer = saved[layer]
        res_grad, feed_parts, feed_vectors, hidden_part = feed_backward(
            flow,
            outer,
            residual,
            vector_of(4, layer),
            vector_of(1, layer),
            gathered_m,
            active,
            slope,
            feed_pieces[layer],
            sizes,
            12 + 4 * layer,
        )
        flow, attend_parts, attend_vectors, joint_part = attention_backward(
            res_grad, gathered_x, qkv, weights_low, context, attend_pieces[layer], sizes, 13 + 4 * layer
        )
        token_sums[layer] = jnp.concatenate([attend_vectors[0:1], feed_vectors[0:5]], axis=0)
        column_sums[layer] = jnp.concatenate(
            [
                joint_part[:, :part].reshape(a_size, z_size, share),
                joint_part[:, 2 * part :].reshape(a_size, z_size, share),
                hidden_part.reshape(a_size, z_size, inner_share),
            ],
            axis=-1,
        )
        layer_sums[layer] = (reduce_pieces(attend_parts, sizes), reduce_pieces(feed_parts, sizes))

    mixed_grad, entry_part, base_part = normed_back(mixed, entry_full, flow)
    slope = gelu_pair(pre)[1]
    conv_low = rounded(mixed_grad * slope)
    (low_parts,) = swap_all(sizes, 3, [by_group(conv_low)], [group_of])
    low_parts = low_parts.reshape(a_size, t_size, z_size, packs, PACK * group_width)
    packed_low = low_parts.transpose(1, 3, 0, 2, 4).reshape(frames // PACK * rows, PACK * group_width)
    half = lax.rem(z, 2)
    own_low = lax.dynamic_index_in_dim(
        packed_low.reshape(-1, PACK, group_width // share, share), half, 2, keepdims=False
    ).reshape(-1, PACK * share)
    halves = grid.reshape(share, taps, 2, share)
    kept = lax.dynamic_index_in_dim(halves, half, 2, keepdims=False)
    given = lax.ppermute(
        lax.dynamic_index_in_dim(halves, 1 - half, 2, keepdims=False), "z", pairs_of(z_size, 1)
    )
    both = jnp.where(half == 0, jnp.stack([kept, given]), jnp.stack([given, kept]))
    both = both.reshape(2 * share, taps, share).transpose(1, 0, 2)
    both = jnp.pad(both[::-1], ((1, 0), (0, 0), (0, 0)))
    feats_part, kernel_own, position_part = conv_backward_packed(
        packed_low, own_low, bounds, shifted_taps(both), even, odd
    )
    position_own = jnp.sum(position_part.reshape(PACK, share), axis=0)

    vector_sums = jnp.concatenate([entry_part, base_part] + token_sums, axis=0)
    vector_sums = vector_sums.reshape(vector_count, devices, share).transpose(1, 0, 2)
    vector_sums = vector_sums.reshape(devices, vector_count * share)
    column_all = jnp.concatenate(column_sums, axis=-1)
    mine = (jnp.arange(t_size) == t)[None, :, None, None]
    column_all = jnp.where(mine, column_all[:, None], 0.0).reshape(devices, -1)
    flat = jnp.concatenate(
        [
            vector_sums,
            column_all,
            jnp.broadcast_to(vocab_sum[None], (devices, vocab)),
        ],
        axis=1,
    )
    room = -flat.shape[1] % 1024
    flat = jnp.pad(flat, ((0, 0), (0, room)))
    flat = jnp.concatenate([flat, head_part.reshape(devices, share * vocab)], axis=1)
    flat = flat.reshape(devices, -1, 128)
    feats_back, sums = swap_all(
        sizes, 4, [by_block(feats_part), flat], [index_of, index_of]
    )
    features_grad = lax.ppermute(mixed_grad, ("t", "z"), turn) + widened(from_channels(feats_back))
    sums = jnp.sum(sums, axis=0).reshape(-1)
    at = vector_count * share
    vector_own = sums[:at].reshape(vector_count, share)
    column_own = sums[at : at + layers * (2 * share + inner_share)].reshape(layers, -1)
    at += layers * (2 * share + inner_share)
    vocab_own = sums[at : at + vocab]
    head_own = sums[-share * vocab :].reshape(share, vocab)

    back_columns = jnp.stack(
        [
            jnp.concatenate(
                [
                    attend_sum[:, : 3 * part].reshape(t_size, share, 3 * part),
                    feed_sum[: t_size * share].reshape(t_size, share, inner),
                ],
                axis=-1,
            )
            for attend_sum, feed_sum in layer_sums
        ],
        axis=1,
    )
    back_columns = widened(lax.all_to_all(rounded(back_columns), "t", 0, 0, tiled=True))
    joint_own = back_columns[..., : 3 * part].reshape(t_size, layers, share, 3, a_size, part // a_size)
    joint_own = joint_own.transpose(1, 2, 3, 4, 0, 5).reshape(layers, share, 3 * width)
    expand_own = back_columns[..., 3 * part :].reshape(t_size, layers, share, a_size, inner // a_size)
    expand_own = expand_own.transpose(1, 2, 3, 0, 4).reshape(layers, share, inner_all)
    output_own = jnp.stack(
        [
            attend_sum[:, 3 * part :].reshape(t_size, share, part).transpose(1, 0, 2).reshape(share, width)
            for attend_sum, _ in layer_sums
        ]
    )
    reduce_own = jnp.stack([feed_sum[t_size * share :] for _, feed_sum in layer_sums])
    per_layer = vector_own[2:].reshape(layers, 6, share)
    return (
        logits[None],
        features_grad[None],
        kernel_own,
        position_own,
        vector_own[0],
        vector_own[1],
        joint_own,
        column_own[:, :share],
        column_own[:, share : 2 * share],
        output_own,
        per_layer[:, 0],
        per_layer[:, 4],
        per_layer[:, 5],
        expand_own,
        column_own[:, 2 * share :],
        reduce_own,
        per_layer[:, 3],
        per_layer[:, 1],
        per_layer[:, 2],
        head_own,
        vocab_own,
    )


def fits(dp_size, seq_size, width):
    head = width // HEADS
    if seq_size != 4 or dp_size % 4:
        return None
    devices = dp_size * seq_size
    share = width // devices
    a_size = dp_size // 4
    if share % 16 or share * 2 != width // CONV_G or (seq_size * share) % head:
        return None
    return (a_size, 4, seq_size)


def placed(mesh, width):
    sizes = fits(mesh.shape["dp"], mesh.shape["seq"], width)
    if sizes is None:
        body, split, over, within = local, "dp", "seq", ("dp", "seq")
    else:
        body = functools.partial(fast_local, sizes)
        mesh = jax.sharding.Mesh(mesh.devices.reshape(sizes), AXES)
        split, over, within = ("a", "t"), "z", AXES
    tokens = P(split, over, None)
    first, first_wide = P(within), P(within, None)
    second, second_wide = P(None, within), P(None, within, None)
    return jax.shard_map(
        body,
        mesh=mesh,
        in_specs=(
            tokens,
            P(split, None),
            first_wide,
            first,
            first,
            first,
            second_wide,
            second,
            second,
            second_wide,
            second,
            second,
            second,
            second_wide,
            second,
            second_wide,
            second,
            second,
            second,
            first_wide,
            P(),
            tokens,
        ),
        out_specs=(
            tokens,
            tokens,
            first_wide,
            first,
            first,
            first,
            second_wide,
            second,
            second,
            second_wide,
            second,
            second,
            second,
            second_wide,
            second,
            second_wide,
            second,
            second,
            second,
            first_wide,
            P(),
        ),
        check_vma=False,
    )


def solution(mesh):
    def whole(*arguments):
        return placed(mesh, arguments[0].shape[2])(*arguments)

    return whole
```

```python
import itertools
import math

import jax
import jax.numpy as jnp
from jax import lax
from jax.experimental import pallas as pl
from jax.experimental.pallas import tpu as pltpu
from jax.sharding import PartitionSpec as P

HEADS = 16
CONV_G = 16


epsilon = 1e-05
masked_score = -1e30


def with_halo(cells, sides, width):
    for axis, dim in sides:
        count = lax.axis_size(axis)
        ends = count - 1
        head = lax.slice_in_dim(cells, 0, width, axis=dim)
        tail = lax.slice_in_dim(cells, cells.shape[dim] - width, cells.shape[dim], axis=dim)
        cells = jnp.concatenate(
            [
                lax.ppermute(tail, axis, [(i, (i + 1) % count) for i in range(ends)]),
                cells,
                lax.ppermute(head, axis, [((i + 1) % count, i) for i in range(ends)]),
            ],
            axis=dim,
        )
    return cells


def layer_norm(tensor, scaling, shifts):
    average = jnp.mean(tensor, axis=-1, keepdims=True)
    centred = tensor - average
    spread = jnp.mean(centred * centred, axis=-1, keepdims=True)
    return centred * lax.rsqrt(spread + epsilon) * scaling + shifts


def norm_pullback(tensor, scaling, upstream):
    _, pullback = jax.vjp(layer_norm, tensor, scaling, jnp.zeros_like(scaling))
    return pullback(upstream)


def gelu_exact(tensor):
    return jax.nn.gelu(tensor, approximate=False)


def rounded(tensor):
    return tensor.astype(jnp.bfloat16)


def widened(tensor):
    return tensor.astype(jnp.float32)


def segment_ids(positions, utterance_ends):
    return jnp.sum(
        (positions[None, :, None] >= utterance_ends[:, None, :]).astype(jnp.int32), axis=2
    )


def unfold(source, source_ids, target_ids, anchors):
    length = target_ids.shape[1]
    pieces = [lax.slice_in_dim(source, anchor, anchor + length, axis=1) for anchor in anchors]
    matches = [
        lax.slice_in_dim(source_ids, anchor, anchor + length, axis=1) == target_ids
        for anchor in anchors
    ]
    stacked = jnp.stack(pieces, axis=2)
    keepers = jnp.stack(matches, axis=2)
    return jnp.where(keepers[..., None], stacked, jnp.zeros_like(stacked))


def conv_forward(halo_feats, halo_ids, frame_ids, kernel_grid, tap_block):
    row_count, frame_count = frame_ids.shape
    groups, group_width, tap_count, inner_width = kernel_grid.shape
    summed = jnp.zeros((row_count, frame_count, groups, group_width), jnp.float32)
    for block_at in range(tap_count // tap_block):
        first_tap = block_at * tap_block
        window = unfold(
            halo_feats,
            halo_ids,
            frame_ids,
            [first_tap + inner_tap for inner_tap in range(tap_block)],
        )
        window = window.reshape(row_count, frame_count, tap_block, groups, inner_width)
        summed = summed + jnp.einsum(
            "rtkgi,goki->rtgo",
            window,
            kernel_grid[:, :, first_tap : first_tap + tap_block, :],
            preferred_element_type=jnp.float32,
        )
    return summed.reshape(row_count, frame_count, groups * group_width)


def conv_backward(halo_grads, halo_feats, halo_ids, frame_ids, kernel_grid, tap_block, conv_low):
    row_count, frame_count = frame_ids.shape
    groups, group_width, tap_count, inner_width = kernel_grid.shape
    input_part = jnp.zeros((row_count, frame_count, groups, inner_width), jnp.float32)
    grouped = conv_low.reshape(row_count, frame_count, groups, group_width)
    kernel_parts = []
    for block_at in range(tap_count // tap_block):
        first_tap = block_at * tap_block
        tap_list = [first_tap + inner_tap for inner_tap in range(tap_block)]
        grads_window = unfold(
            halo_grads, halo_ids, frame_ids, [tap_count - tap_at for tap_at in tap_list]
        )
        grads_window = grads_window.reshape(row_count, frame_count, tap_block, groups, group_width)
        input_part = input_part + jnp.einsum(
            "rtkgo,goki->rtgi",
            grads_window,
            kernel_grid[:, :, first_tap : first_tap + tap_block, :],
            preferred_element_type=jnp.float32,
        )
        feats_window = unfold(halo_feats, halo_ids, frame_ids, tap_list)
        feats_window = feats_window.reshape(row_count, frame_count, tap_block, groups, inner_width)
        kernel_parts.append(
            jnp.einsum(
                "rtgo,rtkgi->goki", grouped, feats_window, preferred_element_type=jnp.float32
            )
        )
    kernel_full = jnp.concatenate(kernel_parts, axis=2).reshape(
        groups * group_width, tap_count * inner_width
    )
    return (input_part.reshape(row_count, frame_count, groups * inner_width), kernel_full)


def split_heads(tensor, head_count):
    return tensor.reshape(
        tensor.shape[0], tensor.shape[1], head_count, tensor.shape[2] // head_count
    )


def attend_scores(queries, all_keys, query_ids, key_ids, head_count):
    scores = jnp.einsum(
        "rqhd,rkhd->rhqk",
        split_heads(queries, head_count),
        split_heads(all_keys, head_count),
        preferred_element_type=jnp.float32,
    )
    allowed = query_ids[:, None, :, None] == key_ids[:, None, None, :]
    return jnp.where(allowed, scores, masked_score)


def attend_forward(queries, all_keys, all_values, frame_ids, row_ids, head_count):
    scores = attend_scores(queries, all_keys, frame_ids, row_ids, head_count)
    row_peak = jnp.max(scores, axis=-1, keepdims=True)
    exponent = jnp.exp(scores - row_peak)
    totals = jnp.sum(exponent, axis=-1, keepdims=True)
    weights_low = rounded(exponent / totals)
    context = jnp.einsum(
        "rhqk,rkhd->rqhd",
        weights_low,
        split_heads(all_values, head_count),
        preferred_element_type=jnp.float32,
    )
    return (rounded(context.reshape(queries.shape)), row_peak + jnp.log(totals))


def attend_backward(
    queries, all_keys, all_values, frame_ids, row_ids, head_count, log_totals, context_low
):
    scores = attend_scores(queries, all_keys, frame_ids, row_ids, head_count)
    attention = jnp.exp(scores - log_totals)
    weights_low = rounded(attention)
    grad_heads = split_heads(context_low, head_count)
    prob_grad = jnp.einsum(
        "rqhd,rkhd->rhqk",
        grad_heads,
        split_heads(all_values, head_count),
        preferred_element_type=jnp.float32,
    )
    row_delta = jnp.sum(attention * prob_grad, axis=-1, keepdims=True)
    score_grad = rounded(attention * (prob_grad - row_delta))
    value_part = jnp.einsum(
        "rhqk,rqhd->rkhd", weights_low, grad_heads, preferred_element_type=jnp.float32
    )
    query_part = jnp.einsum(
        "rhqk,rkhd->rqhd",
        score_grad,
        split_heads(all_keys, head_count),
        preferred_element_type=jnp.float32,
    )
    key_part = jnp.einsum(
        "rhqk,rqhd->rkhd",
        score_grad,
        split_heads(queries, head_count),
        preferred_element_type=jnp.float32,
    )
    return (
        query_part.reshape(queries.shape),
        key_part.reshape(all_keys.shape),
        value_part.reshape(all_values.shape),
    )


def local(
    features,
    utterance_ends,
    kernel_weight,
    position_bias,
    entry_gain,
    base_shift,
    joint_weight,
    query_bias,
    value_bias,
    output_weight,
    attend_bias,
    middle_gain,
    lower_shift,
    expand_weight,
    hidden_bias,
    reduce_weight,
    return_bias,
    final_gain,
    upper_shift,
    head_weight,
    vocab_bias,
    cotangent,
):
    row_count, frame_count, model_dim = features.shape
    frames_all = frame_count * lax.axis_size("seq")
    groups = CONV_G
    group_width = model_dim // groups
    tap_count = kernel_weight.shape[1] // group_width
    half_taps = tap_count // 2
    tap_block = math.gcd(tap_count, 16)
    head_count = HEADS
    query_scale = (model_dim // head_count) ** (-0.5)
    layer_count = joint_weight.shape[0]
    rows_share = model_dim // lax.axis_size(("dp", "seq"))
    anchor = lax.axis_index("seq") * frame_count
    frame_ids = segment_ids(anchor + jnp.arange(frame_count, dtype=jnp.int32), utterance_ends)
    row_ids = segment_ids(jnp.arange(frames_all, dtype=jnp.int32), utterance_ends)
    halo_place = anchor - half_taps + jnp.arange(frame_count + tap_count, dtype=jnp.int32)
    inside = (halo_place >= 0) & (halo_place < frames_all)
    halo_ids = jnp.where(inside[None, :], segment_ids(halo_place, utterance_ends), -1)
    stem = (
        lax.all_gather(kernel_weight, ("dp", "seq"), axis=0, tiled=True),
        lax.all_gather(position_bias, ("dp", "seq"), axis=0, tiled=True),
        lax.all_gather(entry_gain, ("dp", "seq"), axis=0, tiled=True),
        lax.all_gather(base_shift, ("dp", "seq"), axis=0, tiled=True),
        lax.all_gather(head_weight, ("dp", "seq"), axis=0, tiled=True),
    )
    kernel_grid = stem[0].reshape(groups, group_width, tap_count, group_width)
    halo_feats = with_halo(features, (("seq", 1),), half_taps)
    conv_pre = conv_forward(halo_feats, halo_ids, frame_ids, kernel_grid, tap_block) + widened(
        stem[1]
    )
    mixed = widened(features) + gelu_exact(conv_pre)
    hidden = layer_norm(mixed, widened(stem[2]), widened(stem[3]))
    saved = []
    for layer_at in range(layer_count):
        (
            joint_full,
            query_full,
            value_full,
            output_full,
            attend_full,
            middle_full,
            lower_full,
            expand_full,
            hidden_full,
            reduce_full,
            return_full,
            final_full,
            upper_full,
        ) = (
            lax.all_gather(joint_weight[layer_at], ("dp", "seq"), axis=0, tiled=True),
            lax.all_gather(query_bias[layer_at], ("dp", "seq"), axis=0, tiled=True),
            lax.all_gather(value_bias[layer_at], ("dp", "seq"), axis=0, tiled=True),
            lax.all_gather(output_weight[layer_at], ("dp", "seq"), axis=0, tiled=True),
            lax.all_gather(attend_bias[layer_at], ("dp", "seq"), axis=0, tiled=True),
            lax.all_gather(middle_gain[layer_at], ("dp", "seq"), axis=0, tiled=True),
            lax.all_gather(lower_shift[layer_at], ("dp", "seq"), axis=0, tiled=True),
            lax.all_gather(expand_weight[layer_at], ("dp", "seq"), axis=0, tiled=True),
            lax.all_gather(hidden_bias[layer_at], ("dp", "seq"), axis=0, tiled=True),
            lax.all_gather(reduce_weight[layer_at], ("dp", "seq"), axis=0, tiled=True),
            lax.all_gather(return_bias[layer_at], ("dp", "seq"), axis=0, tiled=True),
            lax.all_gather(final_gain[layer_at], ("dp", "seq"), axis=0, tiled=True),
            lax.all_gather(upper_shift[layer_at], ("dp", "seq"), axis=0, tiled=True),
        )
        inputs_low = rounded(hidden)
        joint_out = jnp.einsum(
            "rtd,de->rte", inputs_low, joint_full, preferred_element_type=jnp.float32
        )
        queries = rounded((joint_out[..., :model_dim] + widened(query_full)) * query_scale)
        keys_local = rounded(joint_out[..., model_dim : 2 * model_dim])
        values_local = rounded(joint_out[..., 2 * model_dim :] + widened(value_full))
        all_keys, all_values = (
            lax.all_gather(keys_local, "seq", axis=1, tiled=True),
            lax.all_gather(values_local, "seq", axis=1, tiled=True),
        )
        context, log_totals = attend_forward(
            queries, all_keys, all_values, frame_ids, row_ids, head_count
        )
        attended = jnp.einsum(
            "rtc,cd->rtd", context, output_full, preferred_element_type=jnp.float32
        ) + widened(attend_full)
        residual_one = hidden + attended
        middle = layer_norm(residual_one, widened(middle_full), widened(lower_full))
        middle_low = rounded(middle)
        inner_pre = jnp.einsum(
            "rtd,df->rtf", middle_low, expand_full, preferred_element_type=jnp.float32
        ) + widened(hidden_full)
        activated = rounded(gelu_exact(inner_pre))
        outer = (
            middle
            + jnp.einsum("rtf,fd->rtd", activated, reduce_full, preferred_element_type=jnp.float32)
            + widened(return_full)
        )
        kept_weights = None
        saved.append(
            (
                inputs_low,
                queries,
                all_keys,
                all_values,
                log_totals,
                context,
                residual_one,
                middle_low,
                inner_pre,
                activated,
                outer,
                kept_weights,
            )
        )
        hidden = layer_norm(outer, widened(final_full), widened(upper_full))
    final_low = rounded(hidden)
    logits = jnp.einsum(
        "rtd,dv->rtv", final_low, stem[4], preferred_element_type=jnp.float32
    ) + widened(vocab_bias)
    back_stem = (
        lax.all_gather(kernel_weight, ("dp", "seq"), axis=0, tiled=True),
        lax.all_gather(entry_gain, ("dp", "seq"), axis=0, tiled=True),
        lax.all_gather(head_weight, ("dp", "seq"), axis=0, tiled=True),
    )
    vocab_sum = jnp.sum(widened(cotangent), axis=(0, 1))
    head_part = jnp.einsum("rtd,rtv->dv", final_low, cotangent, preferred_element_type=jnp.float32)
    flow_grad = jnp.einsum(
        "rtv,dv->rtd", cotangent, back_stem[2], preferred_element_type=jnp.float32
    )
    layer_grads = [None] * layer_count
    for layer_at in reversed(range(layer_count)):
        (
            inputs_low,
            queries,
            all_keys,
            all_values,
            log_totals,
            context,
            residual_one,
            middle_low,
            inner_pre,
            activated,
            outer,
            kept_weights,
        ) = saved[layer_at]
        back_weights = (
            lax.all_gather(joint_weight[layer_at], ("dp", "seq"), axis=0, tiled=True),
            lax.all_gather(output_weight[layer_at], ("dp", "seq"), axis=0, tiled=True),
            lax.all_gather(expand_weight[layer_at], ("dp", "seq"), axis=0, tiled=True),
            lax.all_gather(reduce_weight[layer_at], ("dp", "seq"), axis=0, tiled=True),
            lax.all_gather(middle_gain[layer_at], ("dp", "seq"), axis=0, tiled=True),
            lax.all_gather(final_gain[layer_at], ("dp", "seq"), axis=0, tiled=True),
        )
        joint_full, output_full, expand_full, reduce_full, middle_full, final_full = back_weights
        outer_grad, final_part, upper_part = norm_pullback(outer, widened(final_full), flow_grad)
        fed_low = rounded(outer_grad)
        return_part = jnp.sum(widened(fed_low), axis=(0, 1))
        active_grad = jnp.einsum(
            "rtd,fd->rtf", fed_low, reduce_full, preferred_element_type=jnp.float32
        )
        _, gelu_pull = jax.vjp(gelu_exact, inner_pre)
        (inner_grad,) = gelu_pull(active_grad)
        inner_low = rounded(inner_grad)
        hidden_part = jnp.sum(widened(inner_low), axis=(0, 1))
        middle_flow = outer_grad + jnp.einsum(
            "rtf,df->rtd", inner_low, expand_full, preferred_element_type=jnp.float32
        )
        residual_grad, middle_part, lower_part = norm_pullback(
            residual_one, widened(middle_full), middle_flow
        )
        attended_low = rounded(residual_grad)
        attend_part = jnp.sum(widened(attended_low), axis=(0, 1))
        context_low = rounded(
            jnp.einsum("rtd,cd->rtc", attended_low, output_full, preferred_element_type=jnp.float32)
        )
        query_raw, key_raw, value_raw = attend_backward(
            queries, all_keys, all_values, frame_ids, row_ids, head_count, log_totals, context_low
        )
        key_sum, value_sum = (
            lax.psum_scatter(
                key_raw.astype(jnp.bfloat16), "seq", scatter_dimension=1, tiled=True
            ).astype(jnp.float32),
            lax.psum_scatter(
                value_raw.astype(jnp.bfloat16), "seq", scatter_dimension=1, tiled=True
            ).astype(jnp.float32),
        )
        query_low = rounded(widened(rounded(query_raw)) * query_scale)
        key_low = rounded(key_sum)
        value_low = rounded(value_sum)
        query_part = jnp.sum(widened(query_low), axis=(0, 1))
        value_part = jnp.sum(widened(value_low), axis=(0, 1))
        joint_low = jnp.concatenate([query_low, key_low, value_low], axis=-1)
        flow_grad = residual_grad + jnp.einsum(
            "rte,de->rtd", joint_low, joint_full, preferred_element_type=jnp.float32
        )
        ratio = hidden_part.shape[0] // model_dim
        vector_rows = jnp.stack(
            [
                query_part,
                value_part,
                attend_part,
                middle_part,
                lower_part,
                return_part,
                final_part,
                upper_part,
            ],
            axis=1,
        )
        hidden_rows = hidden_part.reshape(model_dim, ratio)

        def layer_term(
            start,
            count,
            inputs_low=inputs_low,
            joint_low=joint_low,
            context=context,
            attended_low=attended_low,
            middle_low=middle_low,
            inner_low=inner_low,
            activated=activated,
            fed_low=fed_low,
            vector_rows=vector_rows,
            hidden_rows=hidden_rows,
            ratio=ratio,
        ):
            joint_rows = jnp.einsum(
                "rtd,rte->de", inputs_low, joint_low, preferred_element_type=jnp.float32
            )
            output_rows = jnp.einsum(
                "rtc,rtd->cd", context, attended_low, preferred_element_type=jnp.float32
            )
            expand_rows = jnp.einsum(
                "rtd,rtf->df", middle_low, inner_low, preferred_element_type=jnp.float32
            )
            reduce_rows = jnp.einsum(
                "rtf,rtd->fd", activated, fed_low, preferred_element_type=jnp.float32
            ).reshape(count, ratio * model_dim)
            return jnp.concatenate(
                [joint_rows, output_rows, expand_rows, reduce_rows, vector_rows, hidden_rows],
                axis=1,
            )

        summed = lax.psum_scatter(
            layer_term(jnp.int32(0), rows_share * lax.axis_size(("dp", "seq"))),
            ("dp", "seq"),
            scatter_dimension=0,
            tiled=True,
        )
        ff_width = ratio * model_dim
        first = 3 * model_dim
        second = first + model_dim
        third = second + ff_width
        fourth = third + ratio * model_dim
        joint_own = summed[:, :first]
        output_own = summed[:, first:second]
        expand_own = summed[:, second:third]
        reduce_own = summed[:, third:fourth].reshape(rows_share * ratio, model_dim)
        vector_own = summed[:, fourth : fourth + 8]
        hidden_own = summed[:, fourth + 8 :].reshape(rows_share * ratio)
        layer_grads[layer_at] = (
            joint_own,
            vector_own[:, 0],
            vector_own[:, 1],
            output_own,
            vector_own[:, 2],
            vector_own[:, 3],
            vector_own[:, 4],
            expand_own,
            hidden_own,
            reduce_own,
            vector_own[:, 5],
            vector_own[:, 6],
            vector_own[:, 7],
        )
    mixed_grad, entry_part, base_part = norm_pullback(mixed, widened(back_stem[1]), flow_grad)
    _, gelu_pull = jax.vjp(gelu_exact, conv_pre)
    (conv_grad,) = gelu_pull(mixed_grad)
    conv_low = rounded(conv_grad)
    position_part = jnp.sum(widened(conv_low), axis=(0, 1))
    halo_grads = with_halo(conv_low, (("seq", 1),), half_taps)
    back_grid = back_stem[0].reshape(groups, group_width, tap_count, group_width)
    input_part, kernel_part = conv_backward(
        halo_grads, halo_feats, halo_ids, frame_ids, back_grid, tap_block, conv_low
    )
    features_grad = mixed_grad + input_part
    vocab_tiled = jnp.tile(vocab_sum, lax.axis_size(("dp", "seq")))
    stem_sums = (
        lax.psum_scatter(kernel_part, ("dp", "seq"), scatter_dimension=0, tiled=True),
        lax.psum_scatter(position_part, ("dp", "seq"), scatter_dimension=0, tiled=True),
        lax.psum_scatter(entry_part, ("dp", "seq"), scatter_dimension=0, tiled=True),
        lax.psum_scatter(base_part, ("dp", "seq"), scatter_dimension=0, tiled=True),
        lax.psum_scatter(head_part, ("dp", "seq"), scatter_dimension=0, tiled=True),
        lax.psum_scatter(vocab_tiled, ("dp", "seq"), scatter_dimension=0, tiled=True),
    )
    stacked = [
        jnp.stack([layer_grads[layer_at][member] for layer_at in range(layer_count)])
        for member in range(13)
    ]
    return (
        logits,
        features_grad,
        stem_sums[0],
        stem_sums[1],
        stem_sums[2],
        stem_sums[3],
        stacked[0],
        stacked[1],
        stacked[2],
        stacked[3],
        stacked[4],
        stacked[5],
        stacked[6],
        stacked[7],
        stacked[8],
        stacked[9],
        stacked[10],
        stacked[11],
        stacked[12],
        stem_sums[4],
        stem_sums[5],
    )


MESH_ID = pl.DeviceIdType.MESH
IN_VMEM = pl.BlockSpec(memory_space=pltpu.VMEM)
ANYWHERE = pl.BlockSpec(memory_space=pl.ANY)
AXES = ("y", "x", "c", "h", "l")
PACK = 8
RANKS = 4


def kernel_params(collective=None):
    if collective is None:
        return pltpu.CompilerParams(vmem_limit_bytes=56 * 2**20)
    return pltpu.CompilerParams(
        vmem_limit_bytes=56 * 2**20, collective_id=collective, has_side_effects=True
    )


def cost(micros):
    return pl.CostEstimate(flops=int(micros * 1.1e9), bytes_accessed=2**20, transcendentals=0)


def greet(peers):
    gate = pltpu.get_barrier_semaphore()
    for peer in peers:
        pl.semaphore_signal(gate, inc=1, device_id=peer, device_id_type=MESH_ID)
    pl.semaphore_wait(gate, len(peers))


def remote(source, target, send, receive, peer):
    return pltpu.make_async_remote_copy(
        source, target, send, receive, device_id=peer, device_id_type=MESH_ID
    )


def bits():
    return tuple(lax.axis_index(axis) for axis in AXES)


def index_of(y, x, c, h, l):
    return y * 16 + x * 8 + c * 4 + h * 2 + l


def turned_of(y, x, c, h, l):
    return index_of(y, h, c, x, l)


def group_of(y, x, c, h, l):
    return index_of(y, x, c, h, l) // 2


def flipped(mask):
    return {
        axis: 1 - lax.axis_index(axis)
        for number, axis in enumerate(AXES)
        if mask >> (len(AXES) - 1 - number) & 1
    }


def swap_all(collective, payloads):
    count = len(payloads)
    total = 2 ** len(AXES)

    def shape_of(array, kind):
        if kind == "group" or kind == "twist":
            return array.shape
        return (total,) + array.shape[1:]

    def kernel(*refs):
        sources, targets = refs[:count], refs[count : 2 * count]
        sends, receives, own_sems = refs[2 * count :]
        y, x, c, h, l = bits()
        me = index_of(y, x, c, h, l)
        t = x * 2 + l
        peers = [flipped(mask) for mask in range(1, total)]
        greet(peers)
        copies = []
        for p, (_, kind) in enumerate(payloads):
            if kind == "twist":

                @pl.when(h == l)
                def _(p=p):
                    pltpu.make_async_copy(sources[p], targets[p], own_sems.at[p]).start()

                @pl.when(h != l)
                def _(p=p):
                    remote(
                        sources[p], targets[p], sends.at[p, 0], receives.at[p, 0], flipped(3)
                    ).start()

                continue
            own = sources[p].at[t] if kind == "group" else sources[p].at[kind(y, x, c, h, l)]
            slot = t if kind == "group" else me
            copy = pltpu.make_async_copy(own, targets[p].at[slot], own_sems.at[p])
            copy.start()
            copies.append(copy)
            masks = (1, 8, 9) if kind == "group" else range(1, total)
            for number, mask in enumerate(masks):
                peer = flipped(mask)
                place = [peer.get(axis, here) for axis, here in zip(AXES, (y, x, c, h, l))]
                wanted = place[1] * 2 + place[4] if kind == "group" else kind(*place)
                copy = remote(
                    sources[p].at[wanted],
                    targets[p].at[slot],
                    sends.at[p, number],
                    receives.at[p, number],
                    peer,
                )
                copy.start()
                copies.append(copy)
        for copy in copies:
            copy.wait()
        for p, (_, kind) in enumerate(payloads):
            if kind == "twist":

                @pl.when(h == l)
                def _(p=p):
                    pltpu.make_async_copy(sources[p], targets[p], own_sems.at[p]).wait()

                @pl.when(h != l)
                def _(p=p):
                    remote(
                        sources[p], targets[p], sends.at[p, 0], receives.at[p, 0], flipped(3)
                    ).wait()

    return pl.pallas_call(
        kernel,
        out_shape=[
            jax.ShapeDtypeStruct(shape_of(array, kind), array.dtype) for array, kind in payloads
        ],
        in_specs=[ANYWHERE] * count,
        out_specs=[ANYWHERE] * count,
        scratch_shapes=[
            pltpu.SemaphoreType.DMA((count, total - 1)),
            pltpu.SemaphoreType.DMA((count, total - 1)),
            pltpu.SemaphoreType.DMA((count,)),
        ],
        compiler_params=kernel_params(collective),
        cost_estimate=cost(20),
    )(*[array for array, _ in payloads])


def rank_lanes(bounds_ref, rows, width):
    lanes = PACK * width
    line = lax.broadcasted_iota(jnp.int32, (rows, lanes), 0) // PACK
    lane = lax.broadcasted_iota(jnp.int32, (rows, lanes), 1) // width
    frame = line * PACK + lane
    rank = jnp.zeros((rows, lanes), jnp.int32)
    for slot in range(bounds_ref.shape[1]):
        rank = rank + (frame >= bounds_ref[:, slot : slot + 1]).astype(jnp.int32)
    return rank


def spread_ranks(wide, packed, rank, first):
    rows = packed.shape[0]
    wide[...] = jnp.zeros_like(wide)
    for number in range(RANKS):
        place = pl.ds(first + number * 64, rows)
        wide[place, :] += jnp.where(rank == number, packed, 0.0)


def collect_ranks(summed, rank, rows):
    result = jnp.zeros((rows, summed.shape[1]), jnp.float32)
    for number in range(RANKS):
        result = jnp.where(rank == number, summed[number * 64 : number * 64 + rows, :], result)
    return result


def toeplitz(even, odd, taps, length):
    total = None
    for step in range(taps.shape[0]):
        source = even if step % 2 == 0 else odd
        part = jnp.dot(
            source[pl.ds((step - step % 2) * 8, length), :],
            taps[step],
            preferred_element_type=jnp.float32,
        )
        total = part if total is None else total + part
    return total


def fill_pair(wide, even, odd):
    length = even.shape[0]
    even[...] = wide[:length, :].astype(jnp.bfloat16)
    odd[...] = wide[8 : 8 + length, :].astype(jnp.bfloat16)


def conv_forward_packed(packed, bounds, taps, bias):
    rows = packed.shape[0]
    length = rows + (RANKS - 1) * 64
    held = length + 128
    steps, depth, width = taps.shape

    def kernel(x_ref, b_ref, k_ref, bias_ref, o_ref, even, odd, wide):
        rank = rank_lanes(b_ref, rows, depth // PACK)
        spread_ranks(wide, x_ref[...].astype(jnp.float32), rank, 64)
        fill_pair(wide, even, odd)
        summed = toeplitz(even, odd, k_ref, length)
        rank_out = rank_lanes(b_ref, rows, width // PACK)
        o_ref[...] = (collect_ranks(summed, rank_out, rows) + bias_ref[...]).astype(jnp.bfloat16)

    return pl.pallas_call(
        kernel,
        out_shape=[
            jax.ShapeDtypeStruct((rows, width), jnp.bfloat16),
            jax.ShapeDtypeStruct((held, depth), jnp.bfloat16),
            jax.ShapeDtypeStruct((held, depth), jnp.bfloat16),
        ],
        in_specs=[IN_VMEM] * 4,
        out_specs=[IN_VMEM] * 3,
        scratch_shapes=[pltpu.VMEM((held + 16, depth), jnp.float32)],
        compiler_params=kernel_params(),
        cost_estimate=cost(10),
    )(packed, bounds, taps, bias)


def conv_backward_packed(packed, own, bounds, taps, even, odd):
    rows, depth = packed.shape
    length = rows + (RANKS - 1) * 64
    held = length + 128
    steps, _, width = taps.shape
    tap_count = (steps - 1) * PACK
    group_width = depth // PACK
    chans = width // PACK

    def kernel(g_ref, own_ref, b_ref, k_ref, even_ref, odd_ref, o_ref, w_ref, s_ref, ge, go, wide, turned):
        rank = rank_lanes(b_ref, rows, depth // PACK)
        spread_ranks(wide, g_ref[...].astype(jnp.float32), rank, 64)
        fill_pair(wide, ge, go)
        summed = toeplitz(ge, go, k_ref, length)
        rank_out = rank_lanes(b_ref, rows, width // PACK)
        o_ref[...] = collect_ranks(summed, rank_out, rows).astype(jnp.bfloat16)
        own_wide = own_ref[...].astype(jnp.float32)
        s_ref[...] = jnp.sum(own_wide, axis=0, keepdims=True)
        spread_ranks(wide.at[:length, :width], own_wide, rank_out, 0)
        across = wide[:length, :width].T.astype(jnp.bfloat16)
        for step in range(steps):
            source = even_ref if step % 2 == 0 else odd_ref
            turned[:, pl.ds(step * depth, depth)] = jnp.dot(
                across,
                source[pl.ds((step - step % 2) * 8, length), :],
                preferred_element_type=jnp.float32,
            )
        total = turned[0:chans, 0 : tap_count * group_width]
        for f in range(1, PACK):
            total = total + turned[
                f * chans : (f + 1) * chans,
                f * group_width : f * group_width + tap_count * group_width,
            ]
        w_ref[...] = total

    return pl.pallas_call(
        kernel,
        out_shape=[
            jax.ShapeDtypeStruct((rows, width), jnp.bfloat16),
            jax.ShapeDtypeStruct((chans, tap_count * group_width), jnp.float32),
            jax.ShapeDtypeStruct((1, width), jnp.float32),
        ],
        in_specs=[IN_VMEM] * 6,
        out_specs=[IN_VMEM] * 3,
        scratch_shapes=[
            pltpu.VMEM((held, depth), jnp.bfloat16),
            pltpu.VMEM((held, depth), jnp.bfloat16),
            pltpu.VMEM((held + 16, depth), jnp.float32),
            pltpu.VMEM((width, steps * depth), jnp.float32),
        ],
        compiler_params=kernel_params(),
        cost_estimate=cost(15),
    )(packed, own, bounds, taps, even, odd)


def shifted_taps(grid):
    taps, depth, width = grid.shape
    steps = 17
    room = steps * PACK
    parts = [
        jnp.pad(grid, ((f, room - taps - f), (0, 0), (0, 0))).reshape(room * depth, width)
        for f in range(PACK)
    ]
    return jnp.concatenate(parts, axis=1).reshape(steps, PACK * depth, PACK * width)


def normed(tensor, gain, shift):
    average = jnp.mean(tensor, axis=-1, keepdims=True)
    centred = tensor - average
    spread = jnp.mean(centred * centred, axis=-1, keepdims=True)
    return centred * lax.rsqrt(spread + epsilon) * gain + shift


def normed_back(tensor, gain, upstream):
    average = jnp.mean(tensor, axis=-1, keepdims=True)
    centred = tensor - average
    spread = jnp.mean(centred * centred, axis=-1, keepdims=True)
    inverse = lax.rsqrt(spread + epsilon)
    unit = centred * inverse
    scaled = upstream * gain
    result = inverse * (
        scaled
        - jnp.mean(scaled, axis=-1, keepdims=True)
        - unit * jnp.mean(scaled * unit, axis=-1, keepdims=True)
    )
    return (
        result,
        jnp.sum(upstream * unit, axis=0, keepdims=True),
        jnp.sum(upstream, axis=0, keepdims=True),
    )


def gelu_pair(tensor):
    half = 0.5 * (1.0 + lax.erf(tensor * (2.0**-0.5)))
    slope = half + tensor * (jnp.exp(-0.5 * tensor * tensor) * ((2.0 * math.pi) ** -0.5))
    return tensor * half, slope


def dot(left, right):
    return jnp.dot(left, right, preferred_element_type=jnp.float32)


def dot_rt(left, right):
    return lax.dot_general(left, right, (((1,), (1,)), ((), ())), preferred_element_type=jnp.float32)


def dot_lt(left, right):
    return lax.dot_general(left, right, (((0,), (0,)), ((), ())), preferred_element_type=jnp.float32)


X_BIT, L_BIT = 8, 1
H_BIT, Y_BIT, C_BIT = 2, 16, 4
PIECES = 8


def group_gather(block, t, sends, receives):
    half = block.shape[1] // 2
    x_peer, l_peer = flipped(X_BIT), flipped(L_BIT)
    own = block.at[t]
    to_x = remote(own, own, sends.at[0], receives.at[0], x_peer)
    to_x.start()
    to_l = remote(own, own, sends.at[1], receives.at[1], l_peer)
    to_l.start()
    to_x.wait_recv()
    other = block.at[lax.bitwise_xor(t, 2), pl.ds(0, half)]
    on_l = remote(other, other, sends.at[2], receives.at[2], l_peer)
    on_l.start()
    to_l.wait_recv()
    other = block.at[lax.bitwise_xor(t, 1), pl.ds(half, half)]
    on_x = remote(other, other, sends.at[3], receives.at[3], x_peer)
    on_x.start()
    on_l.wait_recv()
    on_x.wait_recv()
    for copy in (to_x, to_l, on_l, on_x):
        copy.wait_send()


def group_scatter(part, t, low, got, sends, receives, between=None):
    half = low.shape[1]
    x_peer, l_peer = flipped(X_BIT), flipped(L_BIT)

    def send(slot, value, peer):
        low[slot] = value.astype(jnp.bfloat16)
        copy = remote(low.at[slot], got.at[slot], sends.at[slot], receives.at[slot], peer)
        copy.start()
        return copy

    def arrived(slot):
        return got[slot].astype(jnp.float32)

    far = part(lax.bitwise_xor(t, 3))
    far_x = send(0, far[:half], x_peer)
    far_l = send(1, far[half:], l_peer)
    beside_x = part(lax.bitwise_xor(t, 2))
    near_x = send(2, beside_x[:half], x_peer)
    beside_l = part(lax.bitwise_xor(t, 1))
    near_l = send(3, beside_l[half:], l_peer)
    far_x.wait_recv()
    on_l = send(4, beside_l[:half] + arrived(0), l_peer)
    far_l.wait_recv()
    on_x = send(5, beside_x[half:] + arrived(1), x_peer)
    own = part(t)
    if between is not None:
        between()
    near_x.wait_recv()
    near_l.wait_recv()
    on_l.wait_recv()
    on_x.wait_recv()
    result = jnp.concatenate(
        [own[:half] + arrived(2) + arrived(4), own[half:] + arrived(3) + arrived(5)], axis=0
    )
    for copy in (far_x, far_l, near_x, near_l, on_l, on_x):
        copy.wait_send()
    return result


def group_scratch(n, width):
    return [
        pltpu.VMEM((6, n // 2, width), jnp.bfloat16),
        pltpu.VMEM((6, n // 2, width), jnp.bfloat16),
        pltpu.SemaphoreType.DMA((4,)),
        pltpu.SemaphoreType.DMA((4,)),
        pltpu.SemaphoreType.DMA((6,)),
        pltpu.SemaphoreType.DMA((6,)),
    ]


class Spread:
    def __init__(self, own, held, sends, receives, own_sem):
        self.own, self.held = own, held
        self.sends, self.receives, self.own_sem = sends, receives, own_sem
        y, _, c, h, _ = bits()
        self.me = c * 4 + y * 2 + h
        self.pair = c * 4 + y * 2
        self.four = c * 4

    def copy(self, step):
        pair, four = self.held.at[pl.ds(self.pair, 2)], self.held.at[pl.ds(self.four, 4)]
        source = (self.own, pair, four)[step]
        target = (self.held.at[self.me], pair, four)[step]
        peer = flipped((H_BIT, Y_BIT, C_BIT)[step])
        return remote(source, target, self.sends.at[step], self.receives.at[step], peer)

    def over_h(self):
        pltpu.make_async_copy(self.own, self.held.at[self.me], self.own_sem).start()
        self.copy(0).start()

    def over_y(self):
        pltpu.make_async_copy(self.own, self.held.at[self.me], self.own_sem).wait()
        self.copy(0).wait_recv()
        self.copy(1).start()

    def over_c(self):
        self.copy(1).wait_recv()
        self.copy(2).start()

    def done(self):
        for step in range(3):
            self.copy(step).wait_send()
        self.copy(2).wait_recv()


def slots():
    return [(c, y, h) for c in range(2) for y in range(2) for h in range(2)]


def load_rows(held, target, sem, share, column, width):
    for slot, (c, y, h) in enumerate(slots()):
        for x in range(2):
            pltpu.make_async_copy(
                held.at[slot, pl.ds(x * 2 * share, 2 * share), pl.ds(column, width)],
                target.at[pl.ds((y * 16 + x * 8 + c * 4 + h * 2) * share, 2 * share), :],
                sem,
            ).start()


def load_chunks(held, target, sem, share, column, width):
    for slot, (c, y, h) in enumerate(slots()):
        for chunk in range(4):
            pltpu.make_async_copy(
                held.at[slot, pl.ds(chunk * share, share), pl.ds(column, width)],
                target.at[pl.ds((y * 4 + c * 2 + h) * share, share), pl.ds(chunk * width, width)],
                sem,
            ).start()


def load_blocks(held, target, sem, first, share):
    for slot, (c, y, h) in enumerate(slots()):
        pltpu.make_async_copy(
            held.at[slot, pl.ds(first, share)],
            target.at[pl.ds((y * 4 + c * 2 + h) * share, share), :],
            sem,
        ).start()


def settle(target, sem):
    pltpu.make_async_copy(target, target, sem).wait()


def store_rows(target, grads, share, column):
    y_me, _, c_me, h_me, _ = bits()
    width = grads.shape[1]
    for c, y, h in slots():
        for x in range(2):
            row = (y * 16 + x * 8 + c * 4 + h * 2) * share
            target[
                lax.bitwise_xor(c_me, c),
                lax.bitwise_xor(y_me, y),
                lax.bitwise_xor(h_me, h),
                x * 2 * share : (x + 1) * 2 * share,
                column : column + width,
            ] = grads[row : row + 2 * share, :].astype(jnp.bfloat16)


def store_chunks(target, grads, share, column):
    y_me, _, c_me, h_me, _ = bits()
    width = grads.shape[1] // 4
    for c, y, h in slots():
        row = (y * 4 + c * 2 + h) * share
        for chunk in range(4):
            target[
                lax.bitwise_xor(c_me, c),
                lax.bitwise_xor(y_me, y),
                lax.bitwise_xor(h_me, h),
                chunk * share : (chunk + 1) * share,
                column : column + width,
            ] = grads[row : row + share, chunk * width : (chunk + 1) * width].astype(jnp.bfloat16)


def store_blocks(target, grads, first, share):
    y_me, _, c_me, h_me, _ = bits()
    for c, y, h in slots():
        row = (y * 4 + c * 2 + h) * share
        target[
            lax.bitwise_xor(c_me, c),
            lax.bitwise_xor(y_me, y),
            lax.bitwise_xor(h_me, h),
            first : first + share,
            :,
        ] = grads[row : row + share, :].astype(jnp.bfloat16)


class Gather:
    def __init__(self, parts, got_c, got_y, got_h, sends, receives, result):
        self.parts, self.got = parts, (got_c, got_y, got_h)
        self.sends, self.receives, self.result = sends, receives, result

    def copy(self, step):
        source = (self.parts.at[1], self.parts.at[0, 1], self.parts.at[0, 0, 1])[step]
        return remote(
            source,
            self.got[step],
            self.sends.at[step],
            self.receives.at[step],
            flipped((C_BIT, Y_BIT, H_BIT)[step]),
        )

    def over_c(self):
        self.copy(0).start()

    def over_y(self):
        self.copy(0).wait_recv()
        for y in (1, 0):
            for h in range(2):
                summed = self.parts[0, y, h].astype(jnp.float32) + self.got[0][y, h].astype(jnp.float32)
                self.parts[0, y, h] = summed.astype(jnp.bfloat16)
            if y == 1:
                self.copy(1).start()

    def over_h(self):
        self.copy(1).wait_recv()
        for h in (1, 0):
            summed = self.parts[0, 0, h].astype(jnp.float32) + self.got[1][h].astype(jnp.float32)
            self.parts[0, 0, h] = summed.astype(jnp.bfloat16)
            if h == 1:
                self.copy(2).start()

    def done(self):
        self.copy(2).wait_recv()
        self.result[...] = self.parts[0, 0, 0].astype(jnp.float32) + self.got[2][...].astype(jnp.float32)
        for step in range(3):
            self.copy(step).wait_send()


def greet_core():
    greet([flipped(mask) for mask in (X_BIT, L_BIT, H_BIT, Y_BIT, C_BIT)])


def block_rows(j, n):
    return pl.ds(pl.multiple_of(j * n, n), n)


def core_forward(hidden, seg_col, seg_row, vectors, query_bias, value_bias, hidden_bias, head_turned, vocab_bias, cotangent, bundles, collective):
    n, width = hidden.shape
    layers = query_bias.shape[0]
    count = 4 * n
    part = width // 4
    inner = hidden_bias.shape[1]
    head = width // HEADS
    heads = part // head
    share = width // 32
    inner_share = inner // PIECES
    scale = head**-0.5
    vocab = head_turned.shape[0]
    low, wide = jnp.bfloat16, jnp.float32
    flat = [bundle for pair in bundles for bundle in pair]
    kept = [
        ((layers, 4, n, width), low),
        ((layers, count, 3 * part), low),
        ((layers, heads, count, count), low),
        ((layers, count, part), low),
        ((layers, n, width), wide),
        ((layers, 4, n, width), low),
        ((layers, count, inner), low),
        ((layers, count, inner), low),
        ((layers, n, width), wide),
    ]
    kinds = len(kept)

    def kernel(*refs):
        (h_ref, sc_ref, sr_ref, vec_ref, qb_ref, vb_ref, hb_ref, head_ref, vocab_ref, cot_ref) = refs[:10]
        own = refs[10 : 10 + len(flat)]
        rest = refs[10 + len(flat) :]
        logits_ref, flow_ref, part_ref, sum_ref = rest[:4]
        held = rest[4 : 4 + len(flat)]
        saved = rest[4 + len(flat) : 4 + len(flat) + kinds]
        rest = rest[4 + len(flat) + kinds :]
        (x_all, qkv, weights_low, context, residual, m_all, active, slope, outer) = rest[:kinds]
        (now, wj, wo, we, wr, low_buf, got, gs, gr, ss, sr, bs, br, bo, ws, ks) = rest[kinds:]
        _, x, _, _, l = bits()
        t = x * 2 + l
        greet_core()
        jobs = [
            Spread(own[b], held[b], bs.at[b], br.at[b], bo.at[b]) for b in range(len(flat))
        ]

        def keep(kind, source, layer):
            pltpu.make_async_copy(source.at[layer], saved[kind].at[layer], ks.at[kind, layer]).start()

        jobs[0].over_h()
        jobs[1].over_h()
        jobs[0].over_y()
        jobs[0].over_c()
        jobs[2].over_h()
        jobs[1].over_y()
        now[...] = h_ref[...]
        linked = sc_ref[...] == sr_ref[...]
        for layer in range(layers):
            first, second = jobs[2 * layer], jobs[2 * layer + 1]
            x_all[layer, t] = now[...].astype(low)
            first.done()
            load_rows(held[2 * layer], wj, ws.at[0], share, 0, 3 * part)
            load_chunks(held[2 * layer], wo, ws.at[1], share, 3 * part, part)
            group_gather(x_all.at[layer], t, gs, gr)
            keep(0, x_all, layer)
            settle(wj, ws.at[0])
            joint = dot(x_all[layer].reshape(count, width), wj[...])
            qkv[layer, :, 0:part] = ((joint[:, 0:part] + qb_ref[layer : layer + 1]) * scale).astype(low)
            qkv[layer, :, part : 2 * part] = joint[:, part : 2 * part].astype(low)
            qkv[layer, :, 2 * part :] = (joint[:, 2 * part :] + vb_ref[layer : layer + 1]).astype(low)
            keep(1, qkv, layer)
            for at in range(heads):
                queries = qkv[layer, :, at * head : (at + 1) * head]
                keys = qkv[layer, :, part + at * head : part + (at + 1) * head]
                values = qkv[layer, :, 2 * part + at * head : 2 * part + (at + 1) * head]
                scores = jnp.where(linked, dot_rt(queries, keys), masked_score)
                exponent = jnp.exp(scores - jnp.max(scores, axis=-1, keepdims=True))
                inverse = 1.0 / jnp.sum(exponent, axis=-1, keepdims=True)
                weights_low[layer, at] = (exponent * inverse).astype(low)
                context[layer, :, at * head : (at + 1) * head] = dot(weights_low[layer, at], values).astype(low)
            keep(2, weights_low, layer)
            keep(3, context, layer)
            settle(wo, ws.at[1])

            def advance(layer=layer):
                if layer == 0:
                    jobs[1].over_c()
                    jobs[2].over_y()
                    jobs[3].over_h()
                else:
                    jobs[3].over_c()

            attended = group_scatter(
                lambda j: dot(context[layer, block_rows(j, n), :], wo[...]), t, low_buf, got, ss, sr, advance
            )
            residual[layer] = now[...] + (attended + vec_ref[layer : layer + 1])
            keep(4, residual, layer)
            at = layers + layer
            middle = normed(residual[layer], vec_ref[at : at + 1], vec_ref[at + layers : at + layers + 1])
            now[...] = middle
            m_all[layer, t] = middle.astype(low)
            second.done()
            load_rows(held[2 * layer + 1], we, ws.at[2], share, 0, inner)
            load_blocks(held[2 * layer + 1], wr, ws.at[3], 4 * share, inner_share)
            group_gather(m_all.at[layer], t, gs, gr)
            keep(5, m_all, layer)
            settle(we, ws.at[2])
            if layer == 0:
                jobs[2].over_c()
            made, bent = gelu_pair(dot(m_all[layer].reshape(count, width), we[...]) + hb_ref[layer : layer + 1])
            active[layer] = made.astype(low)
            slope[layer] = bent.astype(low)
            keep(6, active, layer)
            keep(7, slope, layer)
            settle(wr, ws.at[3])

            def advance_more(layer=layer):
                if layer == 0:
                    jobs[3].over_y()

            fed = group_scatter(
                lambda j: dot(active[layer, block_rows(j, n), :], wr[...]), t, low_buf, got, ss, sr, advance_more
            )
            at = 3 * layers + layer
            outer[layer] = now[...] + fed + vec_ref[at : at + 1]
            keep(8, outer, layer)
            at += layers
            now[...] = normed(outer[layer], vec_ref[at : at + 1], vec_ref[at + layers : at + layers + 1])
        final_low = now[...].astype(low)
        logits_ref[...] = dot_rt(final_low, head_ref[...]) + vocab_ref[...]
        flow_ref[...] = dot(cot_ref[...], head_ref[...])
        part_ref[...] = dot_lt(cot_ref[...], final_low)
        sum_ref[...] = jnp.sum(cot_ref[...].astype(wide), axis=0, keepdims=True)
        for kind in range(kinds):
            for layer in range(layers):
                pltpu.make_async_copy(
                    saved[kind].at[layer], saved[kind].at[layer], ks.at[kind, layer]
                ).wait()

    outs = pl.pallas_call(
        kernel,
        out_shape=[
            jax.ShapeDtypeStruct((n, vocab), wide),
            jax.ShapeDtypeStruct((n, width), wide),
            jax.ShapeDtypeStruct((vocab, width), wide),
            jax.ShapeDtypeStruct((1, vocab), wide),
        ]
        + [jax.ShapeDtypeStruct((PIECES,) + bundle.shape, low) for bundle in flat]
        + [jax.ShapeDtypeStruct(shape, kind) for shape, kind in kept],
        in_specs=[IN_VMEM] * 10 + [ANYWHERE] * len(flat),
        out_specs=[IN_VMEM] * 4 + [ANYWHERE] * (len(flat) + kinds),
        scratch_shapes=[pltpu.VMEM(shape, kind) for shape, kind in kept]
        + [
            pltpu.VMEM((n, width), wide),
            pltpu.VMEM((width, 3 * part), low),
            pltpu.VMEM((part, width), low),
            pltpu.VMEM((width, inner), low),
            pltpu.VMEM((inner, width), low),
        ]
        + group_scratch(n, width)
        + [
            pltpu.SemaphoreType.DMA((len(flat), 3)),
            pltpu.SemaphoreType.DMA((len(flat), 3)),
            pltpu.SemaphoreType.DMA((len(flat),)),
            pltpu.SemaphoreType.DMA((4,)),
            pltpu.SemaphoreType.DMA((kinds, layers)),
        ],
        compiler_params=kernel_params(collective),
        cost_estimate=cost(120),
    )(hidden, seg_col, seg_row, vectors, query_bias, value_bias, hidden_bias, head_turned, vocab_bias, cotangent, *flat)
    return outs[:4], outs[4 : 4 + len(flat)], outs[4 + len(flat) :]


def core_backward(flow, vectors, held, saved, collective):
    n, width = flow.shape
    layers = saved[0].shape[0]
    count = 4 * n
    part = width // 4
    inner = saved[6].shape[2]
    head = width // HEADS
    heads = part // head
    share = width // 32
    inner_share = inner // PIECES
    scale = head**-0.5
    low, wide = jnp.bfloat16, jnp.float32
    kinds = len(saved)
    bundles = len(held)
    row_counts = [bundle.shape[1] for bundle in held]

    def kernel(*refs):
        flow_ref, vec_ref = refs[:2]
        held_refs = refs[2 : 2 + bundles]
        saved_refs = refs[2 + bundles : 2 + bundles + kinds]
        rest = refs[2 + bundles + kinds :]
        back_ref, token_ref, joint_ref, hidden_ref = rest[:4]
        results = rest[4 : 4 + bundles]
        rest = rest[4 + bundles :]
        parts = rest[:bundles]
        got_c, got_y, got_h = (rest[k * bundles : (k + 1) * bundles] for k in range(1, 4))
        rest = rest[4 * bundles :]
        (x_all, qkv, weights_low, context, residual, m_all, active, slope, outer) = rest[:kinds]
        (fed, inner_low, grad_low, joint, wj, wo, we, wr, low_buf, got, gs, gr, ss, sr, rs_s, rs_r, ws, ks) = rest[kinds:]
        _, x, _, _, l = bits()
        t = x * 2 + l
        buffers = rest[:kinds]

        def fetch(kind, layer):
            pltpu.make_async_copy(saved_refs[kind].at[layer], buffers[kind], ks.at[kind]).start()

        def need(kind):
            settle(buffers[kind], ks.at[kind])

        def load_feed(layer):
            fetch(8, layer)
            load_blocks(held_refs[2 * layer + 1], wr, ws.at[3], 4 * share, inner_share)
            fetch(7, layer)
            load_rows(held_refs[2 * layer + 1], we, ws.at[2], share, 0, inner)
            for kind in (6, 5, 4):
                fetch(kind, layer)

        def load_attend(layer):
            load_chunks(held_refs[2 * layer], wo, ws.at[1], share, 3 * part, part)
            for kind in (1, 2, 3, 0):
                fetch(kind, layer)
            load_rows(held_refs[2 * layer], wj, ws.at[0], share, 0, 3 * part)

        greet_core()
        load_feed(layers - 1)
        load_attend(layers - 1)
        jobs = [
            Gather(parts[b], got_c[b], got_y[b], got_h[b], rs_s.at[b], rs_r.at[b], results[b])
            for b in range(bundles)
        ]
        back_ref[...] = flow_ref[...]
        for layer in reversed(range(layers)):
            last = layer == layers - 1
            feed_job, attend_job = jobs[2 * layer + 1], jobs[2 * layer]
            sums = token_ref.at[layer]
            sums[6:8] = jnp.zeros((2, width), wide)
            at = 4 * layers + layer
            need(8)
            outer_grad, final_part, upper_part = normed_back(outer[...], vec_ref[at : at + 1], back_ref[...])
            back_ref[...] = outer_grad
            fed_low = outer_grad.astype(low)
            fed[0, t] = fed_low
            sums[0:1] = final_part
            sums[1:2] = upper_part
            sums[2:3] = jnp.sum(fed_low.astype(wide), axis=0, keepdims=True)
            group_gather(fed.at[0], t, gs, gr)
            settle(wr, ws.at[3])
            active_grad = dot_rt(fed[0].reshape(count, width), wr[...])
            need(7)
            inner_low[...] = (active_grad * slope[...].astype(wide)).astype(low)
            hidden_ref[layer : layer + 1] = jnp.sum(inner_low[...].astype(wide), axis=0, keepdims=True)
            settle(we, ws.at[2])
            need(6)
            need(5)

            def feed_weights(layer=layer, last=last, feed_job=feed_job):
                store_blocks(feed_job.parts, dot_lt(active[...], fed[0].reshape(count, width)), 4 * share, inner_share)
                store_rows(feed_job.parts, dot_lt(m_all[...].reshape(count, width), inner_low[...]), share, 0)
                feed_job.over_c()
                if not last:
                    jobs[2 * layer + 2].over_y()
                    jobs[2 * layer + 3].over_h()

            back = group_scatter(
                lambda j: dot_rt(inner_low[block_rows(j, n), :], we[...]), t, low_buf, got, ss, sr, feed_weights
            )
            need(4)
            at = layers + layer
            res_grad, middle_part, lower_part = normed_back(
                residual[...], vec_ref[at : at + 1], back_ref[...] + back
            )
            back_ref[...] = res_grad
            sums[3:4] = middle_part
            sums[4:5] = lower_part
            if layer:
                load_feed(layer - 1)
            own_low = res_grad.astype(low)
            fed[1, t] = own_low
            sums[5:6] = jnp.sum(own_low.astype(wide), axis=0, keepdims=True)
            group_gather(fed.at[1], t, gs, gr)
            settle(wo, ws.at[1])
            grad_low[...] = dot_rt(fed[1].reshape(count, width), wo[...]).astype(low)
            for kind in (1, 2, 3):
                need(kind)
            for at in range(heads):
                mine = slice(at * head, (at + 1) * head)
                queries = qkv[:, mine]
                keys = qkv[:, part + at * head : part + (at + 1) * head]
                values = qkv[:, 2 * part + at * head : 2 * part + (at + 1) * head]
                weights = weights_low[at]
                grads = grad_low[:, mine]
                delta = jnp.sum(grads.astype(wide) * context[:, mine].astype(wide), axis=-1, keepdims=True)
                score_grad = (weights.astype(wide) * (dot_rt(grads, values) - delta)).astype(low)
                joint[:, mine] = (dot(score_grad, keys).astype(low).astype(wide) * scale).astype(low)
                joint[:, part + at * head : part + (at + 1) * head] = dot_lt(score_grad, queries).astype(low)
                joint[:, 2 * part + at * head : 2 * part + (at + 1) * head] = dot_lt(weights, grads).astype(low)
            joint_ref[layer : layer + 1] = jnp.sum(joint[...].astype(wide), axis=0, keepdims=True)
            settle(wj, ws.at[0])
            need(0)

            def attend_weights(layer=layer, last=last, feed_job=feed_job, attend_job=attend_job):
                store_rows(attend_job.parts, dot_lt(x_all[...].reshape(count, width), joint[...]), share, 0)
                store_chunks(attend_job.parts, dot_lt(context[...], fed[1].reshape(count, width)), share, 3 * part)
                attend_job.over_c()
                feed_job.over_y()
                if not last:
                    jobs[2 * layer + 2].over_h()
                    jobs[2 * layer + 3].done()

            back = group_scatter(
                lambda j: dot_rt(joint[block_rows(j, n), :], wj[...]), t, low_buf, got, ss, sr, attend_weights
            )
            back_ref[...] = back_ref[...] + back
            if layer:
                load_attend(layer - 1)
        jobs[0].over_y()
        jobs[1].over_h()
        jobs[2].done()
        jobs[0].over_h()
        jobs[1].done()
        jobs[0].done()

    return pl.pallas_call(
        kernel,
        out_shape=[
            jax.ShapeDtypeStruct((n, width), wide),
            jax.ShapeDtypeStruct((layers, 8, width), wide),
            jax.ShapeDtypeStruct((layers, 3 * part), wide),
            jax.ShapeDtypeStruct((layers, inner), wide),
        ]
        + [jax.ShapeDtypeStruct((rows, width), wide) for rows in row_counts],
        in_specs=[IN_VMEM] * 2 + [ANYWHERE] * (bundles + kinds),
        out_specs=[IN_VMEM] * (4 + bundles),
        scratch_shapes=[pltpu.VMEM((2, 2, 2, rows, width), low) for rows in row_counts]
        + [pltpu.VMEM((2, 2, rows, width), low) for rows in row_counts]
        + [pltpu.VMEM((2, rows, width), low) for rows in row_counts]
        + [pltpu.VMEM((rows, width), low) for rows in row_counts]
        + [pltpu.VMEM(array.shape[1:], array.dtype) for array in saved]
        + [
            pltpu.VMEM((2, 4, n, width), low),
            pltpu.VMEM((count, inner), low),
            pltpu.VMEM((count, part), low),
            pltpu.VMEM((count, 3 * part), low),
            pltpu.VMEM((width, 3 * part), low),
            pltpu.VMEM((part, width), low),
            pltpu.VMEM((width, inner), low),
            pltpu.VMEM((inner, width), low),
        ]
        + group_scratch(n, width)
        + [
            pltpu.SemaphoreType.DMA((bundles, 3)),
            pltpu.SemaphoreType.DMA((bundles, 3)),
            pltpu.SemaphoreType.DMA((4,)),
            pltpu.SemaphoreType.DMA((kinds,)),
        ],
        compiler_params=kernel_params(collective),
        cost_estimate=cost(130),
    )(flow, vectors, *held, *saved)


def fast_local(*arguments):
    (
        features,
        utterance_ends,
        kernel_weight,
        position_bias,
        entry_gain,
        base_shift,
        joint_weight,
        query_bias,
        value_bias,
        output_weight,
        attend_bias,
        middle_gain,
        lower_shift,
        expand_weight,
        hidden_bias,
        reduce_weight,
        return_bias,
        final_gain,
        upper_shift,
        head_weight,
        vocab_bias,
        cotangent,
    ) = arguments
    devices = 32
    _, n, width = features.shape
    blocks = 4
    frames = n * blocks
    rows = 8
    groups = CONV_G
    group_width = width // groups
    share = width // devices
    taps = kernel_weight.shape[1] // group_width
    layers = joint_weight.shape[0]
    inner_all = expand_weight.shape[2]
    inner = inner_all // 4
    inner_share = inner_all // devices
    part = width // 4
    head = width // HEADS
    vocab = head_weight.shape[1]
    packs = n // PACK
    y, x, c, h, l = bits()
    turn = [
        (index_of(*at), turned_of(*at)) for at in itertools.product((0, 1), repeat=len(AXES))
    ]

    joint_turned = joint_weight.reshape(layers, share, 3, 2, 2, 2, 2, head)
    joint_turned = joint_turned.transpose(4, 6, 0, 1, 2, 3, 5, 7).reshape(4, layers, share, 3 * part)
    expand_turned = expand_weight.reshape(layers, share, 2, 2, 2, 2, 2, inner_share)
    expand_turned = expand_turned.transpose(3, 6, 0, 1, 2, 4, 5, 7).reshape(4, layers, share, inner)
    columns = jnp.concatenate([joint_turned, expand_turned], axis=-1)

    whole_rows = jnp.concatenate(
        [entry_gain[None], base_shift[None], attend_bias, middle_gain, lower_shift]
        + [return_bias, final_gain, upper_shift, head_weight.T, query_bias, value_bias]
        + [hidden_bias.reshape(layers * inner_share // share, share)],
        axis=0,
    )
    ends = jnp.concatenate([utterance_ends[0] // 32, utterance_ends[0] % 32])
    flat_rows = jnp.concatenate([whole_rows.reshape(-1), ends.astype(jnp.bfloat16)])
    flat_rows = jnp.pad(flat_rows, (0, -flat_rows.shape[0] % 2048)).reshape(1, -1, 128)

    def by_group(tokens):
        tokens = tokens.reshape(packs, PACK, groups, group_width)
        return tokens.transpose(2, 0, 1, 3).reshape(groups, packs, PACK * group_width)

    def from_channels(received):
        received = received.reshape(devices, packs, PACK, share)
        return received.transpose(1, 2, 0, 3).reshape(n, width)

    def by_block(channels):
        channels = channels.reshape(blocks, packs, rows, PACK * share)
        return channels.transpose(2, 0, 1, 3).reshape(devices, packs, PACK * share)

    arrived, columns, output_rows, small = swap_all(
        1,
        [
            (by_group(features[0]), group_of),
            (columns, "group"),
            (output_weight, "twist"),
            (flat_rows, lambda *place: 0),
        ],
    )
    small = small.reshape(devices, -1)
    taken = whole_rows.shape[0] * share
    gathered = small[:, :taken].reshape(devices, -1, share)
    vector_count = 2 + 6 * layers
    whole = jnp.swapaxes(gathered[:, : vector_count + vocab], 0, 1).reshape(vector_count + vocab, width)
    entry_full, base_full = widened(whole[0:1]), widened(whole[1:2])
    vectors = widened(whole[2:vector_count])
    head_turned = whole[vector_count:]
    own_rows = gathered[:, vector_count + vocab :].reshape(2, 2, 2, 2, 2, -1, share)
    own_rows = lax.dynamic_index_in_dim(own_rows, x, 1, keepdims=False)
    by_head = lax.dynamic_index_in_dim(own_rows[..., : 2 * layers, :], l, 2, keepdims=False)
    by_head = jnp.moveaxis(by_head, 3, 0).reshape(2, layers, part)
    query_full, value_full = widened(by_head[0]), widened(by_head[1])
    hidden_full = lax.dynamic_index_in_dim(own_rows[..., 2 * layers :, :], l, 3, keepdims=False)
    hidden_full = hidden_full.reshape(2, 2, 2, layers, inner_share)
    hidden_full = widened(jnp.moveaxis(hidden_full, 3, 0).reshape(layers, inner))
    all_ends = small[:, taken : taken + 8].astype(jnp.int32)
    all_ends = (all_ends[:, :4] * 32 + all_ends[:, 4:8])[::blocks]
    row_ends = lax.dynamic_slice_in_dim(all_ends, y * 4 + h * 2 + c, 1, axis=0)
    row_ids = segment_ids(jnp.arange(frames, dtype=jnp.int32), row_ends)
    seg_col, seg_row = row_ids.reshape(frames, 1), row_ids
    before = jnp.concatenate([jnp.zeros((rows, 1), jnp.int32), all_ends[:, :-1]], axis=1)
    bounds = jnp.where(all_ends > before, all_ends, frames)
    bounds = jnp.tile(bounds, (frames // PACK, 1))

    bundles = []
    for layer in range(layers):
        joint_rows = columns[:, layer, :, : 3 * part].reshape(4 * share, 3 * part)
        output_part = output_rows[layer].reshape(share, 4, part)
        output_part = output_part.transpose(1, 0, 2).reshape(4 * share, part)
        expand_rows = columns[:, layer, :, 3 * part :].reshape(4 * share, inner)
        bundles.append(
            (
                jnp.concatenate([joint_rows, output_part], axis=1),
                jnp.concatenate([expand_rows, reduce_weight[layer]], axis=0),
            )
        )

    packed = arrived.reshape(rows, frames // PACK, PACK * group_width)
    packed = packed.transpose(1, 0, 2).reshape(frames // PACK * rows, PACK * group_width)
    grid = kernel_weight.reshape(share, taps, group_width)
    conv_pre, even, odd = conv_forward_packed(
        packed,
        bounds,
        shifted_taps(grid.transpose(1, 2, 0)),
        jnp.tile(widened(position_bias), PACK)[None],
    )
    (pre_parts,) = swap_all(2, [(by_block(conv_pre), turned_of)])
    pre = widened(from_channels(pre_parts))
    own_feats = lax.ppermute(features[0], AXES, turn)
    own_cot = lax.ppermute(cotangent[0], AXES, turn)
    mixed = widened(own_feats) + gelu_exact(pre)
    hidden = layer_norm(mixed, entry_full, base_full)

    (logits, flow, head_part, vocab_sum), held, saved = core_forward(
        hidden,
        seg_col,
        seg_row,
        vectors,
        query_full,
        value_full,
        hidden_full,
        head_turned,
        widened(vocab_bias)[None],
        own_cot,
        bundles,
        3,
    )
    logits = lax.ppermute(logits, AXES, turn)
    flow, token_sums, joint_sums, hidden_sums, *layer_sums = core_backward(flow, vectors, held, saved, 4)

    mixed_grad, entry_part, base_part = normed_back(mixed, entry_full, flow)
    slope = gelu_pair(pre)[1]
    conv_low = rounded(mixed_grad * slope)
    (low_parts,) = swap_all(5, [(by_group(conv_low), group_of)])
    low_parts = low_parts.reshape(2, 2, 2, 2, 2, packs, PACK * group_width)
    packed_low = low_parts.transpose(1, 4, 5, 0, 3, 2, 6)
    packed_low = packed_low.reshape(frames // PACK * rows, PACK * group_width)
    own_low = lax.dynamic_index_in_dim(
        packed_low.reshape(-1, PACK, group_width // share, share), l, 2, keepdims=False
    ).reshape(-1, PACK * share)
    halves = grid.reshape(share, taps, 2, share)
    kept = lax.dynamic_index_in_dim(halves, l, 2, keepdims=False)
    given = lax.ppermute(
        lax.dynamic_index_in_dim(halves, 1 - l, 2, keepdims=False), "l", [(0, 1), (1, 0)]
    )
    both = jnp.where(l == 0, jnp.stack([kept, given]), jnp.stack([given, kept]))
    both = both.reshape(2 * share, taps, share).transpose(1, 0, 2)
    both = jnp.pad(both[::-1], ((1, 0), (0, 0), (0, 0)))
    feats_part, kernel_own, position_part = conv_backward_packed(
        packed_low, own_low, bounds, shifted_taps(both), even, odd
    )
    position_own = jnp.sum(position_part.reshape(PACK, share), axis=0)

    vector_sums = jnp.concatenate([entry_part, base_part] + [token_sums[k, :6] for k in range(layers)], axis=0)
    vector_sums = vector_sums.reshape(vector_count, devices, share).transpose(1, 0, 2)
    vector_sums = vector_sums.reshape(devices, vector_count * share)
    place = jnp.arange(2)
    heads_sums = jnp.concatenate(
        [
            joint_sums[:, :part].reshape(layers, 2, 1, 2, 1, 2, share),
            joint_sums[:, 2 * part :].reshape(layers, 2, 1, 2, 1, 2, share),
        ],
        axis=0,
    )
    chosen = (place == x).reshape(2, 1, 1, 1, 1) & (place == l).reshape(2, 1, 1)
    heads_sums = jnp.where(chosen, heads_sums, 0.0)
    chosen = (place == x).reshape(2, 1, 1, 1, 1) & (place == l).reshape(2, 1)
    inner_sums = jnp.where(chosen, hidden_sums.reshape(layers, 2, 1, 2, 2, 1, inner_share), 0.0)

    def per_device(array):
        return jnp.moveaxis(array, 0, 5).reshape(devices, -1)

    flat = jnp.concatenate(
        [
            vector_sums,
            per_device(heads_sums),
            per_device(inner_sums),
            jnp.broadcast_to(vocab_sum, (devices, vocab)),
        ],
        axis=1,
    )
    flat = jnp.pad(flat, ((0, 0), (0, -flat.shape[1] % 1024)))
    head_rows = head_part.reshape(vocab, devices, share).transpose(1, 2, 0).reshape(devices, share * vocab)
    flat = jnp.concatenate([flat, head_rows], axis=1).reshape(devices, -1, 128)

    back_columns = jnp.stack(
        [
            jnp.concatenate(
                [
                    layer_sums[2 * layer][:, : 3 * part].reshape(4, share, 3 * part),
                    layer_sums[2 * layer + 1][: 4 * share].reshape(4, share, inner),
                ],
                axis=-1,
            )
            for layer in range(layers)
        ],
        axis=1,
    )
    output_back = jnp.stack(
        [
            layer_sums[2 * layer][:, 3 * part :].reshape(4, share, part).transpose(1, 0, 2).reshape(share, width)
            for layer in range(layers)
        ]
    )
    feats_back, sums, back_columns, output_own = swap_all(
        6,
        [
            (by_block(feats_part), index_of),
            (flat, index_of),
            (rounded(back_columns), "group"),
            (output_back, "twist"),
        ],
    )
    features_grad = lax.ppermute(mixed_grad, AXES, turn) + widened(from_channels(feats_back))
    sums = jnp.sum(sums, axis=0).reshape(-1)
    at = vector_count * share
    vector_own = sums[:at].reshape(vector_count, share)
    query_own = sums[at : at + layers * share].reshape(layers, share)
    at += layers * share
    value_own = sums[at : at + layers * share].reshape(layers, share)
    at += layers * share
    hidden_own = sums[at : at + layers * inner_share].reshape(layers, inner_share)
    at += layers * inner_share
    vocab_own = sums[at : at + vocab]
    head_own = sums[-share * vocab :].reshape(share, vocab)
    back_columns = widened(back_columns)
    joint_own = back_columns[..., : 3 * part].reshape(2, 2, layers, share, 3, 2, 2, head)
    joint_own = joint_own.transpose(2, 3, 4, 5, 0, 6, 1, 7).reshape(layers, share, 3 * width)
    expand_own = back_columns[..., 3 * part :].reshape(2, 2, layers, share, 2, 2, 2, inner_share)
    expand_own = expand_own.transpose(2, 3, 4, 0, 5, 6, 1, 7).reshape(layers, share, inner_all)
    reduce_own = jnp.stack([layer_sums[2 * layer + 1][4 * share :] for layer in range(layers)])
    per_layer = vector_own[2:].reshape(layers, 6, share)
    return (
        logits[None],
        features_grad[None],
        kernel_own,
        position_own,
        vector_own[0],
        vector_own[1],
        joint_own,
        query_own,
        value_own,
        output_own,
        per_layer[:, 5],
        per_layer[:, 3],
        per_layer[:, 4],
        expand_own,
        hidden_own,
        reduce_own,
        per_layer[:, 2],
        per_layer[:, 0],
        per_layer[:, 1],
        head_own,
        vocab_own,
    )


def fits(dp_size, seq_size, width):
    share = width // 32
    return (
        dp_size == 8
        and seq_size == 4
        and share % 16 == 0
        and share * 2 == width // CONV_G
        and share * 2 == width // HEADS
    )


def placed(mesh, width):
    if fits(mesh.shape["dp"], mesh.shape["seq"], width):
        body = fast_local
        mesh = jax.sharding.Mesh(mesh.devices.reshape((2,) * len(AXES)), AXES)
        split, over, within = AXES[:3], AXES[3:], AXES
    else:
        body, split, over, within = local, "dp", "seq", ("dp", "seq")
    tokens = P(split, over, None)
    first, first_wide = P(within), P(within, None)
    second, second_wide = P(None, within), P(None, within, None)
    return jax.shard_map(
        body,
        mesh=mesh,
        in_specs=(
            tokens,
            P(split, None),
            first_wide,
            first,
            first,
            first,
            second_wide,
            second,
            second,
            second_wide,
            second,
            second,
            second,
            second_wide,
            second,
            second_wide,
            second,
            second,
            second,
            first_wide,
            P(),
            tokens,
        ),
        out_specs=(
            tokens,
            tokens,
            first_wide,
            first,
            first,
            first,
            second_wide,
            second,
            second,
            second_wide,
            second,
            second,
            second,
            second_wide,
            second,
            second_wide,
            second,
            second,
            second,
            first_wide,
            P(),
        ),
        check_vma=False,
    )


def solution(mesh):
    def whole(*arguments):
        return placed(mesh, arguments[0].shape[2])(*arguments)

    return whole
```

```python
import itertools
import math

import jax
import jax.numpy as jnp
from jax import lax
from jax.experimental import pallas as pl
from jax.experimental.pallas import tpu as pltpu
from jax.sharding import PartitionSpec as P

HEADS = 16
CONV_G = 16


epsilon = 1e-05
masked_score = -1e30


def with_halo(cells, sides, width):
    for axis, dim in sides:
        count = lax.axis_size(axis)
        ends = count - 1
        head = lax.slice_in_dim(cells, 0, width, axis=dim)
        tail = lax.slice_in_dim(cells, cells.shape[dim] - width, cells.shape[dim], axis=dim)
        cells = jnp.concatenate(
            [
                lax.ppermute(tail, axis, [(i, (i + 1) % count) for i in range(ends)]),
                cells,
                lax.ppermute(head, axis, [((i + 1) % count, i) for i in range(ends)]),
            ],
            axis=dim,
        )
    return cells


def layer_norm(tensor, scaling, shifts):
    average = jnp.mean(tensor, axis=-1, keepdims=True)
    centred = tensor - average
    spread = jnp.mean(centred * centred, axis=-1, keepdims=True)
    return centred * lax.rsqrt(spread + epsilon) * scaling + shifts


def norm_pullback(tensor, scaling, upstream):
    _, pullback = jax.vjp(layer_norm, tensor, scaling, jnp.zeros_like(scaling))
    return pullback(upstream)


def gelu_exact(tensor):
    return jax.nn.gelu(tensor, approximate=False)


def rounded(tensor):
    return tensor.astype(jnp.bfloat16)


def widened(tensor):
    return tensor.astype(jnp.float32)


def segment_ids(positions, utterance_ends):
    return jnp.sum(
        (positions[None, :, None] >= utterance_ends[:, None, :]).astype(jnp.int32), axis=2
    )


def unfold(source, source_ids, target_ids, anchors):
    length = target_ids.shape[1]
    pieces = [lax.slice_in_dim(source, anchor, anchor + length, axis=1) for anchor in anchors]
    matches = [
        lax.slice_in_dim(source_ids, anchor, anchor + length, axis=1) == target_ids
        for anchor in anchors
    ]
    stacked = jnp.stack(pieces, axis=2)
    keepers = jnp.stack(matches, axis=2)
    return jnp.where(keepers[..., None], stacked, jnp.zeros_like(stacked))


def conv_forward(halo_feats, halo_ids, frame_ids, kernel_grid, tap_block):
    row_count, frame_count = frame_ids.shape
    groups, group_width, tap_count, inner_width = kernel_grid.shape
    summed = jnp.zeros((row_count, frame_count, groups, group_width), jnp.float32)
    for block_at in range(tap_count // tap_block):
        first_tap = block_at * tap_block
        window = unfold(
            halo_feats,
            halo_ids,
            frame_ids,
            [first_tap + inner_tap for inner_tap in range(tap_block)],
        )
        window = window.reshape(row_count, frame_count, tap_block, groups, inner_width)
        summed = summed + jnp.einsum(
            "rtkgi,goki->rtgo",
            window,
            kernel_grid[:, :, first_tap : first_tap + tap_block, :],
            preferred_element_type=jnp.float32,
        )
    return summed.reshape(row_count, frame_count, groups * group_width)


def conv_backward(halo_grads, halo_feats, halo_ids, frame_ids, kernel_grid, tap_block, conv_low):
    row_count, frame_count = frame_ids.shape
    groups, group_width, tap_count, inner_width = kernel_grid.shape
    input_part = jnp.zeros((row_count, frame_count, groups, inner_width), jnp.float32)
    grouped = conv_low.reshape(row_count, frame_count, groups, group_width)
    kernel_parts = []
    for block_at in range(tap_count // tap_block):
        first_tap = block_at * tap_block
        tap_list = [first_tap + inner_tap for inner_tap in range(tap_block)]
        grads_window = unfold(
            halo_grads, halo_ids, frame_ids, [tap_count - tap_at for tap_at in tap_list]
        )
        grads_window = grads_window.reshape(row_count, frame_count, tap_block, groups, group_width)
        input_part = input_part + jnp.einsum(
            "rtkgo,goki->rtgi",
            grads_window,
            kernel_grid[:, :, first_tap : first_tap + tap_block, :],
            preferred_element_type=jnp.float32,
        )
        feats_window = unfold(halo_feats, halo_ids, frame_ids, tap_list)
        feats_window = feats_window.reshape(row_count, frame_count, tap_block, groups, inner_width)
        kernel_parts.append(
            jnp.einsum(
                "rtgo,rtkgi->goki", grouped, feats_window, preferred_element_type=jnp.float32
            )
        )
    kernel_full = jnp.concatenate(kernel_parts, axis=2).reshape(
        groups * group_width, tap_count * inner_width
    )
    return (input_part.reshape(row_count, frame_count, groups * inner_width), kernel_full)


def split_heads(tensor, head_count):
    return tensor.reshape(
        tensor.shape[0], tensor.shape[1], head_count, tensor.shape[2] // head_count
    )


def attend_scores(queries, all_keys, query_ids, key_ids, head_count):
    scores = jnp.einsum(
        "rqhd,rkhd->rhqk",
        split_heads(queries, head_count),
        split_heads(all_keys, head_count),
        preferred_element_type=jnp.float32,
    )
    allowed = query_ids[:, None, :, None] == key_ids[:, None, None, :]
    return jnp.where(allowed, scores, masked_score)


def attend_forward(queries, all_keys, all_values, frame_ids, row_ids, head_count):
    scores = attend_scores(queries, all_keys, frame_ids, row_ids, head_count)
    row_peak = jnp.max(scores, axis=-1, keepdims=True)
    exponent = jnp.exp(scores - row_peak)
    totals = jnp.sum(exponent, axis=-1, keepdims=True)
    weights_low = rounded(exponent / totals)
    context = jnp.einsum(
        "rhqk,rkhd->rqhd",
        weights_low,
        split_heads(all_values, head_count),
        preferred_element_type=jnp.float32,
    )
    return (rounded(context.reshape(queries.shape)), row_peak + jnp.log(totals))


def attend_backward(
    queries, all_keys, all_values, frame_ids, row_ids, head_count, log_totals, context_low
):
    scores = attend_scores(queries, all_keys, frame_ids, row_ids, head_count)
    attention = jnp.exp(scores - log_totals)
    weights_low = rounded(attention)
    grad_heads = split_heads(context_low, head_count)
    prob_grad = jnp.einsum(
        "rqhd,rkhd->rhqk",
        grad_heads,
        split_heads(all_values, head_count),
        preferred_element_type=jnp.float32,
    )
    row_delta = jnp.sum(attention * prob_grad, axis=-1, keepdims=True)
    score_grad = rounded(attention * (prob_grad - row_delta))
    value_part = jnp.einsum(
        "rhqk,rqhd->rkhd", weights_low, grad_heads, preferred_element_type=jnp.float32
    )
    query_part = jnp.einsum(
        "rhqk,rkhd->rqhd",
        score_grad,
        split_heads(all_keys, head_count),
        preferred_element_type=jnp.float32,
    )
    key_part = jnp.einsum(
        "rhqk,rqhd->rkhd",
        score_grad,
        split_heads(queries, head_count),
        preferred_element_type=jnp.float32,
    )
    return (
        query_part.reshape(queries.shape),
        key_part.reshape(all_keys.shape),
        value_part.reshape(all_values.shape),
    )


def local(
    features,
    utterance_ends,
    kernel_weight,
    position_bias,
    entry_gain,
    base_shift,
    joint_weight,
    query_bias,
    value_bias,
    output_weight,
    attend_bias,
    middle_gain,
    lower_shift,
    expand_weight,
    hidden_bias,
    reduce_weight,
    return_bias,
    final_gain,
    upper_shift,
    head_weight,
    vocab_bias,
    cotangent,
):
    row_count, frame_count, model_dim = features.shape
    frames_all = frame_count * lax.axis_size("seq")
    groups = CONV_G
    group_width = model_dim // groups
    tap_count = kernel_weight.shape[1] // group_width
    half_taps = tap_count // 2
    tap_block = math.gcd(tap_count, 16)
    head_count = HEADS
    query_scale = (model_dim // head_count) ** (-0.5)
    layer_count = joint_weight.shape[0]
    rows_share = model_dim // lax.axis_size(("dp", "seq"))
    anchor = lax.axis_index("seq") * frame_count
    frame_ids = segment_ids(anchor + jnp.arange(frame_count, dtype=jnp.int32), utterance_ends)
    row_ids = segment_ids(jnp.arange(frames_all, dtype=jnp.int32), utterance_ends)
    halo_place = anchor - half_taps + jnp.arange(frame_count + tap_count, dtype=jnp.int32)
    inside = (halo_place >= 0) & (halo_place < frames_all)
    halo_ids = jnp.where(inside[None, :], segment_ids(halo_place, utterance_ends), -1)
    stem = (
        lax.all_gather(kernel_weight, ("dp", "seq"), axis=0, tiled=True),
        lax.all_gather(position_bias, ("dp", "seq"), axis=0, tiled=True),
        lax.all_gather(entry_gain, ("dp", "seq"), axis=0, tiled=True),
        lax.all_gather(base_shift, ("dp", "seq"), axis=0, tiled=True),
        lax.all_gather(head_weight, ("dp", "seq"), axis=0, tiled=True),
    )
    kernel_grid = stem[0].reshape(groups, group_width, tap_count, group_width)
    halo_feats = with_halo(features, (("seq", 1),), half_taps)
    conv_pre = conv_forward(halo_feats, halo_ids, frame_ids, kernel_grid, tap_block) + widened(
        stem[1]
    )
    mixed = widened(features) + gelu_exact(conv_pre)
    hidden = layer_norm(mixed, widened(stem[2]), widened(stem[3]))
    saved = []
    for layer_at in range(layer_count):
        (
            joint_full,
            query_full,
            value_full,
            output_full,
            attend_full,
            middle_full,
            lower_full,
            expand_full,
            hidden_full,
            reduce_full,
            return_full,
            final_full,
            upper_full,
        ) = (
            lax.all_gather(joint_weight[layer_at], ("dp", "seq"), axis=0, tiled=True),
            lax.all_gather(query_bias[layer_at], ("dp", "seq"), axis=0, tiled=True),
            lax.all_gather(value_bias[layer_at], ("dp", "seq"), axis=0, tiled=True),
            lax.all_gather(output_weight[layer_at], ("dp", "seq"), axis=0, tiled=True),
            lax.all_gather(attend_bias[layer_at], ("dp", "seq"), axis=0, tiled=True),
            lax.all_gather(middle_gain[layer_at], ("dp", "seq"), axis=0, tiled=True),
            lax.all_gather(lower_shift[layer_at], ("dp", "seq"), axis=0, tiled=True),
            lax.all_gather(expand_weight[layer_at], ("dp", "seq"), axis=0, tiled=True),
            lax.all_gather(hidden_bias[layer_at], ("dp", "seq"), axis=0, tiled=True),
            lax.all_gather(reduce_weight[layer_at], ("dp", "seq"), axis=0, tiled=True),
            lax.all_gather(return_bias[layer_at], ("dp", "seq"), axis=0, tiled=True),
            lax.all_gather(final_gain[layer_at], ("dp", "seq"), axis=0, tiled=True),
            lax.all_gather(upper_shift[layer_at], ("dp", "seq"), axis=0, tiled=True),
        )
        inputs_low = rounded(hidden)
        joint_out = jnp.einsum(
            "rtd,de->rte", inputs_low, joint_full, preferred_element_type=jnp.float32
        )
        queries = rounded((joint_out[..., :model_dim] + widened(query_full)) * query_scale)
        keys_local = rounded(joint_out[..., model_dim : 2 * model_dim])
        values_local = rounded(joint_out[..., 2 * model_dim :] + widened(value_full))
        all_keys, all_values = (
            lax.all_gather(keys_local, "seq", axis=1, tiled=True),
            lax.all_gather(values_local, "seq", axis=1, tiled=True),
        )
        context, log_totals = attend_forward(
            queries, all_keys, all_values, frame_ids, row_ids, head_count
        )
        attended = jnp.einsum(
            "rtc,cd->rtd", context, output_full, preferred_element_type=jnp.float32
        ) + widened(attend_full)
        residual_one = hidden + attended
        middle = layer_norm(residual_one, widened(middle_full), widened(lower_full))
        middle_low = rounded(middle)
        inner_pre = jnp.einsum(
            "rtd,df->rtf", middle_low, expand_full, preferred_element_type=jnp.float32
        ) + widened(hidden_full)
        activated = rounded(gelu_exact(inner_pre))
        outer = (
            middle
            + jnp.einsum("rtf,fd->rtd", activated, reduce_full, preferred_element_type=jnp.float32)
            + widened(return_full)
        )
        kept_weights = None
        saved.append(
            (
                inputs_low,
                queries,
                all_keys,
                all_values,
                log_totals,
                context,
                residual_one,
                middle_low,
                inner_pre,
                activated,
                outer,
                kept_weights,
            )
        )
        hidden = layer_norm(outer, widened(final_full), widened(upper_full))
    final_low = rounded(hidden)
    logits = jnp.einsum(
        "rtd,dv->rtv", final_low, stem[4], preferred_element_type=jnp.float32
    ) + widened(vocab_bias)
    back_stem = (
        lax.all_gather(kernel_weight, ("dp", "seq"), axis=0, tiled=True),
        lax.all_gather(entry_gain, ("dp", "seq"), axis=0, tiled=True),
        lax.all_gather(head_weight, ("dp", "seq"), axis=0, tiled=True),
    )
    vocab_sum = jnp.sum(widened(cotangent), axis=(0, 1))
    head_part = jnp.einsum("rtd,rtv->dv", final_low, cotangent, preferred_element_type=jnp.float32)
    flow_grad = jnp.einsum(
        "rtv,dv->rtd", cotangent, back_stem[2], preferred_element_type=jnp.float32
    )
    layer_grads = [None] * layer_count
    for layer_at in reversed(range(layer_count)):
        (
            inputs_low,
            queries,
            all_keys,
            all_values,
            log_totals,
            context,
            residual_one,
            middle_low,
            inner_pre,
            activated,
            outer,
            kept_weights,
        ) = saved[layer_at]
        back_weights = (
            lax.all_gather(joint_weight[layer_at], ("dp", "seq"), axis=0, tiled=True),
            lax.all_gather(output_weight[layer_at], ("dp", "seq"), axis=0, tiled=True),
            lax.all_gather(expand_weight[layer_at], ("dp", "seq"), axis=0, tiled=True),
            lax.all_gather(reduce_weight[layer_at], ("dp", "seq"), axis=0, tiled=True),
            lax.all_gather(middle_gain[layer_at], ("dp", "seq"), axis=0, tiled=True),
            lax.all_gather(final_gain[layer_at], ("dp", "seq"), axis=0, tiled=True),
        )
        joint_full, output_full, expand_full, reduce_full, middle_full, final_full = back_weights
        outer_grad, final_part, upper_part = norm_pullback(outer, widened(final_full), flow_grad)
        fed_low = rounded(outer_grad)
        return_part = jnp.sum(widened(fed_low), axis=(0, 1))
        active_grad = jnp.einsum(
            "rtd,fd->rtf", fed_low, reduce_full, preferred_element_type=jnp.float32
        )
        _, gelu_pull = jax.vjp(gelu_exact, inner_pre)
        (inner_grad,) = gelu_pull(active_grad)
        inner_low = rounded(inner_grad)
        hidden_part = jnp.sum(widened(inner_low), axis=(0, 1))
        middle_flow = outer_grad + jnp.einsum(
            "rtf,df->rtd", inner_low, expand_full, preferred_element_type=jnp.float32
        )
        residual_grad, middle_part, lower_part = norm_pullback(
            residual_one, widened(middle_full), middle_flow
        )
        attended_low = rounded(residual_grad)
        attend_part = jnp.sum(widened(attended_low), axis=(0, 1))
        context_low = rounded(
            jnp.einsum("rtd,cd->rtc", attended_low, output_full, preferred_element_type=jnp.float32)
        )
        query_raw, key_raw, value_raw = attend_backward(
            queries, all_keys, all_values, frame_ids, row_ids, head_count, log_totals, context_low
        )
        key_sum, value_sum = (
            lax.psum_scatter(
                key_raw.astype(jnp.bfloat16), "seq", scatter_dimension=1, tiled=True
            ).astype(jnp.float32),
            lax.psum_scatter(
                value_raw.astype(jnp.bfloat16), "seq", scatter_dimension=1, tiled=True
            ).astype(jnp.float32),
        )
        query_low = rounded(widened(rounded(query_raw)) * query_scale)
        key_low = rounded(key_sum)
        value_low = rounded(value_sum)
        query_part = jnp.sum(widened(query_low), axis=(0, 1))
        value_part = jnp.sum(widened(value_low), axis=(0, 1))
        joint_low = jnp.concatenate([query_low, key_low, value_low], axis=-1)
        flow_grad = residual_grad + jnp.einsum(
            "rte,de->rtd", joint_low, joint_full, preferred_element_type=jnp.float32
        )
        ratio = hidden_part.shape[0] // model_dim
        vector_rows = jnp.stack(
            [
                query_part,
                value_part,
                attend_part,
                middle_part,
                lower_part,
                return_part,
                final_part,
                upper_part,
            ],
            axis=1,
        )
        hidden_rows = hidden_part.reshape(model_dim, ratio)

        def layer_term(
            start,
            count,
            inputs_low=inputs_low,
            joint_low=joint_low,
            context=context,
            attended_low=attended_low,
            middle_low=middle_low,
            inner_low=inner_low,
            activated=activated,
            fed_low=fed_low,
            vector_rows=vector_rows,
            hidden_rows=hidden_rows,
            ratio=ratio,
        ):
            joint_rows = jnp.einsum(
                "rtd,rte->de", inputs_low, joint_low, preferred_element_type=jnp.float32
            )
            output_rows = jnp.einsum(
                "rtc,rtd->cd", context, attended_low, preferred_element_type=jnp.float32
            )
            expand_rows = jnp.einsum(
                "rtd,rtf->df", middle_low, inner_low, preferred_element_type=jnp.float32
            )
            reduce_rows = jnp.einsum(
                "rtf,rtd->fd", activated, fed_low, preferred_element_type=jnp.float32
            ).reshape(count, ratio * model_dim)
            return jnp.concatenate(
                [joint_rows, output_rows, expand_rows, reduce_rows, vector_rows, hidden_rows],
                axis=1,
            )

        summed = lax.psum_scatter(
            layer_term(jnp.int32(0), rows_share * lax.axis_size(("dp", "seq"))),
            ("dp", "seq"),
            scatter_dimension=0,
            tiled=True,
        )
        ff_width = ratio * model_dim
        first = 3 * model_dim
        second = first + model_dim
        third = second + ff_width
        fourth = third + ratio * model_dim
        joint_own = summed[:, :first]
        output_own = summed[:, first:second]
        expand_own = summed[:, second:third]
        reduce_own = summed[:, third:fourth].reshape(rows_share * ratio, model_dim)
        vector_own = summed[:, fourth : fourth + 8]
        hidden_own = summed[:, fourth + 8 :].reshape(rows_share * ratio)
        layer_grads[layer_at] = (
            joint_own,
            vector_own[:, 0],
            vector_own[:, 1],
            output_own,
            vector_own[:, 2],
            vector_own[:, 3],
            vector_own[:, 4],
            expand_own,
            hidden_own,
            reduce_own,
            vector_own[:, 5],
            vector_own[:, 6],
            vector_own[:, 7],
        )
    mixed_grad, entry_part, base_part = norm_pullback(mixed, widened(back_stem[1]), flow_grad)
    _, gelu_pull = jax.vjp(gelu_exact, conv_pre)
    (conv_grad,) = gelu_pull(mixed_grad)
    conv_low = rounded(conv_grad)
    position_part = jnp.sum(widened(conv_low), axis=(0, 1))
    halo_grads = with_halo(conv_low, (("seq", 1),), half_taps)
    back_grid = back_stem[0].reshape(groups, group_width, tap_count, group_width)
    input_part, kernel_part = conv_backward(
        halo_grads, halo_feats, halo_ids, frame_ids, back_grid, tap_block, conv_low
    )
    features_grad = mixed_grad + input_part
    vocab_tiled = jnp.tile(vocab_sum, lax.axis_size(("dp", "seq")))
    stem_sums = (
        lax.psum_scatter(kernel_part, ("dp", "seq"), scatter_dimension=0, tiled=True),
        lax.psum_scatter(position_part, ("dp", "seq"), scatter_dimension=0, tiled=True),
        lax.psum_scatter(entry_part, ("dp", "seq"), scatter_dimension=0, tiled=True),
        lax.psum_scatter(base_part, ("dp", "seq"), scatter_dimension=0, tiled=True),
        lax.psum_scatter(head_part, ("dp", "seq"), scatter_dimension=0, tiled=True),
        lax.psum_scatter(vocab_tiled, ("dp", "seq"), scatter_dimension=0, tiled=True),
    )
    stacked = [
        jnp.stack([layer_grads[layer_at][member] for layer_at in range(layer_count)])
        for member in range(13)
    ]
    return (
        logits,
        features_grad,
        stem_sums[0],
        stem_sums[1],
        stem_sums[2],
        stem_sums[3],
        stacked[0],
        stacked[1],
        stacked[2],
        stacked[3],
        stacked[4],
        stacked[5],
        stacked[6],
        stacked[7],
        stacked[8],
        stacked[9],
        stacked[10],
        stacked[11],
        stacked[12],
        stem_sums[4],
        stem_sums[5],
    )


MESH_ID = pl.DeviceIdType.MESH
IN_VMEM = pl.BlockSpec(memory_space=pltpu.VMEM)
ANYWHERE = pl.BlockSpec(memory_space=pl.ANY)
AXES = ("y", "x", "c", "h", "l")
Y_BIT, X_BIT, C_BIT, H_BIT, L_BIT = 16, 8, 4, 2, 1
DEVICES = 32
PIECES = 8
PACK = 8
RANKS = 4
LOW, WIDE = jnp.bfloat16, jnp.float32


def kernel_params(collective):
    return pltpu.CompilerParams(
        vmem_limit_bytes=62 * 2**20, collective_id=collective, has_side_effects=True
    )


def cost(micros):
    return pl.CostEstimate(flops=int(micros * 1.1e9), bytes_accessed=2**20, transcendentals=0)


def bits():
    return tuple(lax.axis_index(axis) for axis in AXES)


def index_of(y, x, c, h, l):
    return y * 16 + x * 8 + c * 4 + h * 2 + l


def turned_of(y, x, c, h, l):
    return index_of(y, h, c, x, l)


def flipped(mask):
    return {
        axis: 1 - lax.axis_index(axis)
        for number, axis in enumerate(AXES)
        if mask >> (len(AXES) - 1 - number) & 1
    }


def place_of(mask):
    return [
        1 - here if mask >> (len(AXES) - 1 - number) & 1 else here
        for number, here in enumerate(bits())
    ]


def greet_all():
    gate = pltpu.get_barrier_semaphore()
    for mask in range(1, DEVICES):
        pl.semaphore_signal(gate, inc=1, device_id=flipped(mask), device_id_type=MESH_ID)


def all_greeted():
    pl.semaphore_wait(pltpu.get_barrier_semaphore(), DEVICES - 1)


def remote(source, target, send, receive, peer):
    return pltpu.make_async_remote_copy(
        source, target, send, receive, device_id=peer, device_id_type=MESH_ID
    )


class Swap:
    def __init__(self, block_for, target, sends, receives, own_sem):
        self.block_for, self.target = block_for, target
        self.sends, self.receives, self.own_sem = sends, receives, own_sem

    def own(self):
        place = bits()
        return pltpu.make_async_copy(
            self.block_for(*place), self.target.at[index_of(*place)], self.own_sem
        )

    def copy(self, mask):
        return remote(
            self.block_for(*place_of(mask)),
            self.target.at[index_of(*bits())],
            self.sends.at[mask - 1],
            self.receives.at[mask - 1],
            flipped(mask),
        )

    def start(self):
        self.own().start()
        for mask in range(1, DEVICES):
            self.copy(mask).start()

    def arrived(self):
        self.own().wait()
        for mask in range(1, DEVICES):
            self.copy(mask).wait_recv()

    def sent(self):
        for mask in range(1, DEVICES):
            self.copy(mask).wait_send()


def swap_sems():
    return [
        pltpu.SemaphoreType.DMA((DEVICES - 1,)),
        pltpu.SemaphoreType.DMA((DEVICES - 1,)),
        pltpu.SemaphoreType.DMA,
    ]


class Move:
    def __init__(self, pairs, same, mask, sends, receives):
        self.pairs, self.same, self.mask = pairs, same, mask
        self.sends, self.receives = sends, receives

    def each(self, action):
        @pl.when(self.same)
        def _():
            for number, (source, target) in enumerate(self.pairs):
                copy = pltpu.make_async_copy(source, target, self.receives.at[number])
                copy.start() if action == "start" else copy.wait()

        @pl.when(jnp.logical_not(self.same))
        def _():
            for number, (source, target) in enumerate(self.pairs):
                copy = remote(
                    source,
                    target,
                    self.sends.at[number],
                    self.receives.at[number],
                    flipped(self.mask),
                )
                copy.start() if action == "start" else copy.wait()

    def start(self):
        self.each("start")

    def done(self):
        self.each("wait")


def put_lanes(target, value):
    for q in range(value.shape[1] // 128):
        target[q] = value[:, q * 128 : (q + 1) * 128]


def get_lanes(source, width):
    return jnp.concatenate([source[q] for q in range(width // 128)], axis=1)


def bounds_of(ends, frames):
    before = [jnp.zeros_like(ends[0])] + ends[:-1]
    return [jnp.where(end > last, end, float(frames)) for end, last in zip(ends, before)]


def rank_lanes(bounds, frames, width):
    shape = (frames // PACK, 8, PACK * width)
    frame = lax.broadcasted_iota(jnp.int32, shape, 0) * PACK
    frame = frame + lax.broadcasted_iota(jnp.int32, shape, 2) // width
    rank = jnp.zeros(shape, jnp.int32)
    for bound in bounds:
        rank = rank + (frame >= bound[None].astype(jnp.int32)).astype(jnp.int32)
    return rank.reshape(frames, PACK * width)


def spread_ranks(wide, packed, rank, first):
    lines = packed.shape[0]
    wide[...] = jnp.zeros_like(wide)
    for number in range(RANKS):
        place = pl.ds(first + number * 64, lines)
        wide[place, :] += jnp.where(rank == number, packed, 0.0)


def collect_ranks(summed, rank, lines):
    result = jnp.zeros((lines, summed.shape[1]), WIDE)
    for number in range(RANKS):
        result = jnp.where(rank == number, summed[number * 64 : number * 64 + lines, :], result)
    return result


def fill_pair(wide, even, odd):
    length = even.shape[0]
    even[...] = wide[:length, :].astype(LOW)
    odd[...] = wide[8 : 8 + length, :].astype(LOW)


def shifted(even, odd, step, length):
    source = even if step % 2 == 0 else odd
    return source[pl.ds((step - step % 2) * 8, length), :]


def normed(tensor, gain, shift):
    average = jnp.mean(tensor, axis=-1, keepdims=True)
    centred = tensor - average
    spread = jnp.mean(centred * centred, axis=-1, keepdims=True)
    return centred * lax.rsqrt(spread + epsilon) * gain + shift


def normed_back(tensor, gain, upstream):
    average = jnp.mean(tensor, axis=-1, keepdims=True)
    centred = tensor - average
    spread = jnp.mean(centred * centred, axis=-1, keepdims=True)
    inverse = lax.rsqrt(spread + epsilon)
    unit = centred * inverse
    scaled = upstream * gain
    result = inverse * (
        scaled
        - jnp.mean(scaled, axis=-1, keepdims=True)
        - unit * jnp.mean(scaled * unit, axis=-1, keepdims=True)
    )
    return (
        result,
        jnp.sum(upstream * unit, axis=0, keepdims=True),
        jnp.sum(upstream, axis=0, keepdims=True),
    )


def gelu_pair(tensor):
    half = 0.5 * (1.0 + lax.erf(tensor * (2.0**-0.5)))
    slope = half + tensor * (jnp.exp(-0.5 * tensor * tensor) * ((2.0 * math.pi) ** -0.5))
    return tensor * half, slope


def dot(left, right):
    return jnp.dot(left, right, preferred_element_type=WIDE)


def dot_rt(left, right):
    return lax.dot_general(left, right, (((1,), (1,)), ((), ())), preferred_element_type=WIDE)


def dot_lt(left, right):
    return lax.dot_general(left, right, (((0,), (0,)), ((), ())), preferred_element_type=WIDE)


def group_gather(block, t, sends, receives, ready, use):
    half = block.shape[1] // 2
    x_peer, l_peer = flipped(X_BIT), flipped(L_BIT)
    own = block.at[t]
    to_x = remote(own, own, sends.at[0], receives.at[0], x_peer)
    to_x.start()
    to_l = remote(own, own, sends.at[1], receives.at[1], l_peer)
    to_l.start()
    ready()
    use(t)
    to_x.wait_recv()
    other = block.at[lax.bitwise_xor(t, 2), pl.ds(0, half)]
    on_l = remote(other, other, sends.at[2], receives.at[2], l_peer)
    on_l.start()
    to_l.wait_recv()
    other = block.at[lax.bitwise_xor(t, 1), pl.ds(half, half)]
    on_x = remote(other, other, sends.at[3], receives.at[3], x_peer)
    on_x.start()
    use(lax.bitwise_xor(t, 2))
    use(lax.bitwise_xor(t, 1))
    on_l.wait_recv()
    on_x.wait_recv()
    use(lax.bitwise_xor(t, 3))
    for copy in (to_x, to_l, on_l, on_x):
        copy.wait_send()


def group_scatter(part, t, low, got, sends, receives, between=None):
    half = low.shape[1]
    x_peer, l_peer = flipped(X_BIT), flipped(L_BIT)

    def send(slot, value, peer):
        low[slot] = value.astype(LOW)
        copy = remote(low.at[slot], got.at[slot], sends.at[slot], receives.at[slot], peer)
        copy.start()
        return copy

    def arrived(slot):
        return got[slot].astype(WIDE)

    far = part(lax.bitwise_xor(t, 3))
    far_x = send(0, far[:half], x_peer)
    far_l = send(1, far[half:], l_peer)
    beside_x = part(lax.bitwise_xor(t, 2))
    near_x = send(2, beside_x[:half], x_peer)
    beside_l = part(lax.bitwise_xor(t, 1))
    near_l = send(3, beside_l[half:], l_peer)
    far_x.wait_recv()
    on_l = send(4, beside_l[:half] + arrived(0), l_peer)
    far_l.wait_recv()
    on_x = send(5, beside_x[half:] + arrived(1), x_peer)
    own = part(t)
    if between is not None:
        between()
    near_x.wait_recv()
    near_l.wait_recv()
    on_l.wait_recv()
    on_x.wait_recv()
    result = jnp.concatenate(
        [own[:half] + arrived(2) + arrived(4), own[half:] + arrived(3) + arrived(5)], axis=0
    )
    for copy in (far_x, far_l, near_x, near_l, on_l, on_x):
        copy.wait_send()
    return result


def group_scratch(n, width):
    return [
        pltpu.VMEM((6, n // 2, width), LOW),
        pltpu.VMEM((6, n // 2, width), LOW),
        pltpu.SemaphoreType.DMA((4,)),
        pltpu.SemaphoreType.DMA((4,)),
        pltpu.SemaphoreType.DMA((6,)),
        pltpu.SemaphoreType.DMA((6,)),
    ]


def block_rows(j, n):
    return pl.ds(pl.multiple_of(j * n, n), n)


def slots():
    return [(c, y, h) for c in range(2) for y in range(2) for h in range(2)]


class Spread:
    def __init__(self, held, sends, receives):
        self.held, self.sends, self.receives = held, sends, receives

    def copy(self, step):
        y, _, c, h, _ = bits()
        own = c * 4 + y * 2 + h
        near = c * 4 + y * 2 + 1 - h
        view = self.held.at[(pl.ds(own, 1), pl.ds(own, 1), pl.ds(near, 1), pl.ds(c * 4, 4))[step]]
        peer = flipped((H_BIT, Y_BIT, Y_BIT, C_BIT)[step])
        return remote(view, view, self.sends.at[step], self.receives.at[step], peer)

    def begin(self):
        self.copy(0).start()
        self.copy(1).start()

    def forward(self):
        self.copy(0).wait_recv()
        self.copy(2).start()

    def over_c(self):
        self.copy(1).wait_recv()
        self.copy(2).wait_recv()
        self.copy(3).start()

    def done(self):
        self.copy(3).wait_recv()
        for step in range(4):
            self.copy(step).wait_send()


def load_rows(held, target, sem, share, column, width):
    for slot, (c, y, h) in enumerate(slots()):
        for x in range(2):
            pltpu.make_async_copy(
                held.at[slot, pl.ds(x * 2 * share, 2 * share), pl.ds(column, width)],
                target.at[pl.ds((y * 16 + x * 8 + c * 4 + h * 2) * share, 2 * share), :],
                sem,
            ).start()


def load_chunks(held, target, sem, share, column, width):
    for slot, (c, y, h) in enumerate(slots()):
        for chunk in range(4):
            pltpu.make_async_copy(
                held.at[slot, pl.ds(chunk * share, share), pl.ds(column, width)],
                target.at[pl.ds((y * 4 + c * 2 + h) * share, share), pl.ds(chunk * width, width)],
                sem,
            ).start()


def load_blocks(held, target, sem, first, share):
    for slot, (c, y, h) in enumerate(slots()):
        pltpu.make_async_copy(
            held.at[slot, pl.ds(first, share)],
            target.at[pl.ds((y * 4 + c * 2 + h) * share, share), :],
            sem,
        ).start()


def load_line(held, target, sem, first, width):
    for slot, (c, y, h) in enumerate(slots()):
        pltpu.make_async_copy(
            held.at[slot, pl.ds(first, 16), pl.ds(0, width)],
            target.at[:, pl.ds((y * 4 + c * 2 + h) * width, width)],
            sem,
        ).start()


def settle(target, sem):
    pltpu.make_async_copy(target, target, sem).wait()


def relative(target, c, y, h):
    y_me, _, c_me, h_me, _ = bits()
    return target.at[
        lax.bitwise_xor(c_me, c), lax.bitwise_xor(y_me, y), lax.bitwise_xor(h_me, h)
    ]


def store_rows(target, grads, share, column):
    width = grads.shape[1]
    for c, y, h in slots():
        for x in range(2):
            row = (y * 16 + x * 8 + c * 4 + h * 2) * share
            relative(target, c, y, h)[
                x * 2 * share : (x + 1) * 2 * share, column : column + width
            ] = grads[row : row + 2 * share, :].astype(LOW)


def store_chunks(target, grads, share, column):
    width = grads.shape[1] // 4
    for c, y, h in slots():
        row = (y * 4 + c * 2 + h) * share
        for chunk in range(4):
            relative(target, c, y, h)[
                chunk * share : (chunk + 1) * share, column : column + width
            ] = grads[row : row + share, chunk * width : (chunk + 1) * width].astype(LOW)


def store_blocks(target, grads, first, share):
    for c, y, h in slots():
        row = (y * 4 + c * 2 + h) * share
        relative(target, c, y, h)[first : first + share, :] = grads[row : row + share, :].astype(LOW)


class Gather:
    def __init__(self, parts, got_c, got_y, got_h, sends, receives):
        self.parts, self.got = parts, (got_c, got_y, got_h)
        self.sends, self.receives = sends, receives

    def copy(self, step):
        source = (self.parts.at[1], self.parts.at[0, 1], self.parts.at[0, 0, 1])[step]
        return remote(
            source,
            self.got[step],
            self.sends.at[step],
            self.receives.at[step],
            flipped((C_BIT, Y_BIT, H_BIT)[step]),
        )

    def over_c(self):
        self.copy(0).start()

    def over_y(self):
        self.copy(0).wait_recv()
        for y in (1, 0):
            for h in range(2):
                summed = self.parts[0, y, h].astype(WIDE) + self.got[0][y, h].astype(WIDE)
                self.parts[0, y, h] = summed.astype(LOW)
            if y == 1:
                self.copy(1).start()

    def over_h(self):
        self.copy(1).wait_recv()
        for h in (1, 0):
            summed = self.parts[0, 0, h].astype(WIDE) + self.got[1][h].astype(WIDE)
            self.parts[0, 0, h] = summed.astype(LOW)
            if h == 1:
                self.copy(2).start()

    def done(self):
        self.copy(2).wait_recv()
        for step in range(3):
            self.copy(step).wait_send()

    def total(self, first, last):
        return self.parts[0, 0, 0, first:last, :].astype(WIDE) + self.got[2][first:last, :].astype(WIDE)


class Sizes:
    def __init__(self, n, width, inner, layers, taps, vocab):
        self.n, self.width, self.inner, self.layers = n, width, inner, layers
        self.taps, self.vocab = taps, vocab
        self.count = 4 * n
        self.part = width // 4
        self.head = width // HEADS
        self.heads = self.part // self.head
        self.share = width // DEVICES
        self.inner_share = inner // PIECES
        self.scale = self.head**-0.5
        self.group_width = width // CONV_G
        self.packs = n // PACK
        self.steps = taps // PACK + 1
        self.length = self.count + (RANKS - 1) * 64
        self.lines = self.length + 128
        self.held_rows = (4 * self.share, 4 * self.share, self.inner_share + 16)
        self.grad_rows = (4 * self.share + 16, 4 * self.share, self.inner_share + 16)
        self.bundles = 3 * layers
        self.at = {"entry": 0, "base": 1}
        at = 2
        for name in ("attend", "middle", "lower", "return", "final", "upper"):
            self.at[name] = at
            at += layers
        self.vectors = at
        self.at["head"] = at
        self.at["heads"] = at + vocab
        self.named = at + vocab + 2 * layers
        self.line = -(-(self.named + 1) // 8) * 8
        self.gathered = 64

    def saved(self):
        n, count, layers, width = self.n, self.count, self.layers, self.width
        return [
            ((layers, 4, n, width), LOW),
            ((layers, count, 3 * self.part), LOW),
            ((layers, self.heads * count, count), LOW),
            ((layers, count, self.part), LOW),
            ((layers, n, width), WIDE),
            ((layers, 4, n, width), LOW),
            ((layers, count, self.inner), LOW),
            ((layers, count, self.inner), LOW),
            ((layers, n, width), WIDE),
        ]


def forward(z, features, cot_turned, kernel_weight, small, head_weight, ends_own, hidden_bias, joint_weight, expand_weight, output_weight, reduce_weight):
    kept = z.saved()
    kinds = len(kept)
    layers, n, width, part, inner, share = z.layers, z.n, z.width, z.part, z.inner, z.share
    count, head, heads, packs, gw = z.count, z.head, z.heads, z.packs, z.group_width
    depth, own_width = PACK * gw, PACK * share

    def kernel(*refs):
        (f_ref, cot_ref, k_ref, small_ref, head_ref, e_ref, hb_ref, jw_ref, ew_ref, ow_ref, rw_ref) = refs[:11]
        rest = refs[11:]
        (logits_ref, flow_ref, part_ref, whole, mixed_ref, bend_ref, ends_ref) = rest[:7]
        even_out, odd_out, taps_out = rest[7:10]
        held = rest[10 : 10 + z.bundles]
        saved = rest[10 + z.bundles : 10 + z.bundles + kinds]
        rest = rest[10 + z.bundles + kinds :]
        (x_all, qkv, weights_low, context, residual, m_all, active, slope, outer) = rest[:kinds]
        (now, wj, wo, we, wr, hb, low_buf, got, gs, gr, ss, sr) = rest[kinds : kinds + 12]
        (bs, br, ws, ks, tokens, messages, feats, small_all, packed, wide, even, odd, taps, out_messages) = rest[kinds + 12 : kinds + 26]
        (pres, new_feats, cot, logits_own, cs, cr, rs, fs, ms, mr, lines_out) = rest[kinds + 26 : kinds + 37]
        (cols, hidden_lines, gathering, message) = rest[kinds + 37 : kinds + 41]
        swap1, swap2, swap3 = (rest[kinds + 41 + 3 * k : kinds + 44 + 3 * k] for k in range(3))
        y, x, c, h, l = bits()
        t = x * 2 + l
        slot = c * 4 + y * 2 + h

        put_lanes(tokens, f_ref[...].astype(WIDE))
        for f in range(0, PACK, 2):
            for q in range(width // 128):
                pair = [tokens[q, pl.ds(f + k, packs, stride=PACK), :] for k in range(2)]
                for k in range(2):
                    messages[2 * q + k, :, f * gw : (f + 2) * gw] = jnp.concatenate(
                        [piece[:, k * gw : (k + 1) * gw] for piece in pair], axis=1
                    ).astype(LOW)
        def column_copies():
            copies = []
            for layer in range(layers):
                for kind, (first, span) in enumerate(((0, 3 * part), (3 * part, inner))):
                    target = held[3 * layer + kind].at[slot, pl.ds(t * share, share), pl.ds(0, span)]
                    for number, mask in enumerate((0, L_BIT, X_BIT, X_BIT | L_BIT)):
                        place = place_of(mask)
                        source = cols.at[place[1] * 2 + place[4], layer, :, pl.ds(first, span)]
                        if mask == 0:
                            copy = pltpu.make_async_copy(source, target, cr.at[layer, kind, 0])
                        else:
                            copy = remote(
                                source, target, cs.at[layer, kind, number], cr.at[layer, kind, number], flipped(mask)
                            )
                        copies.append((3 * layer + kind, mask, copy))
            return copies

        def row_copies():
            copies = []
            for layer in range(layers):
                for kind, (source, first) in enumerate(((rw_ref, 0), (hidden_lines, z.inner_share))):
                    target = held[3 * layer + 2].at[slot, pl.ds(first, source.shape[1])]
                    copies.append((3 * layer + 2, pltpu.make_async_copy(source.at[layer], target, rs.at[layer, kind])))
            return copies

        moves = []
        for layer in range(layers):
            pairs = [
                (
                    ow_ref.at[layer, :, pl.ds(chunk * part, part)],
                    held[3 * layer].at[
                        c * 4 + y * 2 + l, pl.ds(chunk * share, share), pl.ds(3 * part, part)
                    ],
                )
                for chunk in range(4)
            ]
            moves.append(Move(pairs, h == l, H_BIT | L_BIT, ms.at[layer], mr.at[layer]))
        column_all, row_all = column_copies(), row_copies()
        greet_all()
        hidden_lines[...] = jnp.zeros_like(hidden_lines)
        for layer in range(layers):
            hidden_lines[layer, :, 0 : z.inner_share] = jnp.broadcast_to(
                hb_ref[layer : layer + 1, :].astype(WIDE), (16, z.inner_share)
            ).astype(LOW)
        for _, copy in row_all:
            copy.start()

        for x_at in range(2):
            for l_at in range(2):
                for layer in range(layers):
                    for which in range(3):
                        for y_at in range(2):
                            cuts = [
                                which * width + (y_at * 8 + x_at * 4 + c_at * 2 + l_at) * head for c_at in range(2)
                            ]
                            at = which * part + y_at * 2 * head
                            cols[x_at * 2 + l_at, layer, :, at : at + 2 * head] = jnp.concatenate(
                                [jw_ref[layer, :, cut : cut + head] for cut in cuts], axis=1
                            )
                    for c_at, y_at, h_at in slots():
                        cut = index_of(y_at, x_at, c_at, h_at, l_at) * z.inner_share
                        at = 3 * part + (y_at * 4 + c_at * 2 + h_at) * z.inner_share
                        cols[x_at * 2 + l_at, layer, :, at : at + z.inner_share] = ew_ref[
                            layer, :, cut : cut + z.inner_share
                        ]
        same = lax.broadcasted_iota(jnp.int32, (share, share), 0) == lax.broadcasted_iota(jnp.int32, (share, share), 1)
        unit = jnp.where(same, 1.0, 0.0).astype(LOW)
        lines_low = small_ref[...].astype(WIDE)
        gathering[...] = jnp.zeros_like(gathering)
        gathering[0 : z.vectors, 0:share] = lines_low[0 : z.vectors]
        gathering[z.vectors : z.at["heads"], 0:share] = dot_lt(head_ref[...], unit)
        gathering[z.at["heads"] : z.named, 0:share] = lines_low[z.vectors : z.vectors + 2 * layers]
        own_ends = e_ref[...]
        gathering[z.named : z.named + 1, 0:4] = lax.shift_right_logical(own_ends, 5).astype(WIDE)
        gathering[z.named : z.named + 1, 4:8] = lax.bitwise_and(own_ends, 31).astype(WIDE)
        per_line = 128 // share
        message_lines = gathering.shape[0] // per_line
        message[...] = jnp.concatenate(
            [gathering[pl.ds(k, message_lines, stride=per_line), :][:, 0:share] for k in range(per_line)], axis=1
        ).astype(LOW)
        position = jnp.concatenate([lines_low[z.vectors + 2 * layers : z.vectors + 2 * layers + 1]] * PACK, axis=1)

        jobs = [Spread(held[b], bs.at[b], br.at[b]) for b in range(z.bundles)]
        all_greeted()

        def launch(layer):
            for number, _, copy in column_all:
                if number // 3 == layer:
                    copy.start()
            moves[layer].start()

        launch(0)
        to_owners = Swap(lambda *place: messages.at[index_of(*place) // 2], feats, *swap1)
        to_owners.start()
        vectors = Swap(lambda *place: message, small_all, *swap2)
        vectors.start()
        frames_move = Move([(f_ref, new_feats), (cot_ref, cot)], x == h, X_BIT | H_BIT, fs.at[0], fs.at[1])
        frames_move.start()
        for layer in range(1, layers):
            launch(layer)

        def own_ready(bundle):
            for number, mask, copy in column_all:
                if number == bundle:
                    if mask:
                        copy.wait_recv()
                        copy.wait_send()
                    else:
                        copy.wait()
            for number, copy in row_all:
                if number == bundle:
                    copy.wait()
            if bundle % 3 == 0:
                moves[bundle // 3].done()
            jobs[bundle].begin()

        own_ready(2)

        def keep(source, target, sem):
            pltpu.make_async_copy(source, target, sem).start()

        span = z.taps * gw
        for step in range(z.steps):
            taps[step] = jnp.zeros((own_width, depth), LOW)
        for f in range(PACK):
            lines = slice(f * share, (f + 1) * share)
            shift = f * gw
            for step in range(z.steps):
                begin = max(step * depth - shift, 0)
                end = min((step + 1) * depth - shift, span)
                at = begin + shift - step * depth
                if begin < end:
                    taps[step, lines, at : at + end - begin] = k_ref[:, begin:end]
        keep(taps, taps_out, ks.at[kinds, 0])

        own_ready(0)
        own_ready(1)
        to_owners.arrived()
        jobs[2].forward()
        vectors.arrived()
        for at in range(DEVICES):
            place = pl.ds((at % 4) * packs * 8 + at // 4, packs, stride=8)
            for q in range(depth // 128):
                packed[q, place, :] = feats[at, :, q * 128 : (q + 1) * 128].astype(WIDE)
        line, lane = z.named * share // 128, z.named * share % 128
        encoded = jnp.concatenate(
            [small_all[4 * row, line : line + 1, :].astype(WIDE) for row in range(8)], axis=0
        )
        ends_ref[...] = encoded
        ends = [
            encoded[:, lane + k : lane + k + 1] * 32.0 + encoded[:, lane + 4 + k : lane + 5 + k]
            for k in range(4)
        ]
        bounds = bounds_of(ends, count)
        spread_ranks(wide, get_lanes(packed, depth), rank_lanes(bounds, count, gw), 64)
        fill_pair(wide, even, odd)
        keep(even, even_out, ks.at[kinds, 1])
        keep(odd, odd_out, ks.at[kinds + 1, 0])
        summed = jnp.zeros((z.length, own_width), WIDE)
        for step in range(z.steps):
            summed = summed + dot_rt(shifted(even, odd, step, z.length), taps[step])
            if step == z.steps // 2:
                jobs[0].forward()
        made = collect_ranks(summed, rank_lanes(bounds, count, share), count) + position
        put_lanes(packed, made)
        for at in range(DEVICES):
            place = pl.ds((at % 4) * packs * 8 + at // 4, packs, stride=8)
            for q in range(own_width // 128):
                out_messages[at, :, q * 128 : (q + 1) * 128] = packed[q, place, :].astype(LOW)
        to_frames = Swap(lambda *place: out_messages.at[turned_of(*place)], pres, *swap3)
        to_frames.start()
        jobs[0].over_c()
        jobs[2].over_c()
        own_ready(3)

        for q in range(width // 128):
            for k in range(per_line):
                cut = slice(k * share, (k + 1) * share)
                lines_out[q, pl.ds(k, message_lines, stride=per_line), :] = jnp.concatenate(
                    [small_all[at, :, cut].astype(WIDE) for at in range(4 * q, 4 * q + 4)], axis=1
                )
        whole[...] = get_lanes(lines_out, width)

        def vector(name, layer=0):
            at = z.at[name] + layer
            return whole[at : at + 1, :]

        heads_lines = jnp.zeros((2 * layers, part), WIDE)
        for x_at in range(2):
            for l_at in range(2):
                cuts = [
                    whole[
                        z.at["heads"] : z.at["heads"] + 2 * layers,
                        (y_at * 16 + x_at * 8 + c_at * 4 + l_at * 2) * share : (y_at * 16 + x_at * 8 + c_at * 4 + l_at * 2 + 2) * share,
                    ]
                    for y_at in range(2)
                    for c_at in range(2)
                ]
                heads_lines = jnp.where(t == x_at * 2 + l_at, jnp.concatenate(cuts, axis=1), heads_lines)
        mine = lax.broadcasted_iota(jnp.int32, (8, 1), 0) == y * 4 + h * 2 + c
        row_ends = [jnp.sum(jnp.where(mine, end, 0.0), axis=0, keepdims=True).astype(jnp.int32) for end in ends]
        across = lax.broadcasted_iota(jnp.int32, (1, count), 1)
        down = lax.broadcasted_iota(jnp.int32, (count, 1), 0)
        across = sum((across >= end).astype(jnp.int32) for end in row_ends)
        down = sum((down >= end).astype(jnp.int32) for end in row_ends)
        linked = down == across

        frames_move.done()
        to_frames.arrived()
        jobs[1].forward()
        own_ready(5)
        own_ready(4)
        for f in range(PACK):
            cut = slice(f * share, (f + 1) * share)
            for q in range(width // 128):
                tokens[q, pl.ds(f, packs, stride=PACK), :] = jnp.concatenate(
                    [pres[at, :, cut].astype(WIDE) for at in range(4 * q, 4 * q + 4)], axis=1
                )
        made, bent = gelu_pair(get_lanes(tokens, width))
        bend_ref[...] = bent
        mixed = new_feats[...].astype(WIDE) + made
        mixed_ref[...] = mixed
        now[...] = normed(mixed, vector("entry"), vector("base"))

        for layer in range(layers):
            first, second, third = jobs[3 * layer : 3 * layer + 3]
            later = jobs[3 * layer + 3 : 3 * layer + 6]
            x_all[layer, t] = now[...].astype(LOW)

            def attend_ready(layer=layer, first=first):
                first.done()
                load_rows(held[3 * layer], wj, ws.at[0], share, 0, 3 * part)
                load_chunks(held[3 * layer], wo, ws.at[1], share, 3 * part, part)
                settle(wj, ws.at[0])

            def attend_use(j, layer=layer):
                lines = block_rows(j, n)
                made = dot(x_all[layer, j], wj[...])
                qkv[layer, lines, 0:part] = ((made[:, 0:part] + heads_lines[layer : layer + 1]) * z.scale).astype(LOW)
                qkv[layer, lines, part : 2 * part] = made[:, part : 2 * part].astype(LOW)
                qkv[layer, lines, 2 * part :] = (
                    made[:, 2 * part :] + heads_lines[layers + layer : layers + layer + 1]
                ).astype(LOW)

            group_gather(x_all.at[layer], t, gs, gr, attend_ready, attend_use)
            if layer == 0:
                second.over_c()
                later[0].forward()
            keep(x_all.at[layer], saved[0].at[layer], ks.at[0, layer])
            keep(qkv.at[layer], saved[1].at[layer], ks.at[1, layer])
            for at in range(heads):
                queries = qkv[layer, :, at * head : (at + 1) * head]
                keys = qkv[layer, :, part + at * head : part + (at + 1) * head]
                values = qkv[layer, :, 2 * part + at * head : 2 * part + (at + 1) * head]
                scores = jnp.where(linked, dot_rt(queries, keys), masked_score)
                exponent = jnp.exp(scores - jnp.max(scores, axis=-1, keepdims=True))
                inverse = 1.0 / jnp.sum(exponent, axis=-1, keepdims=True)
                made = (exponent * inverse).astype(LOW)
                weights_low[layer, at * count : (at + 1) * count, :] = made
                context[layer, :, at * head : (at + 1) * head] = dot(made, values).astype(LOW)
            keep(weights_low.at[layer], saved[2].at[layer], ks.at[2, layer])
            keep(context.at[layer], saved[3].at[layer], ks.at[3, layer])
            settle(wo, ws.at[1])

            def advance(later=later):
                if later:
                    later[0].over_c()

            attended = group_scatter(
                lambda j: dot(context[layer, block_rows(j, n), :], wo[...]), t, low_buf, got, ss, sr, advance
            )
            residual[layer] = now[...] + (attended + vector("attend", layer))
            keep(residual.at[layer], saved[4].at[layer], ks.at[4, layer])
            middle = normed(residual[layer], vector("middle", layer), vector("lower", layer))
            now[...] = middle
            m_all[layer, t] = middle.astype(LOW)

            def feed_ready(layer=layer, second=second, third=third):
                second.done()
                load_rows(held[3 * layer + 1], we, ws.at[2], share, 0, inner)
                third.done()
                load_line(held[3 * layer + 2], hb, ws.at[4], z.inner_share, z.inner_share)
                load_blocks(held[3 * layer + 2], wr, ws.at[3], 0, z.inner_share)
                settle(we, ws.at[2])
                settle(hb, ws.at[4])

            def feed_use(j, layer=layer):
                lines = block_rows(j, n)
                made, bent = gelu_pair(dot(m_all[layer, j], we[...]) + hb[0:1, :].astype(WIDE))
                active[layer, lines, :] = made.astype(LOW)
                slope[layer, lines, :] = bent.astype(LOW)

            group_gather(m_all.at[layer], t, gs, gr, feed_ready, feed_use)
            if later:
                later[2].forward()
            keep(m_all.at[layer], saved[5].at[layer], ks.at[5, layer])
            keep(active.at[layer], saved[6].at[layer], ks.at[6, layer])
            keep(slope.at[layer], saved[7].at[layer], ks.at[7, layer])
            settle(wr, ws.at[3])

            def advance_more(later=later):
                if later:
                    later[1].forward()
                    later[2].over_c()

            fed = group_scatter(
                lambda j: dot(active[layer, block_rows(j, n), :], wr[...]), t, low_buf, got, ss, sr, advance_more
            )
            outer[layer] = now[...] + fed + vector("return", layer)
            keep(outer.at[layer], saved[8].at[layer], ks.at[8, layer])
            now[...] = normed(outer[layer], vector("final", layer), vector("upper", layer))
            if later:
                later[1].over_c()
        final_low = now[...].astype(LOW)
        head_turned = whole[z.at["head"] : z.at["head"] + z.vocab, :].astype(LOW)
        vocab_at = z.vectors + 2 * layers + 1
        vocab_bias = lines_low[vocab_at : vocab_at + 1, :].astype(LOW)
        logits_own[...] = dot_rt(head_turned, final_low) + dot_lt(vocab_bias, jnp.ones((1, n), LOW))
        logits_move = Move([(logits_own, logits_ref)], x == h, X_BIT | H_BIT, fs.at[2], fs.at[3])
        logits_move.start()
        flow_ref[...] = dot_lt(cot[...], head_turned)
        part_ref[...] = dot(cot[...], final_low)
        vocab_sum = dot_rt(jnp.ones((8, n), LOW), cot[...])
        vocab_sum = jnp.concatenate([vocab_sum] * (128 // z.vocab), axis=1)
        whole[z.line : z.line + 8, :] = jnp.concatenate([vocab_sum] * (width // 128), axis=1)
        logits_move.done()
        to_owners.sent()
        vectors.sent()
        to_frames.sent()
        for kind in range(kinds):
            for layer in range(layers):
                settle(saved[kind].at[layer], ks.at[kind, layer])
        settle(taps_out, ks.at[kinds, 0])
        settle(even_out, ks.at[kinds, 1])
        settle(odd_out, ks.at[kinds + 1, 0])

    outs = pl.pallas_call(
        kernel,
        out_shape=[
            jax.ShapeDtypeStruct((z.vocab, n), WIDE),
            jax.ShapeDtypeStruct((n, width), WIDE),
            jax.ShapeDtypeStruct((z.vocab, width), WIDE),
            jax.ShapeDtypeStruct((z.gathered, width), WIDE),
            jax.ShapeDtypeStruct((n, width), WIDE),
            jax.ShapeDtypeStruct((n, width), WIDE),
            jax.ShapeDtypeStruct((8, 128), WIDE),
            jax.ShapeDtypeStruct((z.lines, depth), LOW),
            jax.ShapeDtypeStruct((z.lines, depth), LOW),
            jax.ShapeDtypeStruct((z.steps, own_width, depth), LOW),
        ]
        + [jax.ShapeDtypeStruct((PIECES, z.held_rows[b % 3], width), LOW) for b in range(z.bundles)]
        + [jax.ShapeDtypeStruct(shape, kind) for shape, kind in kept],
        in_specs=[IN_VMEM] * 9 + [ANYWHERE] * 2,
        out_specs=[IN_VMEM] * 7 + [ANYWHERE] * (3 + z.bundles + kinds),
        scratch_shapes=[pltpu.VMEM(shape, kind) for shape, kind in kept]
        + [
            pltpu.VMEM((n, width), WIDE),
            pltpu.VMEM((width, 3 * part), LOW),
            pltpu.VMEM((part, width), LOW),
            pltpu.VMEM((width, inner), LOW),
            pltpu.VMEM((inner, width), LOW),
            pltpu.VMEM((16, inner), LOW),
        ]
        + group_scratch(n, width)
        + [
            pltpu.SemaphoreType.DMA((z.bundles, 4)),
            pltpu.SemaphoreType.DMA((z.bundles, 4)),
            pltpu.SemaphoreType.DMA((5,)),
            pltpu.SemaphoreType.DMA((kinds + 2, layers)),
            pltpu.VMEM((width // 128, n, 128), WIDE),
            pltpu.VMEM((CONV_G, packs, depth), LOW),
            pltpu.VMEM((DEVICES, packs, depth), LOW),
            pltpu.VMEM((DEVICES, z.gathered * share // 128, 128), LOW),
            pltpu.VMEM((depth // 128, count, 128), WIDE),
            pltpu.VMEM((z.lines + 16, depth), WIDE),
            pltpu.VMEM((z.lines, depth), LOW),
            pltpu.VMEM((z.lines, depth), LOW),
            pltpu.VMEM((z.steps, own_width, depth), LOW),
            pltpu.VMEM((DEVICES, packs, own_width), LOW),
            pltpu.VMEM((DEVICES, packs, own_width), LOW),
            pltpu.VMEM((n, width), LOW),
            pltpu.VMEM((z.vocab, n), LOW),
            pltpu.VMEM((z.vocab, n), WIDE),
            pltpu.SemaphoreType.DMA((layers, 2, 4)),
            pltpu.SemaphoreType.DMA((layers, 2, 4)),
            pltpu.SemaphoreType.DMA((layers, 2)),
            pltpu.SemaphoreType.DMA((4, 2)),
            pltpu.SemaphoreType.DMA((layers, 4)),
            pltpu.SemaphoreType.DMA((layers, 4)),
            pltpu.VMEM((width // 128, z.gathered, 128), WIDE),
            pltpu.VMEM((4, layers, share, 3 * part + inner), LOW),
            pltpu.VMEM((layers, 16, width), LOW),
            pltpu.VMEM((z.gathered, 128), WIDE),
            pltpu.VMEM((z.gathered * share // 128, 128), LOW),
        ]
        + swap_sems() * 3,
        compiler_params=kernel_params(1),
        cost_estimate=cost(200),
    )(features, cot_turned, kernel_weight, small, head_weight, ends_own, hidden_bias, joint_weight, expand_weight, output_weight, reduce_weight)
    return outs[:7], outs[7:10], outs[10 : 10 + z.bundles], outs[10 + z.bundles :]


def backward(z, flow, head_sums, whole, mixed, bend, ends, even, odd, taps, held, saved):
    kinds = len(saved)
    layers, n, width, part, inner, share = z.layers, z.n, z.width, z.part, z.inner, z.share
    count, head, heads, packs, gw = z.count, z.head, z.heads, z.packs, z.group_width
    depth, own_width = PACK * gw, PACK * share
    bundles = z.bundles
    row_counts = [z.grad_rows[b % 3] for b in range(bundles)]
    lines = 8 * (-(-(3 + 6 * layers) // 8))
    tap_places = [(half, row, cut) for half in range(2) for row in range(4) for cut in range(2)]

    def kernel(*refs):
        flow_ref, head_ref, whole_ref, mixed_ref, bend_ref, ends_ref = refs[:6]
        even_ref, odd_ref, taps_ref = refs[6:9]
        held_refs = refs[9 : 9 + bundles]
        saved_refs = refs[9 + bundles : 9 + bundles + kinds]
        rest = refs[9 + bundles + kinds :]
        feats_ref, kernel_ref, position_ref, sums_ref, heads_ref = rest[:5]
        joint_ref, expand_ref, reduce_ref, output_ref, small_ref = rest[5:10]
        rest = rest[10:]
        parts = rest[:bundles]
        got_c, got_y, got_h = (rest[k * bundles : (k + 1) * bundles] for k in range(1, 4))
        rest = rest[4 * bundles :]
        buffers = rest[:kinds]
        (x_all, qkv, weights_low, context, residual, m_all, active, slope, outer) = buffers
        rest = rest[kinds:]
        inner_low = slope
        (fed, grad_low, joint, wj, wo, we, wr, low_buf, got, gs, gr, ss, sr) = rest[:13]
        rest = rest[13:]
        (rs_s, rs_r, ws, ks, back, vector_sums, all_sums, all_heads, tokens, out_low, low_parts) = rest[:11]
        (wide, grads_even, grads_odd, collected, out_feats, feat_parts) = rest[11:17]
        even, odd = weights_low.at[pl.ds(0, z.lines)], weights_low.at[pl.ds(2 * count, z.lines)]
        (own_back, columns, column_parts, output_own, small_own, fs, cs, cr, ms, mr) = rest[17:27]
        swaps = [rest[27 + 3 * k : 30 + 3 * k] for k in range(4)]
        y, x, c, h, l = bits()
        t = x * 2 + l

        def fetch(kind, layer):
            pltpu.make_async_copy(saved_refs[kind].at[layer], buffers[kind], ks.at[kind]).start()

        def need(kind):
            settle(buffers[kind], ks.at[kind])

        def load_feed(layer):
            fetch(8, layer)
            load_blocks(held_refs[3 * layer + 2], wr, ws.at[3], 0, z.inner_share)
            fetch(7, layer)
            load_rows(held_refs[3 * layer + 1], we, ws.at[2], share, 0, inner)
            for kind in (6, 5, 4):
                fetch(kind, layer)

        def load_attend(layer):
            load_chunks(held_refs[3 * layer], wo, ws.at[1], share, 3 * part, part)
            for kind in (1, 2, 3, 0):
                fetch(kind, layer)
            load_rows(held_refs[3 * layer], wj, ws.at[0], share, 0, 3 * part)

        def vector(name, layer=0):
            at = z.at[name] + layer
            return whole_ref[at : at + 1, :]

        def lanes_for(source):
            def block_for(*place):
                cut = pl.multiple_of(index_of(*place) * share // 128 * 128, 128)
                return source.at[:, pl.ds(cut, 128)]

            return block_for

        load_feed(layers - 1)
        load_attend(layers - 1)
        greet_all()
        all_greeted()
        heads_swap = Swap(lanes_for(head_ref), all_heads, *swaps[0])
        heads_swap.start()
        jobs = [
            Gather(parts[b], got_c[b], got_y[b], got_h[b], rs_s.at[b], rs_r.at[b]) for b in range(bundles)
        ]

        def column_copies(bundle):
            layer, kind = bundle // 3, bundle % 3
            first, extent = ((0, 3 * part), (3 * part, inner))[kind]
            copies = []
            for number, mask in enumerate((0, L_BIT, X_BIT, X_BIT | L_BIT)):
                place = place_of(mask)
                source = columns.at[layer, pl.ds((place[1] * 2 + place[4]) * share, share), pl.ds(first, extent)]
                target = column_parts.at[t, layer, :, pl.ds(first, extent)]
                if mask == 0:
                    copies.append(pltpu.make_async_copy(source, target, cr.at[layer, kind, 0]))
                else:
                    copies.append(
                        remote(source, target, cs.at[layer, kind, number], cr.at[layer, kind, number], flipped(mask))
                    )
            return copies

        def row_move(layer):
            pairs = [
                (
                    output_own.at[layer, pl.ds(chunk * share, share)],
                    output_ref.at[layer, :, pl.ds(chunk * part, part)],
                )
                for chunk in range(4)
            ]
            pairs.append((small_own.at[layer], small_ref.at[layer]))
            return Move(pairs, h == l, H_BIT | L_BIT, ms.at[layer], mr.at[layer])

        def hand_over(bundle):
            layer, kind = bundle // 3, bundle % 3
            jobs[bundle].done()
            if kind == 0:
                total = jobs[bundle].total(0, 4 * share)
                columns[layer, :, 0 : 3 * part] = total[:, : 3 * part].astype(LOW)
                output_own[layer] = total[:, 3 * part :]
                small_own[layer] = jobs[bundle].total(4 * share, 4 * share + 16)[:, 0:128]
                row_move(layer).start()
            elif kind == 1:
                columns[layer, :, 3 * part :] = jobs[bundle].total(0, 4 * share).astype(LOW)
            else:
                end = z.inner_share
                reduce_ref[layer] = jobs[bundle].total(0, end)
                sums_ref[8 * layer : 8 * layer + 8, :] = jobs[bundle].total(end, end + 16)[0:8, 0:128]
                return
            for copy in column_copies(bundle):
                copy.start()

        back[...] = flow_ref[...]
        vector_sums[...] = jnp.zeros_like(vector_sums)
        vector_sums[2 + 6 * layers : 3 + 6 * layers, :] = whole_ref[z.line : z.line + 1, :]

        for layer in reversed(range(layers)):
            last = layer == layers - 1
            attend_job, expand_job, reduce_job = jobs[3 * layer : 3 * layer + 3]
            after = 3 * layer + 3

            def note(name, value, layer=layer):
                at = z.at[name] + layer
                vector_sums[at : at + 1, :] = value

            need(8)
            outer_grad, final_part, upper_part = normed_back(outer[...], vector("final", layer), back[...])
            back[...] = outer_grad
            fed_low = outer_grad.astype(LOW)
            fed[0, t] = fed_low
            note("final", final_part)
            note("upper", upper_part)
            note("return", jnp.sum(fed_low.astype(WIDE), axis=0, keepdims=True))

            def feed_ready():
                settle(wr, ws.at[3])
                need(7)

            def feed_use(j):
                lines = block_rows(j, n)
                made = dot_rt(fed[0, j], wr[...]) * slope[lines, :].astype(WIDE)
                inner_low[lines, :] = made.astype(LOW)

            group_gather(fed.at[0], t, gs, gr, feed_ready, feed_use)
            if not last:
                jobs[after].over_h()
            settle(we, ws.at[2])
            need(6)
            need(5)

            def feed_weights(after=after, last=last, expand_job=expand_job, reduce_job=reduce_job):
                store_rows(expand_job.parts, dot_lt(m_all[...].reshape(count, width), inner_low[...]), share, 0)
                expand_job.over_c()
                target = reduce_job.parts
                store_blocks(target, dot_lt(active[...], fed[0].reshape(count, width)), 0, z.inner_share)
                hidden_sum = jnp.sum(inner_low[...].astype(WIDE), axis=0, keepdims=True)
                first = z.inner_share
                for c_at, y_at, h_at in slots():
                    at = (y_at * 4 + c_at * 2 + h_at) * z.inner_share
                    view = relative(target, c_at, y_at, h_at)
                    view[first : first + 16, :] = jnp.zeros((16, width), LOW)
                    view[first : first + 16, 0 : z.inner_share] = jnp.broadcast_to(
                        hidden_sum[:, at : at + z.inner_share], (16, z.inner_share)
                    ).astype(LOW)
                reduce_job.over_c()
                if not last:
                    hand_over(after + 1)

            got_back = group_scatter(
                lambda j: dot_rt(inner_low[block_rows(j, n), :], we[...]), t, low_buf, got, ss, sr, feed_weights
            )
            expand_job.over_y()
            reduce_job.over_y()
            need(4)
            res_grad, middle_part, lower_part = normed_back(
                residual[...], vector("middle", layer), back[...] + got_back
            )
            back[...] = res_grad
            note("middle", middle_part)
            note("lower", lower_part)
            if layer:
                load_feed(layer - 1)
            else:
                for step in range(z.steps - 1):
                    half, row, cut = tap_places[step]
                    target = (we, wr)[half].at[pl.ds(row * own_width, own_width), pl.ds(cut * depth, depth)]
                    pltpu.make_async_copy(taps_ref.at[step], target, ws.at[2 + half]).start()
            own_low = res_grad.astype(LOW)
            fed[1, t] = own_low
            note("attend", jnp.sum(own_low.astype(WIDE), axis=0, keepdims=True))

            def attend_ready():
                settle(wo, ws.at[1])

            def attend_use(j):
                grad_low[block_rows(j, n), :] = dot_rt(fed[1, j], wo[...]).astype(LOW)

            group_gather(fed.at[1], t, gs, gr, attend_ready, attend_use)
            expand_job.over_h()
            if not last:
                hand_over(after + 2)
                hand_over(after)
            if layer == 0:
                pltpu.make_async_copy(
                    taps_ref.at[z.steps - 1], wo.at[pl.ds(0, own_width), pl.ds(0, depth)], ws.at[1]
                ).start()
            for kind in (1, 2, 3):
                need(kind)
            for at in range(heads):
                mine = slice(at * head, (at + 1) * head)
                queries = qkv[:, mine]
                keys = qkv[:, part + at * head : part + (at + 1) * head]
                values = qkv[:, 2 * part + at * head : 2 * part + (at + 1) * head]
                weights = weights_low[at * count : (at + 1) * count, :]
                grads = grad_low[:, mine]
                weights_wide = weights.astype(WIDE)
                prob_grad = dot_rt(grads, values)
                delta = jnp.sum(weights_wide * prob_grad, axis=-1, keepdims=True)
                score_grad = (weights_wide * (prob_grad - delta)).astype(LOW)
                joint[:, mine] = (dot(score_grad, keys).astype(LOW).astype(WIDE) * z.scale).astype(LOW)
                joint[:, part + at * head : part + (at + 1) * head] = dot_lt(score_grad, queries).astype(LOW)
                joint[:, 2 * part + at * head : 2 * part + (at + 1) * head] = dot_lt(weights, grads).astype(LOW)
            if layer == 0:
                pltpu.make_async_copy(even_ref, even, ks.at[kinds]).start()
                pltpu.make_async_copy(odd_ref, odd, ks.at[kinds + 1]).start()
            settle(wj, ws.at[0])
            need(0)

            def attend_weights(attend_job=attend_job):
                target = attend_job.parts
                store_rows(target, dot_lt(x_all[...].reshape(count, width), joint[...]), share, 0)
                store_chunks(target, dot_lt(context[...], fed[1].reshape(count, width)), share, 3 * part)
                joint_sum = jnp.sum(joint[...].astype(WIDE), axis=0, keepdims=True)
                for c_at, y_at, h_at in slots():
                    at = (y_at * 4 + c_at * 2 + h_at) * share
                    view = relative(target, c_at, y_at, h_at)
                    line = jnp.concatenate(
                        [
                            joint_sum[:, at : at + share],
                            joint_sum[:, 2 * part + at : 2 * part + at + share],
                            jnp.zeros((1, 128 - 2 * share), WIDE),
                        ],
                        axis=1,
                    )
                    view[4 * share : 4 * share + 16, :] = jnp.zeros((16, width), LOW)
                    view[4 * share : 4 * share + 16, 0:128] = jnp.broadcast_to(line, (16, 128)).astype(LOW)
                attend_job.over_c()

            got_back = group_scatter(
                lambda j: dot_rt(joint[block_rows(j, n), :], wj[...]), t, low_buf, got, ss, sr, attend_weights
            )
            reduce_job.over_h()
            attend_job.over_y()
            back[...] = back[...] + got_back
            if layer:
                load_attend(layer - 1)

        mixed_grad, entry_part, base_part = normed_back(mixed_ref[...], vector("entry"), back[...])
        vector_sums[z.at["entry"] : z.at["entry"] + 1, :] = entry_part
        vector_sums[z.at["base"] : z.at["base"] + 1, :] = base_part
        back[...] = mixed_grad
        put_lanes(tokens, mixed_grad * bend_ref[...])
        for f in range(0, PACK, 4):
            for q in range(width // 128):
                four = [tokens[q, pl.ds(f + k, packs, stride=PACK), :] for k in range(4)]
                for k in range(4):
                    out_low[4 * q + k, :, f * share : (f + 4) * share] = jnp.concatenate(
                        [piece[:, k * share : (k + 1) * share] for piece in four], axis=1
                    ).astype(LOW)
        low_swap = Swap(lambda *place: out_low.at[index_of(*place)], low_parts, *swaps[1])
        low_swap.start()
        sums_swap = Swap(lanes_for(vector_sums), all_sums, *swaps[2])
        sums_swap.start()
        mixed_move = Move([(back, own_back)], x == h, X_BIT | H_BIT, fs.at[0], fs.at[1])
        mixed_move.start()
        encoded = ends_ref[...]
        lane = z.named * share % 128
        bounds = bounds_of(
            [
                encoded[:, lane + k : lane + k + 1] * 32.0 + encoded[:, lane + 4 + k : lane + 5 + k]
                for k in range(4)
            ],
            count,
        )
        pltpu.make_async_copy(even, even, ks.at[kinds]).wait()
        pltpu.make_async_copy(odd, odd, ks.at[kinds + 1]).wait()
        settle(we, ws.at[2])
        settle(wr, ws.at[3])
        settle(wo.at[pl.ds(0, own_width), pl.ds(0, depth)], ws.at[1])
        low_swap.arrived()
        for at, (y_at, x_at, c_at, h_at, l_at) in enumerate(itertools.product((0, 1), repeat=5)):
            row, block = y_at * 4 + h_at * 2 + c_at, x_at * 2 + l_at
            place = pl.ds(block * packs * 8 + row, packs, stride=8)
            for q in range(own_width // 128):
                collected[q, place, :] = low_parts[at, :, q * 128 : (q + 1) * 128].astype(WIDE)
        packed = get_lanes(collected, own_width)
        position_ref[...] = jnp.sum(packed, axis=0, keepdims=True)
        spread_ranks(wide, packed, rank_lanes(bounds, count, share), 64)
        fill_pair(wide, grads_even, grads_odd)
        across = wide[64 : 64 + z.length, :].T.astype(LOW)

        def taps_at(step):
            if step == z.steps - 1:
                return wo[0:own_width, 0:depth]
            half, row, cut = tap_places[step]
            return (we, wr)[half][row * own_width : (row + 1) * own_width, cut * depth : (cut + 1) * depth]

        summed = jnp.zeros((z.length, depth), WIDE)
        for step in range(z.steps):
            summed = summed + dot(shifted(grads_even, grads_odd, step, z.length), taps_at(z.steps - 1 - step))
            if step == z.steps // 2:
                jobs[0].over_h()
        put_lanes(collected, collect_ranks(summed, rank_lanes(bounds, count, gw), count))
        for at in range(DEVICES):
            place = pl.ds((at % 4) * packs * 8 + at // 4, packs, stride=8)
            for q in range(depth // 128):
                out_feats[at, :, q * 128 : (q + 1) * 128] = collected[q, place, :].astype(LOW)
        feats_swap = Swap(lambda *place: out_feats.at[index_of(*place)], feat_parts, *swaps[3])
        feats_swap.start()
        hand_over(1)
        hand_over(2)

        kernel_ref[...] = jnp.zeros_like(kernel_ref)
        for step in range(z.steps):
            made = dot(across, shifted(even, odd, step, z.length))
            for f in range(PACK):
                begin = (step + 1) * depth - f * gw
                kernel_ref[:, begin : begin + depth] += made[f * share : (f + 1) * share, :]
        hand_over(0)

        sums_swap.arrived()
        sums_ref[8 * layers :, :] = jnp.sum(all_sums[...], axis=0)
        heads_swap.arrived()
        heads_ref[...] = jnp.sum(all_heads[...], axis=0)
        feats_swap.arrived()
        for f in range(PACK):
            cut = slice(f * gw, (f + 1) * gw)
            for q in range(width // 128):
                tokens[q, pl.ds(f, packs, stride=PACK), :] = jnp.concatenate(
                    [
                        feat_parts[at, :, cut].astype(WIDE) + feat_parts[at + 1, :, cut].astype(WIDE)
                        for at in (4 * q, 4 * q + 2)
                    ],
                    axis=1,
                )
        mixed_move.done()
        feats_ref[...] = get_lanes(tokens, width) + own_back[...]
        for bundle in (4, 3, 1, 0):
            for copy in column_copies(bundle):
                copy.wait()
            layer, kind = bundle // 3, bundle % 3
            for x_at in range(2):
                for l_at in range(2):
                    piece = column_parts.at[x_at * 2 + l_at, layer]
                    if kind == 0:
                        for which in range(3):
                            for y_at in range(2):
                                for c_at in range(2):
                                    source = which * part + (y_at * 2 + c_at) * head
                                    target = which * width + (y_at * 8 + x_at * 4 + c_at * 2 + l_at) * head
                                    joint_ref[layer, :, target : target + head] = piece[
                                        :, source : source + head
                                    ].astype(WIDE)
                    else:
                        for c_at, y_at, h_at in slots():
                            source = 3 * part + (y_at * 4 + c_at * 2 + h_at) * z.inner_share
                            target = index_of(y_at, x_at, c_at, h_at, l_at) * z.inner_share
                            expand_ref[layer, :, target : target + z.inner_share] = piece[
                                :, source : source + z.inner_share
                            ].astype(WIDE)
        for layer in range(layers):
            row_move(layer).done()
        for swap in (heads_swap, low_swap, sums_swap, feats_swap):
            swap.sent()

    return pl.pallas_call(
        kernel,
        out_shape=[
            jax.ShapeDtypeStruct((n, width), WIDE),
            jax.ShapeDtypeStruct((share, (z.steps + 1) * depth), WIDE),
            jax.ShapeDtypeStruct((1, own_width), WIDE),
            jax.ShapeDtypeStruct((8 * layers + lines, 128), WIDE),
            jax.ShapeDtypeStruct((z.vocab, 128), WIDE),
            jax.ShapeDtypeStruct((layers, share, 3 * width), WIDE),
            jax.ShapeDtypeStruct((layers, share, 4 * inner), WIDE),
            jax.ShapeDtypeStruct((layers, z.inner_share, width), WIDE),
            jax.ShapeDtypeStruct((layers, share, width), WIDE),
            jax.ShapeDtypeStruct((layers, 16, 128), WIDE),
        ],
        in_specs=[IN_VMEM] * 6 + [ANYWHERE] * (3 + bundles + kinds),
        out_specs=[IN_VMEM] * 10,
        scratch_shapes=[pltpu.VMEM((2, 2, 2, rows, width), LOW) for rows in row_counts]
        + [pltpu.VMEM((2, 2, rows, width), LOW) for rows in row_counts]
        + [pltpu.VMEM((2, rows, width), LOW) for rows in row_counts]
        + [pltpu.VMEM((rows, width), LOW) for rows in row_counts]
        + [pltpu.VMEM(array.shape[1:], array.dtype) for array in saved]
        + [
            pltpu.VMEM((2, 4, n, width), LOW),
            pltpu.VMEM((count, part), LOW),
            pltpu.VMEM((count, 3 * part), LOW),
            pltpu.VMEM((width, 3 * part), LOW),
            pltpu.VMEM((part, width), LOW),
            pltpu.VMEM((width, inner), LOW),
            pltpu.VMEM((inner, width), LOW),
        ]
        + group_scratch(n, width)
        + [
            pltpu.SemaphoreType.DMA((bundles, 3)),
            pltpu.SemaphoreType.DMA((bundles, 3)),
            pltpu.SemaphoreType.DMA((4,)),
            pltpu.SemaphoreType.DMA((kinds + 2,)),
            pltpu.VMEM((n, width), WIDE),
            pltpu.VMEM((lines, width), WIDE),
            pltpu.VMEM((DEVICES, lines, 128), WIDE),
            pltpu.VMEM((DEVICES, z.vocab, 128), WIDE),
            pltpu.VMEM((width // 128, n, 128), WIDE),
            pltpu.VMEM((DEVICES, packs, own_width), LOW),
            pltpu.VMEM((DEVICES, packs, own_width), LOW),
            pltpu.VMEM((z.lines + 16, own_width), WIDE),
            pltpu.VMEM((z.lines, own_width), LOW),
            pltpu.VMEM((z.lines, own_width), LOW),
            pltpu.VMEM((depth // 128, count, 128), WIDE),
            pltpu.VMEM((DEVICES, packs, depth), LOW),
            pltpu.VMEM((DEVICES, packs, depth), LOW),
            pltpu.VMEM((n, width), WIDE),
            pltpu.VMEM((layers, 4 * share, 3 * part + inner), LOW),
            pltpu.VMEM((4, layers, share, 3 * part + inner), LOW),
            pltpu.VMEM((layers, 4 * share, part), WIDE),
            pltpu.VMEM((layers, 16, 128), WIDE),
            pltpu.SemaphoreType.DMA((2, 1)),
            pltpu.SemaphoreType.DMA((layers, 2, 4)),
            pltpu.SemaphoreType.DMA((layers, 2, 4)),
            pltpu.SemaphoreType.DMA((layers, 5)),
            pltpu.SemaphoreType.DMA((layers, 5)),
        ]
        + swap_sems() * 4,
        compiler_params=kernel_params(2),
        cost_estimate=cost(220),
    )(flow, head_sums, whole, mixed, bend, ends, even, odd, taps, *held, *saved)


def fast_local(*arguments):
    (
        features,
        utterance_ends,
        kernel_weight,
        position_bias,
        entry_gain,
        base_shift,
        joint_weight,
        query_bias,
        value_bias,
        output_weight,
        attend_bias,
        middle_gain,
        lower_shift,
        expand_weight,
        hidden_bias,
        reduce_weight,
        return_bias,
        final_gain,
        upper_shift,
        head_weight,
        vocab_bias,
        cotangent,
    ) = arguments
    _, n, width = features.shape
    layers, inner_all = joint_weight.shape[0], expand_weight.shape[2]
    vocab = head_weight.shape[1]
    taps = kernel_weight.shape[1] // (width // CONV_G)
    z = Sizes(n, width, inner_all // 4, layers, taps, vocab)
    share = z.share

    small = jnp.concatenate(
        [entry_gain[None], base_shift[None], attend_bias, middle_gain, lower_shift]
        + [return_bias, final_gain, upper_shift, query_bias, value_bias]
        + [position_bias[None], vocab_bias[None]],
        axis=0,
    )
    firsts, conv_saved, held, saved = forward(
        z,
        features[0],
        cotangent[0].T,
        kernel_weight,
        small,
        head_weight,
        utterance_ends,
        hidden_bias,
        joint_weight,
        expand_weight,
        output_weight,
        reduce_weight,
    )
    logits, flow, head_sums, whole, mixed, bend, ends = firsts
    (
        features_grad,
        kernel_wide,
        position_part,
        sums,
        heads_sums,
        joint_own,
        expand_own,
        reduce_own,
        output_own,
        small_own,
    ) = backward(z, flow, head_sums, whole, mixed, bend, ends, *conv_saved, held, saved)
    _, _, _, h, l = bits()
    place = (h * 2 + l) * share
    own_sums = lax.dynamic_slice_in_dim(sums[8 * layers :], place, share, axis=1)
    head_own = lax.dynamic_slice_in_dim(heads_sums, place, share, axis=1).T

    first = PACK * z.group_width

    def own(name):
        return own_sums[z.at[name] : z.at[name] + layers]

    return (
        logits.T[None],
        features_grad[None],
        kernel_wide[:, first : first + kernel_weight.shape[1]],
        jnp.sum(position_part.reshape(PACK, share), axis=0),
        own_sums[0],
        own_sums[1],
        joint_own,
        small_own[:, 0, :share],
        small_own[:, 0, share : 2 * share],
        output_own,
        own("attend"),
        own("middle"),
        own("lower"),
        expand_own,
        sums[0 : 8 * layers : 8, : z.inner_share],
        reduce_own,
        own("return"),
        own("final"),
        own("upper"),
        head_own,
        own_sums[z.vectors],
    )


def fits(dp_size, seq_size, width):
    share = width // 32
    return (
        dp_size == 8
        and seq_size == 4
        and share % 16 == 0
        and share * 2 == width // CONV_G
        and share * 2 == width // HEADS
    )


def placed(mesh, width):
    if fits(mesh.shape["dp"], mesh.shape["seq"], width):
        body = fast_local
        mesh = jax.sharding.Mesh(mesh.devices.reshape((2,) * len(AXES)), AXES)
        split, over, within = AXES[:3], AXES[3:], AXES
    else:
        body, split, over, within = local, "dp", "seq", ("dp", "seq")
    tokens = P(split, over, None)
    first, first_wide = P(within), P(within, None)
    second, second_wide = P(None, within), P(None, within, None)
    return jax.shard_map(
        body,
        mesh=mesh,
        in_specs=(
            tokens,
            P(split, None),
            first_wide,
            first,
            first,
            first,
            second_wide,
            second,
            second,
            second_wide,
            second,
            second,
            second,
            second_wide,
            second,
            second_wide,
            second,
            second,
            second,
            first_wide,
            P(),
            tokens,
        ),
        out_specs=(
            tokens,
            tokens,
            first_wide,
            first,
            first,
            first,
            second_wide,
            second,
            second,
            second_wide,
            second,
            second,
            second,
            second_wide,
            second,
            second_wide,
            second,
            second,
            second,
            first_wide,
            P(),
        ),
        check_vma=False,
    )


def solution(mesh):
    def whole(*arguments):
        return placed(mesh, arguments[0].shape[2])(*arguments)

    return whole
```

```python
import itertools
import math

import jax
import jax.numpy as jnp
from jax import lax
from jax.experimental import pallas as pl
from jax.experimental.pallas import tpu as pltpu
from jax.sharding import PartitionSpec as P

HEADS = 16
CONV_G = 16


epsilon = 1e-05
masked_score = -1e30


def with_halo(cells, sides, width):
    for axis, dim in sides:
        count = lax.axis_size(axis)
        ends = count - 1
        head = lax.slice_in_dim(cells, 0, width, axis=dim)
        tail = lax.slice_in_dim(cells, cells.shape[dim] - width, cells.shape[dim], axis=dim)
        cells = jnp.concatenate(
            [
                lax.ppermute(tail, axis, [(i, (i + 1) % count) for i in range(ends)]),
                cells,
                lax.ppermute(head, axis, [((i + 1) % count, i) for i in range(ends)]),
            ],
            axis=dim,
        )
    return cells


def layer_norm(tensor, scaling, shifts):
    average = jnp.mean(tensor, axis=-1, keepdims=True)
    centred = tensor - average
    spread = jnp.mean(centred * centred, axis=-1, keepdims=True)
    return centred * lax.rsqrt(spread + epsilon) * scaling + shifts


def norm_pullback(tensor, scaling, upstream):
    _, pullback = jax.vjp(layer_norm, tensor, scaling, jnp.zeros_like(scaling))
    return pullback(upstream)


def gelu_exact(tensor):
    return jax.nn.gelu(tensor, approximate=False)


def rounded(tensor):
    return tensor.astype(jnp.bfloat16)


def widened(tensor):
    return tensor.astype(jnp.float32)


def segment_ids(positions, utterance_ends):
    return jnp.sum(
        (positions[None, :, None] >= utterance_ends[:, None, :]).astype(jnp.int32), axis=2
    )


def unfold(source, source_ids, target_ids, anchors):
    length = target_ids.shape[1]
    pieces = [lax.slice_in_dim(source, anchor, anchor + length, axis=1) for anchor in anchors]
    matches = [
        lax.slice_in_dim(source_ids, anchor, anchor + length, axis=1) == target_ids
        for anchor in anchors
    ]
    stacked = jnp.stack(pieces, axis=2)
    keepers = jnp.stack(matches, axis=2)
    return jnp.where(keepers[..., None], stacked, jnp.zeros_like(stacked))


def conv_forward(halo_feats, halo_ids, frame_ids, kernel_grid, tap_block):
    row_count, frame_count = frame_ids.shape
    groups, group_width, tap_count, inner_width = kernel_grid.shape
    summed = jnp.zeros((row_count, frame_count, groups, group_width), jnp.float32)
    for block_at in range(tap_count // tap_block):
        first_tap = block_at * tap_block
        window = unfold(
            halo_feats,
            halo_ids,
            frame_ids,
            [first_tap + inner_tap for inner_tap in range(tap_block)],
        )
        window = window.reshape(row_count, frame_count, tap_block, groups, inner_width)
        summed = summed + jnp.einsum(
            "rtkgi,goki->rtgo",
            window,
            kernel_grid[:, :, first_tap : first_tap + tap_block, :],
            preferred_element_type=jnp.float32,
        )
    return summed.reshape(row_count, frame_count, groups * group_width)


def conv_backward(halo_grads, halo_feats, halo_ids, frame_ids, kernel_grid, tap_block, conv_low):
    row_count, frame_count = frame_ids.shape
    groups, group_width, tap_count, inner_width = kernel_grid.shape
    input_part = jnp.zeros((row_count, frame_count, groups, inner_width), jnp.float32)
    grouped = conv_low.reshape(row_count, frame_count, groups, group_width)
    kernel_parts = []
    for block_at in range(tap_count // tap_block):
        first_tap = block_at * tap_block
        tap_list = [first_tap + inner_tap for inner_tap in range(tap_block)]
        grads_window = unfold(
            halo_grads, halo_ids, frame_ids, [tap_count - tap_at for tap_at in tap_list]
        )
        grads_window = grads_window.reshape(row_count, frame_count, tap_block, groups, group_width)
        input_part = input_part + jnp.einsum(
            "rtkgo,goki->rtgi",
            grads_window,
            kernel_grid[:, :, first_tap : first_tap + tap_block, :],
            preferred_element_type=jnp.float32,
        )
        feats_window = unfold(halo_feats, halo_ids, frame_ids, tap_list)
        feats_window = feats_window.reshape(row_count, frame_count, tap_block, groups, inner_width)
        kernel_parts.append(
            jnp.einsum(
                "rtgo,rtkgi->goki", grouped, feats_window, preferred_element_type=jnp.float32
            )
        )
    kernel_full = jnp.concatenate(kernel_parts, axis=2).reshape(
        groups * group_width, tap_count * inner_width
    )
    return (input_part.reshape(row_count, frame_count, groups * inner_width), kernel_full)


def split_heads(tensor, head_count):
    return tensor.reshape(
        tensor.shape[0], tensor.shape[1], head_count, tensor.shape[2] // head_count
    )


def attend_scores(queries, all_keys, query_ids, key_ids, head_count):
    scores = jnp.einsum(
        "rqhd,rkhd->rhqk",
        split_heads(queries, head_count),
        split_heads(all_keys, head_count),
        preferred_element_type=jnp.float32,
    )
    allowed = query_ids[:, None, :, None] == key_ids[:, None, None, :]
    return jnp.where(allowed, scores, masked_score)


def attend_forward(queries, all_keys, all_values, frame_ids, row_ids, head_count):
    scores = attend_scores(queries, all_keys, frame_ids, row_ids, head_count)
    row_peak = jnp.max(scores, axis=-1, keepdims=True)
    exponent = jnp.exp(scores - row_peak)
    totals = jnp.sum(exponent, axis=-1, keepdims=True)
    weights_low = rounded(exponent / totals)
    context = jnp.einsum(
        "rhqk,rkhd->rqhd",
        weights_low,
        split_heads(all_values, head_count),
        preferred_element_type=jnp.float32,
    )
    return (rounded(context.reshape(queries.shape)), row_peak + jnp.log(totals))


def attend_backward(
    queries, all_keys, all_values, frame_ids, row_ids, head_count, log_totals, context_low
):
    scores = attend_scores(queries, all_keys, frame_ids, row_ids, head_count)
    attention = jnp.exp(scores - log_totals)
    weights_low = rounded(attention)
    grad_heads = split_heads(context_low, head_count)
    prob_grad = jnp.einsum(
        "rqhd,rkhd->rhqk",
        grad_heads,
        split_heads(all_values, head_count),
        preferred_element_type=jnp.float32,
    )
    row_delta = jnp.sum(attention * prob_grad, axis=-1, keepdims=True)
    score_grad = rounded(attention * (prob_grad - row_delta))
    value_part = jnp.einsum(
        "rhqk,rqhd->rkhd", weights_low, grad_heads, preferred_element_type=jnp.float32
    )
    query_part = jnp.einsum(
        "rhqk,rkhd->rqhd",
        score_grad,
        split_heads(all_keys, head_count),
        preferred_element_type=jnp.float32,
    )
    key_part = jnp.einsum(
        "rhqk,rqhd->rkhd",
        score_grad,
        split_heads(queries, head_count),
        preferred_element_type=jnp.float32,
    )
    return (
        query_part.reshape(queries.shape),
        key_part.reshape(all_keys.shape),
        value_part.reshape(all_values.shape),
    )


def local(
    features,
    utterance_ends,
    kernel_weight,
    position_bias,
    entry_gain,
    base_shift,
    joint_weight,
    query_bias,
    value_bias,
    output_weight,
    attend_bias,
    middle_gain,
    lower_shift,
    expand_weight,
    hidden_bias,
    reduce_weight,
    return_bias,
    final_gain,
    upper_shift,
    head_weight,
    vocab_bias,
    cotangent,
):
    row_count, frame_count, model_dim = features.shape
    frames_all = frame_count * lax.axis_size("seq")
    groups = CONV_G
    group_width = model_dim // groups
    tap_count = kernel_weight.shape[1] // group_width
    half_taps = tap_count // 2
    tap_block = math.gcd(tap_count, 16)
    head_count = HEADS
    query_scale = (model_dim // head_count) ** (-0.5)
    layer_count = joint_weight.shape[0]
    rows_share = model_dim // lax.axis_size(("dp", "seq"))
    anchor = lax.axis_index("seq") * frame_count
    frame_ids = segment_ids(anchor + jnp.arange(frame_count, dtype=jnp.int32), utterance_ends)
    row_ids = segment_ids(jnp.arange(frames_all, dtype=jnp.int32), utterance_ends)
    halo_place = anchor - half_taps + jnp.arange(frame_count + tap_count, dtype=jnp.int32)
    inside = (halo_place >= 0) & (halo_place < frames_all)
    halo_ids = jnp.where(inside[None, :], segment_ids(halo_place, utterance_ends), -1)
    stem = (
        lax.all_gather(kernel_weight, ("dp", "seq"), axis=0, tiled=True),
        lax.all_gather(position_bias, ("dp", "seq"), axis=0, tiled=True),
        lax.all_gather(entry_gain, ("dp", "seq"), axis=0, tiled=True),
        lax.all_gather(base_shift, ("dp", "seq"), axis=0, tiled=True),
        lax.all_gather(head_weight, ("dp", "seq"), axis=0, tiled=True),
    )
    kernel_grid = stem[0].reshape(groups, group_width, tap_count, group_width)
    halo_feats = with_halo(features, (("seq", 1),), half_taps)
    conv_pre = conv_forward(halo_feats, halo_ids, frame_ids, kernel_grid, tap_block) + widened(
        stem[1]
    )
    mixed = widened(features) + gelu_exact(conv_pre)
    hidden = layer_norm(mixed, widened(stem[2]), widened(stem[3]))
    saved = []
    for layer_at in range(layer_count):
        (
            joint_full,
            query_full,
            value_full,
            output_full,
            attend_full,
            middle_full,
            lower_full,
            expand_full,
            hidden_full,
            reduce_full,
            return_full,
            final_full,
            upper_full,
        ) = (
            lax.all_gather(joint_weight[layer_at], ("dp", "seq"), axis=0, tiled=True),
            lax.all_gather(query_bias[layer_at], ("dp", "seq"), axis=0, tiled=True),
            lax.all_gather(value_bias[layer_at], ("dp", "seq"), axis=0, tiled=True),
            lax.all_gather(output_weight[layer_at], ("dp", "seq"), axis=0, tiled=True),
            lax.all_gather(attend_bias[layer_at], ("dp", "seq"), axis=0, tiled=True),
            lax.all_gather(middle_gain[layer_at], ("dp", "seq"), axis=0, tiled=True),
            lax.all_gather(lower_shift[layer_at], ("dp", "seq"), axis=0, tiled=True),
            lax.all_gather(expand_weight[layer_at], ("dp", "seq"), axis=0, tiled=True),
            lax.all_gather(hidden_bias[layer_at], ("dp", "seq"), axis=0, tiled=True),
            lax.all_gather(reduce_weight[layer_at], ("dp", "seq"), axis=0, tiled=True),
            lax.all_gather(return_bias[layer_at], ("dp", "seq"), axis=0, tiled=True),
            lax.all_gather(final_gain[layer_at], ("dp", "seq"), axis=0, tiled=True),
            lax.all_gather(upper_shift[layer_at], ("dp", "seq"), axis=0, tiled=True),
        )
        inputs_low = rounded(hidden)
        joint_out = jnp.einsum(
            "rtd,de->rte", inputs_low, joint_full, preferred_element_type=jnp.float32
        )
        queries = rounded((joint_out[..., :model_dim] + widened(query_full)) * query_scale)
        keys_local = rounded(joint_out[..., model_dim : 2 * model_dim])
        values_local = rounded(joint_out[..., 2 * model_dim :] + widened(value_full))
        all_keys, all_values = (
            lax.all_gather(keys_local, "seq", axis=1, tiled=True),
            lax.all_gather(values_local, "seq", axis=1, tiled=True),
        )
        context, log_totals = attend_forward(
            queries, all_keys, all_values, frame_ids, row_ids, head_count
        )
        attended = jnp.einsum(
            "rtc,cd->rtd", context, output_full, preferred_element_type=jnp.float32
        ) + widened(attend_full)
        residual_one = hidden + attended
        middle = layer_norm(residual_one, widened(middle_full), widened(lower_full))
        middle_low = rounded(middle)
        inner_pre = jnp.einsum(
            "rtd,df->rtf", middle_low, expand_full, preferred_element_type=jnp.float32
        ) + widened(hidden_full)
        activated = rounded(gelu_exact(inner_pre))
        outer = (
            middle
            + jnp.einsum("rtf,fd->rtd", activated, reduce_full, preferred_element_type=jnp.float32)
            + widened(return_full)
        )
        kept_weights = None
        saved.append(
            (
                inputs_low,
                queries,
                all_keys,
                all_values,
                log_totals,
                context,
                residual_one,
                middle_low,
                inner_pre,
                activated,
                outer,
                kept_weights,
            )
        )
        hidden = layer_norm(outer, widened(final_full), widened(upper_full))
    final_low = rounded(hidden)
    logits = jnp.einsum(
        "rtd,dv->rtv", final_low, stem[4], preferred_element_type=jnp.float32
    ) + widened(vocab_bias)
    back_stem = (
        lax.all_gather(kernel_weight, ("dp", "seq"), axis=0, tiled=True),
        lax.all_gather(entry_gain, ("dp", "seq"), axis=0, tiled=True),
        lax.all_gather(head_weight, ("dp", "seq"), axis=0, tiled=True),
    )
    vocab_sum = jnp.sum(widened(cotangent), axis=(0, 1))
    head_part = jnp.einsum("rtd,rtv->dv", final_low, cotangent, preferred_element_type=jnp.float32)
    flow_grad = jnp.einsum(
        "rtv,dv->rtd", cotangent, back_stem[2], preferred_element_type=jnp.float32
    )
    layer_grads = [None] * layer_count
    for layer_at in reversed(range(layer_count)):
        (
            inputs_low,
            queries,
            all_keys,
            all_values,
            log_totals,
            context,
            residual_one,
            middle_low,
            inner_pre,
            activated,
            outer,
            kept_weights,
        ) = saved[layer_at]
        back_weights = (
            lax.all_gather(joint_weight[layer_at], ("dp", "seq"), axis=0, tiled=True),
            lax.all_gather(output_weight[layer_at], ("dp", "seq"), axis=0, tiled=True),
            lax.all_gather(expand_weight[layer_at], ("dp", "seq"), axis=0, tiled=True),
            lax.all_gather(reduce_weight[layer_at], ("dp", "seq"), axis=0, tiled=True),
            lax.all_gather(middle_gain[layer_at], ("dp", "seq"), axis=0, tiled=True),
            lax.all_gather(final_gain[layer_at], ("dp", "seq"), axis=0, tiled=True),
        )
        joint_full, output_full, expand_full, reduce_full, middle_full, final_full = back_weights
        outer_grad, final_part, upper_part = norm_pullback(outer, widened(final_full), flow_grad)
        fed_low = rounded(outer_grad)
        return_part = jnp.sum(widened(fed_low), axis=(0, 1))
        active_grad = jnp.einsum(
            "rtd,fd->rtf", fed_low, reduce_full, preferred_element_type=jnp.float32
        )
        _, gelu_pull = jax.vjp(gelu_exact, inner_pre)
        (inner_grad,) = gelu_pull(active_grad)
        inner_low = rounded(inner_grad)
        hidden_part = jnp.sum(widened(inner_low), axis=(0, 1))
        middle_flow = outer_grad + jnp.einsum(
            "rtf,df->rtd", inner_low, expand_full, preferred_element_type=jnp.float32
        )
        residual_grad, middle_part, lower_part = norm_pullback(
            residual_one, widened(middle_full), middle_flow
        )
        attended_low = rounded(residual_grad)
        attend_part = jnp.sum(widened(attended_low), axis=(0, 1))
        context_low = rounded(
            jnp.einsum("rtd,cd->rtc", attended_low, output_full, preferred_element_type=jnp.float32)
        )
        query_raw, key_raw, value_raw = attend_backward(
            queries, all_keys, all_values, frame_ids, row_ids, head_count, log_totals, context_low
        )
        key_sum, value_sum = (
            lax.psum_scatter(
                key_raw.astype(jnp.bfloat16), "seq", scatter_dimension=1, tiled=True
            ).astype(jnp.float32),
            lax.psum_scatter(
                value_raw.astype(jnp.bfloat16), "seq", scatter_dimension=1, tiled=True
            ).astype(jnp.float32),
        )
        query_low = rounded(widened(rounded(query_raw)) * query_scale)
        key_low = rounded(key_sum)
        value_low = rounded(value_sum)
        query_part = jnp.sum(widened(query_low), axis=(0, 1))
        value_part = jnp.sum(widened(value_low), axis=(0, 1))
        joint_low = jnp.concatenate([query_low, key_low, value_low], axis=-1)
        flow_grad = residual_grad + jnp.einsum(
            "rte,de->rtd", joint_low, joint_full, preferred_element_type=jnp.float32
        )
        ratio = hidden_part.shape[0] // model_dim
        vector_rows = jnp.stack(
            [
                query_part,
                value_part,
                attend_part,
                middle_part,
                lower_part,
                return_part,
                final_part,
                upper_part,
            ],
            axis=1,
        )
        hidden_rows = hidden_part.reshape(model_dim, ratio)

        def layer_term(
            start,
            count,
            inputs_low=inputs_low,
            joint_low=joint_low,
            context=context,
            attended_low=attended_low,
            middle_low=middle_low,
            inner_low=inner_low,
            activated=activated,
            fed_low=fed_low,
            vector_rows=vector_rows,
            hidden_rows=hidden_rows,
            ratio=ratio,
        ):
            joint_rows = jnp.einsum(
                "rtd,rte->de", inputs_low, joint_low, preferred_element_type=jnp.float32
            )
            output_rows = jnp.einsum(
                "rtc,rtd->cd", context, attended_low, preferred_element_type=jnp.float32
            )
            expand_rows = jnp.einsum(
                "rtd,rtf->df", middle_low, inner_low, preferred_element_type=jnp.float32
            )
            reduce_rows = jnp.einsum(
                "rtf,rtd->fd", activated, fed_low, preferred_element_type=jnp.float32
            ).reshape(count, ratio * model_dim)
            return jnp.concatenate(
                [joint_rows, output_rows, expand_rows, reduce_rows, vector_rows, hidden_rows],
                axis=1,
            )

        summed = lax.psum_scatter(
            layer_term(jnp.int32(0), rows_share * lax.axis_size(("dp", "seq"))),
            ("dp", "seq"),
            scatter_dimension=0,
            tiled=True,
        )
        ff_width = ratio * model_dim
        first = 3 * model_dim
        second = first + model_dim
        third = second + ff_width
        fourth = third + ratio * model_dim
        joint_own = summed[:, :first]
        output_own = summed[:, first:second]
        expand_own = summed[:, second:third]
        reduce_own = summed[:, third:fourth].reshape(rows_share * ratio, model_dim)
        vector_own = summed[:, fourth : fourth + 8]
        hidden_own = summed[:, fourth + 8 :].reshape(rows_share * ratio)
        layer_grads[layer_at] = (
            joint_own,
            vector_own[:, 0],
            vector_own[:, 1],
            output_own,
            vector_own[:, 2],
            vector_own[:, 3],
            vector_own[:, 4],
            expand_own,
            hidden_own,
            reduce_own,
            vector_own[:, 5],
            vector_own[:, 6],
            vector_own[:, 7],
        )
    mixed_grad, entry_part, base_part = norm_pullback(mixed, widened(back_stem[1]), flow_grad)
    _, gelu_pull = jax.vjp(gelu_exact, conv_pre)
    (conv_grad,) = gelu_pull(mixed_grad)
    conv_low = rounded(conv_grad)
    position_part = jnp.sum(widened(conv_low), axis=(0, 1))
    halo_grads = with_halo(conv_low, (("seq", 1),), half_taps)
    back_grid = back_stem[0].reshape(groups, group_width, tap_count, group_width)
    input_part, kernel_part = conv_backward(
        halo_grads, halo_feats, halo_ids, frame_ids, back_grid, tap_block, conv_low
    )
    features_grad = mixed_grad + input_part
    vocab_tiled = jnp.tile(vocab_sum, lax.axis_size(("dp", "seq")))
    stem_sums = (
        lax.psum_scatter(kernel_part, ("dp", "seq"), scatter_dimension=0, tiled=True),
        lax.psum_scatter(position_part, ("dp", "seq"), scatter_dimension=0, tiled=True),
        lax.psum_scatter(entry_part, ("dp", "seq"), scatter_dimension=0, tiled=True),
        lax.psum_scatter(base_part, ("dp", "seq"), scatter_dimension=0, tiled=True),
        lax.psum_scatter(head_part, ("dp", "seq"), scatter_dimension=0, tiled=True),
        lax.psum_scatter(vocab_tiled, ("dp", "seq"), scatter_dimension=0, tiled=True),
    )
    stacked = [
        jnp.stack([layer_grads[layer_at][member] for layer_at in range(layer_count)])
        for member in range(13)
    ]
    return (
        logits,
        features_grad,
        stem_sums[0],
        stem_sums[1],
        stem_sums[2],
        stem_sums[3],
        stacked[0],
        stacked[1],
        stacked[2],
        stacked[3],
        stacked[4],
        stacked[5],
        stacked[6],
        stacked[7],
        stacked[8],
        stacked[9],
        stacked[10],
        stacked[11],
        stacked[12],
        stem_sums[4],
        stem_sums[5],
    )


MESH_ID = pl.DeviceIdType.MESH
IN_VMEM = pl.BlockSpec(memory_space=pltpu.VMEM)
ANYWHERE = pl.BlockSpec(memory_space=pl.ANY)
AXES = ("y", "x", "c", "h", "l")
Y_BIT, X_BIT, C_BIT, H_BIT, L_BIT = 16, 8, 4, 2, 1
DEVICES = 32
PIECES = 8
PACK = 8
RANKS = 4
LOW, WIDE = jnp.bfloat16, jnp.float32


def kernel_params(collective):
    return pltpu.CompilerParams(
        vmem_limit_bytes=62 * 2**20, collective_id=collective, has_side_effects=True
    )


def cost(micros):
    return pl.CostEstimate(flops=int(micros * 1.1e9), bytes_accessed=2**20, transcendentals=0)


def bits():
    return tuple(lax.axis_index(axis) for axis in AXES)


def index_of(y, x, c, h, l):
    return y * 16 + x * 8 + c * 4 + h * 2 + l


def turned_of(y, x, c, h, l):
    return index_of(h, l, c, y, x)


def flipped(mask):
    return {
        axis: 1 - lax.axis_index(axis)
        for number, axis in enumerate(AXES)
        if mask >> (len(AXES) - 1 - number) & 1
    }


def place_of(mask):
    return [
        1 - here if mask >> (len(AXES) - 1 - number) & 1 else here
        for number, here in enumerate(bits())
    ]


def greet_all():
    gate = pltpu.get_barrier_semaphore()
    for mask in range(1, DEVICES):
        pl.semaphore_signal(gate, inc=1, device_id=flipped(mask), device_id_type=MESH_ID)


def all_greeted():
    pl.semaphore_wait(pltpu.get_barrier_semaphore(), DEVICES - 1)


def remote(source, target, send, receive, peer):
    return pltpu.make_async_remote_copy(
        source, target, send, receive, device_id=peer, device_id_type=MESH_ID
    )


class Swap:
    def __init__(self, block_for, target, sends, receives, own_sem):
        self.block_for, self.target = block_for, target
        self.sends, self.receives, self.own_sem = sends, receives, own_sem

    def own(self):
        place = bits()
        return pltpu.make_async_copy(
            self.block_for(*place), self.target.at[index_of(*place)], self.own_sem
        )

    def copy(self, mask):
        return remote(
            self.block_for(*place_of(mask)),
            self.target.at[index_of(*bits())],
            self.sends.at[mask - 1],
            self.receives.at[mask - 1],
            flipped(mask),
        )

    def start(self):
        self.own().start()
        for mask in range(1, DEVICES):
            self.copy(mask).start()

    def arrived(self):
        self.own().wait()
        for mask in range(1, DEVICES):
            self.copy(mask).wait_recv()

    def sent(self):
        for mask in range(1, DEVICES):
            self.copy(mask).wait_send()


def swap_sems():
    return [
        pltpu.SemaphoreType.DMA((DEVICES - 1,)),
        pltpu.SemaphoreType.DMA((DEVICES - 1,)),
        pltpu.SemaphoreType.DMA,
    ]


class Move:
    def __init__(self, pairs, sends, receives):
        y, x, _, h, l = bits()
        self.pairs, self.sends, self.receives = pairs, sends, receives
        self.same = jnp.logical_and(y == h, x == l)
        self.peer = {"y": h, "x": l, "h": y, "l": x}

    def each(self, action):
        @pl.when(self.same)
        def _():
            for number, (source, target) in enumerate(self.pairs):
                copy = pltpu.make_async_copy(source, target, self.receives.at[number])
                copy.start() if action == "start" else copy.wait()

        @pl.when(jnp.logical_not(self.same))
        def _():
            for number, (source, target) in enumerate(self.pairs):
                copy = remote(
                    source, target, self.sends.at[number], self.receives.at[number], self.peer
                )
                copy.start() if action == "start" else copy.wait()

    def start(self):
        self.each("start")

    def done(self):
        self.each("wait")


def put_lanes(target, value):
    for q in range(value.shape[1] // 128):
        target[q] = value[:, q * 128 : (q + 1) * 128]


def get_lanes(source, width):
    return jnp.concatenate([source[q] for q in range(width // 128)], axis=1)


def bounds_of(ends, frames):
    before = [jnp.zeros_like(ends[0])] + ends[:-1]
    return [jnp.where(end > last, end, float(frames)) for end, last in zip(ends, before)]


def rank_lanes(bounds, frames, width):
    shape = (frames // PACK, 8, PACK * width)
    frame = lax.broadcasted_iota(jnp.int32, shape, 0) * PACK
    frame = frame + lax.broadcasted_iota(jnp.int32, shape, 2) // width
    rank = jnp.zeros(shape, jnp.int32)
    for bound in bounds:
        rank = rank + (frame >= bound[None].astype(jnp.int32)).astype(jnp.int32)
    return rank.reshape(frames, PACK * width)


def spread_ranks(wide, packed, rank, first):
    lines = packed.shape[0]
    wide[...] = jnp.zeros_like(wide)
    for number in range(RANKS):
        place = pl.ds(first + number * 64, lines)
        wide[place, :] += jnp.where(rank == number, packed, 0.0)


def collect_ranks(summed, rank, lines):
    result = jnp.zeros((lines, summed.shape[1]), WIDE)
    for number in range(RANKS):
        result = jnp.where(rank == number, summed[number * 64 : number * 64 + lines, :], result)
    return result


def fill_pair(wide, even, odd):
    length = even.shape[0]
    even[...] = wide[:length, :].astype(LOW)
    odd[...] = wide[8 : 8 + length, :].astype(LOW)


def shifted(even, odd, step, length):
    source = even if step % 2 == 0 else odd
    return source[pl.ds((step - step % 2) * 8, length), :]


def normed(tensor, gain, shift):
    average = jnp.mean(tensor, axis=-1, keepdims=True)
    centred = tensor - average
    spread = jnp.mean(centred * centred, axis=-1, keepdims=True)
    return centred * lax.rsqrt(spread + epsilon) * gain + shift


def normed_back(tensor, gain, upstream):
    average = jnp.mean(tensor, axis=-1, keepdims=True)
    centred = tensor - average
    spread = jnp.mean(centred * centred, axis=-1, keepdims=True)
    inverse = lax.rsqrt(spread + epsilon)
    unit = centred * inverse
    scaled = upstream * gain
    result = inverse * (
        scaled
        - jnp.mean(scaled, axis=-1, keepdims=True)
        - unit * jnp.mean(scaled * unit, axis=-1, keepdims=True)
    )
    return (
        result,
        jnp.sum(upstream * unit, axis=0, keepdims=True),
        jnp.sum(upstream, axis=0, keepdims=True),
    )


def gelu_pair(tensor):
    half = 0.5 * (1.0 + lax.erf(tensor * (2.0**-0.5)))
    slope = half + tensor * (jnp.exp(-0.5 * tensor * tensor) * ((2.0 * math.pi) ** -0.5))
    return tensor * half, slope


def dot(left, right):
    return jnp.dot(left, right, preferred_element_type=WIDE)


def dot_rt(left, right):
    return lax.dot_general(left, right, (((1,), (1,)), ((), ())), preferred_element_type=WIDE)


def dot_lt(left, right):
    return lax.dot_general(left, right, (((0,), (0,)), ((), ())), preferred_element_type=WIDE)


def group_gather(block, t, sends, receives, ready, use):
    half = block.shape[1] // 2
    y_peer, x_peer = flipped(Y_BIT), flipped(X_BIT)
    own = block.at[t]
    to_y = remote(own, own, sends.at[0], receives.at[0], y_peer)
    to_y.start()
    to_x = remote(own, own, sends.at[1], receives.at[1], x_peer)
    to_x.start()
    ready()
    use(t)
    to_y.wait_recv()
    other = block.at[lax.bitwise_xor(t, 2), pl.ds(0, half)]
    on_x = remote(other, other, sends.at[2], receives.at[2], x_peer)
    on_x.start()
    to_x.wait_recv()
    other = block.at[lax.bitwise_xor(t, 1), pl.ds(half, half)]
    on_y = remote(other, other, sends.at[3], receives.at[3], y_peer)
    on_y.start()
    use(lax.bitwise_xor(t, 2))
    use(lax.bitwise_xor(t, 1))
    on_x.wait_recv()
    on_y.wait_recv()
    use(lax.bitwise_xor(t, 3))
    for copy in (to_y, to_x, on_x, on_y):
        copy.wait_send()


def group_scatter(part, t, low, got, sends, receives, between=None):
    half = low.shape[1]
    y_peer, x_peer = flipped(Y_BIT), flipped(X_BIT)

    def send(slot, value, peer):
        low[slot] = value.astype(LOW)
        copy = remote(low.at[slot], got.at[slot], sends.at[slot], receives.at[slot], peer)
        copy.start()
        return copy

    def arrived(slot):
        return got[slot].astype(WIDE)

    far = part(lax.bitwise_xor(t, 3))
    far_y = send(0, far[:half], y_peer)
    far_x = send(1, far[half:], x_peer)
    beside_y = part(lax.bitwise_xor(t, 2))
    near_y = send(2, beside_y[:half], y_peer)
    beside_x = part(lax.bitwise_xor(t, 1))
    near_x = send(3, beside_x[half:], x_peer)
    far_y.wait_recv()
    on_x = send(4, beside_x[:half] + arrived(0), x_peer)
    far_x.wait_recv()
    on_y = send(5, beside_y[half:] + arrived(1), y_peer)
    own = part(t)
    if between is not None:
        between()
    near_y.wait_recv()
    near_x.wait_recv()
    on_x.wait_recv()
    on_y.wait_recv()
    result = jnp.concatenate(
        [own[:half] + arrived(2) + arrived(4), own[half:] + arrived(3) + arrived(5)], axis=0
    )
    for copy in (far_y, far_x, near_y, near_x, on_x, on_y):
        copy.wait_send()
    return result


def group_scratch(n, width):
    return [
        pltpu.VMEM((6, n // 2, width), LOW),
        pltpu.VMEM((6, n // 2, width), LOW),
        pltpu.SemaphoreType.DMA((4,)),
        pltpu.SemaphoreType.DMA((4,)),
        pltpu.SemaphoreType.DMA((6,)),
        pltpu.SemaphoreType.DMA((6,)),
    ]


def block_rows(j, n):
    return pl.ds(pl.multiple_of(j * n, n), n)


def slots():
    return [(c, h, l) for c in range(2) for h in range(2) for l in range(2)]


class Spread:
    def __init__(self, held, sends, receives):
        self.held, self.sends, self.receives = held, sends, receives

    def copy(self, step):
        _, _, c, h, l = bits()
        own = c * 4 + h * 2 + l
        near = c * 4 + (1 - h) * 2 + l
        view = self.held.at[(pl.ds(own, 1), pl.ds(own, 1), pl.ds(near, 1), pl.ds(c * 4, 4))[step]]
        peer = flipped((H_BIT, L_BIT, L_BIT, C_BIT)[step])
        return remote(view, view, self.sends.at[step], self.receives.at[step], peer)

    def begin(self):
        self.copy(0).start()
        self.copy(1).start()

    def forward(self):
        self.copy(0).wait_recv()
        self.copy(2).start()

    def over_c(self):
        self.copy(1).wait_recv()
        self.copy(2).wait_recv()
        self.copy(3).start()

    def done(self):
        self.copy(3).wait_recv()
        for step in range(4):
            self.copy(step).wait_send()


def load_rows(held, target, sem, share, column, width):
    for slot in range(PIECES):
        for at in range(4):
            pltpu.make_async_copy(
                held.at[slot, pl.ds(at * share, share), pl.ds(column, width)],
                target.at[pl.ds((at * PIECES + slot) * share, share), :],
                sem,
            ).start()


def load_chunks(held, target, sem, share, column, width):
    for slot in range(PIECES):
        for chunk in range(4):
            pltpu.make_async_copy(
                held.at[slot, pl.ds(chunk * share, share), pl.ds(column, width)],
                target.at[pl.ds(slot * share, share), pl.ds(chunk * width, width)],
                sem,
            ).start()


def load_blocks(held, target, sem, first, share):
    for slot in range(PIECES):
        pltpu.make_async_copy(
            held.at[slot, pl.ds(first, share)], target.at[pl.ds(slot * share, share), :], sem
        ).start()


def load_line(held, target, sem, first, width):
    for slot in range(PIECES):
        pltpu.make_async_copy(
            held.at[slot, pl.ds(first, 16), pl.ds(0, width)],
            target.at[:, pl.ds(slot * width, width)],
            sem,
        ).start()


def settle(target, sem):
    pltpu.make_async_copy(target, target, sem).wait()


def relative(target, c, h, l):
    _, _, c_me, h_me, l_me = bits()
    return target.at[
        lax.bitwise_xor(c_me, c), lax.bitwise_xor(l_me, l), lax.bitwise_xor(h_me, h)
    ]


def store_rows(target, grads, share, column):
    width = grads.shape[1]
    for slot, place in enumerate(slots()):
        for at in range(4):
            row = (at * PIECES + slot) * share
            relative(target, *place)[at * share : (at + 1) * share, column : column + width] = grads[
                row : row + share, :
            ].astype(LOW)


def store_chunks(target, grads, share, column):
    width = grads.shape[1] // 4
    for slot, place in enumerate(slots()):
        for chunk in range(4):
            relative(target, *place)[
                chunk * share : (chunk + 1) * share, column : column + width
            ] = grads[slot * share : (slot + 1) * share, chunk * width : (chunk + 1) * width].astype(LOW)


def store_blocks(target, grads, first, share):
    for slot, place in enumerate(slots()):
        relative(target, *place)[first : first + share, :] = grads[
            slot * share : (slot + 1) * share, :
        ].astype(LOW)


class Gather:
    def __init__(self, parts, got_c, got_l, got_h, sends, receives):
        self.parts, self.got = parts, (got_c, got_l, got_h)
        self.sends, self.receives = sends, receives

    def copy(self, step):
        source = (self.parts.at[1], self.parts.at[0, 1], self.parts.at[0, 0, 1])[step]
        return remote(
            source,
            self.got[step],
            self.sends.at[step],
            self.receives.at[step],
            flipped((C_BIT, L_BIT, H_BIT)[step]),
        )

    def over_c(self):
        self.copy(0).start()

    def over_l(self):
        self.copy(0).wait_recv()
        for l in (1, 0):
            for h in range(2):
                summed = self.parts[0, l, h].astype(WIDE) + self.got[0][l, h].astype(WIDE)
                self.parts[0, l, h] = summed.astype(LOW)
            if l == 1:
                self.copy(1).start()

    def over_h(self):
        self.copy(1).wait_recv()
        for h in (1, 0):
            summed = self.parts[0, 0, h].astype(WIDE) + self.got[1][h].astype(WIDE)
            self.parts[0, 0, h] = summed.astype(LOW)
            if h == 1:
                self.copy(2).start()

    def done(self):
        self.copy(2).wait_recv()
        for step in range(3):
            self.copy(step).wait_send()

    def total(self, first, last):
        return self.parts[0, 0, 0, first:last, :].astype(WIDE) + self.got[2][first:last, :].astype(WIDE)


class Sizes:
    def __init__(self, n, width, inner, layers, taps, vocab):
        self.n, self.width, self.inner, self.layers = n, width, inner, layers
        self.taps, self.vocab = taps, vocab
        self.count = 4 * n
        self.part = width // 4
        self.head = width // HEADS
        self.heads = self.part // self.head
        self.share = width // DEVICES
        self.inner_share = inner // PIECES
        self.scale = self.head**-0.5
        self.group_width = width // CONV_G
        self.packs = n // PACK
        self.steps = taps // PACK + 1
        self.length = self.count + (RANKS - 1) * 64
        self.lines = self.length + 128
        self.held_rows = (4 * self.share, 4 * self.share, self.inner_share + 16)
        self.grad_rows = (4 * self.share + 16, 4 * self.share, self.inner_share + 16)
        self.bundles = 3 * layers
        self.at = {"entry": 0, "base": 1}
        at = 2
        for name in ("attend", "middle", "lower", "return", "final", "upper"):
            self.at[name] = at
            at += layers
        self.vectors = at
        self.at["head"] = at
        self.at["heads"] = at + vocab
        self.named = at + vocab + 2 * layers
        self.line = -(-(self.named + 1) // 8) * 8
        self.gathered = 64

    def saved(self):
        n, count, layers, width = self.n, self.count, self.layers, self.width
        return [
            ((layers, 4, n, width), LOW),
            ((layers, count, 3 * self.part), LOW),
            ((layers, self.heads * count, count), LOW),
            ((layers, count, self.part), LOW),
            ((layers, n, width), WIDE),
            ((layers, 4, n, width), LOW),
            ((layers, count, self.inner), LOW),
            ((layers, count, self.inner), LOW),
            ((layers, n, width), WIDE),
        ]


def forward(z, features, cot_turned, kernel_weight, small, head_weight, ends_own, hidden_bias, joint_weight, expand_weight, output_weight, reduce_weight):
    kept = z.saved()
    kinds = len(kept)
    layers, n, width, part, inner, share = z.layers, z.n, z.width, z.part, z.inner, z.share
    count, head, heads, packs, gw = z.count, z.head, z.heads, z.packs, z.group_width
    depth, own_width = PACK * gw, PACK * share

    def kernel(*refs):
        (f_ref, cot_ref, k_ref, small_ref, head_ref, e_ref, hb_ref, jw_ref, ew_ref, ow_ref, rw_ref) = refs[:11]
        rest = refs[11:]
        (logits_ref, flow_ref, part_ref, whole, mixed_ref, bend_ref, ends_ref) = rest[:7]
        even_out, odd_out, taps_out = rest[7:10]
        held = rest[10 : 10 + z.bundles]
        saved = rest[10 + z.bundles : 10 + z.bundles + kinds]
        rest = rest[10 + z.bundles + kinds :]
        (x_all, qkv, weights_low, context, residual, m_all, active, slope, outer) = rest[:kinds]
        (now, wj, wo, we, wr, hb, low_buf, got, gs, gr, ss, sr) = rest[kinds : kinds + 12]
        (bs, br, ws, ks, tokens, messages, feats, small_all, packed, wide, even, odd, taps, out_messages) = rest[kinds + 12 : kinds + 26]
        (pres, new_feats, cot, logits_own, cs, cr, rs, fs, lines_out) = rest[kinds + 26 : kinds + 35]
        (hidden_lines, gathering, message) = rest[kinds + 35 : kinds + 38]
        swap1, swap2, swap3 = (rest[kinds + 38 + 3 * k : kinds + 41 + 3 * k] for k in range(3))
        y, x, c, h, l = bits()
        t = y * 2 + x
        slot = c * 4 + h * 2 + l

        put_lanes(tokens, f_ref[...].astype(WIDE))
        for f in range(0, PACK, 2):
            for q in range(width // 128):
                pair = [tokens[q, pl.ds(f + k, packs, stride=PACK), :] for k in range(2)]
                for k in range(2):
                    messages[2 * q + k, :, f * gw : (f + 2) * gw] = jnp.concatenate(
                        [piece[:, k * gw : (k + 1) * gw] for piece in pair], axis=1
                    ).astype(LOW)
        def column_copies():
            copies = []
            for layer in range(layers):
                for number, mask in enumerate((0, X_BIT, Y_BIT, X_BIT | Y_BIT)):
                    place = place_of(mask)
                    user = place[0] * 2 + place[1]
                    lines = pl.ds(pl.multiple_of(t * share, share), share)
                    moved = [
                        (
                            0,
                            jw_ref.at[layer, :, pl.ds(pl.multiple_of(which * width + user * part, part), part)],
                            held[3 * layer].at[slot, lines, pl.ds(which * part, part)],
                        )
                        for which in range(3)
                    ]
                    moved.append(
                        (
                            1,
                            ew_ref.at[layer, :, pl.ds(pl.multiple_of(user * inner, inner), inner)],
                            held[3 * layer + 1].at[slot, lines],
                        )
                    )
                    for at, (kind, source, target) in enumerate(moved):
                        if mask == 0:
                            copy = pltpu.make_async_copy(source, target, cr.at[layer, at, 0])
                        else:
                            copy = remote(
                                source, target, cs.at[layer, at, number], cr.at[layer, at, number], flipped(mask)
                            )
                        copies.append((3 * layer + kind, mask, copy))
            return copies

        def row_copies():
            copies = []
            for layer in range(layers):
                reduce_held = held[3 * layer + 2].at[slot]
                moved = [
                    (2, rw_ref.at[layer], reduce_held.at[pl.ds(0, z.inner_share)]),
                    (2, hidden_lines.at[layer], reduce_held.at[pl.ds(z.inner_share, 16)]),
                ] + [
                    (
                        0,
                        ow_ref.at[layer, :, pl.ds(chunk * part, part)],
                        held[3 * layer].at[slot, pl.ds(chunk * share, share), pl.ds(3 * part, part)],
                    )
                    for chunk in range(4)
                ]
                for at, (kind, source, target) in enumerate(moved):
                    copies.append((3 * layer + kind, pltpu.make_async_copy(source, target, rs.at[layer, at])))
            return copies

        column_all, row_all = column_copies(), row_copies()
        greet_all()
        hidden_lines[...] = jnp.zeros_like(hidden_lines)
        for layer in range(layers):
            hidden_lines[layer, :, 0 : z.inner_share] = jnp.broadcast_to(
                hb_ref[layer : layer + 1, :].astype(WIDE), (16, z.inner_share)
            ).astype(LOW)
        for _, copy in row_all:
            copy.start()

        same = lax.broadcasted_iota(jnp.int32, (share, share), 0) == lax.broadcasted_iota(jnp.int32, (share, share), 1)
        unit = jnp.where(same, 1.0, 0.0).astype(LOW)
        lines_low = small_ref[...].astype(WIDE)
        gathering[...] = jnp.zeros_like(gathering)
        gathering[0 : z.vectors, 0:share] = lines_low[0 : z.vectors]
        gathering[z.vectors : z.at["heads"], 0:share] = dot_lt(head_ref[...], unit)
        gathering[z.at["heads"] : z.named, 0:share] = lines_low[z.vectors : z.vectors + 2 * layers]
        own_ends = e_ref[...]
        gathering[z.named : z.named + 1, 0:4] = lax.shift_right_logical(own_ends, 5).astype(WIDE)
        gathering[z.named : z.named + 1, 4:8] = lax.bitwise_and(own_ends, 31).astype(WIDE)
        per_line = 128 // share
        message_lines = gathering.shape[0] // per_line
        message[...] = jnp.concatenate(
            [gathering[pl.ds(k, message_lines, stride=per_line), :][:, 0:share] for k in range(per_line)], axis=1
        ).astype(LOW)
        position = jnp.concatenate([lines_low[z.vectors + 2 * layers : z.vectors + 2 * layers + 1]] * PACK, axis=1)

        jobs = [Spread(held[b], bs.at[b], br.at[b]) for b in range(z.bundles)]
        all_greeted()

        def launch(layer):
            for number, _, copy in column_all:
                if number // 3 == layer:
                    copy.start()

        to_owners = Swap(lambda *place: messages.at[index_of(*place) // 2], feats, *swap1)
        to_owners.start()
        vectors = Swap(lambda *place: message, small_all, *swap2)
        vectors.start()
        frames_move = Move([(f_ref, new_feats), (cot_ref, cot)], fs.at[0], fs.at[1])
        frames_move.start()
        for layer in range(layers):
            launch(layer)

        def own_ready(bundle):
            for number, mask, copy in column_all:
                if number == bundle:
                    if mask:
                        copy.wait_recv()
                        copy.wait_send()
                    else:
                        copy.wait()
            for number, copy in row_all:
                if number == bundle:
                    copy.wait()
            jobs[bundle].begin()


        def keep(source, target, sem):
            pltpu.make_async_copy(source, target, sem).start()

        span = z.taps * gw
        for step in range(z.steps):
            taps[step] = jnp.zeros((own_width, depth), LOW)
        for f in range(PACK):
            lines = slice(f * share, (f + 1) * share)
            shift = f * gw
            for step in range(z.steps):
                begin = max(step * depth - shift, 0)
                end = min((step + 1) * depth - shift, span)
                at = begin + shift - step * depth
                if begin < end:
                    taps[step, lines, at : at + end - begin] = k_ref[:, begin:end]
        keep(taps, taps_out, ks.at[kinds, 0])

        to_owners.arrived()
        own_ready(0)
        vectors.arrived()
        for at in range(DEVICES):
            place = pl.ds((at % 4) * packs * 8 + at // 4, packs, stride=8)
            for q in range(depth // 128):
                packed[q, place, :] = feats[at, :, q * 128 : (q + 1) * 128].astype(WIDE)
        line, lane = z.named * share // 128, z.named * share % 128
        encoded = jnp.concatenate(
            [small_all[4 * row, line : line + 1, :].astype(WIDE) for row in range(8)], axis=0
        )
        ends_ref[...] = encoded
        ends = [
            encoded[:, lane + k : lane + k + 1] * 32.0 + encoded[:, lane + 4 + k : lane + 5 + k]
            for k in range(4)
        ]
        bounds = bounds_of(ends, count)
        spread_ranks(wide, get_lanes(packed, depth), rank_lanes(bounds, count, gw), 64)
        fill_pair(wide, even, odd)
        keep(even, even_out, ks.at[kinds, 1])
        keep(odd, odd_out, ks.at[kinds + 1, 0])
        summed = jnp.zeros((z.length, own_width), WIDE)
        for step in range(z.steps):
            summed = summed + dot_rt(shifted(even, odd, step, z.length), taps[step])
        made = collect_ranks(summed, rank_lanes(bounds, count, share), count) + position
        put_lanes(packed, made)
        for at in range(DEVICES):
            place = pl.ds((at % 4) * packs * 8 + at // 4, packs, stride=8)
            for q in range(own_width // 128):
                out_messages[at, :, q * 128 : (q + 1) * 128] = packed[q, place, :].astype(LOW)
        to_frames = Swap(lambda *place: out_messages.at[turned_of(*place)], pres, *swap3)
        to_frames.start()
        jobs[0].forward()

        for q in range(width // 128):
            for k in range(per_line):
                cut = slice(k * share, (k + 1) * share)
                lines_out[q, pl.ds(k, message_lines, stride=per_line), :] = jnp.concatenate(
                    [small_all[at, :, cut].astype(WIDE) for at in range(4 * q, 4 * q + 4)], axis=1
                )
        whole[...] = get_lanes(lines_out, width)

        def vector(name, layer=0):
            at = z.at[name] + layer
            return whole[at : at + 1, :]

        heads_lines = whole[z.at["heads"] : z.at["heads"] + 2 * layers, pl.ds(pl.multiple_of(t * part, part), part)]
        mine = lax.broadcasted_iota(jnp.int32, (8, 1), 0) == h * 4 + l * 2 + c
        row_ends = [jnp.sum(jnp.where(mine, end, 0.0), axis=0, keepdims=True).astype(jnp.int32) for end in ends]
        across = lax.broadcasted_iota(jnp.int32, (1, count), 1)
        down = lax.broadcasted_iota(jnp.int32, (count, 1), 0)
        across = sum((across >= end).astype(jnp.int32) for end in row_ends)
        down = sum((down >= end).astype(jnp.int32) for end in row_ends)
        linked = down == across

        frames_move.done()
        to_frames.arrived()
        jobs[0].over_c()
        own_ready(1)
        own_ready(2)
        for f in range(PACK):
            cut = slice(f * share, (f + 1) * share)
            for q in range(width // 128):
                tokens[q, pl.ds(f, packs, stride=PACK), :] = jnp.concatenate(
                    [pres[at, :, cut].astype(WIDE) for at in range(4 * q, 4 * q + 4)], axis=1
                )
        made, bent = gelu_pair(get_lanes(tokens, width))
        bend_ref[...] = bent
        mixed = new_feats[...].astype(WIDE) + made
        mixed_ref[...] = mixed
        now[...] = normed(mixed, vector("entry"), vector("base"))

        for layer in range(layers):
            first, second, third = jobs[3 * layer : 3 * layer + 3]
            later = jobs[3 * layer + 3 : 3 * layer + 6]
            x_all[layer, t] = now[...].astype(LOW)

            def attend_ready(layer=layer, first=first):
                first.done()
                load_rows(held[3 * layer], wj, ws.at[0], share, 0, 3 * part)
                load_chunks(held[3 * layer], wo, ws.at[1], share, 3 * part, part)
                settle(wj, ws.at[0])

            def attend_use(j, layer=layer):
                lines = block_rows(j, n)
                made = dot(x_all[layer, j], wj[...])
                qkv[layer, lines, 0:part] = ((made[:, 0:part] + heads_lines[layer : layer + 1]) * z.scale).astype(LOW)
                qkv[layer, lines, part : 2 * part] = made[:, part : 2 * part].astype(LOW)
                qkv[layer, lines, 2 * part :] = (
                    made[:, 2 * part :] + heads_lines[layers + layer : layers + layer + 1]
                ).astype(LOW)

            group_gather(x_all.at[layer], t, gs, gr, attend_ready, attend_use)
            second.forward()
            if layer == 0:
                own_ready(3)
            keep(x_all.at[layer], saved[0].at[layer], ks.at[0, layer])
            keep(qkv.at[layer], saved[1].at[layer], ks.at[1, layer])
            for at in range(heads):
                queries = qkv[layer, :, at * head : (at + 1) * head]
                keys = qkv[layer, :, part + at * head : part + (at + 1) * head]
                values = qkv[layer, :, 2 * part + at * head : 2 * part + (at + 1) * head]
                scores = jnp.where(linked, dot_rt(queries, keys), masked_score)
                exponent = jnp.exp(scores - jnp.max(scores, axis=-1, keepdims=True))
                inverse = 1.0 / jnp.sum(exponent, axis=-1, keepdims=True)
                made = (exponent * inverse).astype(LOW)
                weights_low[layer, at * count : (at + 1) * count, :] = made
                context[layer, :, at * head : (at + 1) * head] = dot(made, values).astype(LOW)
            keep(weights_low.at[layer], saved[2].at[layer], ks.at[2, layer])
            keep(context.at[layer], saved[3].at[layer], ks.at[3, layer])
            settle(wo, ws.at[1])

            def advance(second=second, third=third):
                second.over_c()
                third.forward()

            attended = group_scatter(
                lambda j: dot(context[layer, block_rows(j, n), :], wo[...]), t, low_buf, got, ss, sr, advance
            )
            third.over_c()
            residual[layer] = now[...] + (attended + vector("attend", layer))
            keep(residual.at[layer], saved[4].at[layer], ks.at[4, layer])
            middle = normed(residual[layer], vector("middle", layer), vector("lower", layer))
            now[...] = middle
            m_all[layer, t] = middle.astype(LOW)

            def feed_ready(layer=layer, second=second, third=third):
                second.done()
                load_rows(held[3 * layer + 1], we, ws.at[2], share, 0, inner)
                third.done()
                load_line(held[3 * layer + 2], hb, ws.at[4], z.inner_share, z.inner_share)
                load_blocks(held[3 * layer + 2], wr, ws.at[3], 0, z.inner_share)
                settle(we, ws.at[2])
                settle(hb, ws.at[4])

            def feed_use(j, layer=layer):
                lines = block_rows(j, n)
                made, bent = gelu_pair(dot(m_all[layer, j], we[...]) + hb[0:1, :].astype(WIDE))
                active[layer, lines, :] = made.astype(LOW)
                slope[layer, lines, :] = bent.astype(LOW)

            group_gather(m_all.at[layer], t, gs, gr, feed_ready, feed_use)
            if later:
                later[0].forward()
                own_ready(4)
                own_ready(5)
            keep(m_all.at[layer], saved[5].at[layer], ks.at[5, layer])
            keep(active.at[layer], saved[6].at[layer], ks.at[6, layer])
            keep(slope.at[layer], saved[7].at[layer], ks.at[7, layer])
            settle(wr, ws.at[3])

            def advance_more(later=later):
                if later:
                    later[0].over_c()

            fed = group_scatter(
                lambda j: dot(active[layer, block_rows(j, n), :], wr[...]), t, low_buf, got, ss, sr, advance_more
            )
            outer[layer] = now[...] + fed + vector("return", layer)
            keep(outer.at[layer], saved[8].at[layer], ks.at[8, layer])
            now[...] = normed(outer[layer], vector("final", layer), vector("upper", layer))
        final_low = now[...].astype(LOW)
        head_turned = whole[z.at["head"] : z.at["head"] + z.vocab, :].astype(LOW)
        vocab_at = z.vectors + 2 * layers + 1
        vocab_bias = lines_low[vocab_at : vocab_at + 1, :].astype(LOW)
        logits_own[...] = dot_rt(head_turned, final_low) + dot_lt(vocab_bias, jnp.ones((1, n), LOW))
        logits_move = Move([(logits_own, logits_ref)], fs.at[2], fs.at[3])
        logits_move.start()
        flow_ref[...] = dot_lt(cot[...], head_turned)
        part_ref[...] = dot(cot[...], final_low)
        vocab_sum = dot_rt(jnp.ones((8, n), LOW), cot[...])
        vocab_sum = jnp.concatenate([vocab_sum] * (128 // z.vocab), axis=1)
        whole[z.line : z.line + 8, :] = jnp.concatenate([vocab_sum] * (width // 128), axis=1)
        logits_move.done()
        to_owners.sent()
        vectors.sent()
        to_frames.sent()
        for kind in range(kinds):
            for layer in range(layers):
                settle(saved[kind].at[layer], ks.at[kind, layer])
        settle(taps_out, ks.at[kinds, 0])
        settle(even_out, ks.at[kinds, 1])
        settle(odd_out, ks.at[kinds + 1, 0])

    outs = pl.pallas_call(
        kernel,
        out_shape=[
            jax.ShapeDtypeStruct((z.vocab, n), WIDE),
            jax.ShapeDtypeStruct((n, width), WIDE),
            jax.ShapeDtypeStruct((z.vocab, width), WIDE),
            jax.ShapeDtypeStruct((z.gathered, width), WIDE),
            jax.ShapeDtypeStruct((n, width), WIDE),
            jax.ShapeDtypeStruct((n, width), WIDE),
            jax.ShapeDtypeStruct((8, 128), WIDE),
            jax.ShapeDtypeStruct((z.lines, depth), LOW),
            jax.ShapeDtypeStruct((z.lines, depth), LOW),
            jax.ShapeDtypeStruct((z.steps, own_width, depth), LOW),
        ]
        + [jax.ShapeDtypeStruct((PIECES, z.held_rows[b % 3], width), LOW) for b in range(z.bundles)]
        + [jax.ShapeDtypeStruct(shape, kind) for shape, kind in kept],
        in_specs=[IN_VMEM] * 11,
        out_specs=[IN_VMEM] * 7 + [ANYWHERE] * (3 + z.bundles + kinds),
        scratch_shapes=[pltpu.VMEM(shape, kind) for shape, kind in kept]
        + [
            pltpu.VMEM((n, width), WIDE),
            pltpu.VMEM((width, 3 * part), LOW),
            pltpu.VMEM((part, width), LOW),
            pltpu.VMEM((width, inner), LOW),
            pltpu.VMEM((inner, width), LOW),
            pltpu.VMEM((16, inner), LOW),
        ]
        + group_scratch(n, width)
        + [
            pltpu.SemaphoreType.DMA((z.bundles, 4)),
            pltpu.SemaphoreType.DMA((z.bundles, 4)),
            pltpu.SemaphoreType.DMA((5,)),
            pltpu.SemaphoreType.DMA((kinds + 2, layers)),
            pltpu.VMEM((width // 128, n, 128), WIDE),
            pltpu.VMEM((CONV_G, packs, depth), LOW),
            pltpu.VMEM((DEVICES, packs, depth), LOW),
            pltpu.VMEM((DEVICES, z.gathered * share // 128, 128), LOW),
            pltpu.VMEM((depth // 128, count, 128), WIDE),
            pltpu.VMEM((z.lines + 16, depth), WIDE),
            pltpu.VMEM((z.lines, depth), LOW),
            pltpu.VMEM((z.lines, depth), LOW),
            pltpu.VMEM((z.steps, own_width, depth), LOW),
            pltpu.VMEM((DEVICES, packs, own_width), LOW),
            pltpu.VMEM((DEVICES, packs, own_width), LOW),
            pltpu.VMEM((n, width), LOW),
            pltpu.VMEM((z.vocab, n), LOW),
            pltpu.VMEM((z.vocab, n), WIDE),
            pltpu.SemaphoreType.DMA((layers, 4, 4)),
            pltpu.SemaphoreType.DMA((layers, 4, 4)),
            pltpu.SemaphoreType.DMA((layers, 6)),
            pltpu.SemaphoreType.DMA((4, 2)),
            pltpu.VMEM((width // 128, z.gathered, 128), WIDE),
            pltpu.VMEM((layers, 16, width), LOW),
            pltpu.VMEM((z.gathered, 128), WIDE),
            pltpu.VMEM((z.gathered * share // 128, 128), LOW),
        ]
        + swap_sems() * 3,
        compiler_params=kernel_params(1),
        cost_estimate=cost(200),
    )(features, cot_turned, kernel_weight, small, head_weight, ends_own, hidden_bias, joint_weight, expand_weight, output_weight, reduce_weight)
    return outs[:7], outs[7:10], outs[10 : 10 + z.bundles], outs[10 + z.bundles :]


def backward(z, flow, head_sums, whole, mixed, bend, ends, even, odd, taps, held, saved):
    kinds = len(saved)
    layers, n, width, part, inner, share = z.layers, z.n, z.width, z.part, z.inner, z.share
    count, head, heads, packs, gw = z.count, z.head, z.heads, z.packs, z.group_width
    depth, own_width = PACK * gw, PACK * share
    bundles = z.bundles
    row_counts = [z.grad_rows[b % 3] for b in range(bundles)]
    lines = 8 * (-(-(3 + 6 * layers) // 8))
    tap_places = [(half, row, cut) for half in range(2) for row in range(4) for cut in range(2)]

    def kernel(*refs):
        flow_ref, head_ref, whole_ref, mixed_ref, bend_ref, ends_ref = refs[:6]
        even_ref, odd_ref, taps_ref = refs[6:9]
        held_refs = refs[9 : 9 + bundles]
        saved_refs = refs[9 + bundles : 9 + bundles + kinds]
        rest = refs[9 + bundles + kinds :]
        feats_ref, kernel_ref, position_ref, sums_ref, heads_ref = rest[:5]
        joint_ref, expand_ref, reduce_ref, output_ref, small_ref = rest[5:10]
        rest = rest[10:]
        parts = rest[:bundles]
        got_c, got_l, got_h = (rest[k * bundles : (k + 1) * bundles] for k in range(1, 4))
        rest = rest[4 * bundles :]
        buffers = rest[:kinds]
        (x_all, qkv, weights_low, context, residual, m_all, active, slope, outer) = buffers
        rest = rest[kinds:]
        inner_low = slope
        (fed, grad_low, joint, wj, wo, we, wr, low_buf, got, gs, gr, ss, sr) = rest[:13]
        rest = rest[13:]
        (rs_s, rs_r, ws, ks, back, vector_sums, all_sums, all_heads, tokens, out_low, low_parts) = rest[:11]
        (wide, grads_even, grads_odd, collected, out_feats, feat_parts) = rest[11:17]
        even, odd = weights_low.at[pl.ds(0, z.lines)], weights_low.at[pl.ds(2 * count, z.lines)]
        (own_back, columns, joint_low, expand_low, fs, cs, cr) = rest[17:24]
        swaps = [rest[24 + 3 * k : 27 + 3 * k] for k in range(4)]
        y, x, c, h, l = bits()
        t = y * 2 + x

        def fetch(kind, layer):
            pltpu.make_async_copy(saved_refs[kind].at[layer], buffers[kind], ks.at[kind]).start()

        def need(kind):
            settle(buffers[kind], ks.at[kind])

        def load_feed(layer):
            fetch(8, layer)
            load_blocks(held_refs[3 * layer + 2], wr, ws.at[3], 0, z.inner_share)
            fetch(7, layer)
            load_rows(held_refs[3 * layer + 1], we, ws.at[2], share, 0, inner)
            for kind in (6, 5, 4):
                fetch(kind, layer)

        def load_attend(layer):
            load_chunks(held_refs[3 * layer], wo, ws.at[1], share, 3 * part, part)
            for kind in (1, 2, 3, 0):
                fetch(kind, layer)
            load_rows(held_refs[3 * layer], wj, ws.at[0], share, 0, 3 * part)

        def vector(name, layer=0):
            at = z.at[name] + layer
            return whole_ref[at : at + 1, :]

        def lanes_for(source):
            def block_for(*place):
                cut = pl.multiple_of(index_of(*place) * share // 128 * 128, 128)
                return source.at[:, pl.ds(cut, 128)]

            return block_for

        greet_all()
        load_feed(layers - 1)
        load_attend(layers - 1)
        all_greeted()
        heads_swap = Swap(lanes_for(head_ref), all_heads, *swaps[0])
        heads_swap.start()
        jobs = [
            Gather(parts[b], got_c[b], got_l[b], got_h[b], rs_s.at[b], rs_r.at[b]) for b in range(bundles)
        ]

        def column_copies(bundle):
            layer, kind = bundle // 3, bundle % 3
            copies = []
            for number, mask in enumerate((0, X_BIT, Y_BIT, X_BIT | Y_BIT)):
                place = place_of(mask)
                owner = place[0] * 2 + place[1]
                lines = pl.ds(pl.multiple_of(owner * share, share), share)
                if kind == 0:
                    moved = [
                        (
                            columns.at[layer, lines, pl.ds(which * part, part)],
                            joint_low.at[layer, :, pl.ds(pl.multiple_of(which * width + t * part, part), part)],
                        )
                        for which in range(3)
                    ]
                else:
                    moved = [
                        (
                            columns.at[layer, lines, pl.ds(3 * part, inner)],
                            expand_low.at[layer, :, pl.ds(pl.multiple_of(t * inner, inner), inner)],
                        )
                    ]
                for at, (source, target) in enumerate(moved):
                    at += 3 * kind
                    if mask == 0:
                        copies.append(pltpu.make_async_copy(source, target, cr.at[layer, at, 0]))
                    else:
                        copies.append(
                            remote(source, target, cs.at[layer, at, number], cr.at[layer, at, number], flipped(mask))
                        )
            return copies

        def hand_over(bundle):
            layer, kind = bundle // 3, bundle % 3
            jobs[bundle].done()
            if kind == 0:
                total = jobs[bundle].total(0, 4 * share)
                columns[layer, :, 0 : 3 * part] = total[:, : 3 * part].astype(LOW)
                for chunk in range(4):
                    output_ref[layer, :, chunk * part : (chunk + 1) * part] = total[
                        chunk * share : (chunk + 1) * share, 3 * part :
                    ]
                small_ref[layer] = jobs[bundle].total(4 * share, 4 * share + 16)[:, 0:128]
            elif kind == 1:
                columns[layer, :, 3 * part :] = jobs[bundle].total(0, 4 * share).astype(LOW)
            else:
                end = z.inner_share
                reduce_ref[layer] = jobs[bundle].total(0, end)
                sums_ref[8 * layer : 8 * layer + 8, :] = jobs[bundle].total(end, end + 16)[0:8, 0:128]
                return
            for copy in column_copies(bundle):
                copy.start()

        back[...] = flow_ref[...]
        vector_sums[...] = jnp.zeros_like(vector_sums)
        vector_sums[2 + 6 * layers : 3 + 6 * layers, :] = whole_ref[z.line : z.line + 1, :]

        for layer in reversed(range(layers)):
            last = layer == layers - 1
            attend_job, expand_job, reduce_job = jobs[3 * layer : 3 * layer + 3]
            after = 3 * layer + 3

            def note(name, value, layer=layer):
                at = z.at[name] + layer
                vector_sums[at : at + 1, :] = value

            need(8)
            outer_grad, final_part, upper_part = normed_back(outer[...], vector("final", layer), back[...])
            back[...] = outer_grad
            fed_low = outer_grad.astype(LOW)
            fed[0, t] = fed_low
            note("final", final_part)
            note("upper", upper_part)
            note("return", jnp.sum(fed_low.astype(WIDE), axis=0, keepdims=True))

            def feed_ready():
                settle(wr, ws.at[3])
                need(7)

            def feed_use(j):
                lines = block_rows(j, n)
                made = dot_rt(fed[0, j], wr[...]) * slope[lines, :].astype(WIDE)
                inner_low[lines, :] = made.astype(LOW)

            group_gather(fed.at[0], t, gs, gr, feed_ready, feed_use)
            if not last:
                jobs[after + 2].over_h()
            settle(we, ws.at[2])
            need(6)
            need(5)

            def feed_weights(after=after, last=last, expand_job=expand_job, reduce_job=reduce_job):
                store_rows(expand_job.parts, dot_lt(m_all[...].reshape(count, width), inner_low[...]), share, 0)
                expand_job.over_c()
                target = reduce_job.parts
                store_blocks(target, dot_lt(active[...], fed[0].reshape(count, width)), 0, z.inner_share)
                hidden_sum = jnp.sum(inner_low[...].astype(WIDE), axis=0, keepdims=True)
                first = z.inner_share
                for slot, place in enumerate(slots()):
                    at = slot * z.inner_share
                    view = relative(target, *place)
                    view[first : first + 16, :] = jnp.zeros((16, width), LOW)
                    view[first : first + 16, 0 : z.inner_share] = jnp.broadcast_to(
                        hidden_sum[:, at : at + z.inner_share], (16, z.inner_share)
                    ).astype(LOW)
                reduce_job.over_c()
                if not last:
                    hand_over(after + 1)

            got_back = group_scatter(
                lambda j: dot_rt(inner_low[block_rows(j, n), :], we[...]), t, low_buf, got, ss, sr, feed_weights
            )
            if not last:
                jobs[after].over_h()
            expand_job.over_l()
            reduce_job.over_l()
            need(4)
            res_grad, middle_part, lower_part = normed_back(
                residual[...], vector("middle", layer), back[...] + got_back
            )
            back[...] = res_grad
            note("middle", middle_part)
            note("lower", lower_part)
            if layer:
                load_feed(layer - 1)
            else:
                for step in range(z.steps - 1):
                    half, row, cut = tap_places[step]
                    target = (we, wr)[half].at[pl.ds(row * own_width, own_width), pl.ds(cut * depth, depth)]
                    pltpu.make_async_copy(taps_ref.at[step], target, ws.at[2 + half]).start()
            own_low = res_grad.astype(LOW)
            fed[1, t] = own_low
            note("attend", jnp.sum(own_low.astype(WIDE), axis=0, keepdims=True))

            def attend_ready():
                settle(wo, ws.at[1])

            def attend_use(j):
                grad_low[block_rows(j, n), :] = dot_rt(fed[1, j], wo[...]).astype(LOW)

            group_gather(fed.at[1], t, gs, gr, attend_ready, attend_use)
            if not last:
                hand_over(after + 2)
            if layer == 0:
                pltpu.make_async_copy(
                    taps_ref.at[z.steps - 1], wo.at[pl.ds(0, own_width), pl.ds(0, depth)], ws.at[1]
                ).start()
            for kind in (1, 2, 3):
                need(kind)
            for at in range(heads):
                mine = slice(at * head, (at + 1) * head)
                queries = qkv[:, mine]
                keys = qkv[:, part + at * head : part + (at + 1) * head]
                values = qkv[:, 2 * part + at * head : 2 * part + (at + 1) * head]
                weights = weights_low[at * count : (at + 1) * count, :]
                grads = grad_low[:, mine]
                weights_wide = weights.astype(WIDE)
                prob_grad = dot_rt(grads, values)
                delta = jnp.sum(weights_wide * prob_grad, axis=-1, keepdims=True)
                score_grad = (weights_wide * (prob_grad - delta)).astype(LOW)
                joint[:, mine] = (dot(score_grad, keys).astype(LOW).astype(WIDE) * z.scale).astype(LOW)
                joint[:, part + at * head : part + (at + 1) * head] = dot_lt(score_grad, queries).astype(LOW)
                joint[:, 2 * part + at * head : 2 * part + (at + 1) * head] = dot_lt(weights, grads).astype(LOW)
            if layer == 0:
                pltpu.make_async_copy(even_ref, even, ks.at[kinds]).start()
                pltpu.make_async_copy(odd_ref, odd, ks.at[kinds + 1]).start()
            settle(wj, ws.at[0])
            need(0)

            def attend_weights(attend_job=attend_job, expand_job=expand_job):
                target = attend_job.parts
                store_rows(target, dot_lt(x_all[...].reshape(count, width), joint[...]), share, 0)
                store_chunks(target, dot_lt(context[...], fed[1].reshape(count, width)), share, 3 * part)
                joint_sum = jnp.sum(joint[...].astype(WIDE), axis=0, keepdims=True)
                for slot, place in enumerate(slots()):
                    at = slot * share
                    view = relative(target, *place)
                    line = jnp.concatenate(
                        [
                            joint_sum[:, at : at + share],
                            joint_sum[:, 2 * part + at : 2 * part + at + share],
                            jnp.zeros((1, 128 - 2 * share), WIDE),
                        ],
                        axis=1,
                    )
                    view[4 * share : 4 * share + 16, :] = jnp.zeros((16, width), LOW)
                    view[4 * share : 4 * share + 16, 0:128] = jnp.broadcast_to(line, (16, 128)).astype(LOW)
                attend_job.over_c()
                expand_job.over_h()

            got_back = group_scatter(
                lambda j: dot_rt(joint[block_rows(j, n), :], wj[...]), t, low_buf, got, ss, sr, attend_weights
            )
            attend_job.over_l()
            back[...] = back[...] + got_back
            if layer:
                load_attend(layer - 1)

        mixed_grad, entry_part, base_part = normed_back(mixed_ref[...], vector("entry"), back[...])
        vector_sums[z.at["entry"] : z.at["entry"] + 1, :] = entry_part
        vector_sums[z.at["base"] : z.at["base"] + 1, :] = base_part
        back[...] = mixed_grad
        put_lanes(tokens, mixed_grad * bend_ref[...])
        for f in range(0, PACK, 4):
            for q in range(width // 128):
                four = [tokens[q, pl.ds(f + k, packs, stride=PACK), :] for k in range(4)]
                for k in range(4):
                    out_low[4 * q + k, :, f * share : (f + 4) * share] = jnp.concatenate(
                        [piece[:, k * share : (k + 1) * share] for piece in four], axis=1
                    ).astype(LOW)
        low_swap = Swap(lambda *place: out_low.at[index_of(*place)], low_parts, *swaps[1])
        low_swap.start()
        sums_swap = Swap(lanes_for(vector_sums), all_sums, *swaps[2])
        sums_swap.start()
        mixed_move = Move([(back, own_back)], fs.at[0], fs.at[1])
        mixed_move.start()
        encoded = ends_ref[...]
        lane = z.named * share % 128
        bounds = bounds_of(
            [
                encoded[:, lane + k : lane + k + 1] * 32.0 + encoded[:, lane + 4 + k : lane + 5 + k]
                for k in range(4)
            ],
            count,
        )
        pltpu.make_async_copy(even, even, ks.at[kinds]).wait()
        pltpu.make_async_copy(odd, odd, ks.at[kinds + 1]).wait()
        settle(we, ws.at[2])
        settle(wr, ws.at[3])
        settle(wo.at[pl.ds(0, own_width), pl.ds(0, depth)], ws.at[1])
        jobs[2].over_h()
        hand_over(3)
        low_swap.arrived()
        for at, (y_at, x_at, c_at, h_at, l_at) in enumerate(itertools.product((0, 1), repeat=5)):
            row, block = h_at * 4 + l_at * 2 + c_at, y_at * 2 + x_at
            place = pl.ds(block * packs * 8 + row, packs, stride=8)
            for q in range(own_width // 128):
                collected[q, place, :] = low_parts[at, :, q * 128 : (q + 1) * 128].astype(WIDE)
        packed = get_lanes(collected, own_width)
        position_ref[...] = jnp.sum(packed, axis=0, keepdims=True)
        spread_ranks(wide, packed, rank_lanes(bounds, count, share), 64)
        fill_pair(wide, grads_even, grads_odd)
        across = wide[64 : 64 + z.length, :].T.astype(LOW)

        def taps_at(step):
            if step == z.steps - 1:
                return wo[0:own_width, 0:depth]
            half, row, cut = tap_places[step]
            return (we, wr)[half][row * own_width : (row + 1) * own_width, cut * depth : (cut + 1) * depth]

        summed = jnp.zeros((z.length, depth), WIDE)
        for step in range(z.steps):
            summed = summed + dot(shifted(grads_even, grads_odd, step, z.length), taps_at(z.steps - 1 - step))
            if step == z.steps // 2:
                jobs[0].over_h()
        put_lanes(collected, collect_ranks(summed, rank_lanes(bounds, count, gw), count))
        for at in range(DEVICES):
            place = pl.ds((at % 4) * packs * 8 + at // 4, packs, stride=8)
            for q in range(depth // 128):
                out_feats[at, :, q * 128 : (q + 1) * 128] = collected[q, place, :].astype(LOW)
        feats_swap = Swap(lambda *place: out_feats.at[index_of(*place)], feat_parts, *swaps[3])
        feats_swap.start()
        hand_over(1)

        kernel_ref[...] = jnp.zeros_like(kernel_ref)
        for step in range(z.steps):
            made = dot(across, shifted(even, odd, step, z.length))
            for f in range(PACK):
                begin = (step + 1) * depth - f * gw
                kernel_ref[:, begin : begin + depth] += made[f * share : (f + 1) * share, :]
        hand_over(2)
        hand_over(0)

        sums_swap.arrived()
        sums_ref[8 * layers :, :] = jnp.sum(all_sums[...], axis=0)
        heads_swap.arrived()
        heads_ref[...] = jnp.sum(all_heads[...], axis=0)
        feats_swap.arrived()
        for f in range(PACK):
            cut = slice(f * gw, (f + 1) * gw)
            for q in range(width // 128):
                tokens[q, pl.ds(f, packs, stride=PACK), :] = jnp.concatenate(
                    [
                        feat_parts[at, :, cut].astype(WIDE) + feat_parts[at + 1, :, cut].astype(WIDE)
                        for at in (4 * q, 4 * q + 2)
                    ],
                    axis=1,
                )
        mixed_move.done()
        feats_ref[...] = get_lanes(tokens, width) + own_back[...]
        for bundle in (4, 3, 1, 0):
            for copy in column_copies(bundle):
                copy.wait()
            layer, kind = bundle // 3, bundle % 3
            if kind == 0:
                joint_ref[layer] = joint_low[layer].astype(WIDE)
            else:
                expand_ref[layer] = expand_low[layer].astype(WIDE)
        for swap in (heads_swap, low_swap, sums_swap, feats_swap):
            swap.sent()

    return pl.pallas_call(
        kernel,
        out_shape=[
            jax.ShapeDtypeStruct((n, width), WIDE),
            jax.ShapeDtypeStruct((share, (z.steps + 1) * depth), WIDE),
            jax.ShapeDtypeStruct((1, own_width), WIDE),
            jax.ShapeDtypeStruct((8 * layers + lines, 128), WIDE),
            jax.ShapeDtypeStruct((z.vocab, 128), WIDE),
            jax.ShapeDtypeStruct((layers, share, 3 * width), WIDE),
            jax.ShapeDtypeStruct((layers, share, 4 * inner), WIDE),
            jax.ShapeDtypeStruct((layers, z.inner_share, width), WIDE),
            jax.ShapeDtypeStruct((layers, share, width), WIDE),
            jax.ShapeDtypeStruct((layers, 16, 128), WIDE),
        ],
        in_specs=[IN_VMEM] * 6 + [ANYWHERE] * (3 + bundles + kinds),
        out_specs=[IN_VMEM] * 10,
        scratch_shapes=[pltpu.VMEM((2, 2, 2, rows, width), LOW) for rows in row_counts]
        + [pltpu.VMEM((2, 2, rows, width), LOW) for rows in row_counts]
        + [pltpu.VMEM((2, rows, width), LOW) for rows in row_counts]
        + [pltpu.VMEM((rows, width), LOW) for rows in row_counts]
        + [pltpu.VMEM(array.shape[1:], array.dtype) for array in saved]
        + [
            pltpu.VMEM((2, 4, n, width), LOW),
            pltpu.VMEM((count, part), LOW),
            pltpu.VMEM((count, 3 * part), LOW),
            pltpu.VMEM((width, 3 * part), LOW),
            pltpu.VMEM((part, width), LOW),
            pltpu.VMEM((width, inner), LOW),
            pltpu.VMEM((inner, width), LOW),
        ]
        + group_scratch(n, width)
        + [
            pltpu.SemaphoreType.DMA((bundles, 3)),
            pltpu.SemaphoreType.DMA((bundles, 3)),
            pltpu.SemaphoreType.DMA((4,)),
            pltpu.SemaphoreType.DMA((kinds + 2,)),
            pltpu.VMEM((n, width), WIDE),
            pltpu.VMEM((lines, width), WIDE),
            pltpu.VMEM((DEVICES, lines, 128), WIDE),
            pltpu.VMEM((DEVICES, z.vocab, 128), WIDE),
            pltpu.VMEM((width // 128, n, 128), WIDE),
            pltpu.VMEM((DEVICES, packs, own_width), LOW),
            pltpu.VMEM((DEVICES, packs, own_width), LOW),
            pltpu.VMEM((z.lines + 16, own_width), WIDE),
            pltpu.VMEM((z.lines, own_width), LOW),
            pltpu.VMEM((z.lines, own_width), LOW),
            pltpu.VMEM((depth // 128, count, 128), WIDE),
            pltpu.VMEM((DEVICES, packs, depth), LOW),
            pltpu.VMEM((DEVICES, packs, depth), LOW),
            pltpu.VMEM((n, width), WIDE),
            pltpu.VMEM((layers, 4 * share, 3 * part + inner), LOW),
            pltpu.VMEM((layers, share, 3 * width), LOW),
            pltpu.VMEM((layers, share, 4 * inner), LOW),
            pltpu.SemaphoreType.DMA((2, 1)),
            pltpu.SemaphoreType.DMA((layers, 4, 4)),
            pltpu.SemaphoreType.DMA((layers, 4, 4)),
        ]
        + swap_sems() * 4,
        compiler_params=kernel_params(2),
        cost_estimate=cost(220),
    )(flow, head_sums, whole, mixed, bend, ends, even, odd, taps, *held, *saved)


def finish(z, arrays, position_part, sums, heads_sums, small_own):
    layers, share, span = z.layers, z.share, z.taps * z.group_width
    count = len(arrays)
    names = ("attend", "middle", "lower", "return", "final", "upper")

    def kernel(*refs):
        sources, (position_ref, sums_ref, heads_ref, small_ref) = refs[:count], refs[count : count + 4]
        targets = refs[count + 4 : 2 * count + 4]
        line_refs, pair_refs = refs[2 * count + 4 : 2 * count + 8], refs[2 * count + 8 : -1]
        head_ref = refs[-1]
        for at in range(count):
            if at == 0:
                targets[at][0] = sources[at][...]
            elif at == 1:
                targets[at][...] = sources[at][:, PACK * z.group_width : PACK * z.group_width + span]
            else:
                targets[at][...] = sources[at][...]
        _, _, _, h, l = bits()

        def own(value):
            result = value[:, 0:share]
            for at in range(1, 4):
                result = jnp.where(h * 2 + l == at, value[:, at * share : (at + 1) * share], result)
            return result

        mine = own(sums_ref[8 * layers :, :])
        total = position_ref[:, 0:share]
        for f in range(1, PACK):
            total = total + position_ref[:, f * share : (f + 1) * share]
        line_refs[0][...] = total
        for number, at in enumerate((z.at["entry"], z.at["base"], z.vectors)):
            line_refs[1 + number][...] = mine[at : at + 1]
        for layer in range(layers):
            here = slice(layer, layer + 1)
            pair_refs[0][here, :] = small_ref[layer, 0:1, 0:share]
            pair_refs[1][here, :] = small_ref[layer, 0:1, share : 2 * share]
            for number, name in enumerate(names):
                at = z.at[name] + layer
                pair_refs[2 + number][here, :] = mine[at : at + 1]
            pair_refs[-1][here, :] = sums_ref[8 * layer : 8 * layer + 1, 0 : z.inner_share]
        head_ref[...] = own(heads_ref[...])

    shapes = [array.shape for array in arrays]
    shapes[0] = (1,) + shapes[0]
    shapes[1] = (share, span)
    outs = pl.pallas_call(
        kernel,
        out_shape=[jax.ShapeDtypeStruct(shape, WIDE) for shape in shapes]
        + [
            jax.ShapeDtypeStruct(shape, WIDE)
            for shape in [(1, share)] * 4
            + [(layers, share)] * (2 + len(names))
            + [(layers, z.inner_share), (z.vocab, share)]
        ],
        in_specs=[IN_VMEM] * (count + 4),
        out_specs=[IN_VMEM] * (count + 8 + len(names)),
        compiler_params=pltpu.CompilerParams(vmem_limit_bytes=62 * 2**20),
        cost_estimate=cost(5),
    )(*arrays, position_part, sums, heads_sums, small_own)
    lines = [line.reshape(share) for line in outs[count : count + 4]]
    return *outs[:count], lines, outs[count + 4 : -1], outs[-1].T


def fast_local(*arguments):
    (
        features,
        utterance_ends,
        kernel_weight,
        position_bias,
        entry_gain,
        base_shift,
        joint_weight,
        query_bias,
        value_bias,
        output_weight,
        attend_bias,
        middle_gain,
        lower_shift,
        expand_weight,
        hidden_bias,
        reduce_weight,
        return_bias,
        final_gain,
        upper_shift,
        head_weight,
        vocab_bias,
        cotangent,
    ) = arguments
    _, n, width = features.shape
    layers, inner_all = joint_weight.shape[0], expand_weight.shape[2]
    vocab = head_weight.shape[1]
    taps = kernel_weight.shape[1] // (width // CONV_G)
    z = Sizes(n, width, inner_all // 4, layers, taps, vocab)

    small = jnp.concatenate(
        [entry_gain[None], base_shift[None], attend_bias, middle_gain, lower_shift]
        + [return_bias, final_gain, upper_shift, query_bias, value_bias]
        + [position_bias[None], vocab_bias[None]],
        axis=0,
    )
    firsts, conv_saved, held, saved = forward(
        z,
        features[0],
        cotangent[0].T,
        kernel_weight,
        small,
        head_weight,
        utterance_ends,
        hidden_bias,
        joint_weight,
        expand_weight,
        output_weight,
        reduce_weight,
    )
    logits, flow, head_sums, whole, mixed, bend, ends = firsts
    (
        features_grad,
        kernel_wide,
        position_part,
        sums,
        heads_sums,
        joint_own,
        expand_own,
        reduce_own,
        output_own,
        small_own,
    ) = backward(z, flow, head_sums, whole, mixed, bend, ends, *conv_saved, held, saved)
    (
        features_grad,
        kernel_own,
        joint_own,
        expand_own,
        reduce_own,
        output_own,
        lines,
        pairs,
        head_own,
    ) = finish(
        z,
        [features_grad, kernel_wide, joint_own, expand_own, reduce_own, output_own],
        position_part,
        sums,
        heads_sums,
        small_own,
    )
    return (
        logits.T[None],
        features_grad,
        kernel_own,
        lines[0],
        lines[1],
        lines[2],
        joint_own,
        pairs[0],
        pairs[1],
        output_own,
        pairs[2],
        pairs[3],
        pairs[4],
        expand_own,
        pairs[8],
        reduce_own,
        pairs[5],
        pairs[6],
        pairs[7],
        head_own,
        lines[3],
    )


def fits(dp_size, seq_size, width):
    share = width // 32
    return (
        dp_size == 8
        and seq_size == 4
        and share % 16 == 0
        and share * 2 == width // CONV_G
        and share * 2 == width // HEADS
    )


def placed(mesh, width):
    if fits(mesh.shape["dp"], mesh.shape["seq"], width):
        body = fast_local
        mesh = jax.sharding.Mesh(mesh.devices.reshape((2,) * len(AXES)), AXES)
        split, over, within = AXES[:3], AXES[3:], AXES
    else:
        body, split, over, within = local, "dp", "seq", ("dp", "seq")
    tokens = P(split, over, None)
    first, first_wide = P(within), P(within, None)
    second, second_wide = P(None, within), P(None, within, None)
    return jax.shard_map(
        body,
        mesh=mesh,
        in_specs=(
            tokens,
            P(split, None),
            first_wide,
            first,
            first,
            first,
            second_wide,
            second,
            second,
            second_wide,
            second,
            second,
            second,
            second_wide,
            second,
            second_wide,
            second,
            second,
            second,
            first_wide,
            P(),
            tokens,
        ),
        out_specs=(
            tokens,
            tokens,
            first_wide,
            first,
            first,
            first,
            second_wide,
            second,
            second,
            second_wide,
            second,
            second,
            second,
            second_wide,
            second,
            second_wide,
            second,
            second,
            second,
            first_wide,
            P(),
        ),
        check_vma=False,
    )


def solution(mesh):
    def whole(*arguments):
        return placed(mesh, arguments[0].shape[2])(*arguments)

    return whole
```

```python
import itertools
import math

import jax
import jax.numpy as jnp
from jax import lax
from jax.experimental import pallas as pl
from jax.experimental.pallas import tpu as pltpu
from jax.sharding import PartitionSpec as P

HEADS = 16
CONV_G = 16


epsilon = 1e-05
masked_score = -1e30


def with_halo(cells, sides, width):
    for axis, dim in sides:
        count = lax.axis_size(axis)
        ends = count - 1
        head = lax.slice_in_dim(cells, 0, width, axis=dim)
        tail = lax.slice_in_dim(cells, cells.shape[dim] - width, cells.shape[dim], axis=dim)
        cells = jnp.concatenate(
            [
                lax.ppermute(tail, axis, [(i, (i + 1) % count) for i in range(ends)]),
                cells,
                lax.ppermute(head, axis, [((i + 1) % count, i) for i in range(ends)]),
            ],
            axis=dim,
        )
    return cells


def layer_norm(tensor, scaling, shifts):
    average = jnp.mean(tensor, axis=-1, keepdims=True)
    centred = tensor - average
    spread = jnp.mean(centred * centred, axis=-1, keepdims=True)
    return centred * lax.rsqrt(spread + epsilon) * scaling + shifts


def norm_pullback(tensor, scaling, upstream):
    _, pullback = jax.vjp(layer_norm, tensor, scaling, jnp.zeros_like(scaling))
    return pullback(upstream)


def gelu_exact(tensor):
    return jax.nn.gelu(tensor, approximate=False)


def rounded(tensor):
    return tensor.astype(jnp.bfloat16)


def widened(tensor):
    return tensor.astype(jnp.float32)


def segment_ids(positions, utterance_ends):
    return jnp.sum(
        (positions[None, :, None] >= utterance_ends[:, None, :]).astype(jnp.int32), axis=2
    )


def unfold(source, source_ids, target_ids, anchors):
    length = target_ids.shape[1]
    pieces = [lax.slice_in_dim(source, anchor, anchor + length, axis=1) for anchor in anchors]
    matches = [
        lax.slice_in_dim(source_ids, anchor, anchor + length, axis=1) == target_ids
        for anchor in anchors
    ]
    stacked = jnp.stack(pieces, axis=2)
    keepers = jnp.stack(matches, axis=2)
    return jnp.where(keepers[..., None], stacked, jnp.zeros_like(stacked))


def conv_forward(halo_feats, halo_ids, frame_ids, kernel_grid, tap_block):
    row_count, frame_count = frame_ids.shape
    groups, group_width, tap_count, inner_width = kernel_grid.shape
    summed = jnp.zeros((row_count, frame_count, groups, group_width), jnp.float32)
    for block_at in range(tap_count // tap_block):
        first_tap = block_at * tap_block
        window = unfold(
            halo_feats,
            halo_ids,
            frame_ids,
            [first_tap + inner_tap for inner_tap in range(tap_block)],
        )
        window = window.reshape(row_count, frame_count, tap_block, groups, inner_width)
        summed = summed + jnp.einsum(
            "rtkgi,goki->rtgo",
            window,
            kernel_grid[:, :, first_tap : first_tap + tap_block, :],
            preferred_element_type=jnp.float32,
        )
    return summed.reshape(row_count, frame_count, groups * group_width)


def conv_backward(halo_grads, halo_feats, halo_ids, frame_ids, kernel_grid, tap_block, conv_low):
    row_count, frame_count = frame_ids.shape
    groups, group_width, tap_count, inner_width = kernel_grid.shape
    input_part = jnp.zeros((row_count, frame_count, groups, inner_width), jnp.float32)
    grouped = conv_low.reshape(row_count, frame_count, groups, group_width)
    kernel_parts = []
    for block_at in range(tap_count // tap_block):
        first_tap = block_at * tap_block
        tap_list = [first_tap + inner_tap for inner_tap in range(tap_block)]
        grads_window = unfold(
            halo_grads, halo_ids, frame_ids, [tap_count - tap_at for tap_at in tap_list]
        )
        grads_window = grads_window.reshape(row_count, frame_count, tap_block, groups, group_width)
        input_part = input_part + jnp.einsum(
            "rtkgo,goki->rtgi",
            grads_window,
            kernel_grid[:, :, first_tap : first_tap + tap_block, :],
            preferred_element_type=jnp.float32,
        )
        feats_window = unfold(halo_feats, halo_ids, frame_ids, tap_list)
        feats_window = feats_window.reshape(row_count, frame_count, tap_block, groups, inner_width)
        kernel_parts.append(
            jnp.einsum(
                "rtgo,rtkgi->goki", grouped, feats_window, preferred_element_type=jnp.float32
            )
        )
    kernel_full = jnp.concatenate(kernel_parts, axis=2).reshape(
        groups * group_width, tap_count * inner_width
    )
    return (input_part.reshape(row_count, frame_count, groups * inner_width), kernel_full)


def split_heads(tensor, head_count):
    return tensor.reshape(
        tensor.shape[0], tensor.shape[1], head_count, tensor.shape[2] // head_count
    )


def attend_scores(queries, all_keys, query_ids, key_ids, head_count):
    scores = jnp.einsum(
        "rqhd,rkhd->rhqk",
        split_heads(queries, head_count),
        split_heads(all_keys, head_count),
        preferred_element_type=jnp.float32,
    )
    allowed = query_ids[:, None, :, None] == key_ids[:, None, None, :]
    return jnp.where(allowed, scores, masked_score)


def attend_forward(queries, all_keys, all_values, frame_ids, row_ids, head_count):
    scores = attend_scores(queries, all_keys, frame_ids, row_ids, head_count)
    row_peak = jnp.max(scores, axis=-1, keepdims=True)
    exponent = jnp.exp(scores - row_peak)
    totals = jnp.sum(exponent, axis=-1, keepdims=True)
    weights_low = rounded(exponent / totals)
    context = jnp.einsum(
        "rhqk,rkhd->rqhd",
        weights_low,
        split_heads(all_values, head_count),
        preferred_element_type=jnp.float32,
    )
    return (rounded(context.reshape(queries.shape)), row_peak + jnp.log(totals))


def attend_backward(
    queries, all_keys, all_values, frame_ids, row_ids, head_count, log_totals, context_low
):
    scores = attend_scores(queries, all_keys, frame_ids, row_ids, head_count)
    attention = jnp.exp(scores - log_totals)
    weights_low = rounded(attention)
    grad_heads = split_heads(context_low, head_count)
    prob_grad = jnp.einsum(
        "rqhd,rkhd->rhqk",
        grad_heads,
        split_heads(all_values, head_count),
        preferred_element_type=jnp.float32,
    )
    row_delta = jnp.sum(attention * prob_grad, axis=-1, keepdims=True)
    score_grad = rounded(attention * (prob_grad - row_delta))
    value_part = jnp.einsum(
        "rhqk,rqhd->rkhd", weights_low, grad_heads, preferred_element_type=jnp.float32
    )
    query_part = jnp.einsum(
        "rhqk,rkhd->rqhd",
        score_grad,
        split_heads(all_keys, head_count),
        preferred_element_type=jnp.float32,
    )
    key_part = jnp.einsum(
        "rhqk,rqhd->rkhd",
        score_grad,
        split_heads(queries, head_count),
        preferred_element_type=jnp.float32,
    )
    return (
        query_part.reshape(queries.shape),
        key_part.reshape(all_keys.shape),
        value_part.reshape(all_values.shape),
    )


def local(
    features,
    utterance_ends,
    kernel_weight,
    position_bias,
    entry_gain,
    base_shift,
    joint_weight,
    query_bias,
    value_bias,
    output_weight,
    attend_bias,
    middle_gain,
    lower_shift,
    expand_weight,
    hidden_bias,
    reduce_weight,
    return_bias,
    final_gain,
    upper_shift,
    head_weight,
    vocab_bias,
    cotangent,
):
    row_count, frame_count, model_dim = features.shape
    frames_all = frame_count * lax.axis_size("seq")
    groups = CONV_G
    group_width = model_dim // groups
    tap_count = kernel_weight.shape[1] // group_width
    half_taps = tap_count // 2
    tap_block = math.gcd(tap_count, 16)
    head_count = HEADS
    query_scale = (model_dim // head_count) ** (-0.5)
    layer_count = joint_weight.shape[0]
    rows_share = model_dim // lax.axis_size(("dp", "seq"))
    anchor = lax.axis_index("seq") * frame_count
    frame_ids = segment_ids(anchor + jnp.arange(frame_count, dtype=jnp.int32), utterance_ends)
    row_ids = segment_ids(jnp.arange(frames_all, dtype=jnp.int32), utterance_ends)
    halo_place = anchor - half_taps + jnp.arange(frame_count + tap_count, dtype=jnp.int32)
    inside = (halo_place >= 0) & (halo_place < frames_all)
    halo_ids = jnp.where(inside[None, :], segment_ids(halo_place, utterance_ends), -1)
    stem = (
        lax.all_gather(kernel_weight, ("dp", "seq"), axis=0, tiled=True),
        lax.all_gather(position_bias, ("dp", "seq"), axis=0, tiled=True),
        lax.all_gather(entry_gain, ("dp", "seq"), axis=0, tiled=True),
        lax.all_gather(base_shift, ("dp", "seq"), axis=0, tiled=True),
        lax.all_gather(head_weight, ("dp", "seq"), axis=0, tiled=True),
    )
    kernel_grid = stem[0].reshape(groups, group_width, tap_count, group_width)
    halo_feats = with_halo(features, (("seq", 1),), half_taps)
    conv_pre = conv_forward(halo_feats, halo_ids, frame_ids, kernel_grid, tap_block) + widened(
        stem[1]
    )
    mixed = widened(features) + gelu_exact(conv_pre)
    hidden = layer_norm(mixed, widened(stem[2]), widened(stem[3]))
    saved = []
    for layer_at in range(layer_count):
        (
            joint_full,
            query_full,
            value_full,
            output_full,
            attend_full,
            middle_full,
            lower_full,
            expand_full,
            hidden_full,
            reduce_full,
            return_full,
            final_full,
            upper_full,
        ) = (
            lax.all_gather(joint_weight[layer_at], ("dp", "seq"), axis=0, tiled=True),
            lax.all_gather(query_bias[layer_at], ("dp", "seq"), axis=0, tiled=True),
            lax.all_gather(value_bias[layer_at], ("dp", "seq"), axis=0, tiled=True),
            lax.all_gather(output_weight[layer_at], ("dp", "seq"), axis=0, tiled=True),
            lax.all_gather(attend_bias[layer_at], ("dp", "seq"), axis=0, tiled=True),
            lax.all_gather(middle_gain[layer_at], ("dp", "seq"), axis=0, tiled=True),
            lax.all_gather(lower_shift[layer_at], ("dp", "seq"), axis=0, tiled=True),
            lax.all_gather(expand_weight[layer_at], ("dp", "seq"), axis=0, tiled=True),
            lax.all_gather(hidden_bias[layer_at], ("dp", "seq"), axis=0, tiled=True),
            lax.all_gather(reduce_weight[layer_at], ("dp", "seq"), axis=0, tiled=True),
            lax.all_gather(return_bias[layer_at], ("dp", "seq"), axis=0, tiled=True),
            lax.all_gather(final_gain[layer_at], ("dp", "seq"), axis=0, tiled=True),
            lax.all_gather(upper_shift[layer_at], ("dp", "seq"), axis=0, tiled=True),
        )
        inputs_low = rounded(hidden)
        joint_out = jnp.einsum(
            "rtd,de->rte", inputs_low, joint_full, preferred_element_type=jnp.float32
        )
        queries = rounded((joint_out[..., :model_dim] + widened(query_full)) * query_scale)
        keys_local = rounded(joint_out[..., model_dim : 2 * model_dim])
        values_local = rounded(joint_out[..., 2 * model_dim :] + widened(value_full))
        all_keys, all_values = (
            lax.all_gather(keys_local, "seq", axis=1, tiled=True),
            lax.all_gather(values_local, "seq", axis=1, tiled=True),
        )
        context, log_totals = attend_forward(
            queries, all_keys, all_values, frame_ids, row_ids, head_count
        )
        attended = jnp.einsum(
            "rtc,cd->rtd", context, output_full, preferred_element_type=jnp.float32
        ) + widened(attend_full)
        residual_one = hidden + attended
        middle = layer_norm(residual_one, widened(middle_full), widened(lower_full))
        middle_low = rounded(middle)
        inner_pre = jnp.einsum(
            "rtd,df->rtf", middle_low, expand_full, preferred_element_type=jnp.float32
        ) + widened(hidden_full)
        activated = rounded(gelu_exact(inner_pre))
        outer = (
            middle
            + jnp.einsum("rtf,fd->rtd", activated, reduce_full, preferred_element_type=jnp.float32)
            + widened(return_full)
        )
        kept_weights = None
        saved.append(
            (
                inputs_low,
                queries,
                all_keys,
                all_values,
                log_totals,
                context,
                residual_one,
                middle_low,
                inner_pre,
                activated,
                outer,
                kept_weights,
            )
        )
        hidden = layer_norm(outer, widened(final_full), widened(upper_full))
    final_low = rounded(hidden)
    logits = jnp.einsum(
        "rtd,dv->rtv", final_low, stem[4], preferred_element_type=jnp.float32
    ) + widened(vocab_bias)
    back_stem = (
        lax.all_gather(kernel_weight, ("dp", "seq"), axis=0, tiled=True),
        lax.all_gather(entry_gain, ("dp", "seq"), axis=0, tiled=True),
        lax.all_gather(head_weight, ("dp", "seq"), axis=0, tiled=True),
    )
    vocab_sum = jnp.sum(widened(cotangent), axis=(0, 1))
    head_part = jnp.einsum("rtd,rtv->dv", final_low, cotangent, preferred_element_type=jnp.float32)
    flow_grad = jnp.einsum(
        "rtv,dv->rtd", cotangent, back_stem[2], preferred_element_type=jnp.float32
    )
    layer_grads = [None] * layer_count
    for layer_at in reversed(range(layer_count)):
        (
            inputs_low,
            queries,
            all_keys,
            all_values,
            log_totals,
            context,
            residual_one,
            middle_low,
            inner_pre,
            activated,
            outer,
            kept_weights,
        ) = saved[layer_at]
        back_weights = (
            lax.all_gather(joint_weight[layer_at], ("dp", "seq"), axis=0, tiled=True),
            lax.all_gather(output_weight[layer_at], ("dp", "seq"), axis=0, tiled=True),
            lax.all_gather(expand_weight[layer_at], ("dp", "seq"), axis=0, tiled=True),
            lax.all_gather(reduce_weight[layer_at], ("dp", "seq"), axis=0, tiled=True),
            lax.all_gather(middle_gain[layer_at], ("dp", "seq"), axis=0, tiled=True),
            lax.all_gather(final_gain[layer_at], ("dp", "seq"), axis=0, tiled=True),
        )
        joint_full, output_full, expand_full, reduce_full, middle_full, final_full = back_weights
        outer_grad, final_part, upper_part = norm_pullback(outer, widened(final_full), flow_grad)
        fed_low = rounded(outer_grad)
        return_part = jnp.sum(widened(fed_low), axis=(0, 1))
        active_grad = jnp.einsum(
            "rtd,fd->rtf", fed_low, reduce_full, preferred_element_type=jnp.float32
        )
        _, gelu_pull = jax.vjp(gelu_exact, inner_pre)
        (inner_grad,) = gelu_pull(active_grad)
        inner_low = rounded(inner_grad)
        hidden_part = jnp.sum(widened(inner_low), axis=(0, 1))
        middle_flow = outer_grad + jnp.einsum(
            "rtf,df->rtd", inner_low, expand_full, preferred_element_type=jnp.float32
        )
        residual_grad, middle_part, lower_part = norm_pullback(
            residual_one, widened(middle_full), middle_flow
        )
        attended_low = rounded(residual_grad)
        attend_part = jnp.sum(widened(attended_low), axis=(0, 1))
        context_low = rounded(
            jnp.einsum("rtd,cd->rtc", attended_low, output_full, preferred_element_type=jnp.float32)
        )
        query_raw, key_raw, value_raw = attend_backward(
            queries, all_keys, all_values, frame_ids, row_ids, head_count, log_totals, context_low
        )
        key_sum, value_sum = (
            lax.psum_scatter(
                key_raw.astype(jnp.bfloat16), "seq", scatter_dimension=1, tiled=True
            ).astype(jnp.float32),
            lax.psum_scatter(
                value_raw.astype(jnp.bfloat16), "seq", scatter_dimension=1, tiled=True
            ).astype(jnp.float32),
        )
        query_low = rounded(widened(rounded(query_raw)) * query_scale)
        key_low = rounded(key_sum)
        value_low = rounded(value_sum)
        query_part = jnp.sum(widened(query_low), axis=(0, 1))
        value_part = jnp.sum(widened(value_low), axis=(0, 1))
        joint_low = jnp.concatenate([query_low, key_low, value_low], axis=-1)
        flow_grad = residual_grad + jnp.einsum(
            "rte,de->rtd", joint_low, joint_full, preferred_element_type=jnp.float32
        )
        ratio = hidden_part.shape[0] // model_dim
        vector_rows = jnp.stack(
            [
                query_part,
                value_part,
                attend_part,
                middle_part,
                lower_part,
                return_part,
                final_part,
                upper_part,
            ],
            axis=1,
        )
        hidden_rows = hidden_part.reshape(model_dim, ratio)

        def layer_term(
            start,
            count,
            inputs_low=inputs_low,
            joint_low=joint_low,
            context=context,
            attended_low=attended_low,
            middle_low=middle_low,
            inner_low=inner_low,
            activated=activated,
            fed_low=fed_low,
            vector_rows=vector_rows,
            hidden_rows=hidden_rows,
            ratio=ratio,
        ):
            joint_rows = jnp.einsum(
                "rtd,rte->de", inputs_low, joint_low, preferred_element_type=jnp.float32
            )
            output_rows = jnp.einsum(
                "rtc,rtd->cd", context, attended_low, preferred_element_type=jnp.float32
            )
            expand_rows = jnp.einsum(
                "rtd,rtf->df", middle_low, inner_low, preferred_element_type=jnp.float32
            )
            reduce_rows = jnp.einsum(
                "rtf,rtd->fd", activated, fed_low, preferred_element_type=jnp.float32
            ).reshape(count, ratio * model_dim)
            return jnp.concatenate(
                [joint_rows, output_rows, expand_rows, reduce_rows, vector_rows, hidden_rows],
                axis=1,
            )

        summed = lax.psum_scatter(
            layer_term(jnp.int32(0), rows_share * lax.axis_size(("dp", "seq"))),
            ("dp", "seq"),
            scatter_dimension=0,
            tiled=True,
        )
        ff_width = ratio * model_dim
        first = 3 * model_dim
        second = first + model_dim
        third = second + ff_width
        fourth = third + ratio * model_dim
        joint_own = summed[:, :first]
        output_own = summed[:, first:second]
        expand_own = summed[:, second:third]
        reduce_own = summed[:, third:fourth].reshape(rows_share * ratio, model_dim)
        vector_own = summed[:, fourth : fourth + 8]
        hidden_own = summed[:, fourth + 8 :].reshape(rows_share * ratio)
        layer_grads[layer_at] = (
            joint_own,
            vector_own[:, 0],
            vector_own[:, 1],
            output_own,
            vector_own[:, 2],
            vector_own[:, 3],
            vector_own[:, 4],
            expand_own,
            hidden_own,
            reduce_own,
            vector_own[:, 5],
            vector_own[:, 6],
            vector_own[:, 7],
        )
    mixed_grad, entry_part, base_part = norm_pullback(mixed, widened(back_stem[1]), flow_grad)
    _, gelu_pull = jax.vjp(gelu_exact, conv_pre)
    (conv_grad,) = gelu_pull(mixed_grad)
    conv_low = rounded(conv_grad)
    position_part = jnp.sum(widened(conv_low), axis=(0, 1))
    halo_grads = with_halo(conv_low, (("seq", 1),), half_taps)
    back_grid = back_stem[0].reshape(groups, group_width, tap_count, group_width)
    input_part, kernel_part = conv_backward(
        halo_grads, halo_feats, halo_ids, frame_ids, back_grid, tap_block, conv_low
    )
    features_grad = mixed_grad + input_part
    vocab_tiled = jnp.tile(vocab_sum, lax.axis_size(("dp", "seq")))
    stem_sums = (
        lax.psum_scatter(kernel_part, ("dp", "seq"), scatter_dimension=0, tiled=True),
        lax.psum_scatter(position_part, ("dp", "seq"), scatter_dimension=0, tiled=True),
        lax.psum_scatter(entry_part, ("dp", "seq"), scatter_dimension=0, tiled=True),
        lax.psum_scatter(base_part, ("dp", "seq"), scatter_dimension=0, tiled=True),
        lax.psum_scatter(head_part, ("dp", "seq"), scatter_dimension=0, tiled=True),
        lax.psum_scatter(vocab_tiled, ("dp", "seq"), scatter_dimension=0, tiled=True),
    )
    stacked = [
        jnp.stack([layer_grads[layer_at][member] for layer_at in range(layer_count)])
        for member in range(13)
    ]
    return (
        logits,
        features_grad,
        stem_sums[0],
        stem_sums[1],
        stem_sums[2],
        stem_sums[3],
        stacked[0],
        stacked[1],
        stacked[2],
        stacked[3],
        stacked[4],
        stacked[5],
        stacked[6],
        stacked[7],
        stacked[8],
        stacked[9],
        stacked[10],
        stacked[11],
        stacked[12],
        stem_sums[4],
        stem_sums[5],
    )


MESH_ID = pl.DeviceIdType.MESH
IN_VMEM = pl.BlockSpec(memory_space=pltpu.VMEM)
ANYWHERE = pl.BlockSpec(memory_space=pl.ANY)
AXES = ("y", "x", "c", "h", "l")
Y_BIT, X_BIT, C_BIT, H_BIT, L_BIT = 16, 8, 4, 2, 1
DEVICES = 32
PIECES = 8
PACK = 8
RANKS = 4
LOW, WIDE = jnp.bfloat16, jnp.float32


def kernel_params(collective):
    return pltpu.CompilerParams(
        vmem_limit_bytes=62 * 2**20, collective_id=collective, has_side_effects=True
    )


def cost(micros):
    return pl.CostEstimate(flops=int(micros * 1.1e9), bytes_accessed=2**20, transcendentals=0)


def bits():
    return tuple(lax.axis_index(axis) for axis in AXES)


def index_of(y, x, c, h, l):
    return y * 16 + x * 8 + c * 4 + h * 2 + l


def turned_of(y, x, c, h, l):
    return index_of(h, l, c, y, x)


def flipped(mask):
    return {
        axis: 1 - lax.axis_index(axis)
        for number, axis in enumerate(AXES)
        if mask >> (len(AXES) - 1 - number) & 1
    }


def place_of(mask):
    return [
        1 - here if mask >> (len(AXES) - 1 - number) & 1 else here
        for number, here in enumerate(bits())
    ]


def greet_all():
    gate = pltpu.get_barrier_semaphore()
    for mask in range(1, DEVICES):
        pl.semaphore_signal(gate, inc=1, device_id=flipped(mask), device_id_type=MESH_ID)


def all_greeted():
    pl.semaphore_wait(pltpu.get_barrier_semaphore(), DEVICES - 1)


def remote(source, target, send, receive, peer):
    return pltpu.make_async_remote_copy(
        source, target, send, receive, device_id=peer, device_id_type=MESH_ID
    )


class Swap:
    def __init__(self, block_for, target, sends, receives, own_sem):
        self.block_for, self.target = block_for, target
        self.sends, self.receives, self.own_sem = sends, receives, own_sem

    def own(self):
        place = bits()
        return pltpu.make_async_copy(
            self.block_for(*place), self.target.at[index_of(*place)], self.own_sem
        )

    def copy(self, mask):
        return remote(
            self.block_for(*place_of(mask)),
            self.target.at[index_of(*bits())],
            self.sends.at[mask - 1],
            self.receives.at[mask - 1],
            flipped(mask),
        )

    def start(self):
        self.own().start()
        for mask in range(1, DEVICES):
            self.copy(mask).start()

    def arrived(self):
        self.own().wait()
        for mask in range(1, DEVICES):
            self.copy(mask).wait_recv()

    def sent(self):
        for mask in range(1, DEVICES):
            self.copy(mask).wait_send()


def swap_sems():
    return [
        pltpu.SemaphoreType.DMA((DEVICES - 1,)),
        pltpu.SemaphoreType.DMA((DEVICES - 1,)),
        pltpu.SemaphoreType.DMA,
    ]


class Move:
    def __init__(self, pairs, sends, receives):
        y, x, _, h, l = bits()
        self.pairs, self.sends, self.receives = pairs, sends, receives
        self.same = jnp.logical_and(y == h, x == l)
        self.peer = {"y": h, "x": l, "h": y, "l": x}

    def each(self, action):
        @pl.when(self.same)
        def _():
            for number, (source, target) in enumerate(self.pairs):
                copy = pltpu.make_async_copy(source, target, self.receives.at[number])
                copy.start() if action == "start" else copy.wait()

        @pl.when(jnp.logical_not(self.same))
        def _():
            for number, (source, target) in enumerate(self.pairs):
                copy = remote(
                    source, target, self.sends.at[number], self.receives.at[number], self.peer
                )
                copy.start() if action == "start" else copy.wait()

    def start(self):
        self.each("start")

    def done(self):
        self.each("wait")


def put_lanes(target, value):
    for q in range(value.shape[1] // 128):
        target[q] = value[:, q * 128 : (q + 1) * 128]


def get_lanes(source, width):
    return jnp.concatenate([source[q] for q in range(width // 128)], axis=1)


def bounds_of(ends, frames):
    before = [jnp.zeros_like(ends[0])] + ends[:-1]
    return [jnp.where(end > last, end, float(frames)) for end, last in zip(ends, before)]


def rank_lanes(bounds, frames, width):
    shape = (frames // PACK, 8, PACK * width)
    frame = lax.broadcasted_iota(jnp.int32, shape, 0) * PACK
    frame = frame + lax.broadcasted_iota(jnp.int32, shape, 2) // width
    rank = jnp.zeros(shape, jnp.int32)
    for bound in bounds:
        rank = rank + (frame >= bound[None].astype(jnp.int32)).astype(jnp.int32)
    return rank.reshape(frames, PACK * width)


def spread_ranks(wide, packed, rank, first):
    lines = packed.shape[0]
    wide[...] = jnp.zeros_like(wide)
    for number in range(RANKS):
        place = pl.ds(first + number * 64, lines)
        wide[place, :] += jnp.where(rank == number, packed, 0.0)


def collect_ranks(summed, rank, lines):
    result = jnp.zeros((lines, summed.shape[1]), WIDE)
    for number in range(RANKS):
        result = jnp.where(rank == number, summed[number * 64 : number * 64 + lines, :], result)
    return result


def fill_pair(wide, even, odd):
    length = even.shape[0]
    even[...] = wide[:length, :].astype(LOW)
    odd[...] = wide[8 : 8 + length, :].astype(LOW)


def shifted(even, odd, step, length):
    source = even if step % 2 == 0 else odd
    return source[pl.ds((step - step % 2) * 8, length), :]


def normed(tensor, gain, shift):
    average = jnp.mean(tensor, axis=-1, keepdims=True)
    centred = tensor - average
    spread = jnp.mean(centred * centred, axis=-1, keepdims=True)
    return centred * lax.rsqrt(spread + epsilon) * gain + shift


def normed_back(tensor, gain, upstream):
    average = jnp.mean(tensor, axis=-1, keepdims=True)
    centred = tensor - average
    spread = jnp.mean(centred * centred, axis=-1, keepdims=True)
    inverse = lax.rsqrt(spread + epsilon)
    unit = centred * inverse
    scaled = upstream * gain
    result = inverse * (
        scaled
        - jnp.mean(scaled, axis=-1, keepdims=True)
        - unit * jnp.mean(scaled * unit, axis=-1, keepdims=True)
    )
    return (
        result,
        jnp.sum(upstream * unit, axis=0, keepdims=True),
        jnp.sum(upstream, axis=0, keepdims=True),
    )


def gelu_pair(tensor):
    half = 0.5 * (1.0 + lax.erf(tensor * (2.0**-0.5)))
    slope = half + tensor * (jnp.exp(-0.5 * tensor * tensor) * ((2.0 * math.pi) ** -0.5))
    return tensor * half, slope


def dot(left, right):
    return jnp.dot(left, right, preferred_element_type=WIDE)


def dot_rt(left, right):
    return lax.dot_general(left, right, (((1,), (1,)), ((), ())), preferred_element_type=WIDE)


def dot_lt(left, right):
    return lax.dot_general(left, right, (((0,), (0,)), ((), ())), preferred_element_type=WIDE)


def group_gather(block, t, sends, receives, ready, use):
    half = block.shape[1] // 2
    y_peer, x_peer = flipped(Y_BIT), flipped(X_BIT)
    own = block.at[t]
    to_y = remote(own, own, sends.at[0], receives.at[0], y_peer)
    to_y.start()
    to_x = remote(own, own, sends.at[1], receives.at[1], x_peer)
    to_x.start()
    ready()
    use(t)
    to_y.wait_recv()
    other = block.at[lax.bitwise_xor(t, 2), pl.ds(0, half)]
    on_x = remote(other, other, sends.at[2], receives.at[2], x_peer)
    on_x.start()
    to_x.wait_recv()
    other = block.at[lax.bitwise_xor(t, 1), pl.ds(half, half)]
    on_y = remote(other, other, sends.at[3], receives.at[3], y_peer)
    on_y.start()
    use(lax.bitwise_xor(t, 2))
    use(lax.bitwise_xor(t, 1))
    on_x.wait_recv()
    on_y.wait_recv()
    use(lax.bitwise_xor(t, 3))
    for copy in (to_y, to_x, on_x, on_y):
        copy.wait_send()


def group_scatter(part, t, low, got, sends, receives, between=None):
    half = low.shape[1]
    y_peer, x_peer = flipped(Y_BIT), flipped(X_BIT)

    def send(slot, value, peer):
        low[slot] = value.astype(LOW)
        copy = remote(low.at[slot], got.at[slot], sends.at[slot], receives.at[slot], peer)
        copy.start()
        return copy

    def arrived(slot):
        return got[slot].astype(WIDE)

    far = part(lax.bitwise_xor(t, 3))
    far_y = send(0, far[:half], y_peer)
    far_x = send(1, far[half:], x_peer)
    beside_y = part(lax.bitwise_xor(t, 2))
    near_y = send(2, beside_y[:half], y_peer)
    beside_x = part(lax.bitwise_xor(t, 1))
    near_x = send(3, beside_x[half:], x_peer)
    far_y.wait_recv()
    on_x = send(4, beside_x[:half] + arrived(0), x_peer)
    far_x.wait_recv()
    on_y = send(5, beside_y[half:] + arrived(1), y_peer)
    own = part(t)
    if between is not None:
        between()
    near_y.wait_recv()
    near_x.wait_recv()
    on_x.wait_recv()
    on_y.wait_recv()
    result = jnp.concatenate(
        [own[:half] + arrived(2) + arrived(4), own[half:] + arrived(3) + arrived(5)], axis=0
    )
    for copy in (far_y, far_x, near_y, near_x, on_x, on_y):
        copy.wait_send()
    return result


def group_scratch(n, width):
    return [
        pltpu.VMEM((6, n // 2, width), LOW),
        pltpu.VMEM((6, n // 2, width), LOW),
        pltpu.SemaphoreType.DMA((4,)),
        pltpu.SemaphoreType.DMA((4,)),
        pltpu.SemaphoreType.DMA((6,)),
        pltpu.SemaphoreType.DMA((6,)),
    ]


def block_rows(j, n):
    return pl.ds(pl.multiple_of(j * n, n), n)


def slots():
    return [(c, h, l) for c in range(2) for h in range(2) for l in range(2)]


class Spread:
    def __init__(self, held, sends, receives):
        self.held, self.sends, self.receives = held, sends, receives

    def copy(self, step):
        _, _, c, h, l = bits()
        own = c * 4 + h * 2 + l
        near = c * 4 + (1 - h) * 2 + l
        view = self.held.at[(pl.ds(own, 1), pl.ds(own, 1), pl.ds(near, 1), pl.ds(c * 4, 4))[step]]
        peer = flipped((H_BIT, L_BIT, L_BIT, C_BIT)[step])
        return remote(view, view, self.sends.at[step], self.receives.at[step], peer)

    def begin(self):
        self.copy(0).start()
        self.copy(1).start()

    def forward(self):
        self.copy(0).wait_recv()
        self.copy(2).start()

    def over_c(self):
        self.copy(1).wait_recv()
        self.copy(2).wait_recv()
        self.copy(3).start()

    def done(self):
        self.copy(3).wait_recv()
        for step in range(4):
            self.copy(step).wait_send()


def load_rows(held, target, sem, share, column, width):
    for slot in range(PIECES):
        for at in range(4):
            pltpu.make_async_copy(
                held.at[slot, pl.ds(at * share, share), pl.ds(column, width)],
                target.at[pl.ds((at * PIECES + slot) * share, share), :],
                sem,
            ).start()


def load_chunks(held, target, sem, share, column, width):
    for slot in range(PIECES):
        for chunk in range(4):
            pltpu.make_async_copy(
                held.at[slot, pl.ds(chunk * share, share), pl.ds(column, width)],
                target.at[pl.ds(slot * share, share), pl.ds(chunk * width, width)],
                sem,
            ).start()


def load_blocks(held, target, sem, first, share):
    for slot in range(PIECES):
        pltpu.make_async_copy(
            held.at[slot, pl.ds(first, share)], target.at[pl.ds(slot * share, share), :], sem
        ).start()


def load_line(held, target, sem, first, width):
    for slot in range(PIECES):
        pltpu.make_async_copy(
            held.at[slot, pl.ds(first, 16), pl.ds(0, width)],
            target.at[:, pl.ds(slot * width, width)],
            sem,
        ).start()


def settle(target, sem):
    pltpu.make_async_copy(target, target, sem).wait()


def relative(target, c, h, l):
    _, _, c_me, h_me, l_me = bits()
    return target.at[
        lax.bitwise_xor(c_me, c), lax.bitwise_xor(l_me, l), lax.bitwise_xor(h_me, h)
    ]


def store_rows(target, grads, share, column):
    width = grads.shape[1]
    for slot, place in enumerate(slots()):
        for at in range(4):
            row = (at * PIECES + slot) * share
            relative(target, *place)[at * share : (at + 1) * share, column : column + width] = grads[
                row : row + share, :
            ].astype(LOW)


def store_chunks(target, grads, share, column):
    width = grads.shape[1] // 4
    for slot, place in enumerate(slots()):
        for chunk in range(4):
            relative(target, *place)[
                chunk * share : (chunk + 1) * share, column : column + width
            ] = grads[slot * share : (slot + 1) * share, chunk * width : (chunk + 1) * width].astype(LOW)


def store_blocks(target, grads, first, share):
    for slot, place in enumerate(slots()):
        relative(target, *place)[first : first + share, :] = grads[
            slot * share : (slot + 1) * share, :
        ].astype(LOW)


class Gather:
    def __init__(self, parts, got_c, got_l, got_h, sends, receives):
        self.parts, self.got = parts, (got_c, got_l, got_h)
        self.sends, self.receives = sends, receives

    def copy(self, step):
        source = (self.parts.at[1], self.parts.at[0, 1], self.parts.at[0, 0, 1])[step]
        return remote(
            source,
            self.got[step],
            self.sends.at[step],
            self.receives.at[step],
            flipped((C_BIT, L_BIT, H_BIT)[step]),
        )

    def over_c(self):
        self.copy(0).start()

    def over_l(self):
        self.copy(0).wait_recv()
        for l in (1, 0):
            for h in range(2):
                summed = self.parts[0, l, h].astype(WIDE) + self.got[0][l, h].astype(WIDE)
                self.parts[0, l, h] = summed.astype(LOW)
            if l == 1:
                self.copy(1).start()

    def over_h(self):
        self.copy(1).wait_recv()
        for h in (1, 0):
            summed = self.parts[0, 0, h].astype(WIDE) + self.got[1][h].astype(WIDE)
            self.parts[0, 0, h] = summed.astype(LOW)
            if h == 1:
                self.copy(2).start()

    def done(self):
        self.copy(2).wait_recv()
        for step in range(3):
            self.copy(step).wait_send()

    def total(self, first, last):
        return self.parts[0, 0, 0, first:last, :].astype(WIDE) + self.got[2][first:last, :].astype(WIDE)


class Sizes:
    def __init__(self, n, width, inner, layers, taps, vocab):
        self.n, self.width, self.inner, self.layers = n, width, inner, layers
        self.taps, self.vocab = taps, vocab
        self.count = 4 * n
        self.part = width // 4
        self.head = width // HEADS
        self.heads = self.part // self.head
        self.share = width // DEVICES
        self.inner_share = inner // PIECES
        self.scale = self.head**-0.5
        self.group_width = width // CONV_G
        self.packs = n // PACK
        self.steps = taps // PACK + 1
        self.length = self.count + (RANKS - 1) * 64
        self.lines = self.length + 128
        self.held_rows = (4 * self.share, 4 * self.share, self.inner_share + 16)
        self.grad_rows = (4 * self.share + 16, 4 * self.share, self.inner_share + 16)
        self.bundles = 3 * layers
        self.at = {"entry": 0, "base": 1}
        at = 2
        for name in ("attend", "middle", "lower", "return", "final", "upper"):
            self.at[name] = at
            at += layers
        self.vectors = at
        self.at["head"] = at
        self.at["heads"] = at + vocab
        self.named = at + vocab + 2 * layers
        self.line = -(-(self.named + 1) // 8) * 8
        self.gathered = 64

    def saved(self):
        n, count, layers, width = self.n, self.count, self.layers, self.width
        return [
            ((layers, 4, n, width), LOW),
            ((layers, count, 3 * self.part), LOW),
            ((layers, self.heads * count, count), LOW),
            ((layers, count, self.part), LOW),
            ((layers, n, width), WIDE),
            ((layers, 4, n, width), LOW),
            ((layers, count, self.inner), LOW),
            ((layers, count, self.inner), LOW),
            ((layers, n, width), WIDE),
        ]


def forward(z, features, cot_turned, kernel_weight, small, head_weight, ends_own, hidden_bias, joint_weight, expand_weight, output_weight, reduce_weight):
    kept = z.saved()
    kinds = len(kept)
    layers, n, width, part, inner, share = z.layers, z.n, z.width, z.part, z.inner, z.share
    count, head, heads, packs, gw = z.count, z.head, z.heads, z.packs, z.group_width
    depth, own_width = PACK * gw, PACK * share

    def kernel(*refs):
        (f_ref, cot_ref, k_ref, small_ref, head_ref, e_ref, hb_ref, jw_ref, ew_ref, ow_ref, rw_ref) = refs[:11]
        rest = refs[11:]
        (logits_ref, flow_ref, part_ref, whole, mixed_ref, bend_ref, ends_ref) = rest[:7]
        even_out, odd_out, taps_out = rest[7:10]
        held = rest[10 : 10 + z.bundles]
        saved = rest[10 + z.bundles : 10 + z.bundles + kinds]
        rest = rest[10 + z.bundles + kinds :]
        (x_all, qkv, weights_low, context, residual, m_all, active, slope, outer) = rest[:kinds]
        (now, wj, wo, we, wr, hb, low_buf, got, gs, gr, ss, sr) = rest[kinds : kinds + 12]
        (bs, br, ws, ks, tokens, messages, feats, small_all, packed, wide, even, odd, taps, out_messages) = rest[kinds + 12 : kinds + 26]
        (pres, new_feats, cot, logits_own, cs, cr, rs, fs, lines_out) = rest[kinds + 26 : kinds + 35]
        (hidden_lines, gathering, message) = rest[kinds + 35 : kinds + 38]
        swap1, swap2, swap3 = (rest[kinds + 38 + 3 * k : kinds + 41 + 3 * k] for k in range(3))
        y, x, c, h, l = bits()
        t = y * 2 + x
        slot = c * 4 + h * 2 + l

        put_lanes(tokens, f_ref[...].astype(WIDE))
        for f in range(0, PACK, 2):
            for q in range(width // 128):
                pair = [tokens[q, pl.ds(f + k, packs, stride=PACK), :] for k in range(2)]
                for k in range(2):
                    messages[2 * q + k, :, f * gw : (f + 2) * gw] = jnp.concatenate(
                        [piece[:, k * gw : (k + 1) * gw] for piece in pair], axis=1
                    ).astype(LOW)
        def column_copies():
            copies = []
            for layer in range(layers):
                for number, mask in enumerate((0, X_BIT, Y_BIT, X_BIT | Y_BIT)):
                    place = place_of(mask)
                    user = place[0] * 2 + place[1]
                    lines = pl.ds(pl.multiple_of(t * share, share), share)
                    moved = [
                        (
                            0,
                            jw_ref.at[layer, :, pl.ds(pl.multiple_of(which * width + user * part, part), part)],
                            held[3 * layer].at[slot, lines, pl.ds(which * part, part)],
                        )
                        for which in range(3)
                    ]
                    moved.append(
                        (
                            1,
                            ew_ref.at[layer, :, pl.ds(pl.multiple_of(user * inner, inner), inner)],
                            held[3 * layer + 1].at[slot, lines],
                        )
                    )
                    for at, (kind, source, target) in enumerate(moved):
                        if mask == 0:
                            copy = pltpu.make_async_copy(source, target, cr.at[layer, at, 0])
                        else:
                            copy = remote(
                                source, target, cs.at[layer, at, number], cr.at[layer, at, number], flipped(mask)
                            )
                        copies.append((3 * layer + kind, mask, copy))
            return copies

        def row_copies():
            copies = []
            for layer in range(layers):
                reduce_held = held[3 * layer + 2].at[slot]
                moved = [
                    (2, rw_ref.at[layer], reduce_held.at[pl.ds(0, z.inner_share)]),
                    (2, hidden_lines.at[layer], reduce_held.at[pl.ds(z.inner_share, 16)]),
                ] + [
                    (
                        0,
                        ow_ref.at[layer, :, pl.ds(chunk * part, part)],
                        held[3 * layer].at[slot, pl.ds(chunk * share, share), pl.ds(3 * part, part)],
                    )
                    for chunk in range(4)
                ]
                for at, (kind, source, target) in enumerate(moved):
                    copies.append((3 * layer + kind, pltpu.make_async_copy(source, target, rs.at[layer, at])))
            return copies

        column_all, row_all = column_copies(), row_copies()
        greet_all()
        hidden_lines[...] = jnp.zeros_like(hidden_lines)
        for layer in range(layers):
            hidden_lines[layer, :, 0 : z.inner_share] = jnp.broadcast_to(
                hb_ref[layer : layer + 1, :].astype(WIDE), (16, z.inner_share)
            ).astype(LOW)
        for _, copy in row_all:
            copy.start()

        same = lax.broadcasted_iota(jnp.int32, (share, share), 0) == lax.broadcasted_iota(jnp.int32, (share, share), 1)
        unit = jnp.where(same, 1.0, 0.0).astype(LOW)
        lines_low = small_ref[...].astype(WIDE)
        gathering[...] = jnp.zeros_like(gathering)
        gathering[0 : z.vectors, 0:share] = lines_low[0 : z.vectors]
        gathering[z.vectors : z.at["heads"], 0:share] = dot_lt(head_ref[...], unit)
        gathering[z.at["heads"] : z.named, 0:share] = lines_low[z.vectors : z.vectors + 2 * layers]
        own_ends = e_ref[...]
        gathering[z.named : z.named + 1, 0:4] = lax.shift_right_logical(own_ends, 5).astype(WIDE)
        gathering[z.named : z.named + 1, 4:8] = lax.bitwise_and(own_ends, 31).astype(WIDE)
        per_line = 128 // share
        message_lines = gathering.shape[0] // per_line
        message[...] = jnp.concatenate(
            [gathering[pl.ds(k, message_lines, stride=per_line), :][:, 0:share] for k in range(per_line)], axis=1
        ).astype(LOW)
        position = jnp.concatenate([lines_low[z.vectors + 2 * layers : z.vectors + 2 * layers + 1]] * PACK, axis=1)

        jobs = [Spread(held[b], bs.at[b], br.at[b]) for b in range(z.bundles)]
        all_greeted()

        def launch(layer):
            for number, _, copy in column_all:
                if number // 3 == layer:
                    copy.start()

        to_owners = Swap(lambda *place: messages.at[index_of(*place) // 2], feats, *swap1)
        to_owners.start()
        vectors = Swap(lambda *place: message, small_all, *swap2)
        vectors.start()
        frames_move = Move([(f_ref, new_feats), (cot_ref, cot)], fs.at[0], fs.at[1])
        frames_move.start()
        for layer in range(layers):
            launch(layer)

        def own_ready(bundle):
            for number, mask, copy in column_all:
                if number == bundle:
                    if mask:
                        copy.wait_recv()
                        copy.wait_send()
                    else:
                        copy.wait()
            for number, copy in row_all:
                if number == bundle:
                    copy.wait()
            jobs[bundle].begin()


        def keep(source, target, sem):
            pltpu.make_async_copy(source, target, sem).start()

        span = z.taps * gw
        for step in range(z.steps):
            taps[step] = jnp.zeros((own_width, depth), LOW)
        for f in range(PACK):
            lines = slice(f * share, (f + 1) * share)
            shift = f * gw
            for step in range(z.steps):
                begin = max(step * depth - shift, 0)
                end = min((step + 1) * depth - shift, span)
                at = begin + shift - step * depth
                if begin < end:
                    taps[step, lines, at : at + end - begin] = k_ref[:, begin:end]
        keep(taps, taps_out, ks.at[kinds, 0])

        to_owners.arrived()
        own_ready(0)
        vectors.arrived()
        for at in range(DEVICES):
            place = pl.ds((at % 4) * packs * 8 + at // 4, packs, stride=8)
            for q in range(depth // 128):
                packed[q, place, :] = feats[at, :, q * 128 : (q + 1) * 128].astype(WIDE)
        line, lane = z.named * share // 128, z.named * share % 128
        encoded = jnp.concatenate(
            [small_all[4 * row, line : line + 1, :].astype(WIDE) for row in range(8)], axis=0
        )
        ends_ref[...] = encoded
        ends = [
            encoded[:, lane + k : lane + k + 1] * 32.0 + encoded[:, lane + 4 + k : lane + 5 + k]
            for k in range(4)
        ]
        bounds = bounds_of(ends, count)
        spread_ranks(wide, get_lanes(packed, depth), rank_lanes(bounds, count, gw), 64)
        fill_pair(wide, even, odd)
        keep(even, even_out, ks.at[kinds, 1])
        keep(odd, odd_out, ks.at[kinds + 1, 0])
        summed = jnp.zeros((z.length, own_width), WIDE)
        for step in range(z.steps):
            summed = summed + dot_rt(shifted(even, odd, step, z.length), taps[step])
        made = collect_ranks(summed, rank_lanes(bounds, count, share), count) + position
        put_lanes(packed, made)
        for at in range(DEVICES):
            place = pl.ds((at % 4) * packs * 8 + at // 4, packs, stride=8)
            for q in range(own_width // 128):
                out_messages[at, :, q * 128 : (q + 1) * 128] = packed[q, place, :].astype(LOW)
        to_frames = Swap(lambda *place: out_messages.at[turned_of(*place)], pres, *swap3)
        to_frames.start()
        jobs[0].forward()

        for q in range(width // 128):
            for k in range(per_line):
                cut = slice(k * share, (k + 1) * share)
                lines_out[q, pl.ds(k, message_lines, stride=per_line), :] = jnp.concatenate(
                    [small_all[at, :, cut].astype(WIDE) for at in range(4 * q, 4 * q + 4)], axis=1
                )
        whole[...] = get_lanes(lines_out, width)

        def vector(name, layer=0):
            at = z.at[name] + layer
            return whole[at : at + 1, :]

        heads_lines = whole[z.at["heads"] : z.at["heads"] + 2 * layers, pl.ds(pl.multiple_of(t * part, part), part)]
        mine = lax.broadcasted_iota(jnp.int32, (8, 1), 0) == h * 4 + l * 2 + c
        row_ends = [jnp.sum(jnp.where(mine, end, 0.0), axis=0, keepdims=True).astype(jnp.int32) for end in ends]
        across = lax.broadcasted_iota(jnp.int32, (1, count), 1)
        down = lax.broadcasted_iota(jnp.int32, (count, 1), 0)
        across = sum((across >= end).astype(jnp.int32) for end in row_ends)
        down = sum((down >= end).astype(jnp.int32) for end in row_ends)
        linked = down == across

        frames_move.done()
        to_frames.arrived()
        jobs[0].over_c()
        own_ready(1)
        own_ready(2)
        for f in range(PACK):
            cut = slice(f * share, (f + 1) * share)
            for q in range(width // 128):
                tokens[q, pl.ds(f, packs, stride=PACK), :] = jnp.concatenate(
                    [pres[at, :, cut].astype(WIDE) for at in range(4 * q, 4 * q + 4)], axis=1
                )
        made, bent = gelu_pair(get_lanes(tokens, width))
        bend_ref[...] = bent
        mixed = new_feats[...].astype(WIDE) + made
        mixed_ref[...] = mixed
        now[...] = normed(mixed, vector("entry"), vector("base"))

        for layer in range(layers):
            first, second, third = jobs[3 * layer : 3 * layer + 3]
            later = jobs[3 * layer + 3 : 3 * layer + 6]
            x_all[layer, t] = now[...].astype(LOW)

            def attend_ready(layer=layer, first=first):
                first.done()
                load_rows(held[3 * layer], wj, ws.at[0], share, 0, 3 * part)
                load_chunks(held[3 * layer], wo, ws.at[1], share, 3 * part, part)
                settle(wj, ws.at[0])

            def attend_use(j, layer=layer):
                lines = block_rows(j, n)
                made = dot(x_all[layer, j], wj[...])
                qkv[layer, lines, 0:part] = ((made[:, 0:part] + heads_lines[layer : layer + 1]) * z.scale).astype(LOW)
                qkv[layer, lines, part : 2 * part] = made[:, part : 2 * part].astype(LOW)
                qkv[layer, lines, 2 * part :] = (
                    made[:, 2 * part :] + heads_lines[layers + layer : layers + layer + 1]
                ).astype(LOW)

            group_gather(x_all.at[layer], t, gs, gr, attend_ready, attend_use)
            second.forward()
            if layer == 0:
                own_ready(3)
            keep(x_all.at[layer], saved[0].at[layer], ks.at[0, layer])
            keep(qkv.at[layer], saved[1].at[layer], ks.at[1, layer])
            for at in range(heads):
                queries = qkv[layer, :, at * head : (at + 1) * head]
                keys = qkv[layer, :, part + at * head : part + (at + 1) * head]
                values = qkv[layer, :, 2 * part + at * head : 2 * part + (at + 1) * head]
                scores = jnp.where(linked, dot_rt(queries, keys), masked_score)
                exponent = jnp.exp(scores - jnp.max(scores, axis=-1, keepdims=True))
                inverse = 1.0 / jnp.sum(exponent, axis=-1, keepdims=True)
                made = (exponent * inverse).astype(LOW)
                weights_low[layer, at * count : (at + 1) * count, :] = made
                context[layer, :, at * head : (at + 1) * head] = dot(made, values).astype(LOW)
            keep(weights_low.at[layer], saved[2].at[layer], ks.at[2, layer])
            keep(context.at[layer], saved[3].at[layer], ks.at[3, layer])
            settle(wo, ws.at[1])

            def advance(second=second, third=third):
                second.over_c()
                third.forward()

            attended = group_scatter(
                lambda j: dot(context[layer, block_rows(j, n), :], wo[...]), t, low_buf, got, ss, sr, advance
            )
            third.over_c()
            residual[layer] = now[...] + (attended + vector("attend", layer))
            keep(residual.at[layer], saved[4].at[layer], ks.at[4, layer])
            middle = normed(residual[layer], vector("middle", layer), vector("lower", layer))
            now[...] = middle
            m_all[layer, t] = middle.astype(LOW)

            def feed_ready(layer=layer, second=second, third=third):
                second.done()
                load_rows(held[3 * layer + 1], we, ws.at[2], share, 0, inner)
                third.done()
                load_line(held[3 * layer + 2], hb, ws.at[4], z.inner_share, z.inner_share)
                load_blocks(held[3 * layer + 2], wr, ws.at[3], 0, z.inner_share)
                settle(we, ws.at[2])
                settle(hb, ws.at[4])

            def feed_use(j, layer=layer):
                lines = block_rows(j, n)
                made, bent = gelu_pair(dot(m_all[layer, j], we[...]) + hb[0:1, :].astype(WIDE))
                active[layer, lines, :] = made.astype(LOW)
                slope[layer, lines, :] = bent.astype(LOW)

            group_gather(m_all.at[layer], t, gs, gr, feed_ready, feed_use)
            if later:
                later[0].forward()
                own_ready(4)
                own_ready(5)
            keep(m_all.at[layer], saved[5].at[layer], ks.at[5, layer])
            keep(active.at[layer], saved[6].at[layer], ks.at[6, layer])
            keep(slope.at[layer], saved[7].at[layer], ks.at[7, layer])
            settle(wr, ws.at[3])

            def advance_more(later=later):
                if later:
                    later[0].over_c()

            fed = group_scatter(
                lambda j: dot(active[layer, block_rows(j, n), :], wr[...]), t, low_buf, got, ss, sr, advance_more
            )
            outer[layer] = now[...] + fed + vector("return", layer)
            keep(outer.at[layer], saved[8].at[layer], ks.at[8, layer])
            now[...] = normed(outer[layer], vector("final", layer), vector("upper", layer))
        final_low = now[...].astype(LOW)
        head_turned = whole[z.at["head"] : z.at["head"] + z.vocab, :].astype(LOW)
        vocab_at = z.vectors + 2 * layers + 1
        vocab_bias = lines_low[vocab_at : vocab_at + 1, :].astype(LOW)
        logits_own[...] = dot_rt(head_turned, final_low) + dot_lt(vocab_bias, jnp.ones((1, n), LOW))
        logits_move = Move([(logits_own, logits_ref)], fs.at[2], fs.at[3])
        logits_move.start()
        flow_ref[...] = dot_lt(cot[...], head_turned)
        part_ref[...] = dot(cot[...], final_low).astype(LOW)
        vocab_sum = dot_rt(jnp.ones((8, n), LOW), cot[...])
        vocab_sum = jnp.concatenate([vocab_sum] * (128 // z.vocab), axis=1)
        whole[z.line : z.line + 8, :] = jnp.concatenate([vocab_sum] * (width // 128), axis=1)
        logits_move.done()
        to_owners.sent()
        vectors.sent()
        to_frames.sent()
        for kind in range(kinds):
            for layer in range(layers):
                settle(saved[kind].at[layer], ks.at[kind, layer])
        settle(taps_out, ks.at[kinds, 0])
        settle(even_out, ks.at[kinds, 1])
        settle(odd_out, ks.at[kinds + 1, 0])

    outs = pl.pallas_call(
        kernel,
        out_shape=[
            jax.ShapeDtypeStruct((z.vocab, n), WIDE),
            jax.ShapeDtypeStruct((n, width), WIDE),
            jax.ShapeDtypeStruct((z.vocab, width), LOW),
            jax.ShapeDtypeStruct((z.gathered, width), WIDE),
            jax.ShapeDtypeStruct((n, width), WIDE),
            jax.ShapeDtypeStruct((n, width), WIDE),
            jax.ShapeDtypeStruct((8, 128), WIDE),
            jax.ShapeDtypeStruct((z.lines, depth), LOW),
            jax.ShapeDtypeStruct((z.lines, depth), LOW),
            jax.ShapeDtypeStruct((z.steps, own_width, depth), LOW),
        ]
        + [jax.ShapeDtypeStruct((PIECES, z.held_rows[b % 3], width), LOW) for b in range(z.bundles)]
        + [jax.ShapeDtypeStruct(shape, kind) for shape, kind in kept],
        in_specs=[IN_VMEM] * 11,
        out_specs=[IN_VMEM] * 7 + [ANYWHERE] * (3 + z.bundles + kinds),
        scratch_shapes=[pltpu.VMEM(shape, kind) for shape, kind in kept]
        + [
            pltpu.VMEM((n, width), WIDE),
            pltpu.VMEM((width, 3 * part), LOW),
            pltpu.VMEM((part, width), LOW),
            pltpu.VMEM((width, inner), LOW),
            pltpu.VMEM((inner, width), LOW),
            pltpu.VMEM((16, inner), LOW),
        ]
        + group_scratch(n, width)
        + [
            pltpu.SemaphoreType.DMA((z.bundles, 4)),
            pltpu.SemaphoreType.DMA((z.bundles, 4)),
            pltpu.SemaphoreType.DMA((5,)),
            pltpu.SemaphoreType.DMA((kinds + 2, layers)),
            pltpu.VMEM((width // 128, n, 128), WIDE),
            pltpu.VMEM((CONV_G, packs, depth), LOW),
            pltpu.VMEM((DEVICES, packs, depth), LOW),
            pltpu.VMEM((DEVICES, z.gathered * share // 128, 128), LOW),
            pltpu.VMEM((depth // 128, count, 128), WIDE),
            pltpu.VMEM((z.lines + 16, depth), WIDE),
            pltpu.VMEM((z.lines, depth), LOW),
            pltpu.VMEM((z.lines, depth), LOW),
            pltpu.VMEM((z.steps, own_width, depth), LOW),
            pltpu.VMEM((DEVICES, packs, own_width), LOW),
            pltpu.VMEM((DEVICES, packs, own_width), LOW),
            pltpu.VMEM((n, width), LOW),
            pltpu.VMEM((z.vocab, n), LOW),
            pltpu.VMEM((z.vocab, n), WIDE),
            pltpu.SemaphoreType.DMA((layers, 4, 4)),
            pltpu.SemaphoreType.DMA((layers, 4, 4)),
            pltpu.SemaphoreType.DMA((layers, 6)),
            pltpu.SemaphoreType.DMA((4, 2)),
            pltpu.VMEM((width // 128, z.gathered, 128), WIDE),
            pltpu.VMEM((layers, 16, width), LOW),
            pltpu.VMEM((z.gathered, 128), WIDE),
            pltpu.VMEM((z.gathered * share // 128, 128), LOW),
        ]
        + swap_sems() * 3,
        compiler_params=kernel_params(1),
        cost_estimate=cost(200),
    )(features, cot_turned, kernel_weight, small, head_weight, ends_own, hidden_bias, joint_weight, expand_weight, output_weight, reduce_weight)
    return outs[:7], outs[7:10], outs[10 : 10 + z.bundles], outs[10 + z.bundles :]


def backward(z, flow, head_sums, whole, mixed, bend, ends, even, odd, taps, held, saved):
    kinds = len(saved)
    layers, n, width, part, inner, share = z.layers, z.n, z.width, z.part, z.inner, z.share
    count, head, heads, packs, gw = z.count, z.head, z.heads, z.packs, z.group_width
    depth, own_width = PACK * gw, PACK * share
    bundles = z.bundles
    row_counts = [z.grad_rows[b % 3] for b in range(bundles)]
    lines = 8 * (-(-(3 + 6 * layers) // 8))
    tap_places = [(half, row, cut) for half in range(2) for row in range(4) for cut in range(2)]

    def kernel(*refs):
        flow_ref, head_ref, whole_ref, mixed_ref, bend_ref, ends_ref = refs[:6]
        even_ref, odd_ref, taps_ref = refs[6:9]
        held_refs = refs[9 : 9 + bundles]
        saved_refs = refs[9 + bundles : 9 + bundles + kinds]
        rest = refs[9 + bundles + kinds :]
        feats_ref, kernel_ref, position_ref, sums_ref, heads_ref = rest[:5]
        joint_ref, expand_ref, reduce_ref, output_ref, small_ref = rest[5:10]
        rest = rest[10:]
        parts = rest[:bundles]
        got_c, got_l, got_h = (rest[k * bundles : (k + 1) * bundles] for k in range(1, 4))
        rest = rest[4 * bundles :]
        buffers = rest[:kinds]
        (x_all, qkv, weights_low, context, residual, m_all, active, slope, outer) = buffers
        rest = rest[kinds:]
        inner_low = slope
        (fed, grad_low, joint, wj, wo, we, wr, low_buf, got, gs, gr, ss, sr) = rest[:13]
        rest = rest[13:]
        (rs_s, rs_r, ws, ks, back, vector_sums, all_sums, all_heads, tokens, out_low, low_parts) = rest[:11]
        (wide, grads_even, grads_odd, collected, out_feats, feat_parts) = rest[11:17]
        even, odd = weights_low.at[pl.ds(0, z.lines)], weights_low.at[pl.ds(2 * count, z.lines)]
        (own_back, columns, joint_low, expand_low, fs, cs, cr) = rest[17:24]
        swaps = [rest[24 + 3 * k : 27 + 3 * k] for k in range(4)]
        y, x, c, h, l = bits()
        t = y * 2 + x

        def fetch(kind, layer):
            pltpu.make_async_copy(saved_refs[kind].at[layer], buffers[kind], ks.at[kind]).start()

        def need(kind):
            settle(buffers[kind], ks.at[kind])

        def load_feed(layer):
            fetch(8, layer)
            load_blocks(held_refs[3 * layer + 2], wr, ws.at[3], 0, z.inner_share)
            fetch(7, layer)
            load_rows(held_refs[3 * layer + 1], we, ws.at[2], share, 0, inner)
            for kind in (6, 5, 4):
                fetch(kind, layer)

        def load_attend(layer):
            load_chunks(held_refs[3 * layer], wo, ws.at[1], share, 3 * part, part)
            for kind in (1, 2, 3, 0):
                fetch(kind, layer)
            load_rows(held_refs[3 * layer], wj, ws.at[0], share, 0, 3 * part)

        def vector(name, layer=0):
            at = z.at[name] + layer
            return whole_ref[at : at + 1, :]

        def lanes_for(source):
            def block_for(*place):
                cut = pl.multiple_of(index_of(*place) * share // 128 * 128, 128)
                return source.at[:, pl.ds(cut, 128)]

            return block_for

        greet_all()
        load_feed(layers - 1)
        load_attend(layers - 1)
        all_greeted()
        heads_swap = Swap(lanes_for(head_ref), all_heads, *swaps[0])
        heads_swap.start()
        jobs = [
            Gather(parts[b], got_c[b], got_l[b], got_h[b], rs_s.at[b], rs_r.at[b]) for b in range(bundles)
        ]

        def column_copies(bundle):
            layer, kind = bundle // 3, bundle % 3
            copies = []
            for number, mask in enumerate((0, X_BIT, Y_BIT, X_BIT | Y_BIT)):
                place = place_of(mask)
                owner = place[0] * 2 + place[1]
                lines = pl.ds(pl.multiple_of(owner * share, share), share)
                if kind == 0:
                    moved = [
                        (
                            columns.at[layer, lines, pl.ds(which * part, part)],
                            joint_low.at[layer, :, pl.ds(pl.multiple_of(which * width + t * part, part), part)],
                        )
                        for which in range(3)
                    ]
                else:
                    moved = [
                        (
                            columns.at[layer, lines, pl.ds(3 * part, inner)],
                            expand_low.at[layer, :, pl.ds(pl.multiple_of(t * inner, inner), inner)],
                        )
                    ]
                for at, (source, target) in enumerate(moved):
                    at += 3 * kind
                    if mask == 0:
                        copies.append(pltpu.make_async_copy(source, target, cr.at[layer, at, 0]))
                    else:
                        copies.append(
                            remote(source, target, cs.at[layer, at, number], cr.at[layer, at, number], flipped(mask))
                        )
            return copies

        def hand_over(bundle):
            layer, kind = bundle // 3, bundle % 3
            jobs[bundle].done()
            if kind == 0:
                total = jobs[bundle].total(0, 4 * share)
                columns[layer, :, 0 : 3 * part] = total[:, : 3 * part].astype(LOW)
                for chunk in range(4):
                    output_ref[layer, :, chunk * part : (chunk + 1) * part] = total[
                        chunk * share : (chunk + 1) * share, 3 * part :
                    ]
                small_ref[layer] = jobs[bundle].total(4 * share, 4 * share + 16)[:, 0:128]
            elif kind == 1:
                columns[layer, :, 3 * part :] = jobs[bundle].total(0, 4 * share).astype(LOW)
            else:
                end = z.inner_share
                reduce_ref[layer] = jobs[bundle].total(0, end)
                sums_ref[8 * layer : 8 * layer + 8, :] = jobs[bundle].total(end, end + 16)[0:8, 0:128]
                return
            for copy in column_copies(bundle):
                copy.start()

        back[...] = flow_ref[...]
        vector_sums[...] = jnp.zeros_like(vector_sums)
        vector_sums[2 + 6 * layers : 3 + 6 * layers, :] = whole_ref[z.line : z.line + 1, :]

        for layer in reversed(range(layers)):
            last = layer == layers - 1
            attend_job, expand_job, reduce_job = jobs[3 * layer : 3 * layer + 3]
            after = 3 * layer + 3

            def note(name, value, layer=layer):
                at = z.at[name] + layer
                vector_sums[at : at + 1, :] = value

            need(8)
            outer_grad, final_part, upper_part = normed_back(outer[...], vector("final", layer), back[...])
            back[...] = outer_grad
            fed_low = outer_grad.astype(LOW)
            fed[0, t] = fed_low
            note("final", final_part)
            note("upper", upper_part)
            note("return", jnp.sum(fed_low.astype(WIDE), axis=0, keepdims=True))

            def feed_ready():
                settle(wr, ws.at[3])
                need(7)

            def feed_use(j):
                lines = block_rows(j, n)
                made = dot_rt(fed[0, j], wr[...]) * slope[lines, :].astype(WIDE)
                inner_low[lines, :] = made.astype(LOW)

            group_gather(fed.at[0], t, gs, gr, feed_ready, feed_use)
            if not last:
                jobs[after + 2].over_h()
            settle(we, ws.at[2])
            need(6)
            need(5)

            def feed_weights(after=after, last=last, expand_job=expand_job, reduce_job=reduce_job):
                store_rows(expand_job.parts, dot_lt(m_all[...].reshape(count, width), inner_low[...]), share, 0)
                expand_job.over_c()
                target = reduce_job.parts
                store_blocks(target, dot_lt(active[...], fed[0].reshape(count, width)), 0, z.inner_share)
                hidden_sum = jnp.sum(inner_low[...].astype(WIDE), axis=0, keepdims=True)
                first = z.inner_share
                for slot, place in enumerate(slots()):
                    at = slot * z.inner_share
                    view = relative(target, *place)
                    view[first : first + 16, :] = jnp.zeros((16, width), LOW)
                    view[first : first + 16, 0 : z.inner_share] = jnp.broadcast_to(
                        hidden_sum[:, at : at + z.inner_share], (16, z.inner_share)
                    ).astype(LOW)
                reduce_job.over_c()
                if not last:
                    hand_over(after + 1)

            got_back = group_scatter(
                lambda j: dot_rt(inner_low[block_rows(j, n), :], we[...]), t, low_buf, got, ss, sr, feed_weights
            )
            if not last:
                jobs[after].over_h()
            expand_job.over_l()
            reduce_job.over_l()
            need(4)
            res_grad, middle_part, lower_part = normed_back(
                residual[...], vector("middle", layer), back[...] + got_back
            )
            back[...] = res_grad
            note("middle", middle_part)
            note("lower", lower_part)
            if layer:
                load_feed(layer - 1)
            else:
                for step in range(z.steps - 1):
                    half, row, cut = tap_places[step]
                    target = (we, wr)[half].at[pl.ds(row * own_width, own_width), pl.ds(cut * depth, depth)]
                    pltpu.make_async_copy(taps_ref.at[step], target, ws.at[2 + half]).start()
            own_low = res_grad.astype(LOW)
            fed[1, t] = own_low
            note("attend", jnp.sum(own_low.astype(WIDE), axis=0, keepdims=True))

            def attend_ready():
                settle(wo, ws.at[1])

            def attend_use(j):
                grad_low[block_rows(j, n), :] = dot_rt(fed[1, j], wo[...]).astype(LOW)

            group_gather(fed.at[1], t, gs, gr, attend_ready, attend_use)
            if not last:
                hand_over(after + 2)
            if layer == 0:
                pltpu.make_async_copy(
                    taps_ref.at[z.steps - 1], wo.at[pl.ds(0, own_width), pl.ds(0, depth)], ws.at[1]
                ).start()
            for kind in (1, 2, 3):
                need(kind)
            for at in range(heads):
                mine = slice(at * head, (at + 1) * head)
                queries = qkv[:, mine]
                keys = qkv[:, part + at * head : part + (at + 1) * head]
                values = qkv[:, 2 * part + at * head : 2 * part + (at + 1) * head]
                weights = weights_low[at * count : (at + 1) * count, :]
                grads = grad_low[:, mine]
                weights_wide = weights.astype(WIDE)
                prob_grad = dot_rt(grads, values)
                delta = jnp.sum(weights_wide * prob_grad, axis=-1, keepdims=True)
                score_grad = (weights_wide * (prob_grad - delta)).astype(LOW)
                joint[:, mine] = (dot(score_grad, keys).astype(LOW).astype(WIDE) * z.scale).astype(LOW)
                joint[:, part + at * head : part + (at + 1) * head] = dot_lt(score_grad, queries).astype(LOW)
                joint[:, 2 * part + at * head : 2 * part + (at + 1) * head] = dot_lt(weights, grads).astype(LOW)
            if layer == 0:
                pltpu.make_async_copy(even_ref, even, ks.at[kinds]).start()
                pltpu.make_async_copy(odd_ref, odd, ks.at[kinds + 1]).start()
            settle(wj, ws.at[0])
            need(0)

            def attend_weights(attend_job=attend_job, expand_job=expand_job):
                target = attend_job.parts
                store_rows(target, dot_lt(x_all[...].reshape(count, width), joint[...]), share, 0)
                store_chunks(target, dot_lt(context[...], fed[1].reshape(count, width)), share, 3 * part)
                joint_sum = jnp.sum(joint[...].astype(WIDE), axis=0, keepdims=True)
                for slot, place in enumerate(slots()):
                    at = slot * share
                    view = relative(target, *place)
                    line = jnp.concatenate(
                        [
                            joint_sum[:, at : at + share],
                            joint_sum[:, 2 * part + at : 2 * part + at + share],
                            jnp.zeros((1, 128 - 2 * share), WIDE),
                        ],
                        axis=1,
                    )
                    view[4 * share : 4 * share + 16, :] = jnp.zeros((16, width), LOW)
                    view[4 * share : 4 * share + 16, 0:128] = jnp.broadcast_to(line, (16, 128)).astype(LOW)
                attend_job.over_c()
                expand_job.over_h()

            got_back = group_scatter(
                lambda j: dot_rt(joint[block_rows(j, n), :], wj[...]), t, low_buf, got, ss, sr, attend_weights
            )
            attend_job.over_l()
            back[...] = back[...] + got_back
            if layer:
                load_attend(layer - 1)

        mixed_grad, entry_part, base_part = normed_back(mixed_ref[...], vector("entry"), back[...])
        vector_sums[z.at["entry"] : z.at["entry"] + 1, :] = entry_part
        vector_sums[z.at["base"] : z.at["base"] + 1, :] = base_part
        m_all[0] = mixed_grad.astype(LOW)
        put_lanes(tokens, mixed_grad * bend_ref[...])
        for f in range(0, PACK, 4):
            for q in range(width // 128):
                four = [tokens[q, pl.ds(f + k, packs, stride=PACK), :] for k in range(4)]
                for k in range(4):
                    out_low[4 * q + k, :, f * share : (f + 4) * share] = jnp.concatenate(
                        [piece[:, k * share : (k + 1) * share] for piece in four], axis=1
                    ).astype(LOW)
        low_swap = Swap(lambda *place: out_low.at[index_of(*place)], low_parts, *swaps[1])
        low_swap.start()
        sums_swap = Swap(lanes_for(vector_sums), all_sums, *swaps[2])
        mixed_move = Move([(m_all.at[0], own_back)], fs.at[0], fs.at[1])
        encoded = ends_ref[...]
        lane = z.named * share % 128
        bounds = bounds_of(
            [
                encoded[:, lane + k : lane + k + 1] * 32.0 + encoded[:, lane + 4 + k : lane + 5 + k]
                for k in range(4)
            ],
            count,
        )
        pltpu.make_async_copy(even, even, ks.at[kinds]).wait()
        pltpu.make_async_copy(odd, odd, ks.at[kinds + 1]).wait()
        settle(we, ws.at[2])
        settle(wr, ws.at[3])
        settle(wo.at[pl.ds(0, own_width), pl.ds(0, depth)], ws.at[1])
        jobs[2].over_h()
        hand_over(3)
        low_swap.arrived()
        sums_swap.start()
        mixed_move.start()
        for at, (y_at, x_at, c_at, h_at, l_at) in enumerate(itertools.product((0, 1), repeat=5)):
            row, block = h_at * 4 + l_at * 2 + c_at, y_at * 2 + x_at
            place = pl.ds(block * packs * 8 + row, packs, stride=8)
            for q in range(own_width // 128):
                collected[q, place, :] = low_parts[at, :, q * 128 : (q + 1) * 128].astype(WIDE)
        packed = get_lanes(collected, own_width)
        position_ref[...] = jnp.sum(packed, axis=0, keepdims=True)
        spread_ranks(wide, packed, rank_lanes(bounds, count, share), 64)
        fill_pair(wide, grads_even, grads_odd)
        across = wide[64 : 64 + z.length, :].T.astype(LOW)

        def taps_at(step):
            if step == z.steps - 1:
                return wo[0:own_width, 0:depth]
            half, row, cut = tap_places[step]
            return (we, wr)[half][row * own_width : (row + 1) * own_width, cut * depth : (cut + 1) * depth]

        summed = jnp.zeros((z.length, depth), WIDE)
        for step in range(z.steps):
            summed = summed + dot(shifted(grads_even, grads_odd, step, z.length), taps_at(z.steps - 1 - step))
            if step == z.steps // 2:
                jobs[0].over_h()
        put_lanes(collected, collect_ranks(summed, rank_lanes(bounds, count, gw), count))
        for at in range(DEVICES):
            place = pl.ds((at % 4) * packs * 8 + at // 4, packs, stride=8)
            for q in range(depth // 128):
                out_feats[at, :, q * 128 : (q + 1) * 128] = collected[q, place, :].astype(LOW)
        feats_swap = Swap(lambda *place: out_feats.at[index_of(*place)], feat_parts, *swaps[3])
        feats_swap.start()
        hand_over(1)

        kernel_ref[...] = jnp.zeros_like(kernel_ref)
        for step in range(z.steps):
            made = dot(across, shifted(even, odd, step, z.length))
            for f in range(PACK):
                begin = (step + 1) * depth - f * gw
                kernel_ref[:, begin : begin + depth] += made[f * share : (f + 1) * share, :]
        hand_over(2)
        hand_over(0)

        sums_swap.arrived()
        sums_ref[8 * layers :, :] = jnp.sum(all_sums[...], axis=0)
        heads_swap.arrived()
        heads_ref[...] = jnp.sum(all_heads[...].astype(WIDE), axis=0)
        feats_swap.arrived()
        for f in range(PACK):
            cut = slice(f * gw, (f + 1) * gw)
            for q in range(width // 128):
                tokens[q, pl.ds(f, packs, stride=PACK), :] = jnp.concatenate(
                    [
                        feat_parts[at, :, cut].astype(WIDE) + feat_parts[at + 1, :, cut].astype(WIDE)
                        for at in (4 * q, 4 * q + 2)
                    ],
                    axis=1,
                )
        mixed_move.done()
        feats_ref[...] = get_lanes(tokens, width) + own_back[...].astype(WIDE)
        for bundle in (4, 3, 1, 0):
            for copy in column_copies(bundle):
                copy.wait()
            layer, kind = bundle // 3, bundle % 3
            if kind == 0:
                joint_ref[layer] = joint_low[layer].astype(WIDE)
            else:
                expand_ref[layer] = expand_low[layer].astype(WIDE)
        for swap in (heads_swap, low_swap, sums_swap, feats_swap):
            swap.sent()

    return pl.pallas_call(
        kernel,
        out_shape=[
            jax.ShapeDtypeStruct((n, width), WIDE),
            jax.ShapeDtypeStruct((share, (z.steps + 1) * depth), WIDE),
            jax.ShapeDtypeStruct((1, own_width), WIDE),
            jax.ShapeDtypeStruct((8 * layers + lines, 128), WIDE),
            jax.ShapeDtypeStruct((z.vocab, 128), WIDE),
            jax.ShapeDtypeStruct((layers, share, 3 * width), WIDE),
            jax.ShapeDtypeStruct((layers, share, 4 * inner), WIDE),
            jax.ShapeDtypeStruct((layers, z.inner_share, width), WIDE),
            jax.ShapeDtypeStruct((layers, share, width), WIDE),
            jax.ShapeDtypeStruct((layers, 16, 128), WIDE),
        ],
        in_specs=[IN_VMEM] * 6 + [ANYWHERE] * (3 + bundles + kinds),
        out_specs=[IN_VMEM] * 10,
        scratch_shapes=[pltpu.VMEM((2, 2, 2, rows, width), LOW) for rows in row_counts]
        + [pltpu.VMEM((2, 2, rows, width), LOW) for rows in row_counts]
        + [pltpu.VMEM((2, rows, width), LOW) for rows in row_counts]
        + [pltpu.VMEM((rows, width), LOW) for rows in row_counts]
        + [pltpu.VMEM(array.shape[1:], array.dtype) for array in saved]
        + [
            pltpu.VMEM((2, 4, n, width), LOW),
            pltpu.VMEM((count, part), LOW),
            pltpu.VMEM((count, 3 * part), LOW),
            pltpu.VMEM((width, 3 * part), LOW),
            pltpu.VMEM((part, width), LOW),
            pltpu.VMEM((width, inner), LOW),
            pltpu.VMEM((inner, width), LOW),
        ]
        + group_scratch(n, width)
        + [
            pltpu.SemaphoreType.DMA((bundles, 3)),
            pltpu.SemaphoreType.DMA((bundles, 3)),
            pltpu.SemaphoreType.DMA((4,)),
            pltpu.SemaphoreType.DMA((kinds + 2,)),
            pltpu.VMEM((n, width), WIDE),
            pltpu.VMEM((lines, width), WIDE),
            pltpu.VMEM((DEVICES, lines, 128), WIDE),
            pltpu.VMEM((DEVICES, z.vocab, 128), LOW),
            pltpu.VMEM((width // 128, n, 128), WIDE),
            pltpu.VMEM((DEVICES, packs, own_width), LOW),
            pltpu.VMEM((DEVICES, packs, own_width), LOW),
            pltpu.VMEM((z.lines + 16, own_width), WIDE),
            pltpu.VMEM((z.lines, own_width), LOW),
            pltpu.VMEM((z.lines, own_width), LOW),
            pltpu.VMEM((depth // 128, count, 128), WIDE),
            pltpu.VMEM((DEVICES, packs, depth), LOW),
            pltpu.VMEM((DEVICES, packs, depth), LOW),
            pltpu.VMEM((n, width), LOW),
            pltpu.VMEM((layers, 4 * share, 3 * part + inner), LOW),
            pltpu.VMEM((layers, share, 3 * width), LOW),
            pltpu.VMEM((layers, share, 4 * inner), LOW),
            pltpu.SemaphoreType.DMA((2, 1)),
            pltpu.SemaphoreType.DMA((layers, 4, 4)),
            pltpu.SemaphoreType.DMA((layers, 4, 4)),
        ]
        + swap_sems() * 4,
        compiler_params=kernel_params(2),
        cost_estimate=cost(220),
    )(flow, head_sums, whole, mixed, bend, ends, even, odd, taps, *held, *saved)


def finish(z, arrays, position_part, sums, heads_sums, small_own):
    layers, share, span = z.layers, z.share, z.taps * z.group_width
    count = len(arrays)
    names = ("attend", "middle", "lower", "return", "final", "upper")

    def kernel(*refs):
        sources, (position_ref, sums_ref, heads_ref, small_ref) = refs[:count], refs[count : count + 4]
        targets = refs[count + 4 : 2 * count + 4]
        line_refs, pair_refs = refs[2 * count + 4 : 2 * count + 8], refs[2 * count + 8 : -1]
        head_ref = refs[-1]
        for at in range(count):
            if at == 0:
                targets[at][0] = sources[at][...]
            elif at == 1:
                targets[at][...] = sources[at][:, PACK * z.group_width : PACK * z.group_width + span]
            else:
                targets[at][...] = sources[at][...]
        _, _, _, h, l = bits()

        def own(value):
            result = value[:, 0:share]
            for at in range(1, 4):
                result = jnp.where(h * 2 + l == at, value[:, at * share : (at + 1) * share], result)
            return result

        mine = own(sums_ref[8 * layers :, :])
        total = position_ref[:, 0:share]
        for f in range(1, PACK):
            total = total + position_ref[:, f * share : (f + 1) * share]
        line_refs[0][...] = total
        for number, at in enumerate((z.at["entry"], z.at["base"], z.vectors)):
            line_refs[1 + number][...] = mine[at : at + 1]
        for layer in range(layers):
            here = slice(layer, layer + 1)
            pair_refs[0][here, :] = small_ref[layer, 0:1, 0:share]
            pair_refs[1][here, :] = small_ref[layer, 0:1, share : 2 * share]
            for number, name in enumerate(names):
                at = z.at[name] + layer
                pair_refs[2 + number][here, :] = mine[at : at + 1]
            pair_refs[-1][here, :] = sums_ref[8 * layer : 8 * layer + 1, 0 : z.inner_share]
        head_ref[...] = own(heads_ref[...])

    shapes = [array.shape for array in arrays]
    shapes[0] = (1,) + shapes[0]
    shapes[1] = (share, span)
    outs = pl.pallas_call(
        kernel,
        out_shape=[jax.ShapeDtypeStruct(shape, WIDE) for shape in shapes]
        + [
            jax.ShapeDtypeStruct(shape, WIDE)
            for shape in [(1, share)] * 4
            + [(layers, share)] * (2 + len(names))
            + [(layers, z.inner_share), (z.vocab, share)]
        ],
        in_specs=[IN_VMEM] * (count + 4),
        out_specs=[IN_VMEM] * (count + 8 + len(names)),
        compiler_params=pltpu.CompilerParams(vmem_limit_bytes=62 * 2**20),
        cost_estimate=cost(5),
    )(*arrays, position_part, sums, heads_sums, small_own)
    lines = [line.reshape(share) for line in outs[count : count + 4]]
    return *outs[:count], lines, outs[count + 4 : -1], outs[-1].T


def fast_local(*arguments):
    (
        features,
        utterance_ends,
        kernel_weight,
        position_bias,
        entry_gain,
        base_shift,
        joint_weight,
        query_bias,
        value_bias,
        output_weight,
        attend_bias,
        middle_gain,
        lower_shift,
        expand_weight,
        hidden_bias,
        reduce_weight,
        return_bias,
        final_gain,
        upper_shift,
        head_weight,
        vocab_bias,
        cotangent,
    ) = arguments
    _, n, width = features.shape
    layers, inner_all = joint_weight.shape[0], expand_weight.shape[2]
    vocab = head_weight.shape[1]
    taps = kernel_weight.shape[1] // (width // CONV_G)
    z = Sizes(n, width, inner_all // 4, layers, taps, vocab)

    small = jnp.concatenate(
        [entry_gain[None], base_shift[None], attend_bias, middle_gain, lower_shift]
        + [return_bias, final_gain, upper_shift, query_bias, value_bias]
        + [position_bias[None], vocab_bias[None]],
        axis=0,
    )
    firsts, conv_saved, held, saved = forward(
        z,
        features[0],
        cotangent[0].T,
        kernel_weight,
        small,
        head_weight,
        utterance_ends,
        hidden_bias,
        joint_weight,
        expand_weight,
        output_weight,
        reduce_weight,
    )
    logits, flow, head_sums, whole, mixed, bend, ends = firsts
    (
        features_grad,
        kernel_wide,
        position_part,
        sums,
        heads_sums,
        joint_own,
        expand_own,
        reduce_own,
        output_own,
        small_own,
    ) = backward(z, flow, head_sums, whole, mixed, bend, ends, *conv_saved, held, saved)
    (
        features_grad,
        kernel_own,
        joint_own,
        expand_own,
        reduce_own,
        output_own,
        lines,
        pairs,
        head_own,
    ) = finish(
        z,
        [features_grad, kernel_wide, joint_own, expand_own, reduce_own, output_own],
        position_part,
        sums,
        heads_sums,
        small_own,
    )
    return (
        logits.T[None],
        features_grad,
        kernel_own,
        lines[0],
        lines[1],
        lines[2],
        joint_own,
        pairs[0],
        pairs[1],
        output_own,
        pairs[2],
        pairs[3],
        pairs[4],
        expand_own,
        pairs[8],
        reduce_own,
        pairs[5],
        pairs[6],
        pairs[7],
        head_own,
        lines[3],
    )


def fits(dp_size, seq_size, width):
    share = width // 32
    return (
        dp_size == 8
        and seq_size == 4
        and share % 16 == 0
        and share * 2 == width // CONV_G
        and share * 2 == width // HEADS
    )


def placed(mesh, width):
    if fits(mesh.shape["dp"], mesh.shape["seq"], width):
        body = fast_local
        mesh = jax.sharding.Mesh(mesh.devices.reshape((2,) * len(AXES)), AXES)
        split, over, within = AXES[:3], AXES[3:], AXES
    else:
        body, split, over, within = local, "dp", "seq", ("dp", "seq")
    tokens = P(split, over, None)
    first, first_wide = P(within), P(within, None)
    second, second_wide = P(None, within), P(None, within, None)
    return jax.shard_map(
        body,
        mesh=mesh,
        in_specs=(
            tokens,
            P(split, None),
            first_wide,
            first,
            first,
            first,
            second_wide,
            second,
            second,
            second_wide,
            second,
            second,
            second,
            second_wide,
            second,
            second_wide,
            second,
            second,
            second,
            first_wide,
            P(),
            tokens,
        ),
        out_specs=(
            tokens,
            tokens,
            first_wide,
            first,
            first,
            first,
            second_wide,
            second,
            second,
            second_wide,
            second,
            second,
            second,
            second_wide,
            second,
            second_wide,
            second,
            second,
            second,
            first_wide,
            P(),
        ),
        check_vma=False,
    )


def solution(mesh):
    def whole(*arguments):
        return placed(mesh, arguments[0].shape[2])(*arguments)

    return whole
```
